128 devices in a mesh: ctx: 16 (over y, z_lo, core), mp: 8 (over x, z_hi).
Axes of the slice: x: 4, y: 4, z: 4 (z_hi: 2, z_lo: 2; z = z_hi * 2 + z_lo), core: 2. Of those that a mesh axis runs over, the one named last changes fastest.
Arguments:
- tokens: bfloat16 [8192, 2048], P('ctx'), may hold values from -6 to 6
- cotangent: bfloat16 [8192, 2048], P('ctx'), may hold values from -6 to 6
- gain_attn: float32 [2048], replicated, may hold values from 0.5 to 1.5
- w_query: bfloat16 [2048, 2048], P(None, 'mp'), may hold values from -0.125 to 0.125
- w_key: bfloat16 [2048, 2048], P(None, 'mp'), may hold values from -0.125 to 0.125
- w_value: bfloat16 [2048, 2048], P(None, 'mp'), may hold values from -0.125 to 0.125
- w_out: bfloat16 [2048, 2048], P('mp'), may hold values from -0.5 to 0.5
- gain_moe: float32 [2048], replicated, may hold values from 0.5 to 1.5
- w_router: bfloat16 [2048, 64], replicated, may hold values from -0.0625 to 0.0625
- shared_gate: bfloat16 [2048, 2816], P(None, 'mp'), may hold values from -0.125 to 0.125
- shared_up: bfloat16 [2048, 2816], P(None, 'mp'), may hold values from -0.125 to 0.125
- shared_down: bfloat16 [2816, 2048], P('mp'), may hold values from -0.109375 to 0.109375
- expert_gate: bfloat16 [3, 2048, 1408], P(None, None, 'mp'), may hold values from -0.125 to 0.125
- expert_up: bfloat16 [3, 2048, 1408], P(None, None, 'mp'), may hold values from -0.125 to 0.125
- expert_down: bfloat16 [3, 1408, 2048], P(None, 'mp'), may hold values from -6 to 6
- expert_ids: int32 [8192, 6], P('ctx'), may hold values from 0 to 63, as said below
- pair_order: int32 [16], replicated, may hold values from 0 to 15, each once
Outputs:
- output: bfloat16 [8192, 2048], P('ctx')
- grad_tokens: bfloat16 [8192, 2048], P('ctx')
- grad_gain_attn: float32 [2048], replicated
- grad_w_query: float32 [2048, 2048], P(None, 'mp')
- grad_w_key: float32 [2048, 2048], P(None, 'mp')
- grad_w_value: float32 [2048, 2048], P(None, 'mp')
- grad_w_out: float32 [2048, 2048], P('mp')
- grad_gain_moe: float32 [2048], replicated
- grad_w_router: float32 [2048, 64], replicated
- grad_shared_gate: float32 [2048, 2816], P(None, 'mp')
- grad_shared_up: float32 [2048, 2816], P(None, 'mp')
- grad_shared_down: float32 [2816, 2048], P('mp')
- grad_expert_gate: float32 [3, 2048, 1408], P(None, None, 'mp')
- grad_expert_up: float32 [3, 2048, 1408], P(None, None, 'mp')
- grad_expert_down: float32 [3, 1408, 2048], P(None, 'mp')
The draws below stay inside these ranges and needn't reach their ends.
Inputs may be any that keep to these rules, and one draw needn't show every extreme that they name: `expert_ids`: each row names 6 different experts. In the rows of one device (aligned blocks of 512 rows) each expert below 3 is named by at most 32 rows, and in every block one of them by exactly 32. A permutation: ctx device i holds blocks pair_order[i] and 31 - pair_order[i] of the sequence.
All inputs are finite; a program needn't handle non-finite values.
Results may differ from the reference program's by a relative error of at most 0.028.
Values may be sent and summed in bfloat16 or wider, within the bound.
A program may use at most 320 MiB of HBM per device.

```python
import jax
import jax.numpy as jnp
from jax import lax

D = 2048
HEADS = 16
HD = 128
FF = 1408
EXPERTS = 64
TOP = 6
E_HELD = 3
CAP = 32
TOK_DEV = 512
SH_FF = 2816
TOKENS = 8192
PAIRS = 16


def draw_expert_ids(key, part):
    key = jax.random.fold_in(key, 11)
    blocks = TOKENS // TOK_DEV
    key_count, key_full, key_pick, key_other = jax.random.split(key, 4)
    load_count = jax.random.randint(key_count, (blocks, E_HELD), CAP // 2, CAP + 1)
    busiest = jax.random.randint(key_full, (blocks, 1), 0, E_HELD)
    held_range = jnp.arange(E_HELD, dtype=jnp.int32)
    load_count = jnp.where(held_range[None, :] == busiest, CAP, load_count)
    pick_keys = jax.random.split(key_pick, blocks * E_HELD)
    ranking = jax.vmap(lambda sub_key: jax.random.permutation(sub_key, TOK_DEV))(pick_keys).reshape(blocks, E_HELD, TOK_DEV)
    picked = jnp.transpose(ranking < load_count[:, :, None], (0, 2, 1))
    held_score = jnp.where(picked, 2 ** 28 + held_range[None, None, :], -1 - held_range[None, None, :])
    others = jax.random.randint(key_other, (blocks, TOK_DEV, EXPERTS - E_HELD), 0, 2 ** 20) * EXPERTS + jnp.arange(E_HELD, EXPERTS, dtype=jnp.int32)[None, None, :]
    ranked = jnp.concatenate([held_score.astype(jnp.int32), others.astype(jnp.int32)], axis=-1)
    chosen = lax.top_k(ranked, TOP)[1]
    return chosen.reshape(TOKENS, TOP).astype(jnp.int32)


def level_of(stream_key, dims, shards, low, largest):
    level, own = 1.0, jax.random.fold_in(stream_key, 6)
    for axis_at, shards_of in shards:
        steps = jnp.exp(jax.random.uniform(jax.random.fold_in(own, axis_at), (shards_of,), jnp.float32, low / len(shards), largest / len(shards)))
        level = level * jnp.repeat(steps, dims[axis_at] // shards_of).reshape([-1 if axis == axis_at else 1 for axis in range(len(dims))])
    return level


def bell_draw(key, dims, spread, bound, cuts=(), kind=jnp.bfloat16):
    array = jax.random.normal(key, dims, jnp.float32) * spread
    if len(cuts) > 0:
        array = level_of(key, dims, cuts, -0.22, 0.18) * array
    return jnp.clip(array, min=-bound, max=bound).astype(kind)


def setup_inputs(seed: int = 0) -> dict:
    key_list = jax.random.split(jax.random.key(seed), 18)
    return {
        "tokens": bell_draw(key_list[0], (TOKENS, D), 1.0, 6.0, ((0, 16),)),
        "cotangent": bell_draw(key_list[1], (TOKENS, D), 1.0, 6.0, ((0, 16),)),
        "gain_attn": jnp.clip(1.0 + 0.1 * jax.random.normal(key_list[2], (D,), jnp.float32), 0.5, 1.5),
        "w_query": bell_draw(key_list[3], (D, HEADS * HD), D ** -0.5, 0.125, ((1, 8),)),
        "w_key": bell_draw(key_list[4], (D, HEADS * HD), D ** -0.5, 0.125, ((1, 8),)),
        "w_value": bell_draw(key_list[5], (D, HEADS * HD), D ** -0.5, 0.125, ((1, 8),)),
        "w_out": bell_draw(key_list[6], (HEADS * HD, D), (HEADS * HD // 16) ** -0.5, 0.5, ((0, 8),)),
        "gain_moe": jnp.clip(1.0 + 0.1 * jax.random.normal(key_list[7], (D,), jnp.float32), 0.5, 1.5),
        "w_router": bell_draw(key_list[8], (D, EXPERTS), (4 * D) ** -0.5, 0.0625),
        "shared_gate": bell_draw(key_list[9], (D, SH_FF), D ** -0.5, 0.125, ((1, 8),)),
        "shared_up": bell_draw(key_list[10], (D, SH_FF), D ** -0.5, 0.125, ((1, 8),)),
        "shared_down": bell_draw(key_list[11], (SH_FF, D), SH_FF ** -0.5, 0.109375, ((0, 8),)),
        "expert_gate": bell_draw(key_list[12], (E_HELD, D, FF), D ** -0.5, 0.125, ((2, 8),)),
        "expert_up": bell_draw(key_list[13], (E_HELD, D, FF), D ** -0.5, 0.125, ((2, 8),)),
        "expert_down": bell_draw(key_list[14], (E_HELD, FF, D), 1.0, 6.0, ((1, 8),)),
        "expert_ids": draw_expert_ids(jax.random.fold_in(key_list[17], 71), 0),
        "pair_order": jax.random.permutation(key_list[16], PAIRS).astype(jnp.int32),
    }


EPSILON = 1e-06
ROPE_BASE = 10000.0
PRECISE = lax.Precision.HIGHEST

@jax.custom_vjp
def low(v):
    return lax.optimization_barrier(v.astype(jnp.bfloat16)).astype(jnp.float32)

@jax.custom_vjp
def low_back(v):
    return v

def low_keep(v):
    return (low(v), None)

def low_pass(kept, grad):
    return (grad,)

def back_keep(v):
    return (v, None)

def back_low(kept, grad):
    return (low(grad),)
low.defvjp(low_keep, low_pass)
low_back.defvjp(back_keep, back_low)

def product(left, right):
    return jnp.dot(left, right, precision=PRECISE, preferred_element_type=jnp.float32)

def rms_norm(values, gain_vec):
    return values * lax.rsqrt(lax.optimization_barrier(jnp.mean(values * values, axis=-1, keepdims=True)) + EPSILON) * gain_vec

def rotate(values, angle_cos, angle_sin):
    half_dim = values.shape[-1] // 2
    first_half = values[..., :half_dim]
    second_half = values[..., half_dim:]
    return jnp.concatenate([first_half * angle_cos - second_half * angle_sin, second_half * angle_cos + first_half * angle_sin], axis=-1)

def angles(position, head_dim):
    index_range = jnp.arange(head_dim // 2, dtype=jnp.float32)
    inverse = ROPE_BASE ** (-2.0 * index_range / head_dim)
    phase = position.astype(jnp.float32)[:, None] * inverse[None, :]
    return (jnp.cos(phase)[:, None, :], jnp.sin(phase)[:, None, :])

def positions(pair_order, row_count):
    pair_count = pair_order.shape[0]
    half_rows = row_count // 2
    within = jnp.arange(row_count, dtype=jnp.int32)
    first_block = pair_order[:, None] * half_rows + within[None, :]
    second_block = (2 * pair_count - 1 - pair_order[:, None]) * half_rows + within[None, :] - half_rows
    return jnp.where(within[None, :] < half_rows, first_block, second_block).reshape(-1).astype(jnp.int32)

def dispatch_table(expert_ids, row_count):
    blocks = expert_ids.shape[0] // row_count
    grouped = expert_ids.reshape(blocks, row_count, -1)
    chosen = jnp.any(grouped[:, :, :, None] == jnp.arange(E_HELD, dtype=jnp.int32)[None, None, None, :], axis=2)
    held_flag = chosen.astype(jnp.int32)
    slot_index = (jnp.cumsum(held_flag, axis=1) - 1).astype(jnp.int32)
    placed = chosen[:, :, :, None] & (slot_index[:, :, :, None] == jnp.arange(CAP, dtype=jnp.int32)[None, None, None, :])
    return placed.astype(jnp.float32)

def attend(queries, key_rows, value_rows, position):
    block_rows = min(512, TOKENS)
    block_count = TOKENS // block_rows
    head_count = queries.shape[1]

    def one_block(pieces):
        query_block, pos_block = pieces
        scores = low_back(jnp.einsum('qhd,khd->hqk', query_block, key_rows, precision=PRECISE))
        visible = position[None, None, :] <= pos_block[None, :, None]
        scores = jnp.where(visible, scores, -1e+30)
        weights = low(jnp.exp(scores - jax.nn.logsumexp(scores, axis=-1, keepdims=True)))
        return jnp.einsum('hqk,khd->qhd', weights, value_rows, precision=PRECISE)
    attended = lax.map(jax.checkpoint(one_block), (queries.reshape(block_count, block_rows, head_count, -1), position.reshape(block_count, block_rows)))
    return attended.reshape(TOKENS, head_count * queries.shape[2])

def block_forward(source, gain_attn, w_query, w_key, w_value, w_out, gain_moe, w_router, shared_gate, shared_up, shared_down, expert_gate, expert_up, expert_down, angle_cos, angle_sin, position, placed):
    shape_heads = (TOKENS, HEADS, HD)
    normed = low(rms_norm(source, gain_attn))
    queries = low(rotate(low_back(product(normed, w_query)).reshape(shape_heads), angle_cos, angle_sin) * HD ** (-0.5))
    key_rows = low(rotate(low_back(product(normed, w_key)).reshape(shape_heads), angle_cos, angle_sin))
    value_rows = low(low_back(product(normed, w_value))).reshape(shape_heads)
    attended = low(low_back(attend(queries, key_rows, value_rows, position)))
    mixed = source + low_back(product(attended, w_out))
    normed_moe = low(rms_norm(mixed, gain_moe))
    router_probs = jax.nn.softmax(low_back(product(normed_moe, w_router)), axis=-1)
    shared_hidden = low(jax.nn.silu(low_back(product(normed_moe, shared_gate))) * low_back(product(normed_moe, shared_up)))
    branch = product(shared_hidden, shared_down)
    blocks = placed.shape[0]
    feature_count = normed_moe.shape[1]
    grouped = normed_moe.reshape(blocks, -1, feature_count)
    expert_in = jnp.einsum('btec,btd->ebcd', placed, grouped, precision=PRECISE).reshape(E_HELD, -1, feature_count)
    held_probs = router_probs.reshape(blocks, -1, router_probs.shape[1])[:, :, :E_HELD]
    gate_slot = jnp.einsum('btec,bte->ebc', placed, held_probs, precision=PRECISE)
    gate_vals = low_back(jnp.einsum('end,edf->enf', expert_in, expert_gate, precision=PRECISE))
    up_vals = low_back(jnp.einsum('end,edf->enf', expert_in, expert_up, precision=PRECISE))
    expert_hidden = low(jax.nn.silu(gate_vals) * up_vals)
    expert_out = low_back(jnp.einsum('enf,efd->end', expert_hidden, expert_down, precision=PRECISE)).reshape(E_HELD, blocks, -1, feature_count)
    routed = jnp.einsum('btec,ebc,ebcd->btd', placed, gate_slot, expert_out, precision=PRECISE).reshape(mixed.shape)
    return mixed + branch + routed

def reference(tokens, cotangent, gain_attn, w_query, w_key, w_value, w_out, gain_moe, w_router, shared_gate, shared_up, shared_down, expert_gate, expert_up, expert_down, expert_ids, pair_order):
    position = positions(pair_order, TOK_DEV)
    angle_cos, angle_sin = angles(position, HD)
    placed = dispatch_table(expert_ids, TOK_DEV)
    floats = tuple((operand.astype(jnp.float32) for operand in (tokens, gain_attn, w_query, w_key, w_value, w_out, gain_moe, w_router, shared_gate, shared_up, shared_down, expert_gate, expert_up, expert_down)))

    def forward(*inputs):
        return block_forward(*inputs, angle_cos, angle_sin, position, placed)
    result, pullback = jax.vjp(forward, *floats)
    gradients = pullback(cotangent.astype(jnp.float32))
    return (result.astype(jnp.bfloat16), gradients[0].astype(jnp.bfloat16), gradients[1], gradients[2], gradients[3], gradients[4], gradients[5], gradients[6], gradients[7], gradients[8], gradients[9], gradients[10], gradients[11], gradients[12], gradients[13])
```

```python
import functools

import jax
import jax.numpy as jnp
from jax import lax
from jax.experimental import pallas as pl
from jax.experimental.pallas import tpu as pltpu
from jax.sharding import PartitionSpec as P

HD = 128
CAP = 32
EPSILON = 1e-06
ROPE_BASE = 10000.0
PRECISE = lax.Precision.HIGHEST
MESH = pl.DeviceIdType.MESH
BF = jnp.bfloat16
F32 = jnp.float32
D = 2048
R1 = 2640
R2 = 1088
VM = 60 * 2**20


def contract(pattern, left, right):
    return jnp.einsum(pattern, left, right, preferred_element_type=F32)


def exact_contract(pattern, left, right):
    return jnp.einsum(pattern, left, right, precision=PRECISE, preferred_element_type=F32)


def nt(a, b):
    return lax.dot_general(a, b, (((1,), (1,)), ((), ())), preferred_element_type=F32)


def nn(a, b):
    return lax.dot_general(a, b, (((1,), (0,)), ((), ())), preferred_element_type=F32)


def tn(a, b):
    return lax.dot_general(a, b, (((0,), (0,)), ((), ())), preferred_element_type=F32)


def rel8(i, d):
    ring = lax.rem(lax.div(i, 2) + d // 2 if isinstance(d, int) else lax.div(i, 2) + lax.div(d, 2), 4)
    pair = lax.rem(lax.rem(i, 2) + (d % 2 if isinstance(d, int) else lax.rem(d, 2)), 2)
    return ring * 2 + pair


def where_am_i():
    c = lax.axis_index("ctx")
    return c, lax.div(c, 2), lax.rem(c, 2), lax.axis_index("mp")


def remote(src, dst, ssem, rsem, dev):
    return pltpu.make_async_remote_copy(
        src_ref=src, dst_ref=dst, send_sem=ssem, recv_sem=rsem, device_id=dev, device_id_type=MESH
    )


def entry_barrier(ctx=True, mp=True):
    c, chip, core, m = where_am_i()
    bar = pltpu.get_barrier_semaphore()
    count = 0
    if ctx:
        pl.semaphore_signal(bar, inc=1, device_id={"ctx": chip * 2 + 1 - core}, device_id_type=MESH)
        count += 1
        for d in range(1, 8):
            pl.semaphore_signal(
                bar, inc=1, device_id={"ctx": rel8(chip, d) * 2 + core}, device_id_type=MESH
            )
            count += 1
    if mp:
        for d in range(1, 8):
            pl.semaphore_signal(bar, inc=1, device_id={"mp": rel8(m, d)}, device_id_type=MESH)
            count += 1
    pl.semaphore_wait(bar, count)


def mp_send_parts(parts, landing, ssem, rsem):
    m = lax.axis_index("mp")
    for d in range(1, 8):
        t = rel8(m, d)
        remote(parts.at[t], landing.at[m], ssem.at[d - 1], rsem.at[m], {"mp": t}).start()


def mp_send_same(src, landing, ssem, rsem):
    m = lax.axis_index("mp")
    for d in range(1, 8):
        t = rel8(m, d)
        remote(src, landing.at[m], ssem.at[d - 1], rsem.at[m], {"mp": t}).start()


def mp_wait_recv(landing, ssem, rsem, d):
    m = lax.axis_index("mp")
    t = rel8(m, d)
    remote(landing.at[t], landing.at[t], ssem.at[0], rsem.at[t], {"mp": t}).wait_recv()
    return t


def mp_wait_send(src, ssem):
    m = lax.axis_index("mp")
    for d in range(1, 8):
        remote(src, src, ssem.at[d - 1], ssem.at[d - 1], {"mp": rel8(m, d)}).wait_send()


def k1_kernel(
    sel, q, kv, tok, wout, gain,
    moe, mixed, lse, ot, kvall,
    st_m, st_l, st_a, att, parts, land,
    s_loc, s_sib, s_dir, s_rel, r_kv, s_mp, r_mp, s_ag, r_ag,
):
    c, chip, core, m = where_am_i()
    sib = chip * 2 + 1 - core
    entry_barrier()
    remote(kv, kvall.at[c], s_sib, r_kv.at[c], {"ctx": sib}).start()
    for d in range(1, 8):
        t = rel8(chip, d) * 2 + core
        remote(kv, kvall.at[c], s_dir.at[d - 1], r_kv.at[c], {"ctx": t}).start()
    own = pltpu.make_async_copy(kv, kvall.at[c], s_loc)
    own.start()

    st_m[...] = jnp.full_like(st_m, -1e30)
    st_l[...] = jnp.zeros_like(st_l)
    st_a[...] = jnp.zeros_like(st_a)

    def step(n, h, st, v):
        m0 = st_m[n, h]
        mn = jnp.maximum(m0, jnp.max(st, axis=0, keepdims=True))
        p = jnp.exp(st - mn)
        al = jnp.exp(m0 - mn)
        st_m[n, h] = mn
        st_l[n, h] = al * st_l[n, h] + jnp.sum(p, axis=0, keepdims=True)
        st_a[n, h] = al * st_a[n, h] + tn(v, p.astype(BF))

    def pick(s, h, st, v):
        m0 = jnp.where(s == 0, st_m[0, h], st_m[1, h])
        l0 = jnp.where(s == 0, st_l[0, h], st_l[1, h])
        a0 = st_a[s, h]
        mn = jnp.maximum(m0, jnp.max(st, axis=0, keepdims=True))
        p = jnp.exp(st - mn)
        al = jnp.exp(m0 - mn)
        l1 = al * l0 + jnp.sum(p, axis=0, keepdims=True)
        a1 = al * a0 + tn(v, p.astype(BF))
        for n in range(2):
            st_m[n, h] = jnp.where(s == n, mn, st_m[n, h])
            st_l[n, h] = jnp.where(s == n, l1, st_l[n, h])
            st_a[n, h] = jnp.where(s == n, a1, st_a[n, h])

    def block(j):
        s = sel[j]
        for h in range(2):
            cols = pl.ds(h * HD, HD)
            step(2, h, nt(kvall[j, 0, 0, :, cols], q[1, :, cols]), kvall[j, 1, 0, :, cols])
            ks = jnp.where(s == 0, kvall[j, 0, 0, :, cols], kvall[j, 0, 1, :, cols])
            vs = jnp.where(s == 0, kvall[j, 1, 0, :, cols], kvall[j, 1, 1, :, cols])
            pick(s, h, nt(ks, q[s, :, cols]), vs)

    tri = lax.broadcasted_iota(jnp.int32, (256, 256), 0) <= lax.broadcasted_iota(
        jnp.int32, (256, 256), 1
    )
    for h in range(2):
        cols = pl.ds(h * HD, HD)
        step(2, h, nt(kv[0, 0, :, cols], q[1, :, cols]), kv[1, 0, :, cols])
        for n in range(2):
            st = jnp.where(tri, nt(kv[0, n, :, cols], q[n, :, cols]), -1e30)
            step(n, h, st, kv[1, n, :, cols])

    def wait_block(j):
        remote(kvall.at[j], kvall.at[j], s_sib, r_kv.at[j], {"ctx": sib}).wait_recv()

    wait_block(sib)
    block(sib)

    def chips(i, carry):
        p = rel8(chip, i + 1)
        mine = p * 2 + core
        wait_block(mine)
        remote(kvall.at[mine], kvall.at[mine], s_rel.at[i], r_kv.at[mine], {"ctx": sib}).start()
        block(mine)
        other = p * 2 + 1 - core
        wait_block(other)
        block(other)
        return carry

    lax.fori_loop(0, 7, chips, 0)

    for h in range(2):
        for n in range(2):
            m0, l0, a0 = st_m[n, h], st_l[n, h], st_a[n, h]
            if n == 1:
                m2, l2, a2 = st_m[2, h], st_l[2, h], st_a[2, h]
                mn = jnp.maximum(m0, m2)
                e0, e2 = jnp.exp(m0 - mn), jnp.exp(m2 - mn)
                m0, l0, a0 = mn, e0 * l0 + e2 * l2, e0 * a0 + e2 * a2
            lse[n, h] = m0 + jnp.log(l0)
            o = a0 / l0
            ot[n, h] = o
            att[pl.ds(n * 256, 256), pl.ds(h * HD, HD)] = jnp.transpose(o).astype(BF)

    def out_cols(i, carry):
        cols = pl.ds(pl.multiple_of(i * 256, 256), 256)
        parts[:, :, cols] = nn(att[...], wout[:, cols]).reshape(8, 64, 256).astype(BF)
        return carry

    lax.fori_loop(0, 8, out_cols, 0)
    mp_send_parts(parts, land, s_mp, r_mp)
    total = tok[...].astype(F32) + parts[m].astype(F32)
    for d in range(1, 8):
        total = total + land[mp_wait_recv(land, s_mp, r_mp, d)].astype(F32)
    mixed[...] = total
    normed = total * lax.rsqrt(jnp.mean(total * total, axis=-1, keepdims=True) + EPSILON)
    moe[m] = (normed * gain[...]).astype(BF)
    mp_send_same(moe.at[m], moe, s_ag, r_ag)

    own.wait()
    remote(kv, kv, s_sib, s_sib, {"ctx": sib}).wait_send()
    for d in range(7):
        remote(kv, kv, s_dir.at[d], s_dir.at[d], {"ctx": sib}).wait_send()
        remote(kv, kv, s_rel.at[d], s_rel.at[d], {"ctx": sib}).wait_send()
    mp_wait_send(parts.at[0], s_mp)
    for d in range(1, 8):
        mp_wait_recv(moe, s_ag, r_ag, d)
    mp_wait_send(moe.at[0], s_ag)


def sds(shape, dtype):
    return jax.ShapeDtypeStruct(shape, dtype)


VMEM_SPEC = pl.BlockSpec(memory_space=pltpu.VMEM)
SMEM_SPEC = pl.BlockSpec(memory_space=pltpu.SMEM)
ANY_SPEC = pl.BlockSpec(memory_space=pl.ANY)
DMA = pltpu.SemaphoreType.DMA


def params(cid):
    return pltpu.CompilerParams(collective_id=cid, has_side_effects=True, vmem_limit_bytes=VM)


def attention_forward(sel, q, kv, tok_mine, w_out, gain):
    return pl.pallas_call(
        k1_kernel,
        name="attend_forward",
        out_shape=(
            sds((8, 64, D), BF),
            sds((64, D), F32),
            sds((2, 2, 1, 256), F32),
            sds((2, 2, HD, 256), F32),
            sds((16, 2, 2, 256, 256), BF),
        ),
        in_specs=[SMEM_SPEC] + [VMEM_SPEC] * 5,
        out_specs=(VMEM_SPEC,) * 5,
        scratch_shapes=[
            pltpu.VMEM((3, 2, 1, 256), F32),
            pltpu.VMEM((3, 2, 1, 256), F32),
            pltpu.VMEM((3, 2, HD, 256), F32),
            pltpu.VMEM((512, 256), BF),
            pltpu.VMEM((8, 64, D), BF),
            pltpu.VMEM((8, 64, D), BF),
            DMA, DMA, DMA((7,)), DMA((7,)), DMA((16,)),
            DMA((7,)), DMA((8,)), DMA((7,)), DMA((8,)),
        ],
        compiler_params=params(1),
    )(sel, q, kv, tok_mine, w_out, gain)


def w_sibling_sends(w, sibbuf, ssem, rsem):
    c, chip, core, m = where_am_i()
    sib = chip * 2 + 1 - core
    for k in range(8):
        cols = pl.ds(pl.multiple_of((2 * k + 1 - core) * HD, HD), HD)
        remote(w.at[:, cols], sibbuf.at[k], ssem.at[k], rsem.at[k], {"ctx": sib}).start()


def w_scatter(w, sibbuf, sums, land, ssem_sib, rsem_sib, ssem, rsem, rows, tile):
    c, chip, core, m = where_am_i()
    sib = chip * 2 + 1 - core

    def one(i, carry):
        k = rel8(chip, i + 1)
        remote(
            sibbuf.at[k], sibbuf.at[k], ssem_sib.at[0], rsem_sib.at[k], {"ctx": sib}
        ).wait_recv()
        cols = pl.ds(pl.multiple_of((2 * k + core) * HD, HD), HD)

        def add(r, carry):
            rr = pl.ds(pl.multiple_of(r * tile, 16), tile)
            sums[k, rr, :] = (w[rr, cols].astype(F32) + sibbuf[k, rr, :].astype(F32)).astype(BF)
            return carry

        lax.fori_loop(0, rows // tile, add, 0)

        @pl.when(i < 7)
        def _():
            remote(
                sums.at[k], land.at[chip], ssem.at[i], rsem.at[chip], {"ctx": k * 2 + core}
            ).start()

        return carry

    lax.fori_loop(0, 8, one, 0)


def w_total(sums, land, fin, ssem, rsem, rows, tile):
    c, chip, core, m = where_am_i()
    for d in range(1, 8):
        k = rel8(chip, d)
        remote(land.at[k], land.at[k], ssem.at[0], rsem.at[k], {"ctx": k * 2 + core}).wait_recv()

    def add(r, carry):
        rr = pl.ds(pl.multiple_of(r * tile, 16), tile)
        total = sums[chip, rr, :].astype(F32)
        for d in range(1, 8):
            total = total + land[rel8(chip, d), rr, :].astype(F32)
        fin[rr, :] = total.astype(BF)
        return carry

    lax.fori_loop(0, rows // tile, add, 0)


def w_scatter_drain(sibbuf, sums, ssem_sib, ssem):
    c, chip, core, m = where_am_i()
    sib = chip * 2 + 1 - core
    for k in range(8):
        remote(sibbuf.at[k], sibbuf.at[k], ssem_sib.at[k], ssem_sib.at[k], {"ctx": sib}).wait_send()
    for d in range(7):
        remote(sums.at[d], sums.at[d], ssem.at[d], ssem.at[d], {"ctx": sib}).wait_send()


def window(ref, j):
    return ref.at[:, pl.ds(pl.multiple_of(j * HD, HD), HD)]


def w_gather_start(fin, out, s_loc, s_sib, s_dir, rsem):
    c, chip, core, m = where_am_i()
    sib = chip * 2 + 1 - core
    for d in range(1, 8):
        t = rel8(chip, d) * 2 + core
        remote(fin, window(out, c), s_dir.at[d - 1], rsem.at[c], {"ctx": t}).start()
    remote(fin, window(out, c), s_sib, rsem.at[c], {"ctx": sib}).start()
    pltpu.make_async_copy(fin, window(out, c), s_loc).start()


def w_gather_relay(out, s_rel, rsem, i):
    c, chip, core, m = where_am_i()
    sib = chip * 2 + 1 - core
    j = rel8(chip, i + 1) * 2 + core
    win = window(out, j)
    remote(win, win, s_rel.at[i], rsem.at[j], {"ctx": sib}).wait_recv()
    remote(win, win, s_rel.at[i], rsem.at[j], {"ctx": sib}).start()


def w_gather_drain(fin, out, s_loc, s_sib, s_dir, s_rel, rsem):
    c, chip, core, m = where_am_i()
    sib = chip * 2 + 1 - core
    pltpu.make_async_copy(fin, window(out, c), s_loc).wait()
    remote(fin, fin, s_sib, s_sib, {"ctx": sib}).wait_send()
    for d in range(7):
        remote(fin, fin, s_dir.at[d], s_dir.at[d], {"ctx": sib}).wait_send()
        remote(fin, fin, s_rel.at[d], s_rel.at[d], {"ctx": sib}).wait_send()
    remote(window(out, sib), window(out, sib), s_sib, rsem.at[sib], {"ctx": sib}).wait_recv()
    for d in range(1, 8):
        j = rel8(chip, d) * 2 + 1 - core
        remote(window(out, j), window(out, j), s_sib, rsem.at[j], {"ctx": sib}).wait_recv()


def k2_kernel(
    gmi, gate_part, mixed, cot, gain, w_router, probs, slots, w1,
    g_attn, g_mixed, gain_part, gate_sum, fin,
    land, gate_land, sibbuf, sums, wland,
    s_mp, r_mp, s_gate, r_gate, s_ag, r_ag, s_wsib, r_wsib, s_w, r_w,
):
    c, chip, core, m = where_am_i()
    entry_barrier()
    mp_send_parts(gmi, land, s_mp, r_mp)
    mp_send_same(gate_part, gate_land, s_gate, r_gate)
    w_sibling_sends(w1, sibbuf, s_wsib, r_wsib)
    w_scatter(w1, sibbuf, sums, wland, s_wsib, r_wsib, s_w, r_w, R1, 528)

    gate = gate_part[...]
    for d in range(1, 8):
        gate = gate + gate_land[mp_wait_recv(gate_land, s_gate, r_gate, d)]
    gate_sum[...] = gate
    lane = lax.broadcasted_iota(jnp.int32, (HD, 64), 0)
    col = lax.broadcasted_iota(jnp.int32, (HD, 64), 1)
    member = jnp.where((lane >= col * CAP) & (lane < (col + 1) * CAP) & (col < 3), 1.0, 0.0)
    grad_probs = lax.dot_general(
        slots[...] * gate, member, (((1,), (0,)), ((), ())),
        precision=PRECISE, preferred_element_type=F32,
    )
    pr = probs[...]
    logits = (pr * (grad_probs - jnp.sum(grad_probs * pr, axis=-1, keepdims=True))).astype(BF)

    total = nt(logits, w_router[...]) + gmi[m].astype(F32)
    for d in range(1, 8):
        total = total + land[mp_wait_recv(land, s_mp, r_mp, d)].astype(F32)
    mx = mixed[...]
    n = lax.rsqrt(jnp.mean(mx * mx, axis=-1, keepdims=True) + EPSILON)
    gain_part[...] = jnp.sum(total * mx * n, axis=0, keepdims=True)
    gg = total * gain[...]
    gm = cot[...].astype(F32) + n * gg - mx * (n * n * n) * jnp.mean(gg * mx, axis=-1, keepdims=True)
    g_mixed[...] = gm
    g_attn[m] = gm.astype(BF)
    mp_send_same(g_attn.at[m], g_attn, s_ag, r_ag)

    w_total(sums, wland, fin, s_w, r_w, R1, 528)
    w_scatter_drain(sibbuf, sums, s_wsib, s_w)
    mp_wait_send(gmi.at[0], s_mp)
    mp_wait_send(gate_part, s_gate)
    for d in range(1, 8):
        mp_wait_recv(g_attn, s_ag, r_ag, d)
    mp_wait_send(g_attn.at[0], s_ag)


def second_norm_backward(gmi, gate_part, mixed, cot, gain, w_router, probs, slots, w1):
    return pl.pallas_call(
        k2_kernel,
        name="second_norm_backward",
        out_shape=(
            sds((8, 64, D), BF),
            sds((64, D), F32),
            sds((1, D), F32),
            sds((1, HD), F32),
            sds((R1, HD), BF),
        ),
        in_specs=[VMEM_SPEC] * 9,
        out_specs=(VMEM_SPEC,) * 5,
        scratch_shapes=[
            pltpu.VMEM((8, 64, D), BF),
            pltpu.VMEM((8, 1, HD), F32),
            pltpu.VMEM((8, R1, HD), BF),
            pltpu.VMEM((8, R1, HD), BF),
            pltpu.VMEM((8, R1, HD), BF),
            DMA((7,)), DMA((8,)), DMA((7,)), DMA((8,)), DMA((7,)), DMA((8,)),
            DMA((8,)), DMA((8,)), DMA((7,)), DMA((8,)),
        ],
        compiler_params=params(2),
    )(gmi, gate_part, mixed, cot, gain, w_router, probs, slots, w1)


def k3_kernel(
    sel, q, kvall, lse, ot, g_attn, wout, moe_part, mixed, fin,
    output, w1, dq, dkv,
    do, delta, dqt, cur, to_sib, from_sib, to_far, from_far, oland,
    s_sib, r_sib, s_far, r_far, s_mp, r_mp, s_ag, r_ag, s_loc, s_wsib, s_wdir, s_wrel, r_w,
):
    c, chip, core, m = where_am_i()
    sib = chip * 2 + 1 - core
    entry_barrier()
    mp_send_parts(moe_part, oland, s_mp, r_mp)
    w_gather_start(fin, w1, s_loc, s_wsib, s_wdir, r_w)

    g_att = nt(g_attn[...], wout[...])
    for n in range(2):
        for h in range(2):
            piece = g_att[n * 256 : n * 256 + 256, h * HD : h * HD + HD].astype(BF)
            do[n, h] = piece
            dot_t = jnp.transpose(piece.astype(F32))
            delta[n, h] = jnp.sum(dot_t * ot[n, h], axis=0, keepdims=True)
    dqt[...] = jnp.zeros_like(dqt)

    def terms(h, k, v, qq, dd, ls, de, mask):
        p = jnp.exp(nt(k, qq) - ls)
        if mask is not None:
            p = jnp.where(mask, p, 0.0)
        ds = (p * (nt(v, dd) - de)).astype(BF)
        return nn(ds, qq), nn(p.astype(BF), dd), tn(k, ds)

    def block(j, store):
        s = sel[j]
        for h in range(2):
            cols = pl.ds(h * HD, HD)
            dk0, dv0, dq0 = terms(
                h, kvall[j, 0, 0, :, cols], kvall[j, 1, 0, :, cols], q[1, :, cols], do[1, h],
                lse[1, h], delta[1, h], None,
            )
            dqt[2, h] += dq0
            ls = jnp.where(s == 0, lse[0, h], lse[1, h])
            de = jnp.where(s == 0, delta[0, h], delta[1, h])
            dk1, dv1, dq1 = terms(
                h, kvall[j, 0, s, :, cols], kvall[j, 1, s, :, cols], q[s, :, cols], do[s, h],
                ls, de, None,
            )
            for n in range(2):
                dqt[n, h] += jnp.where(s == n, dq1, 0.0)
            store(0, 0, cols, dk0 + jnp.where(s == 0, dk1, 0.0))
            store(1, 0, cols, dv0 + jnp.where(s == 0, dv1, 0.0))
            store(0, 1, cols, jnp.where(s == 1, dk1, 0.0))
            store(1, 1, cols, jnp.where(s == 1, dv1, 0.0))

    def finish(i):
        k = rel8(chip, i + 1)
        remote(from_sib.at[k], from_sib.at[k], s_sib.at[0], r_sib.at[k], {"ctx": sib}).wait_recv()
        for a in range(2):
            for n in range(2):
                to_far[k, a, n] = (to_far[k, a, n].astype(F32) + from_sib[k, a, n].astype(F32)).astype(BF)
        remote(to_far.at[k], from_far.at[chip], s_far.at[i], r_far.at[chip], {"ctx": k * 2 + core}).start()

    def chips(i, carry):
        k = rel8(chip, i + 1)

        def to_sibling(a, n, cols, val):
            to_sib[k, a, n, :, cols] = val.astype(BF)

        block(k * 2 + 1 - core, to_sibling)
        remote(to_sib.at[k], from_sib.at[k], s_sib.at[k], r_sib.at[k], {"ctx": sib}).start()

        def to_chip(a, n, cols, val):
            to_far[k, a, n, :, cols] = val.astype(BF)

        block(k * 2 + core, to_chip)

        @pl.when(i > 0)
        def _():
            finish(i - 1)

        return carry

    lax.fori_loop(0, 7, chips, 0)

    def to_sibling(a, n, cols, val):
        to_sib[chip, a, n, :, cols] = val.astype(BF)

    block(sib, to_sibling)
    remote(to_sib.at[chip], from_sib.at[chip], s_sib.at[chip], r_sib.at[chip], {"ctx": sib}).start()
    finish(6)

    tri = lax.broadcasted_iota(jnp.int32, (256, 256), 0) <= lax.broadcasted_iota(
        jnp.int32, (256, 256), 1
    )
    for h in range(2):
        cols = pl.ds(h * HD, HD)
        k0, v0 = kvall[c, 0, 0, :, cols], kvall[c, 1, 0, :, cols]
        dk0, dv0, dq0 = terms(h, k0, v0, q[1, :, cols], do[1, h], lse[1, h], delta[1, h], None)
        dqt[2, h] += dq0
        for n in range(2):
            kn, vn = kvall[c, 0, n, :, cols], kvall[c, 1, n, :, cols]
            dk1, dv1, dq1 = terms(h, kn, vn, q[n, :, cols], do[n, h], lse[n, h], delta[n, h], tri)
            dqt[n, h] += dq1
            cur[0, n, :, cols] = dk0 + dk1 if n == 0 else dk1
            cur[1, n, :, cols] = dv0 + dv1 if n == 0 else dv1
    for h in range(2):
        dq[0, :, pl.ds(h * HD, HD)] = jnp.transpose(dqt[0, h])
        dq[1, :, pl.ds(h * HD, HD)] = jnp.transpose(dqt[1, h] + dqt[2, h])

    total = mixed[...] + moe_part[m].astype(F32)
    for d in range(1, 8):
        total = total + oland[mp_wait_recv(oland, s_mp, r_mp, d)].astype(F32)
    output[m] = total.astype(BF)
    mp_send_same(output.at[m], output, s_ag, r_ag)

    def relay(i, carry):
        w_gather_relay(w1, s_wrel, r_w, i)
        return carry

    lax.fori_loop(0, 7, relay, 0)

    remote(from_sib.at[chip], from_sib.at[chip], s_sib.at[0], r_sib.at[chip], {"ctx": sib}).wait_recv()
    for d in range(1, 8):
        k = rel8(chip, d)
        remote(from_far.at[k], from_far.at[k], s_sib.at[0], r_far.at[k], {"ctx": sib}).wait_recv()

    def add(i, carry):
        a, n = lax.div(i, 2), lax.rem(i, 2)
        t = cur[a, n] + from_sib[chip, a, n].astype(F32)
        for d in range(1, 8):
            t = t + from_far[rel8(chip, d), a, n].astype(F32)
        dkv[a, n] = t
        return carry

    lax.fori_loop(0, 4, add, 0)

    for k in range(8):
        remote(to_sib.at[k], to_sib.at[k], s_sib.at[k], s_sib.at[k], {"ctx": sib}).wait_send()
    for d in range(7):
        remote(to_far.at[d], to_far.at[d], s_far.at[d], s_far.at[d], {"ctx": sib}).wait_send()
    mp_wait_send(moe_part.at[0], s_mp)
    for d in range(1, 8):
        mp_wait_recv(output, s_ag, r_ag, d)
    mp_wait_send(output.at[0], s_ag)
    w_gather_drain(fin, w1, s_loc, s_wsib, s_wdir, s_wrel, r_w)


def attention_backward(sel, q, kvall, lse, ot, g_attn, w_out, moe_part, mixed, fin):
    return pl.pallas_call(
        k3_kernel,
        name="attend_backward",
        out_shape=(
            sds((8, 64, D), BF),
            sds((R1, D), BF),
            sds((2, 256, 256), F32),
            sds((2, 2, 256, 256), F32),
        ),
        in_specs=[SMEM_SPEC] + [VMEM_SPEC] * 9,
        out_specs=(VMEM_SPEC, ANY_SPEC, VMEM_SPEC, VMEM_SPEC),
        scratch_shapes=[
            pltpu.VMEM((2, 2, 256, HD), BF),
            pltpu.VMEM((2, 2, 1, 256), F32),
            pltpu.VMEM((3, 2, HD, 256), F32),
            pltpu.VMEM((2, 2, 256, 256), F32),
            pltpu.VMEM((8, 2, 2, 256, 256), BF),
            pltpu.VMEM((8, 2, 2, 256, 256), BF),
            pltpu.VMEM((8, 2, 2, 256, 256), BF),
            pltpu.VMEM((8, 2, 2, 256, 256), BF),
            pltpu.VMEM((8, 64, D), BF),
            DMA((8,)), DMA((8,)), DMA((7,)), DMA((8,)),
            DMA((7,)), DMA((8,)), DMA((7,)), DMA((8,)),
            DMA, DMA, DMA((7,)), DMA((7,)), DMA((16,)),
        ],
        compiler_params=params(3),
    )(sel, q, kvall, lse, ot, g_attn, w_out, moe_part, mixed, fin)


def k4_kernel(
    gni, tok, g_mixed, gain, gain_moe_part, w2,
    g_tokens, w2out, gains,
    land, sibbuf, sums, wland, fin, gmine, gland, gpart, gfar,
    s_mp, r_mp, s_ag, r_ag, s_wsib, r_wsib, s_w, r_w, s_loc, s_gsib, s_gdir, s_grel, r_g,
    s_gm, r_gm, s_gs, r_gs, s_gc, r_gc,
):
    c, chip, core, m = where_am_i()
    sib = chip * 2 + 1 - core
    entry_barrier()
    mp_send_parts(gni, land, s_mp, r_mp)
    w_sibling_sends(w2, sibbuf, s_wsib, r_wsib)
    w_scatter(w2, sibbuf, sums, wland, s_wsib, r_wsib, s_w, r_w, R2, 544)

    total = gni[m].astype(F32)
    for d in range(1, 8):
        total = total + land[mp_wait_recv(land, s_mp, r_mp, d)].astype(F32)
    src = tok[...].astype(F32)
    n = lax.rsqrt(jnp.mean(src * src, axis=-1, keepdims=True) + EPSILON)
    gg = total * gain[...]
    gs = n * gg - src * (n * n * n) * jnp.mean(gg * src, axis=-1, keepdims=True)
    g_tokens[m] = (g_mixed[...] + gs).astype(BF)
    mp_send_same(g_tokens.at[m], g_tokens, s_ag, r_ag)
    gmine[pl.ds(0, 1), :] = gain_moe_part[...]
    gmine[pl.ds(1, 1), :] = jnp.sum(total * src * n, axis=0, keepdims=True)
    mp_send_same(gmine, gland, s_gm, r_gm)

    w_total(sums, wland, fin, s_w, r_w, R2, 544)
    w_gather_start(fin, w2out, s_loc, s_gsib, s_gdir, r_g)

    gsum = gmine[...]
    for d in range(1, 8):
        gsum = gsum + gland[mp_wait_recv(gland, s_gm, r_gm, d)]
    gpart[0] = gsum
    remote(gpart.at[0], gpart.at[1], s_gs, r_gs, {"ctx": sib}).start()
    remote(gpart.at[0], gpart.at[1], s_gs, r_gs, {"ctx": sib}).wait_recv()
    gpart[2] = gpart[0] + gpart[1]
    for d in range(1, 8):
        k = rel8(chip, d)
        remote(gpart.at[2], gfar.at[chip], s_gc.at[d - 1], r_gc.at[chip], {"ctx": k * 2 + core}).start()
    gfar[chip] = gpart[2]
    for d in range(1, 8):
        k = rel8(chip, d)
        remote(gfar.at[k], gfar.at[k], s_gs, r_gc.at[k], {"ctx": sib}).wait_recv()
    gsum = gfar[0]
    for k in range(1, 8):
        gsum = gsum + gfar[k]
    gains[...] = gsum

    def relay(i, carry):
        w_gather_relay(w2out, s_grel, r_g, i)
        return carry

    lax.fori_loop(0, 7, relay, 0)
    remote(gpart.at[0], gpart.at[1], s_gs, r_gs, {"ctx": sib}).wait_send()
    for d in range(7):
        remote(gpart.at[2], gpart.at[2], s_gc.at[d], s_gc.at[d], {"ctx": sib}).wait_send()
    mp_wait_send(gmine, s_gm)
    w_scatter_drain(sibbuf, sums, s_wsib, s_w)
    mp_wait_send(gni.at[0], s_mp)
    for d in range(1, 8):
        mp_wait_recv(g_tokens, s_ag, r_ag, d)
    mp_wait_send(g_tokens.at[0], s_ag)
    w_gather_drain(fin, w2out, s_loc, s_gsib, s_gdir, s_grel, r_g)


def first_norm_backward(gni, tok, g_mixed, gain, gain_moe_part, w2):
    return pl.pallas_call(
        k4_kernel,
        name="first_norm_backward",
        out_shape=(sds((8, 64, D), BF), sds((R2, D), BF), sds((2, D), F32)),
        in_specs=[VMEM_SPEC] * 6,
        out_specs=(VMEM_SPEC, ANY_SPEC, VMEM_SPEC),
        scratch_shapes=[
            pltpu.VMEM((8, 64, D), BF),
            pltpu.VMEM((8, R2, HD), BF),
            pltpu.VMEM((8, R2, HD), BF),
            pltpu.VMEM((8, R2, HD), BF),
            pltpu.VMEM((R2, HD), BF),
            pltpu.VMEM((2, D), F32),
            pltpu.VMEM((8, 2, D), F32),
            pltpu.VMEM((3, 2, D), F32),
            pltpu.VMEM((8, 2, D), F32),
            DMA((7,)), DMA((8,)), DMA((7,)), DMA((8,)),
            DMA((8,)), DMA((8,)), DMA((7,)), DMA((8,)),
            DMA, DMA, DMA((7,)), DMA((7,)), DMA((16,)),
            DMA((7,)), DMA((8,)), DMA, DMA, DMA((7,)), DMA((8,)),
        ],
        compiler_params=params(4),
    )(gni, tok, g_mixed, gain, gain_moe_part, w2)


def rms_norm(values, gain_vec):
    return (
        values * lax.rsqrt(jnp.mean(values * values, axis=-1, keepdims=True) + EPSILON) * gain_vec
    )


def swiglu(gate_vals, up_vals):
    return jax.nn.silu(gate_vals) * up_vals


def rotate(values, angle_cos, angle_sin):
    half_dim = values.shape[-1] // 2
    first_half = values[..., :half_dim]
    second_half = values[..., half_dim:]
    return jnp.concatenate(
        [
            first_half * angle_cos - second_half * angle_sin,
            second_half * angle_cos + first_half * angle_sin,
        ],
        axis=-1,
    )


def angles(position, head_dim):
    index_range = jnp.arange(head_dim // 2, dtype=F32)
    inverse = ROPE_BASE ** (-2.0 * index_range / head_dim)
    phase = position.astype(F32)[:, None] * inverse[None, :]
    return (jnp.cos(phase)[:, None, :], jnp.sin(phase)[:, None, :])


def dispatch_table(expert_ids, held_count, slot_count):
    chosen = jnp.any(
        expert_ids[:, :, None] == jnp.arange(held_count, dtype=jnp.int32)[None, None, :], axis=1
    )
    held_flag = chosen.astype(jnp.int32)
    slot_index = jnp.cumsum(held_flag, axis=0) - 1
    placed = chosen[:, :, None] & (
        slot_index[:, :, None] == jnp.arange(slot_count, dtype=jnp.int32)[None, None, :]
    )
    return placed.astype(F32)


def on_device(
    tokens, cotangent, gain_attn, w_query, w_key, w_value, w_out, gain_moe, w_router,
    shared_gate, shared_up, shared_down, expert_gate, expert_up, expert_down, expert_ids, pair_order,
):
    rows = tokens.shape[0]
    head_shape = (rows, 2, HD)
    member = lax.axis_index("ctx")
    mine = lax.axis_index("mp")
    pair = lax.dynamic_index_in_dim(pair_order, member, keepdims=False)
    within = jnp.arange(rows, dtype=jnp.int32)
    pos = jnp.where(within < 256, pair * 256 + within, (31 - pair) * 256 + within - 256)
    cos_mine, sin_mine = angles(pos, HD)
    sel = jnp.where(pair_order < pair, 0, 1).astype(jnp.int32)
    scale = HD ** (-0.5)
    source = tokens.astype(F32)
    normed_low = rms_norm(source, gain_attn).astype(BF)
    q_lin = nn(normed_low, w_query).reshape(head_shape)
    k_lin = nn(normed_low, w_key).reshape(head_shape)
    v_low = nn(normed_low, w_value).astype(BF)
    q_rot = (rotate(q_lin, cos_mine, sin_mine) * scale).astype(BF).reshape(2, 256, 256)
    k_rot = rotate(k_lin, cos_mine, sin_mine).astype(BF).reshape(2, 256, 256)
    kv = jnp.stack([k_rot, v_low.reshape(2, 256, 256)])
    tok_mine = lax.dynamic_slice_in_dim(tokens, mine * 64, 64)
    cot_mine = lax.dynamic_slice_in_dim(cotangent, mine * 64, 64)
    moe_all, mixed, lse, ot, kvall = attention_forward(
        sel, q_rot, kv, tok_mine, w_out, gain_moe[None]
    )
    moe_low = moe_all.reshape(rows, D)
    attended_low = ot.transpose(0, 3, 1, 2).reshape(rows, 256).astype(BF)

    router_probs = jax.nn.softmax(nn(moe_low, w_router), axis=-1)
    shared_g = nn(moe_low, shared_gate)
    shared_u = nn(moe_low, shared_up)
    shared_act, shared_pull = jax.vjp(swiglu, shared_g, shared_u)
    shared_hidden = shared_act.astype(BF)
    held = expert_gate.shape[0]
    slot_table = dispatch_table(expert_ids, held, CAP)
    table_low = slot_table.astype(BF)
    expert_in = contract("tec,td->ecd", table_low, moe_low).astype(BF)
    gate_slot = exact_contract("tec,te->ec", slot_table, router_probs[:, :held])
    expert_g = contract("ecd,edf->ecf", expert_in, expert_gate)
    expert_u = contract("ecd,edf->ecf", expert_in, expert_up)
    expert_act, expert_pull = jax.vjp(swiglu, expert_g, expert_u)
    expert_hidden = expert_act.astype(BF)
    expert_part = contract("ecf,efd->ecd", expert_hidden, expert_down)
    gated_part = gate_slot[:, :, None] * expert_part
    moe_part = nn(shared_hidden, shared_down) + exact_contract("tec,ecd->td", slot_table, gated_part)
    moe_part = moe_part.astype(BF).reshape(8, 64, D)

    grad_shared_hidden = contract("td,fd->tf", cotangent, shared_down)
    g_shared_g, g_shared_u = shared_pull(grad_shared_hidden)
    g_sg = g_shared_g.astype(BF)
    g_su = g_shared_u.astype(BF)
    grad_moe_in = contract("tf,df->td", g_sg, shared_gate) + contract("tf,df->td", g_su, shared_up)
    grad_slot = contract("tec,td->ecd", table_low, cotangent)
    grad_expert_out = (gate_slot[:, :, None] * grad_slot).astype(BF)
    gate_grad_part = jnp.sum(grad_slot * expert_part, axis=-1)
    grad_expert_hidden = contract("ecd,efd->ecf", grad_expert_out, expert_down)
    g_expert_g, g_expert_u = expert_pull(grad_expert_hidden)
    g_eg = g_expert_g.astype(BF)
    g_eu = g_expert_u.astype(BF)
    grad_expert_in = contract("ecf,edf->ecd", g_eg, expert_gate) + contract(
        "ecf,edf->ecd", g_eu, expert_up
    )
    grad_moe_in = grad_moe_in + exact_contract("tec,ecd->td", slot_table, grad_expert_in)
    grad_moe_in = grad_moe_in.astype(BF).reshape(8, 64, D)
    w1 = jnp.concatenate(
        [
            contract("tf,td->fd", g_sg, moe_low).astype(BF),
            contract("tf,td->fd", g_su, moe_low).astype(BF),
            contract("tf,td->fd", shared_hidden, cotangent).astype(BF),
            contract("ecf,ecd->efd", g_eg, expert_in).astype(BF).reshape(-1, D),
            contract("ecf,ecd->efd", g_eu, expert_in).astype(BF).reshape(-1, D),
            contract("ecf,ecd->efd", expert_hidden, grad_expert_out).astype(BF).reshape(-1, D),
        ]
    )

    gate_part = jnp.pad(gate_grad_part.reshape(1, -1), ((0, 0), (0, HD - held * CAP)))
    slots = jnp.pad(slot_table.reshape(rows, -1), ((0, 0), (0, HD - held * CAP)))
    slots_mine = lax.dynamic_slice_in_dim(slots, mine * 64, 64)
    probs_mine = lax.dynamic_slice_in_dim(router_probs, mine * 64, 64)
    g_attn, g_mixed, gain_moe_part, gate_sum, fin = second_norm_backward(
        grad_moe_in, gate_part, mixed, cot_mine, gain_moe[None], w_router, probs_mine, slots_mine, w1
    )
    grad_held = exact_contract(
        "tec,ec->te", slot_table, gate_sum[0, : held * CAP].reshape(held, CAP)
    )
    grad_probs = jnp.pad(grad_held, ((0, 0), (0, router_probs.shape[1] - held)))
    g_logits = (
        router_probs * (grad_probs - jnp.sum(grad_probs * router_probs, axis=-1, keepdims=True))
    ).astype(BF)

    g_attn = g_attn.reshape(rows, D)
    output, w1, dq, dkv = attention_backward(
        sel, q_rot, kvall, lse, ot, g_attn, w_out, moe_part, mixed, fin
    )
    grad_q_lin = (
        rotate(dq.reshape(head_shape) * scale, cos_mine, -sin_mine).reshape(rows, -1).astype(BF)
    )
    grad_k_lin = (
        rotate(dkv[0].reshape(head_shape), cos_mine, -sin_mine).reshape(rows, -1).astype(BF)
    )
    grad_v_lin = dkv[1].reshape(rows, -1).astype(BF)
    grad_normed = (
        contract("tk,dk->td", grad_q_lin, w_query)
        + contract("tk,dk->td", grad_k_lin, w_key)
        + contract("tk,dk->td", grad_v_lin, w_value)
    )
    grad_normed = grad_normed.astype(BF).reshape(8, 64, D)
    w2 = jnp.concatenate(
        [
            contract("tk,td->kd", grad_q_lin, normed_low).astype(BF),
            contract("tk,td->kd", grad_k_lin, normed_low).astype(BF),
            contract("tk,td->kd", grad_v_lin, normed_low).astype(BF),
            contract("tk,td->kd", attended_low, g_attn).astype(BF),
            contract("te,td->ed", g_logits, moe_low).astype(BF),
        ]
    )
    g_tokens, w2, gains = first_norm_backward(
        grad_normed, tok_mine, g_mixed, gain_attn[None], gain_moe_part, w2
    )
    w1 = w1.astype(F32)
    w2 = w2.astype(F32)
    return (
        output.reshape(rows, D),
        g_tokens.reshape(rows, D),
        gains[1],
        w2[:256].T,
        w2[256:512].T,
        w2[512:768].T,
        w2[768:1024],
        gains[0],
        w2[1024:].T,
        w1[:352].T,
        w1[352:704].T,
        w1[704:1056],
        w1[1056:1584].reshape(3, 176, D).transpose(0, 2, 1),
        w1[1584:2112].reshape(3, 176, D).transpose(0, 2, 1),
        w1[2112:].reshape(3, 176, D),
    )


def solution(mesh):
    in_specs = (
        P("ctx", None),
        P("ctx", None),
        P(),
        P(None, "mp"),
        P(None, "mp"),
        P(None, "mp"),
        P("mp", None),
        P(),
        P(),
        P(None, "mp"),
        P(None, "mp"),
        P("mp", None),
        P(None, None, "mp"),
        P(None, None, "mp"),
        P(None, "mp", None),
        P("ctx", None),
        P(),
    )
    out_specs = (
        P("ctx", None),
        P("ctx", None),
        P(),
        P(None, "mp"),
        P(None, "mp"),
        P(None, "mp"),
        P("mp", None),
        P(),
        P(),
        P(None, "mp"),
        P(None, "mp"),
        P("mp", None),
        P(None, None, "mp"),
        P(None, None, "mp"),
        P(None, "mp", None),
    )
    return jax.shard_map(
        on_device, mesh=mesh, in_specs=in_specs, out_specs=out_specs, check_vma=False
    )
```

```python
import jax
import jax.numpy as jnp
from jax import lax
from jax.experimental import pallas as pl
from jax.experimental.pallas import tpu as pltpu
from jax.sharding import PartitionSpec as P

HD = 128
CAP = 32
EPSILON = 1e-06
ROPE_BASE = 10000.0
PRECISE = lax.Precision.HIGHEST
MESH = pl.DeviceIdType.MESH
BF = jnp.bfloat16
F32 = jnp.float32
D = 2048
SH = 352
EF = 176
R1 = 3 * SH + 9 * EF
R2 = 64 + 4 * 256
VM = 60 * 2**20
NEG = -1e30


def nt(a, b):
    return lax.dot_general(a, b, (((1,), (1,)), ((), ())), preferred_element_type=F32)


def nn(a, b):
    return lax.dot_general(a, b, (((1,), (0,)), ((), ())), preferred_element_type=F32)


def tn(a, b):
    return lax.dot_general(a, b, (((0,), (0,)), ((), ())), preferred_element_type=F32)


def turned(a):
    return jnp.transpose(a.astype(F32)).astype(BF)


def place():
    c = lax.axis_index("ctx")
    return lax.div(c, 4), lax.rem(lax.div(c, 2), 2), lax.rem(c, 2), lax.axis_index("mp")


def chip_at(dy, t):
    y, z, core, m = place()
    return lax.rem(y + dy, 4) * 2 + lax.rem(z + t, 2)


def peer(dy, t):
    y, z, core, m = place()
    return {"ctx": chip_at(dy, t) * 2 + core}


def sibling():
    y, z, core, m = place()
    return {"ctx": chip_at(0, 0) * 2 + 1 - core}


def mp_at(d):
    m = lax.axis_index("mp")
    return lax.rem(lax.div(m, 2) + d // 2, 4) * 2 + lax.rem(lax.rem(m, 2) + d % 2, 2)


def remote(src, dst, ssem, rsem, dev):
    return pltpu.make_async_remote_copy(
        src_ref=src, dst_ref=dst, send_sem=ssem, recv_sem=rsem, device_id=dev, device_id_type=MESH
    )


def greet(far=False):
    bar = pltpu.get_barrier_semaphore()
    devs = [sibling(), peer(0, 1), peer(1, 0), peer(3, 0)] + ([peer(2, 0)] if far else [])
    devs += [{"mp": mp_at(d)} for d in range(1, 8)]
    for dev in devs:
        pl.semaphore_signal(bar, inc=1, device_id=dev, device_id_type=MESH)
    return len(devs)


def all_in(count):
    pl.semaphore_wait(pltpu.get_barrier_semaphore(), count)


def mp_send_parts(parts, landing, ssem, rsem):
    m = lax.axis_index("mp")
    for d in range(1, 8):
        t = mp_at(d)
        remote(parts.at[t], landing.at[m], ssem.at[d - 1], rsem.at[m], {"mp": t}).start()


def mp_send_same(src, landing, ssem, rsem):
    m = lax.axis_index("mp")
    for d in range(1, 8):
        remote(src, landing.at[m], ssem.at[d - 1], rsem.at[m], {"mp": mp_at(d)}).start()


def mp_wait_recv(landing, ssem, rsem, d):
    t = mp_at(d)
    remote(landing.at[t], landing.at[t], ssem.at[0], rsem.at[t], {"mp": t}).wait_recv()
    return t


def mp_wait_send(src, ssem):
    for d in range(1, 8):
        remote(src, src, ssem.at[d - 1], ssem.at[d - 1], {"mp": mp_at(d)}).wait_send()


class Gather:
    def __init__(self, buf, sems):
        self.buf, (self.s, self.r) = buf, sems
        y, z, self.core, m = place()

    @staticmethod
    def sems():
        return (pltpu.SemaphoreType.DMA((15,)), pltpu.SemaphoreType.DMA((16,)))

    def send(self, src, chip, n, dev):
        dst = self.buf.at[chip, self.core]
        remote(src, dst, self.s.at[n], self.r.at[chip * 2 + self.core], dev).start()

    def start(self, src):
        chip = chip_at(0, 0)
        for n, dev in enumerate([peer(0, 1), peer(1, 0), peer(3, 0), sibling()]):
            self.send(src, chip, n, dev)

    def wait(self, chip, core):
        ref = self.buf.at[chip, core]
        remote(ref, ref, self.s.at[0], self.r.at[chip * 2 + core], sibling()).wait_recv()

    def hop(self, dy, t):
        chip = chip_at(dy, t)
        self.wait(chip, self.core)
        src = self.buf.at[chip, self.core]
        n, devs = {
            (0, 1): (4, [peer(1, 0), peer(3, 0), sibling()]),
            (3, 0): (7, [peer(1, 0), sibling()]),
            (1, 0): (9, [sibling()]),
            (3, 1): (10, [sibling()]),
            (1, 1): (11, [peer(3, 0), sibling()]),
            (2, 0): (13, [sibling()]),
            (2, 1): (14, [sibling()]),
        }[dy, t]
        for i, dev in enumerate(devs):
            self.send(src, chip, n + i, dev)
        return chip

    def other_core(self, dy, t):
        chip = chip_at(dy, t)
        self.wait(chip, 1 - self.core)

    def drain(self):
        ref = self.buf.at[0, 0]
        for n in range(15):
            remote(ref, ref, self.s.at[n], self.s.at[n], sibling()).wait_send()


HOPS = ((0, 1), (3, 0), (1, 0), (3, 1), (1, 1), (2, 0), (2, 1))


def add_rows(dst, srcs, tile):
    def body(r, carry):
        rr = pl.ds(pl.multiple_of(r * tile, 16), tile)
        total = srcs[0][rr, :].astype(F32)
        for s in srcs[1:]:
            total = total + s[rr, :].astype(F32)
        dst[rr, :] = total.astype(dst.dtype)
        return carry

    lax.fori_loop(0, dst.shape[0] // tile, body, 0)


class Scatter:
    def __init__(self, refs, tile):
        (
            self.to_sib, self.from_sib, self.sums, self.half, self.pairs,
            self.s_sib, self.r_sib, self.s_half, self.r_half, self.s_pair, self.r_pair,
        ) = refs
        self.tile = tile
        self.y, self.z, self.core, m = place()

    @staticmethod
    def scratch(rows, cols):
        dma = pltpu.SemaphoreType.DMA
        eight = pltpu.VMEM((8, rows, cols), BF)
        return (
            eight, eight, eight, pltpu.VMEM((2, rows, cols), BF), pltpu.VMEM((2, 2, rows, cols), BF),
            dma((8,)), dma((8,)), dma((2,)), dma((2,)), dma((2,)), dma((2,)),
        )

    def add(self, dst, srcs):
        add_rows(dst, srcs, self.tile)

    def to_sibling(self, chip):
        remote(
            self.to_sib.at[chip], self.from_sib.at[chip], self.s_sib.at[chip], self.r_sib.at[chip], sibling()
        ).start()

    def merge(self, chip):
        got = self.from_sib.at[chip]
        remote(got, got, self.s_sib.at[0], self.r_sib.at[chip], sibling()).wait_recv()
        self.add(self.sums.at[chip], [self.sums.at[chip], got])

    def far(self):
        for t, dy in ((0, 1), (1, 3)):
            remote(
                self.sums.at[chip_at(2, t)], self.half.at[t], self.s_half.at[t], self.r_half.at[t], peer(dy, 0)
            ).start()

    def near(self, way):
        dy = 1 if way == 0 else 3
        got = self.half.at[way]
        remote(got, got, self.s_half.at[0], self.r_half.at[way], sibling()).wait_recv()
        mid = self.sums.at[chip_at(dy, way)]
        self.add(mid, [mid, got])
        both = self.sums.at[pl.ds(lax.rem(self.y + dy, 4) * 2, 2)]
        remote(both, self.pairs.at[way], self.s_pair.at[way], self.r_pair.at[way], peer(dy, 0)).start()

    def own(self, dst):
        for way in range(2):
            got = self.pairs.at[way]
            remote(got, got, self.s_pair.at[0], self.r_pair.at[way], sibling()).wait_recv()
        for t in (1, 0):
            zz = lax.rem(self.z + t, 2)
            self.add(
                dst.at[t], [self.sums.at[chip_at(0, t)], self.pairs.at[0, zz], self.pairs.at[1, zz]]
            )

    def drain(self):
        one, two = self.sums.at[0], self.pairs.at[0]
        for k in range(8):
            remote(one, one, self.s_sib.at[k], self.s_sib.at[k], sibling()).wait_send()
        for k in range(2):
            remote(one, one, self.s_half.at[k], self.s_half.at[k], sibling()).wait_send()
            remote(two, two, self.s_pair.at[k], self.s_pair.at[k], sibling()).wait_send()


def sds(shape, dtype):
    return jax.ShapeDtypeStruct(shape, dtype)


VMEM_SPEC = pl.BlockSpec(memory_space=pltpu.VMEM)
SMEM_SPEC = pl.BlockSpec(memory_space=pltpu.SMEM)
ANY_SPEC = pl.BlockSpec(memory_space=pl.ANY)
DMA = pltpu.SemaphoreType.DMA
MP_SEMS = (DMA((7,)), DMA((8,)))
PARTS = pltpu.VMEM((8, 64, D), BF)


def params(cid):
    return pltpu.CompilerParams(collective_id=cid, has_side_effects=True, vmem_limit_bytes=VM)


def rolled(x):
    return pltpu.roll(x, 64, axis=1)


def k1_kernel(
    sel, tokens, wq, wk, wv, wo, cosf, sinf, gain_a, gain_m,
    moe, mixed, lse, ot, q, kvall, normed, att,
    tok, w3, wov, st_m, st_l, st_a, parts, land, s_in, g_sems, mp1, mp2,
):
    y, z, core, m = place()
    chip = chip_at(0, 0)
    loads = [
        pltpu.make_async_copy(a, b, s_in.at[i])
        for i, (a, b) in enumerate(
            [(tokens, tok), (wk, w3.at[0]), (wv, w3.at[1]), (wq, w3.at[2]), (wo, wov)]
        )
    ]
    for cp in loads:
        cp.start()
    count = greet()
    loads[0].wait()

    def norm_rows(i, carry):
        rr = pl.ds(pl.multiple_of(i * 128, 128), 128)
        x = tok[rr, :].astype(F32)
        n = lax.rsqrt(jnp.mean(x * x, axis=-1, keepdims=True) + EPSILON)
        normed[rr, :] = (x * n * gain_a[...]).astype(BF)
        return carry

    lax.fori_loop(0, 4, norm_rows, 0)
    own = kvall.at[chip, core]

    def turn(lin, rr, h):
        x = lin[:, h * HD : h * HD + HD]
        return x * cosf[rr, :] + rolled(x) * sinf[rr, :]

    loads[1].wait()
    loads[2].wait()

    def keys_values(n, carry):
        rr = pl.ds(pl.multiple_of(n * 256, 256), 256)
        lin = nn(normed[rr, :], w3[0])
        for h in range(2):
            own[0, n, :, pl.ds(h * HD, HD)] = turn(lin, rr, h).astype(BF)
        own[1, n] = nn(normed[rr, :], w3[1]).astype(BF)
        return carry

    lax.fori_loop(0, 2, keys_values, 0)
    all_in(count)
    gather = Gather(kvall, g_sems)
    gather.start(own)
    loads[3].wait()

    def queries(n, carry):
        rr = pl.ds(pl.multiple_of(n * 256, 256), 256)
        lin = nn(normed[rr, :], w3[2])
        for h in range(2):
            q[n, :, pl.ds(h * HD, HD)] = (turn(lin, rr, h) * (HD**-0.5)).astype(BF)
        return carry

    lax.fori_loop(0, 2, queries, 0)

    st_m[...] = jnp.full_like(st_m, NEG)
    st_l[...] = jnp.zeros_like(st_l)
    st_a[...] = jnp.zeros_like(st_a)

    def online(olds, sts, vs):
        mn = [jnp.maximum(o[0], jnp.max(s, axis=0, keepdims=True)) for o, s in zip(olds, sts)]
        ps = [jnp.exp(s - a) for s, a in zip(sts, mn)]
        al = [jnp.exp(o[0] - a) for o, a in zip(olds, mn)]
        ls = [a * o[1] + jnp.sum(p, axis=0, keepdims=True) for a, o, p in zip(al, olds, ps)]
        ac = [a * o[2] + tn(v, p.astype(BF)) for a, o, v, p in zip(al, olds, vs, ps)]
        return list(zip(mn, ls, ac))

    def keep(n, h, new):
        st_m[n, h], st_l[n, h], st_a[n, h] = new

    def block(k, cr):
        s = sel[k * 2 + cr]
        sts, vs, olds = [], [], []
        for h in range(2):
            cols = pl.ds(h * HD, HD)
            k0, k1 = kvall[k, cr, 0, 0, :, cols], kvall[k, cr, 0, 1, :, cols]
            v0, v1 = kvall[k, cr, 1, 0, :, cols], kvall[k, cr, 1, 1, :, cols]
            sts += [nt(k0, q[1, :, cols]), nt(jnp.where(s == 0, k0, k1), q[s, :, cols])]
            vs += [v0, jnp.where(s == 0, v0, v1)]
            olds.append((st_m[2, h], st_l[2, h], st_a[2, h]))
            olds.append(
                (
                    jnp.where(s == 0, st_m[0, h], st_m[1, h]),
                    jnp.where(s == 0, st_l[0, h], st_l[1, h]),
                    st_a[s, h],
                )
            )
        new = online(olds, sts, vs)
        for h in range(2):
            keep(2, h, new[2 * h])
            b = new[2 * h + 1]
            for n in range(2):
                st_m[n, h] = jnp.where(s == n, b[0], st_m[n, h])
                st_l[n, h] = jnp.where(s == n, b[1], st_l[n, h])
                st_a[n, h] = jnp.where(s == n, b[2], st_a[n, h])

    tri = lax.broadcasted_iota(jnp.int32, (256, 256), 0) <= lax.broadcasted_iota(
        jnp.int32, (256, 256), 1
    )
    for h in range(2):
        cols = pl.ds(h * HD, HD)
        names = [2, 0, 1]
        sts = [nt(own[0, 0, :, cols], q[1, :, cols])]
        sts += [jnp.where(tri, nt(own[0, n, :, cols], q[n, :, cols]), NEG) for n in range(2)]
        vs = [own[1, 0, :, cols], own[1, 0, :, cols], own[1, 1, :, cols]]
        olds = [(st_m[n, h], st_l[n, h], st_a[n, h]) for n in names]
        for n, new in zip(names, online(olds, sts, vs)):
            keep(n, h, new)

    gather.wait(chip, 1 - core)
    block(chip, 1 - core)
    for dy, t in HOPS:
        k = gather.hop(dy, t)

        def cores(i, carry):
            cr = lax.rem(core + i, 2)

            @pl.when(i == 1)
            def _():
                gather.wait(k, cr)

            block(k, cr)
            return carry

        lax.fori_loop(0, 2, cores, 0)

    for h in range(2):
        for n in range(2):
            m0, l0, a0 = st_m[n, h], st_l[n, h], st_a[n, h]
            if n == 1:
                m2, l2, a2 = st_m[2, h], st_l[2, h], st_a[2, h]
                mn = jnp.maximum(m0, m2)
                e0, e2 = jnp.exp(m0 - mn), jnp.exp(m2 - mn)
                m0, l0, a0 = mn, e0 * l0 + e2 * l2, e0 * a0 + e2 * a2
            lse[n, h] = m0 + jnp.log(l0)
            o = a0 / l0
            ot[n, h] = o
            att[pl.ds(n * 256, 256), pl.ds(h * HD, HD)] = jnp.transpose(o).astype(BF)

    loads[4].wait()

    def out_cols(i, carry):
        cols = pl.ds(pl.multiple_of(i * 256, 256), 256)
        parts[:, :, cols] = nn(att[...], wov[:, cols]).reshape(8, 64, 256).astype(BF)
        return carry

    lax.fori_loop(0, 8, out_cols, 0)
    mp_send_parts(parts, land, *mp1)
    total = tok[pl.ds(pl.multiple_of(m * 64, 64), 64), :].astype(F32) + parts[m].astype(F32)
    for d in range(1, 8):
        total = total + land[mp_wait_recv(land, *mp1, d)].astype(F32)
    mixed[...] = total
    n = lax.rsqrt(jnp.mean(total * total, axis=-1, keepdims=True) + EPSILON)
    moe[m] = (total * n * gain_m[...]).astype(BF)
    mp_send_same(moe.at[m], moe, *mp2)

    gather.drain()
    mp_wait_send(parts.at[0], mp1[0])
    for d in range(1, 8):
        mp_wait_recv(moe, *mp2, d)
    mp_wait_send(moe.at[0], mp2[0])


def attention_forward(sel, tokens, wq, wk, wv, wo, cosf, sinf, gain_a, gain_m):
    return pl.pallas_call(
        k1_kernel,
        name="attend_forward",
        out_shape=(
            sds((8, 64, D), BF),
            sds((64, D), F32),
            sds((2, 2, 1, 256), F32),
            sds((2, 2, HD, 256), F32),
            sds((2, 256, 256), BF),
            sds((8, 2, 2, 2, 256, 256), BF),
            sds((512, D), BF),
            sds((512, 256), BF),
        ),
        in_specs=[SMEM_SPEC] + [ANY_SPEC] * 5 + [VMEM_SPEC] * 4,
        out_specs=(VMEM_SPEC,) * 8,
        scratch_shapes=[
            pltpu.VMEM((512, D), BF),
            pltpu.VMEM((3, D, 256), BF),
            pltpu.VMEM((256, D), BF),
            pltpu.VMEM((3, 2, 1, 256), F32),
            pltpu.VMEM((3, 2, 1, 256), F32),
            pltpu.VMEM((3, 2, HD, 256), F32),
            PARTS, PARTS, DMA((5,)), Gather.sems(), MP_SEMS, MP_SEMS,
        ],
        compiler_params=params(1),
    )(sel, tokens, wq, wk, wv, wo, cosf, sinf, gain_a, gain_m)


def swish_parts(g, u):
    s = 1.0 / (1.0 + jnp.exp(-g))
    return s, g * s


def to_column(row):
    return jnp.transpose(jnp.broadcast_to(row, (HD, HD)))[:, 0:1]


def to_row(col):
    return jnp.transpose(jnp.broadcast_to(col, (HD, HD)))[0:1, :]


def k2_kernel(
    ids, moe, mixed, gain, w_router, cot, sg, su, sd, eg, eu, ed,
    g_attn, g_mixed, gain_part, wown, moe_part, g_logits,
    wsg, wsu, wsd, weg, weu, wed, cotv, tb, tbt, pr, gt, ut, hs, gsg, gsu,
    ein, gsl, geo, gated, eo, gein, ge3, ue3, he3, tmp, amat, blk, gate_part, gmi, land, gate_land,
    s_in, rs_refs, mp1, mp2, mp3,
):
    y, z, core, m = place()
    loads = [
        pltpu.make_async_copy(a, b, s_in.at[i])
        for i, (a, b) in enumerate(
            [(sg, wsg), (su, wsu), (eg, weg), (eu, weu), (ed, wed), (sd, wsd), (cot, cotv)]
        )
    ]
    for cp in loads:
        cp.start()
    count = greet()

    slot = lax.broadcasted_iota(jnp.int32, (HD, 512), 0)
    holder = lax.div(slot, CAP)
    chosen = holder == ids[0:1, :]
    for k in range(1, 6):
        chosen = chosen | (holder == ids[k : k + 1, :])
    chosen = jnp.where(chosen & (slot < 3 * CAP), 1.0, 0.0)
    upto = lax.broadcasted_iota(jnp.int32, (512, 512), 0) <= lax.broadcasted_iota(
        jnp.int32, (512, 512), 1
    )
    place_of = nn(chosen.astype(BF), jnp.where(upto, 1.0, 0.0).astype(BF)) - 1.0
    table_t = jnp.where(place_of == lax.rem(slot, CAP).astype(F32), chosen, 0.0)
    tbt[...] = table_t.astype(BF)
    table = jnp.transpose(table_t)
    tb[...] = table.astype(BF)
    expert = lax.div(lax.broadcasted_iota(jnp.int32, (512, HD), 1), CAP)

    logits = nt(moe[...], w_router[...])
    e = jnp.exp(logits - jnp.max(logits, axis=-1, keepdims=True))
    probs = e / jnp.sum(e, axis=-1, keepdims=True)
    pr[...] = probs
    px = jnp.where(expert == 0, probs[:, 0:1], jnp.where(expert == 1, probs[:, 1:2], probs[:, 2:3]))
    gate_col = to_column(jnp.sum(table * px, axis=0, keepdims=True))

    hs[...] = jnp.zeros_like(hs)
    gsg[...] = jnp.zeros_like(gsg)
    gsu[...] = jnp.zeros_like(gsu)
    eo[...] = jnp.zeros_like(eo)
    gein[...] = jnp.zeros_like(gein)
    tmp[...] = jnp.zeros_like(tmp)

    def gather_in(i, carry):
        cols = pl.ds(pl.multiple_of(i * 512, 512), 512)
        ein[:, cols] = nn(tbt[...], moe[:, cols]).astype(BF)
        return carry

    lax.fori_loop(0, 4, gather_in, 0)
    loads[0].wait()
    loads[1].wait()

    def shared_in(i, carry):
        rr = pl.ds(pl.multiple_of(i * 256, 256), 256)
        g, u = nt(moe[rr, :], wsg[...]), nt(moe[rr, :], wsu[...])
        gt[rr, :] = g
        ut[rr, :] = u
        hs[rr, 0:SH] = (swish_parts(g, u)[1] * u).astype(BF)
        return carry

    lax.fori_loop(0, 2, shared_in, 0)
    for cp in loads[2:5]:
        cp.wait()
    for k in range(3):
        rr = pl.ds(k * CAP, CAP)
        g, u = nt(ein[rr, :], weg[k]), nt(ein[rr, :], weu[k])
        ge3[k] = g
        ue3[k] = u
        hid = (swish_parts(g, u)[1] * u).astype(BF)
        he3[k] = hid
        eo[rr, :] = nn(hid, wed[k])
    loads[5].wait()
    loads[6].wait()

    def slots_in(i, carry):
        cols = pl.ds(pl.multiple_of(i * 512, 512), 512)
        g = nn(tbt[...], cotv[:, cols])
        gsl[:, cols] = g.astype(BF)
        geo[:, cols] = (gate_col * g).astype(BF)
        gated[:, cols] = (gate_col * eo[:, cols]).astype(BF)
        return carry

    lax.fori_loop(0, 4, slots_in, 0)
    gate_part[...] = to_row(jnp.sum(eo[...] * gsl[...].astype(F32), axis=1, keepdims=True))
    all_in(count)
    mp_send_same(gate_part, gate_land, *mp1)

    def shared_back(i, carry):
        rr = pl.ds(pl.multiple_of(i * 256, 256), 256)
        gh = nt(cotv[rr, :], wsd[...])
        g, u = gt[rr, :], ut[rr, :]
        s, sw = swish_parts(g, u)
        gsg[rr, 0:SH] = (gh * u * s * (1.0 + g * (1.0 - s))).astype(BF)
        gsu[rr, 0:SH] = (gh * sw).astype(BF)
        return carry

    lax.fori_loop(0, 2, shared_back, 0)

    def put_block(i, k, val):
        rr = pl.ds(k * CAP, CAP)
        tmp[k, rr, 0:EF] = val.astype(F32)
        blk[pl.ds(EF * i, EF), :] = jnp.transpose(tmp[k])[0:EF].astype(BF)

    for k in range(3):
        rr = pl.ds(k * CAP, CAP)
        gh = nt(geo[rr, :], wed[k])
        g, u = ge3[k], ue3[k]
        s, sw = swish_parts(g, u)
        geg = (gh * u * s * (1.0 + g * (1.0 - s))).astype(BF)
        geu = (gh * sw).astype(BF)
        gein[rr, :] = (nn(geg, weg[k]) + nn(geu, weu[k])).astype(BF)
        put_block(k, k, geg)
        put_block(3 + k, k, geu)
        put_block(6 + k, k, he3[k])

    def back_cols(i, carry):
        cols = pl.ds(pl.multiple_of(i * 256, 256), 256)
        g = nn(gsg[:, 0:SH], wsg[:, cols]) + nn(gsu[:, 0:SH], wsu[:, cols]) + nn(tb[...], gein[:, cols])
        gmi[:, :, cols] = g.reshape(8, 64, 256).astype(BF)
        return carry

    lax.fori_loop(0, 8, back_cols, 0)
    mp_send_parts(gmi, land, *mp2)

    amat[pl.ds(0, SH), :] = turned(gsg[...])[0:SH]
    amat[pl.ds(SH, SH), :] = turned(gsu[...])[0:SH]
    amat[pl.ds(2 * SH, SH), :] = turned(hs[...])[0:SH]
    rs = Scatter(rs_refs, 528)

    def piece(k):
        cols = pl.ds(pl.multiple_of(k * 256, 256), 256)
        for off, rows, lhs, rhs in (
            (0, 2 * SH, amat.at[pl.ds(0, 2 * SH)], moe),
            (2 * SH, SH, amat.at[pl.ds(2 * SH, SH)], cotv),
            (3 * SH, 6 * EF, blk.at[pl.ds(0, 6 * EF)], ein),
            (3 * SH + 6 * EF, 3 * EF, blk.at[pl.ds(6 * EF, 3 * EF)], geo),
        ):
            val = nn(lhs[...], rhs[:, cols]).astype(BF)
            one, two = val[:, 0:HD], val[:, HD:]
            rs.sums[k, pl.ds(off, rows), :] = jnp.where(core == 0, one, two)
            rs.to_sib[k, pl.ds(off, rows), :] = jnp.where(core == 0, two, one)
        rs.to_sibling(k)

    def pieces(i, carry):
        j = lax.div(i, 2)
        dy = lax.rem(2 - j + 3 * lax.div(j * (j - 1), 2), 4)
        piece(chip_at(dy, lax.rem(i, 2)))

        @pl.when(i == 2)
        def _():
            rs.merge(chip_at(2, 0))
            rs.merge(chip_at(2, 1))
            rs.far()

        return carry

    lax.fori_loop(0, 8, pieces, 0)

    def out_cols(i, carry):
        cols = pl.ds(pl.multiple_of(i * 256, 256), 256)
        o = nn(hs[:, 0:SH], wsd[:, cols]) + nn(tb[...], gated[:, cols])
        moe_part[:, :, cols] = o.reshape(8, 64, 256).astype(BF)
        return carry

    lax.fori_loop(0, 8, out_cols, 0)

    gate = gate_part[...]
    for d in range(1, 8):
        gate = gate + gate_land[mp_wait_recv(gate_land, *mp1, d)]
    lane2 = lax.broadcasted_iota(jnp.int32, (HD, 64), 0)
    col2 = lax.broadcasted_iota(jnp.int32, (HD, 64), 1)
    member = jnp.where((lax.div(lane2, CAP) == col2) & (col2 < 3), 1.0, 0.0)
    gate_probs = lax.dot_general(
        tb[...].astype(F32) * gate, member, (((1,), (0,)), ((), ())),
        precision=PRECISE, preferred_element_type=F32,
    )
    prob = pr[...]
    g_logits[...] = (prob * (gate_probs - jnp.sum(gate_probs * prob, axis=-1, keepdims=True))).astype(BF)

    for way, dy in ((0, 1), (1, 3)):
        rs.merge(chip_at(dy, 0))
        rs.merge(chip_at(dy, 1))
        rs.near(way)
    rs.merge(chip_at(0, 1))
    rs.merge(chip_at(0, 0))

    mine = pl.ds(pl.multiple_of(m * 64, 64), 64)
    total = nn(g_logits[mine, :], w_router[...]) + gmi[m].astype(F32)
    for d in range(1, 8):
        total = total + land[mp_wait_recv(land, *mp2, d)].astype(F32)
    mx = mixed[...]
    n = lax.rsqrt(jnp.mean(mx * mx, axis=-1, keepdims=True) + EPSILON)
    gain_part[...] = jnp.sum(total * mx * n, axis=0, keepdims=True)
    gg = total * gain[...]
    gm = cotv[mine, :].astype(F32) + n * gg
    gm = gm - mx * (n * n * n) * jnp.mean(gg * mx, axis=-1, keepdims=True)
    g_mixed[...] = gm
    g_attn[m] = gm.astype(BF)
    mp_send_same(g_attn.at[m], g_attn, *mp3)

    rs.own(wown)
    rs.drain()
    mp_wait_send(gmi.at[0], mp2[0])
    mp_wait_send(gate_part, mp1[0])
    for d in range(1, 8):
        mp_wait_recv(g_attn, *mp3, d)
    mp_wait_send(g_attn.at[0], mp3[0])


def experts(ids, moe, mixed, gain, w_router, cot, sg, su, sd, eg, eu, ed):
    vm = pltpu.VMEM
    return pl.pallas_call(
        k2_kernel,
        name="experts",
        out_shape=(
            sds((8, 64, D), BF),
            sds((64, D), F32),
            sds((1, D), F32),
            sds((2, R1, HD), BF),
            sds((8, 64, D), BF),
            sds((512, 64), BF),
        ),
        in_specs=[VMEM_SPEC] * 5 + [ANY_SPEC] * 7,
        out_specs=(VMEM_SPEC,) * 6,
        scratch_shapes=[
            vm((SH, D), BF), vm((SH, D), BF), vm((SH, D), BF),
            vm((3, EF, D), BF), vm((3, EF, D), BF), vm((3, EF, D), BF),
            vm((512, D), BF), vm((512, HD), BF), vm((HD, 512), BF), vm((512, 64), F32),
            vm((512, SH), F32), vm((512, SH), F32),
            vm((512, 384), BF), vm((512, 384), BF), vm((512, 384), BF),
            vm((HD, D), BF), vm((HD, D), BF), vm((HD, D), BF), vm((HD, D), BF),
            vm((HD, D), F32), vm((HD, D), BF),
            vm((3, CAP, EF), F32), vm((3, CAP, EF), F32), vm((3, CAP, EF), BF),
            vm((3, HD, 256), F32), vm((3 * SH, 512), BF), vm((9 * EF, HD), BF),
            vm((1, HD), F32), PARTS, PARTS, vm((8, 1, HD), F32),
            DMA((7,)), Scatter.scratch(R1, HD), MP_SEMS, MP_SEMS, MP_SEMS,
        ],
        compiler_params=params(2),
    )(ids, moe, mixed, gain, w_router, cot, sg, su, sd, eg, eu, ed)


def k3_kernel(
    sel, q, kvall, lse, ot, g_attn, wout, moe_part, mixed, wown, cosf, sinf,
    output, w1, glin,
    do, delta, dqt, oland, zbuf, fin, dkz, dkv,
    s_loc, s_z, r_z, s_z2, r_z2, g_sems, rs_refs, mp1, mp2,
):
    y, z, core, m = place()
    chip = chip_at(0, 0)
    count = greet()
    g_att = nt(g_attn[...], wout[...])
    for n in range(2):
        for h in range(2):
            piece = g_att[n * 256 : n * 256 + 256, h * HD : h * HD + HD].astype(BF)
            do[n, h] = piece
            delta[n, h] = jnp.sum(jnp.transpose(piece.astype(F32)) * ot[n, h], axis=0, keepdims=True)
    dqt[...] = jnp.zeros_like(dqt)
    all_in(count)
    mp_send_parts(moe_part, oland, *mp1)
    remote(wown.at[1], zbuf, s_z, r_z, peer(0, 1)).start()
    rs = Scatter(rs_refs, 256)
    gather = Gather(w1, g_sems)

    def terms(items):
        ps = [nt(k, qq) - ls for k, v, qq, dd, ls, de, mask in items]
        ps = [jnp.exp(p) for p in ps]
        ps = [p if i[6] is None else jnp.where(i[6], p, 0.0) for p, i in zip(ps, items)]
        ds = [(p * (nt(i[1], i[3]) - i[5])).astype(BF) for p, i in zip(ps, items)]
        dv = [nn(p.astype(BF), i[3]) for p, i in zip(ps, items)]
        dk = [nn(d, i[2]) for d, i in zip(ds, items)]
        dq = [tn(i[0], d) for d, i in zip(ds, items)]
        return list(zip(dk, dv, dq))

    def block(k, cr, dst):
        s = sel[k * 2 + cr]
        items = []
        for h in range(2):
            cols = pl.ds(h * HD, HD)
            items.append(
                (kvall[k, cr, 0, 0, :, cols], kvall[k, cr, 1, 0, :, cols], q[1, :, cols], do[1, h],
                 lse[1, h], delta[1, h], None)
            )
            items.append(
                (kvall[k, cr, 0, s, :, cols], kvall[k, cr, 1, s, :, cols], q[s, :, cols], do[s, h],
                 jnp.where(s == 0, lse[0, h], lse[1, h]), jnp.where(s == 0, delta[0, h], delta[1, h]), None)
            )
        got = terms(items)
        for h in range(2):
            cols = pl.ds(h * HD, HD)
            always, picked = got[2 * h], got[2 * h + 1]
            dqt[2, h] += always[2]
            for n in range(2):
                dqt[n, h] += jnp.where(s == n, picked[2], 0.0)
            for a in range(2):
                low = always[a] + jnp.where(s == 0, picked[a], 0.0)
                high = jnp.where(s == 1, picked[a], 0.0)
                dst[pl.ds(a * 512, 256), cols] = low.astype(BF)
                dst[pl.ds(a * 512 + 256, 256), cols] = high.astype(BF)

    def both_cores(k):
        block(k, 1 - core, rs.to_sib.at[k])
        rs.to_sibling(k)
        block(k, core, rs.sums.at[k])

    def ring_place(dy):
        def one(t, carry):
            both_cores(chip_at(dy, t))
            return carry

        lax.fori_loop(0, 2, one, 0)
        rs.merge(chip_at(dy, 0))
        rs.merge(chip_at(dy, 1))

    ring_place(2)
    rs.far()
    ring_place(1)
    rs.near(0)
    ring_place(3)
    rs.near(1)

    remote(zbuf, zbuf, s_z, r_z, peer(0, 1)).wait_recv()
    add_rows(fin, [wown.at[0], zbuf], 528)
    gather.start(fin)
    local = pltpu.make_async_copy(fin, w1.at[chip, core], s_loc)
    local.start()

    both_cores(chip_at(0, 1))
    block(chip, 1 - core, rs.to_sib.at[chip])
    rs.to_sibling(chip)
    tri = lax.broadcasted_iota(jnp.int32, (256, 256), 0) <= lax.broadcasted_iota(
        jnp.int32, (256, 256), 1
    )
    for h in range(2):
        cols = pl.ds(h * HD, HD)
        kk = [kvall[chip, core, 0, n, :, cols] for n in range(2)]
        vv = [kvall[chip, core, 1, n, :, cols] for n in range(2)]
        items = [(kk[0], vv[0], q[1, :, cols], do[1, h], lse[1, h], delta[1, h], None)]
        for n in range(2):
            items.append((kk[n], vv[n], q[n, :, cols], do[n, h], lse[n, h], delta[n, h], tri))
        got = terms(items)
        dqt[2, h] += got[0][2]
        for n in range(2):
            dqt[n, h] += got[1 + n][2]
        for a in range(2):
            rs.sums[chip, pl.ds(a * 512, 256), cols] = (got[0][a] + got[1][a]).astype(BF)
            rs.sums[chip, pl.ds(a * 512 + 256, 256), cols] = got[2][a].astype(BF)
    rs.merge(chip_at(0, 1))
    rs.merge(chip)

    def back(x, rr):
        return (x * cosf[rr, :] - rolled(x) * sinf[rr, :]).astype(BF)

    for h in range(2):
        for n in range(2):
            rr = pl.ds(n * 256, 256)
            g = dqt[n, h] if n == 0 else dqt[1, h] + dqt[2, h]
            glin[0, rr, pl.ds(h * HD, HD)] = back(jnp.transpose(g) * (HD**-0.5), rr)

    total = mixed[...] + moe_part[m].astype(F32)
    for d in range(1, 8):
        total = total + oland[mp_wait_recv(oland, *mp1, d)].astype(F32)
    output[m] = total.astype(BF)
    mp_send_same(output.at[m], output, *mp2)

    gather.hop(0, 1)
    gather.hop(3, 0)
    gather.hop(1, 0)
    rs.own(dkz)
    remote(dkz.at[1], dkv, s_z2, r_z2, peer(0, 1)).start()
    remote(dkv, dkv, s_z2, r_z2, peer(0, 1)).wait_recv()
    for n in range(2):
        rr = pl.ds(n * 256, 256)
        for h in range(2):
            cols = pl.ds(h * HD, HD)
            kr = pl.ds(n * 256, 256)
            vr = pl.ds(512 + n * 256, 256)
            g = dkz[0, kr, cols].astype(F32) + dkv[kr, cols].astype(F32)
            glin[1, rr, cols] = back(g, rr)
            glin[2, rr, cols] = (dkz[0, vr, cols].astype(F32) + dkv[vr, cols].astype(F32)).astype(BF)
    for dy, t in HOPS[3:]:
        gather.hop(dy, t)

    remote(dkv, dkv, s_z2, s_z2, peer(0, 1)).wait_send()
    remote(zbuf, zbuf, s_z, s_z, peer(0, 1)).wait_send()
    rs.drain()
    mp_wait_send(moe_part.at[0], mp1[0])
    for d in range(1, 8):
        mp_wait_recv(output, *mp2, d)
    mp_wait_send(output.at[0], mp2[0])
    local.wait()
    gather.wait(chip, 1 - core)
    for dy, t in HOPS:
        gather.other_core(dy, t)
    gather.drain()


def attention_backward(sel, q, kvall, lse, ot, g_attn, wout, moe_part, mixed, wown, cosf, sinf):
    vm = pltpu.VMEM
    return pl.pallas_call(
        k3_kernel,
        name="attend_backward",
        out_shape=(sds((8, 64, D), BF), sds((8, 2, R1, HD), BF), sds((3, 512, 256), BF)),
        in_specs=[SMEM_SPEC] + [VMEM_SPEC] * 11,
        out_specs=(VMEM_SPEC, ANY_SPEC, VMEM_SPEC),
        scratch_shapes=[
            vm((2, 2, 256, HD), BF), vm((2, 2, 1, 256), F32), vm((3, 2, HD, 256), F32),
            PARTS, vm((R1, HD), BF), vm((R1, HD), BF), vm((2, 1024, 256), BF), vm((1024, 256), BF),
            DMA, DMA, DMA, DMA, DMA, Gather.sems(), Scatter.scratch(1024, 256), MP_SEMS, MP_SEMS,
        ],
        compiler_params=params(3),
    )(sel, q, kvall, lse, ot, g_attn, wout, moe_part, mixed, wown, cosf, sinf)


def k4_kernel(
    glin, att, g_attn, g_logits, moe, normed, g_mixed, gain, gain_moe_part, tokens, wq, wk, wv,
    g_tokens, w2out, gains,
    tok, w3, amat, gni, land, zbuf, fin, wown, gmine, gland, gsteps, gfar,
    s_in, s_loc, s_z, r_z, s_gx, r_gx, s_gy, r_gy, g_sems, rs_refs, mp1, mp2, mp3,
):
    y, z, core, m = place()
    chip = chip_at(0, 0)
    loads = [
        pltpu.make_async_copy(a, w3.at[i], s_in.at[i]) for i, a in enumerate((wq, wk, wv))
    ]
    mine = pl.ds(pl.multiple_of(m * 64, 64), 64)
    loads.append(pltpu.make_async_copy(tokens.at[mine, :], tok, s_in.at[3]))
    for cp in loads:
        cp.start()
    count = greet(far=True)
    for cp in loads:
        cp.wait()

    def back_cols(i, carry):
        cols = pl.ds(pl.multiple_of(i * 256, 256), 256)
        g = nt(glin[0], w3[0, cols, :]) + nt(glin[1], w3[1, cols, :]) + nt(glin[2], w3[2, cols, :])
        gni[:, :, cols] = g.reshape(8, 64, 256).astype(BF)
        return carry

    lax.fori_loop(0, 8, back_cols, 0)
    all_in(count)
    mp_send_parts(gni, land, *mp1)

    amat[pl.ds(0, 64), :] = turned(g_logits[...])
    for i in range(3):
        amat[pl.ds(64 + 256 * i, 256), :] = turned(glin[i])
    amat[pl.ds(832, 256), :] = turned(att[...])
    rs = Scatter(rs_refs, 544)

    def piece(k):
        cols = pl.ds(pl.multiple_of(k * 256, 256), 256)
        for off, rows, rhs in ((0, 64, moe), (64, 768, normed), (832, 256, g_attn)):
            val = nn(amat[pl.ds(off, rows), :], rhs[:, cols]).astype(BF)
            one, two = val[:, 0:HD], val[:, HD:]
            rs.sums[k, pl.ds(off, rows), :] = jnp.where(core == 0, one, two)
            rs.to_sib[k, pl.ds(off, rows), :] = jnp.where(core == 0, two, one)
        rs.to_sibling(k)

    def pieces(i, carry):
        j = lax.div(i, 2)
        dy = lax.rem(2 - j + 3 * lax.div(j * (j - 1), 2), 4)
        piece(chip_at(dy, lax.rem(i, 2)))

        @pl.when(i == 2)
        def _():
            rs.merge(chip_at(2, 0))
            rs.merge(chip_at(2, 1))
            rs.far()

        return carry

    lax.fori_loop(0, 8, pieces, 0)
    for way, dy in ((0, 1), (1, 3)):
        rs.merge(chip_at(dy, 0))
        rs.merge(chip_at(dy, 1))
        rs.near(way)
    rs.merge(chip_at(0, 1))
    rs.merge(chip_at(0, 0))

    total = gni[m].astype(F32)
    for d in range(1, 8):
        total = total + land[mp_wait_recv(land, *mp1, d)].astype(F32)
    src = tok[...].astype(F32)
    n = lax.rsqrt(jnp.mean(src * src, axis=-1, keepdims=True) + EPSILON)
    gg = total * gain[...]
    gs = n * gg - src * (n * n * n) * jnp.mean(gg * src, axis=-1, keepdims=True)
    g_tokens[m] = (g_mixed[...] + gs).astype(BF)
    mp_send_same(g_tokens.at[m], g_tokens, *mp2)
    gmine[pl.ds(0, 1), :] = gain_moe_part[...]
    gmine[pl.ds(1, 1), :] = jnp.sum(total * src * n, axis=0, keepdims=True)
    mp_send_same(gmine, gland, *mp3)

    rs.own(wown)
    remote(wown.at[1], zbuf, s_z, r_z, peer(0, 1)).start()

    gsum = gmine[...]
    for d in range(1, 8):
        gsum = gsum + gland[mp_wait_recv(gland, *mp3, d)]
    for i, dev in enumerate((sibling(), peer(0, 1))):
        gsteps[2 * i] = gsum
        cp = remote(gsteps.at[2 * i], gsteps.at[2 * i + 1], s_gx.at[i], r_gx.at[i], dev)
        cp.start()
        cp.wait_recv()
        gsum = gsum + gsteps[2 * i + 1]
    gfar[y] = gsum
    for d in range(1, 4):
        remote(gfar.at[y], gfar.at[y], s_gy.at[d - 1], r_gy.at[y], peer(d, 0)).start()

    remote(zbuf, zbuf, s_z, r_z, peer(0, 1)).wait_recv()
    add_rows(fin, [wown.at[0], zbuf], 544)
    gather = Gather(w2out, g_sems)
    gather.start(fin)
    local = pltpu.make_async_copy(fin, w2out.at[chip, core], s_loc)
    local.start()

    for d in range(1, 4):
        yy = lax.rem(y + d, 4)
        remote(gfar.at[yy], gfar.at[yy], s_gy.at[0], r_gy.at[yy], peer(d, 0)).wait_recv()
    gains[...] = gfar[0] + gfar[1] + gfar[2] + gfar[3]

    for dy, t in HOPS:
        gather.hop(dy, t)
    for i, dev in enumerate((sibling(), peer(0, 1))):
        remote(gsteps.at[0], gsteps.at[0], s_gx.at[i], s_gx.at[i], dev).wait_send()
    for d in range(1, 4):
        remote(gfar.at[0], gfar.at[0], s_gy.at[d - 1], s_gy.at[d - 1], peer(d, 0)).wait_send()
    remote(zbuf, zbuf, s_z, s_z, peer(0, 1)).wait_send()
    rs.drain()
    mp_wait_send(gmine, mp3[0])
    mp_wait_send(gni.at[0], mp1[0])
    for d in range(1, 8):
        mp_wait_recv(g_tokens, *mp2, d)
    mp_wait_send(g_tokens.at[0], mp2[0])
    local.wait()
    gather.wait(chip, 1 - core)
    for dy, t in HOPS:
        gather.other_core(dy, t)
    gather.drain()


def first_norm_backward(*args):
    vm = pltpu.VMEM
    return pl.pallas_call(
        k4_kernel,
        name="first_norm_backward",
        out_shape=(sds((8, 64, D), BF), sds((8, 2, R2, HD), BF), sds((2, D), F32)),
        in_specs=[VMEM_SPEC] * 9 + [ANY_SPEC] * 4,
        out_specs=(VMEM_SPEC, ANY_SPEC, VMEM_SPEC),
        scratch_shapes=[
            vm((64, D), BF), vm((3, D, 256), BF), vm((R2, 512), BF), PARTS, PARTS, vm((R2, HD), BF), vm((R2, HD), BF),
            vm((2, R2, HD), BF), vm((2, D), F32), vm((8, 2, D), F32), vm((4, 2, D), F32), vm((4, 2, D), F32),
            DMA((4,)), DMA, DMA, DMA, DMA((2,)), DMA((2,)), DMA((3,)), DMA((4,)),
            Gather.sems(), Scatter.scratch(R2, HD), MP_SEMS, MP_SEMS, MP_SEMS,
        ],
        compiler_params=params(4),
    )(*args)


def widen_kernel(w1, w2, gq, gk, gv, go, gr, sg, su, sd, eg, eu, ed):
    def flip(src, off):
        return jnp.transpose(src[0, 0, pl.ds(off, 256), :].astype(F32))

    gr[...] = w2[0, 0, pl.ds(0, 64), :].astype(F32)
    gq[...] = flip(w2, 64)
    gk[...] = flip(w2, 320)
    gv[...] = flip(w2, 576)
    go[...] = w2[0, 0, pl.ds(832, 256), :].astype(F32)
    sg[...] = w1[0, 0, pl.ds(0, SH), :].astype(F32)
    su[...] = w1[0, 0, pl.ds(SH, SH), :].astype(F32)
    sd[...] = w1[0, 0, pl.ds(2 * SH, SH), :].astype(F32)
    for k in range(3):
        eg[k] = w1[0, 0, pl.ds(3 * SH + EF * k, EF), :].astype(F32)
        eu[k] = w1[0, 0, pl.ds(3 * SH + EF * (3 + k), EF), :].astype(F32)
        ed[k] = w1[0, 0, pl.ds(3 * SH + EF * (6 + k), EF), :].astype(F32)


def widen(w1, w2):
    def rows(width):
        return sds((D, width), F32), pl.BlockSpec((HD, width), lambda i: (i, 0))

    def cols(height):
        return sds((height, D), F32), pl.BlockSpec((height, HD), lambda i: (0, i))

    three = sds((3, EF, D), F32), pl.BlockSpec((3, EF, HD), lambda i: (0, 0, i))
    outs = [rows(256), rows(256), rows(256), cols(256), cols(64), cols(SH), cols(SH), cols(SH)]
    outs += [three, three, three]
    return pl.pallas_call(
        widen_kernel,
        name="widen",
        grid=(16,),
        out_shape=[o[0] for o in outs],
        in_specs=[
            pl.BlockSpec((1, 1, R1, HD), lambda i: (i // 2, i % 2, 0, 0)),
            pl.BlockSpec((1, 1, R2, HD), lambda i: (i // 2, i % 2, 0, 0)),
        ],
        out_specs=[o[1] for o in outs],
        compiler_params=pltpu.CompilerParams(vmem_limit_bytes=VM),
    )(w1, w2)


def on_device(
    tokens, cotangent, gain_attn, w_query, w_key, w_value, w_out, gain_moe, w_router,
    shared_gate, shared_up, shared_down, expert_gate, expert_up, expert_down, expert_ids, pair_order,
):
    rows = tokens.shape[0]
    member = lax.axis_index("ctx")
    pair = lax.dynamic_index_in_dim(pair_order, member, keepdims=False)
    within = jnp.arange(rows, dtype=jnp.int32)
    pos = jnp.where(within < 256, pair * 256 + within, (31 - pair) * 256 + within - 256)
    inverse = ROPE_BASE ** (-2.0 * jnp.arange(HD // 2, dtype=F32) / HD)
    phase = pos.astype(F32)[:, None] * jnp.concatenate([inverse, inverse])[None, :]
    sign = jnp.where(jnp.arange(HD) < HD // 2, -1.0, 1.0).astype(F32)
    cosf = jnp.cos(phase)
    sinf = jnp.sin(phase) * sign[None, :]
    sel = jnp.where(pair_order < pair, 0, 1).astype(jnp.int32)

    moe, mixed, lse, ot, q, kvall, normed, att = attention_forward(
        sel, tokens, w_query, w_key, w_value, w_out, cosf, sinf, gain_attn[None], gain_moe[None]
    )
    moe = moe.reshape(rows, D)
    g_attn, g_mixed, gain_moe_part, wown, moe_part, g_logits = experts(
        expert_ids.T, moe, mixed, gain_moe[None], w_router.T, cotangent, shared_gate.T, shared_up.T, shared_down,
        expert_gate.transpose(0, 2, 1), expert_up.transpose(0, 2, 1), expert_down,
    )
    g_attn = g_attn.reshape(rows, D)
    output, w1, glin = attention_backward(
        sel, q, kvall, lse, ot, g_attn, w_out, moe_part, mixed, wown, cosf, sinf
    )
    g_tokens, w2, gains = first_norm_backward(
        glin, att, g_attn, g_logits, moe, normed, g_mixed, gain_attn[None], gain_moe_part,
        tokens, w_query, w_key, w_value,
    )
    gq, gk, gv, go, gr, sg, su, sd, eg, eu, ed = widen(w1, w2)
    return (
        output.reshape(rows, D), g_tokens.reshape(rows, D), gains[1],
        gq, gk, gv, go, gains[0], gr.T, sg.T, su.T, sd, eg.transpose(0, 2, 1), eu.transpose(0, 2, 1), ed,
    )


def solution(mesh):
    in_specs = (
        P("ctx", None), P("ctx", None), P(), P(None, "mp"), P(None, "mp"), P(None, "mp"),
        P("mp", None), P(), P(), P(None, "mp"), P(None, "mp"), P("mp", None),
        P(None, None, "mp"), P(None, None, "mp"), P(None, "mp", None), P("ctx", None), P(),
    )
    out_specs = (
        P("ctx", None), P("ctx", None), P(), P(None, "mp"), P(None, "mp"), P(None, "mp"),
        P("mp", None), P(), P(), P(None, "mp"), P(None, "mp"), P("mp", None),
        P(None, None, "mp"), P(None, None, "mp"), P(None, "mp", None),
    )
    return jax.shard_map(
        on_device, mesh=mesh, in_specs=in_specs, out_specs=out_specs, check_vma=False
    )
```

```python
import jax
import jax.numpy as jnp
from jax import lax
from jax.experimental import pallas as pl
from jax.experimental.pallas import tpu as pltpu
from jax.sharding import PartitionSpec as P

HD = 128
CAP = 32
EPSILON = 1e-06
ROPE_BASE = 10000.0
PRECISE = lax.Precision.HIGHEST
MESH = pl.DeviceIdType.MESH
BF = jnp.bfloat16
F32 = jnp.float32
D = 2048
SH = 352
EF = 176
R1 = 3 * SH + 9 * EF
RA = 3 * SH
R2 = 64 + 4 * 256
VM = 60 * 2**20
NEG = -1e30


def nt(a, b):
    return lax.dot_general(a, b, (((1,), (1,)), ((), ())), preferred_element_type=F32)


def nn(a, b):
    return lax.dot_general(a, b, (((1,), (0,)), ((), ())), preferred_element_type=F32)


def tn(a, b):
    return lax.dot_general(a, b, (((0,), (0,)), ((), ())), preferred_element_type=F32)


def turned(a):
    return jnp.transpose(a.astype(F32)).astype(BF)


def place():
    c = lax.axis_index("ctx")
    return lax.div(c, 4), lax.rem(lax.div(c, 2), 2), lax.rem(c, 2), lax.axis_index("mp")


def chip_at(dy, t):
    y, z, core, m = place()
    return lax.rem(y + dy, 4) * 2 + lax.rem(z + t, 2)


def peer(dy, t):
    y, z, core, m = place()
    return {"ctx": chip_at(dy, t) * 2 + core}


def sibling():
    y, z, core, m = place()
    return {"ctx": chip_at(0, 0) * 2 + 1 - core}


def mp_at(d):
    m = lax.axis_index("mp")
    return lax.rem(lax.div(m, 2) + d // 2, 4) * 2 + lax.rem(lax.rem(m, 2) + d % 2, 2)


def remote(src, dst, ssem, rsem, dev):
    return pltpu.make_async_remote_copy(
        src_ref=src, dst_ref=dst, send_sem=ssem, recv_sem=rsem, device_id=dev, device_id_type=MESH
    )


def greet(far=False):
    bar = pltpu.get_barrier_semaphore()
    devs = [sibling(), peer(0, 1), peer(1, 0), peer(3, 0)] + ([peer(2, 0)] if far else [])
    devs += [{"mp": mp_at(d)} for d in range(1, 8)]
    for dev in devs:
        pl.semaphore_signal(bar, inc=1, device_id=dev, device_id_type=MESH)
    return len(devs)


def all_in(count):
    pl.semaphore_wait(pltpu.get_barrier_semaphore(), count)


def mp_send_same(src, landing, ssem, rsem):
    m = lax.axis_index("mp")
    for d in range(1, 8):
        remote(src, landing.at[m], ssem.at[d - 1], rsem.at[m], {"mp": mp_at(d)}).start()


def mp_wait_recv(landing, ssem, rsem, d):
    t = mp_at(d)
    remote(landing.at[t], landing.at[t], ssem.at[0], rsem.at[t], {"mp": t}).wait_recv()
    return t


def mp_wait_send(src, ssem):
    for d in range(1, 8):
        remote(src, src, ssem.at[d - 1], ssem.at[d - 1], {"mp": mp_at(d)}).wait_send()


def mp_place():
    m = lax.axis_index("mp")
    return lax.div(m, 2), lax.rem(m, 2)


def x_peer(dx):
    x, zh = mp_place()
    return {"mp": lax.rem(x + dx, 4) * 2 + zh}


def zh_peer():
    x, zh = mp_place()
    return {"mp": x * 2 + 1 - zh}


class MpSum:
    def __init__(self, parts, refs, ca):
        self.parts, self.ca = parts, ca
        self.xa, self.za, self.zb, self.xs, self.xr, self.s, self.r = refs
        self.x, self.zh = mp_place()
        self.a, self.b = pl.ds(0, ca), pl.ds(ca, D - ca)

    @staticmethod
    def scratch(ca):
        cb, vm = D - ca, pltpu.VMEM
        return (
            vm((3, 2, 64, ca), BF), vm((2, 64, ca), BF), vm((4, 64, cb), BF),
            vm((3, 64, cb), BF), vm((3, 64, cb), BF),
            pltpu.SemaphoreType.DMA((11,)), pltpu.SemaphoreType.DMA((11,)),
        )

    def copy(self, n, src, dst, dev):
        return remote(src, dst, self.s.at[n], self.r.at[n], dev)

    def a_copy(self, dx):
        far = lax.rem(self.x + dx, 4)
        src = self.parts.at[pl.ds(far * 2, 2), :, self.a]
        return self.copy(dx - 1, src, self.xa.at[dx - 1], x_peer(dx))

    def b_copy(self, x):
        src = self.parts.at[x * 2 + 1 - self.zh, :, self.b]
        return self.copy(4 + x, src, self.zb.at[x], zh_peer())

    def x_copy(self, dx):
        return self.copy(7 + dx, self.xs.at[dx - 1], self.xr.at[dx - 1], x_peer(dx))

    def z_copy(self):
        return self.copy(3, self.za.at[0], self.za.at[1], zh_peer())

    def start_a(self):
        for dx in range(1, 4):
            self.a_copy(dx).start()

    def start_b(self):
        for x in range(4):
            self.b_copy(x).start()

    def middle(self):
        for x in range(4):
            self.b_copy(x).wait_recv()
        for dx in range(1, 4):
            far = lax.rem(self.x + dx, 4)
            val = self.parts[far * 2 + self.zh, :, self.b].astype(F32) + self.zb[far].astype(F32)
            self.xs[dx - 1] = val.astype(BF)
            self.x_copy(dx).start()
        for dx in range(1, 4):
            self.a_copy(dx).wait_recv()
        self.za[0] = self.over_x(1 - self.zh).astype(BF)
        self.z_copy().start()

    def over_x(self, zz):
        val = self.parts[self.x * 2 + zz, :, self.a].astype(F32)
        for n in range(3):
            val = val + self.xa[n, zz].astype(F32)
        return val

    def finish(self):
        one = self.over_x(self.zh)
        two = self.parts[self.x * 2 + self.zh, :, self.b].astype(F32) + self.zb[self.x].astype(F32)
        for dx in range(1, 4):
            self.x_copy(dx).wait_recv()
            two = two + self.xr[dx - 1].astype(F32)
        self.z_copy().wait_recv()
        one = one + self.za[1].astype(F32)
        return jnp.concatenate([one, two], axis=1)

    def drain(self):
        for dx in range(1, 4):
            self.a_copy(dx).wait_send()
            self.x_copy(dx).wait_send()
        for x in range(4):
            self.b_copy(x).wait_send()
        self.z_copy().wait_send()


class MpGather:
    def __init__(self, out, sems, ca):
        self.out, (self.s, self.r) = out, sems
        self.x, self.zh = mp_place()
        self.a, self.b = pl.ds(0, ca), pl.ds(ca, D - ca)

    @staticmethod
    def sems():
        return (pltpu.SemaphoreType.DMA((14,)), pltpu.SemaphoreType.DMA((14,)))

    def copy(self, n, x, zh, cols, dev):
        ref = self.out.at[x * 2 + zh, :, cols]
        return remote(ref, ref, self.s.at[n], self.r.at[n], dev)

    def start(self):
        x, zh = self.x, self.zh
        self.copy(0, x, zh, self.a, zh_peer()).start()
        for dx in range(1, 4):
            self.copy(dx, x, zh, self.b, x_peer(dx)).start()
        self.copy(4, x, zh, self.b, zh_peer()).start()
        for dx in range(1, 4):
            self.copy(4 + dx, x, zh, self.a, x_peer(dx)).start()

    def relay(self):
        x, zh = self.x, self.zh
        self.copy(0, x, 1 - zh, self.a, zh_peer()).wait_recv()
        for dx in range(1, 4):
            self.copy(7 + dx, x, 1 - zh, self.a, x_peer(dx)).start()
        for dx in (1, 3, 2):
            back = lax.rem(x + 4 - dx, 4)
            self.copy(dx, back, zh, self.b, x_peer(dx)).wait_recv()
            self.copy(10 + dx, back, zh, self.b, zh_peer()).start()

    def finish(self):
        x, zh = self.x, self.zh
        self.copy(4, x, 1 - zh, self.b, zh_peer()).wait_recv()
        for dx in range(1, 4):
            back = lax.rem(x + 4 - dx, 4)
            self.copy(4 + dx, back, zh, self.a, x_peer(dx)).wait_recv()
            self.copy(7 + dx, back, 1 - zh, self.a, x_peer(dx)).wait_recv()
            self.copy(10 + dx, back, 1 - zh, self.b, zh_peer()).wait_recv()
        for n in range(14):
            cols = self.a if n in (0, 5, 6, 7, 8, 9, 10) else self.b
            self.copy(n, x, zh, cols, zh_peer()).wait_send()


class Gather:
    def __init__(self, buf, sems):
        self.buf, (self.s, self.r) = buf, sems
        y, z, self.core, m = place()

    @staticmethod
    def sems():
        return (pltpu.SemaphoreType.DMA((15,)), pltpu.SemaphoreType.DMA((16,)))

    def send(self, src, chip, n, dev):
        dst = self.buf.at[chip, self.core]
        remote(src, dst, self.s.at[n], self.r.at[chip * 2 + self.core], dev).start()

    def start(self, src):
        chip = chip_at(0, 0)
        for n, dev in enumerate([peer(0, 1), peer(1, 0), peer(3, 0), sibling()]):
            self.send(src, chip, n, dev)

    def wait(self, chip, core):
        ref = self.buf.at[chip, core]
        remote(ref, ref, self.s.at[0], self.r.at[chip * 2 + core], sibling()).wait_recv()

    def hop(self, dy, t):
        chip = chip_at(dy, t)
        self.wait(chip, self.core)
        src = self.buf.at[chip, self.core]
        n, devs = {
            (0, 1): (4, [peer(1, 0), peer(3, 0), sibling()]),
            (3, 0): (7, [peer(1, 0), sibling()]),
            (1, 0): (9, [sibling()]),
            (3, 1): (10, [sibling()]),
            (1, 1): (11, [peer(3, 0), sibling()]),
            (2, 0): (13, [sibling()]),
            (2, 1): (14, [sibling()]),
        }[dy, t]
        for i, dev in enumerate(devs):
            self.send(src, chip, n + i, dev)
        return chip

    def other_core(self, dy, t):
        chip = chip_at(dy, t)
        self.wait(chip, 1 - self.core)

    def drain(self):
        ref = self.buf.at[0, 0]
        for n in range(15):
            remote(ref, ref, self.s.at[n], self.s.at[n], sibling()).wait_send()


HOPS = ((0, 1), (3, 0), (1, 0), (3, 1), (1, 1), (2, 0), (2, 1))


def add_rows(dst, srcs, tile):
    def body(r, carry):
        rr = pl.ds(pl.multiple_of(r * tile, 16), tile)
        total = srcs[0][rr, :].astype(F32)
        for s in srcs[1:]:
            total = total + s[rr, :].astype(F32)
        dst[rr, :] = total.astype(dst.dtype)
        return carry

    lax.fori_loop(0, dst.shape[0] // tile, body, 0)


class Scatter:
    def __init__(self, refs, tile):
        (
            self.to_sib, self.from_sib, self.sums, self.half, self.pairs,
            self.s_sib, self.r_sib, self.s_half, self.r_half, self.s_pair, self.r_pair,
        ) = refs
        self.tile = tile
        self.y, self.z, self.core, m = place()

    @staticmethod
    def scratch(rows, cols):
        dma = pltpu.SemaphoreType.DMA
        eight = pltpu.VMEM((8, rows, cols), BF)
        return (
            eight, eight, eight, pltpu.VMEM((2, rows, cols), BF), pltpu.VMEM((2, 2, rows, cols), BF),
            dma((8,)), dma((8,)), dma((2,)), dma((2,)), dma((2,)), dma((2,)),
        )

    def add(self, dst, srcs):
        add_rows(dst, srcs, self.tile)

    def to_sibling(self, chip):
        remote(
            self.to_sib.at[chip], self.from_sib.at[chip], self.s_sib.at[chip], self.r_sib.at[chip], sibling()
        ).start()

    def merge(self, chip):
        got = self.from_sib.at[chip]
        remote(got, got, self.s_sib.at[0], self.r_sib.at[chip], sibling()).wait_recv()
        self.add(self.sums.at[chip], [self.sums.at[chip], got])

    def far(self):
        for t, dy in ((0, 1), (1, 3)):
            remote(
                self.sums.at[chip_at(2, t)], self.half.at[t], self.s_half.at[t], self.r_half.at[t], peer(dy, 0)
            ).start()

    def near(self, way):
        dy = 1 if way == 0 else 3
        got = self.half.at[way]
        remote(got, got, self.s_half.at[0], self.r_half.at[way], sibling()).wait_recv()
        mid = self.sums.at[chip_at(dy, way)]
        self.add(mid, [mid, got])
        both = self.sums.at[pl.ds(lax.rem(self.y + dy, 4) * 2, 2)]
        remote(both, self.pairs.at[way], self.s_pair.at[way], self.r_pair.at[way], peer(dy, 0)).start()

    def own(self, dst):
        for way in range(2):
            got = self.pairs.at[way]
            remote(got, got, self.s_pair.at[0], self.r_pair.at[way], sibling()).wait_recv()
        for t in (1, 0):
            zz = lax.rem(self.z + t, 2)
            self.add(
                dst.at[t], [self.sums.at[chip_at(0, t)], self.pairs.at[0, zz], self.pairs.at[1, zz]]
            )

    def drain(self):
        one, two = self.sums.at[0], self.pairs.at[0]
        for k in range(8):
            remote(one, one, self.s_sib.at[k], self.s_sib.at[k], sibling()).wait_send()
        for k in range(2):
            remote(one, one, self.s_half.at[k], self.s_half.at[k], sibling()).wait_send()
            remote(two, two, self.s_pair.at[k], self.s_pair.at[k], sibling()).wait_send()


def sds(shape, dtype):
    return jax.ShapeDtypeStruct(shape, dtype)


VMEM_SPEC = pl.BlockSpec(memory_space=pltpu.VMEM)
SMEM_SPEC = pl.BlockSpec(memory_space=pltpu.SMEM)
ANY_SPEC = pl.BlockSpec(memory_space=pl.ANY)
DMA = pltpu.SemaphoreType.DMA
MP_SEMS = (DMA((7,)), DMA((8,)))
CA = 1024
CO = 1792
PARTS = pltpu.VMEM((8, 64, D), BF)


def params(cid):
    return pltpu.CompilerParams(collective_id=cid, has_side_effects=True, vmem_limit_bytes=VM)


def rolled(x):
    return pltpu.roll(x, 64, axis=1)


def pick_of(order, k, cr):
    return jnp.where(order[k * 2 + cr] < order[lax.axis_index("ctx")], 0, 1)


def k1_kernel(
    order, tokens, wq, wk, wv, wo, inverse, gain_a, gain_m,
    moe, mixed, lse, ot, q, kvall, normed, att, cosf, sinf,
    tok, w3, wov, st_m, st_l, st_a, parts, s_in, g_sems, sum_refs, ag_sems,
):
    y, z, core, m = place()
    chip = chip_at(0, 0)
    loads = [
        pltpu.make_async_copy(a, b, s_in.at[i])
        for i, (a, b) in enumerate(
            [(tokens, tok), (wk, w3.at[0]), (wv, w3.at[1]), (wq, w3.at[2]), (wo, wov)]
        )
    ]
    for cp in loads:
        cp.start()
    count = greet()
    pair = order[lax.axis_index("ctx")]
    sign = jnp.where(lax.broadcasted_iota(jnp.int32, (1, HD), 1) < HD // 2, -1.0, 1.0)
    for n, first in enumerate((pair, 31 - pair)):
        pos = (lax.broadcasted_iota(jnp.int32, (256, HD), 0) + first * 256).astype(F32)
        phase = pos * inverse[...]
        cosf[pl.ds(n * 256, 256), :] = jnp.cos(phase)
        sinf[pl.ds(n * 256, 256), :] = jnp.sin(phase) * sign
    loads[0].wait()

    def norm_rows(i, carry):
        rr = pl.ds(pl.multiple_of(i * 128, 128), 128)
        x = tok[rr, :].astype(F32)
        n = lax.rsqrt(jnp.mean(x * x, axis=-1, keepdims=True) + EPSILON)
        normed[rr, :] = (x * n * gain_a[...]).astype(BF)
        return carry

    lax.fori_loop(0, 4, norm_rows, 0)
    own = kvall.at[chip, core]

    def turn(lin, rr, h):
        x = lin[:, h * HD : h * HD + HD]
        return x * cosf[rr, :] + rolled(x) * sinf[rr, :]

    loads[1].wait()
    loads[2].wait()

    def keys_values(n, carry):
        rr = pl.ds(pl.multiple_of(n * 256, 256), 256)
        lin = nn(normed[rr, :], w3[0])
        for h in range(2):
            own[0, n, :, pl.ds(h * HD, HD)] = turn(lin, rr, h).astype(BF)
        own[1, n] = nn(normed[rr, :], w3[1]).astype(BF)
        return carry

    lax.fori_loop(0, 2, keys_values, 0)
    all_in(count)
    gather = Gather(kvall, g_sems)
    gather.start(own)
    loads[3].wait()

    def queries(n, carry):
        rr = pl.ds(pl.multiple_of(n * 256, 256), 256)
        lin = nn(normed[rr, :], w3[2])
        for h in range(2):
            q[n, :, pl.ds(h * HD, HD)] = (turn(lin, rr, h) * (HD**-0.5)).astype(BF)
        return carry

    lax.fori_loop(0, 2, queries, 0)

    st_m[...] = jnp.full_like(st_m, NEG)
    st_l[...] = jnp.zeros_like(st_l)
    st_a[...] = jnp.zeros_like(st_a)

    def online(olds, sts, vs):
        mn = [jnp.maximum(o[0], jnp.max(s, axis=0, keepdims=True)) for o, s in zip(olds, sts)]
        ps = [jnp.exp(s - a) for s, a in zip(sts, mn)]
        al = [jnp.exp(o[0] - a) for o, a in zip(olds, mn)]
        ls = [a * o[1] + jnp.sum(p, axis=0, keepdims=True) for a, o, p in zip(al, olds, ps)]
        ac = [a * o[2] + tn(v, p.astype(BF)) for a, o, v, p in zip(al, olds, vs, ps)]
        return list(zip(mn, ls, ac))

    def keep(n, h, new):
        st_m[n, h], st_l[n, h], st_a[n, h] = new

    def block(k, cr):
        s = pick_of(order, k, cr)
        sts, vs, olds = [], [], []
        for h in range(2):
            cols = pl.ds(h * HD, HD)
            k0, k1 = kvall[k, cr, 0, 0, :, cols], kvall[k, cr, 0, 1, :, cols]
            v0, v1 = kvall[k, cr, 1, 0, :, cols], kvall[k, cr, 1, 1, :, cols]
            sts += [nt(k0, q[1, :, cols]), nt(jnp.where(s == 0, k0, k1), q[s, :, cols])]
            vs += [v0, jnp.where(s == 0, v0, v1)]
            olds.append((st_m[2, h], st_l[2, h], st_a[2, h]))
            olds.append(
                (
                    jnp.where(s == 0, st_m[0, h], st_m[1, h]),
                    jnp.where(s == 0, st_l[0, h], st_l[1, h]),
                    st_a[s, h],
                )
            )
        new = online(olds, sts, vs)
        for h in range(2):
            keep(2, h, new[2 * h])
            b = new[2 * h + 1]
            for n in range(2):
                st_m[n, h] = jnp.where(s == n, b[0], st_m[n, h])
                st_l[n, h] = jnp.where(s == n, b[1], st_l[n, h])
                st_a[n, h] = jnp.where(s == n, b[2], st_a[n, h])

    tri = lax.broadcasted_iota(jnp.int32, (256, 256), 0) <= lax.broadcasted_iota(
        jnp.int32, (256, 256), 1
    )
    for h in range(2):
        cols = pl.ds(h * HD, HD)
        names = [2, 0, 1]
        sts = [nt(own[0, 0, :, cols], q[1, :, cols])]
        sts += [jnp.where(tri, nt(own[0, n, :, cols], q[n, :, cols]), NEG) for n in range(2)]
        vs = [own[1, 0, :, cols], own[1, 0, :, cols], own[1, 1, :, cols]]
        olds = [(st_m[n, h], st_l[n, h], st_a[n, h]) for n in names]
        for n, new in zip(names, online(olds, sts, vs)):
            keep(n, h, new)

    gather.wait(chip, 1 - core)
    block(chip, 1 - core)
    for dy, t in HOPS:
        k = gather.hop(dy, t)

        def cores(i, carry):
            cr = lax.rem(core + i, 2)

            @pl.when(i == 1)
            def _():
                gather.wait(k, cr)

            block(k, cr)
            return carry

        lax.fori_loop(0, 2, cores, 0)

    for h in range(2):
        for n in range(2):
            m0, l0, a0 = st_m[n, h], st_l[n, h], st_a[n, h]
            if n == 1:
                m2, l2, a2 = st_m[2, h], st_l[2, h], st_a[2, h]
                mn = jnp.maximum(m0, m2)
                e0, e2 = jnp.exp(m0 - mn), jnp.exp(m2 - mn)
                m0, l0, a0 = mn, e0 * l0 + e2 * l2, e0 * a0 + e2 * a2
            lse[n, h] = m0 + jnp.log(l0)
            o = a0 / l0
            ot[n, h] = o
            att[pl.ds(n * 256, 256), pl.ds(h * HD, HD)] = jnp.transpose(o).astype(BF)

    loads[4].wait()

    def out_cols(i, carry):
        cols = pl.ds(pl.multiple_of(i * 256, 256), 256)
        parts[:, :, cols] = nn(att[...], wov[:, cols]).reshape(8, 64, 256).astype(BF)
        return carry

    mps = MpSum(parts, sum_refs, CA)
    lax.fori_loop(0, CA // 256, out_cols, 0)
    mps.start_a()
    lax.fori_loop(CA // 256, 8, out_cols, 0)
    mps.start_b()
    mps.middle()
    total = tok[pl.ds(pl.multiple_of(m * 64, 64), 64), :].astype(F32) + mps.finish()
    mixed[...] = total
    n = lax.rsqrt(jnp.mean(total * total, axis=-1, keepdims=True) + EPSILON)
    moe[m] = (total * n * gain_m[...]).astype(BF)
    mpg = MpGather(moe, ag_sems, CA)
    mpg.start()
    mpg.relay()

    gather.drain()
    mps.drain()
    mpg.finish()


def attention_forward(order, tokens, wq, wk, wv, wo, inverse, gain_a, gain_m):
    return pl.pallas_call(
        k1_kernel,
        name="attend_forward",
        out_shape=(
            sds((8, 64, D), BF),
            sds((64, D), F32),
            sds((2, 2, 1, 256), F32),
            sds((2, 2, HD, 256), F32),
            sds((2, 256, 256), BF),
            sds((8, 2, 2, 2, 256, 256), BF),
            sds((512, D), BF),
            sds((512, 256), BF),
            sds((512, HD), F32),
            sds((512, HD), F32),
        ),
        in_specs=[SMEM_SPEC] + [ANY_SPEC] * 5 + [VMEM_SPEC] * 3,
        out_specs=(VMEM_SPEC,) * 10,
        scratch_shapes=[
            pltpu.VMEM((512, D), BF),
            pltpu.VMEM((3, D, 256), BF),
            pltpu.VMEM((256, D), BF),
            pltpu.VMEM((3, 2, 1, 256), F32),
            pltpu.VMEM((3, 2, 1, 256), F32),
            pltpu.VMEM((3, 2, HD, 256), F32),
            PARTS, DMA((5,)), Gather.sems(), MpSum.scratch(CA), MpGather.sems(),
        ],
        compiler_params=params(1),
    )(order, tokens, wq, wk, wv, wo, inverse, gain_a, gain_m)


def swish_parts(g, u):
    s = 1.0 / (1.0 + jnp.exp(-g))
    return s, g * s


def to_column(row):
    return jnp.transpose(jnp.broadcast_to(row, (HD, HD)))[:, 0:1]


def to_row(col):
    return jnp.transpose(jnp.broadcast_to(col, (HD, HD)))[0:1, :]


def k2_kernel(
    ids, moe, mixed, gain, w_router, cot, sg, su, sd, eg, eu, ed,
    g_attn, g_mixed, gain_part, wown, moe_part, g_logits,
    wsg, wsu, wsd, weg, weu, wed, cotv, tb, tbt, pr, gt, ut, hs, gsg, gsu,
    ein, gsl, geo, gated, eo, gein, ge3, ue3, he3, tmp, amat, blk, gate_part, gmi, gate_land,
    s_in, rs_refs, mp1, sum_refs, ag_sems,
):
    y, z, core, m = place()
    loads = [
        pltpu.make_async_copy(a, b, s_in.at[i])
        for i, (a, b) in enumerate(
            [(sg, wsg), (su, wsu), (eg, weg), (eu, weu), (ed, wed), (sd, wsd), (cot, cotv)]
        )
    ]
    for cp in loads:
        cp.start()
    count = greet()

    slot = lax.broadcasted_iota(jnp.int32, (HD, 512), 0)
    holder = lax.div(slot, CAP)
    chosen = holder == ids[0:1, :]
    for k in range(1, 6):
        chosen = chosen | (holder == ids[k : k + 1, :])
    chosen = jnp.where(chosen & (slot < 3 * CAP), 1.0, 0.0)
    upto = lax.broadcasted_iota(jnp.int32, (512, 512), 0) <= lax.broadcasted_iota(
        jnp.int32, (512, 512), 1
    )
    place_of = nn(chosen.astype(BF), jnp.where(upto, 1.0, 0.0).astype(BF)) - 1.0
    table_t = jnp.where(place_of == lax.rem(slot, CAP).astype(F32), chosen, 0.0)
    tbt[...] = table_t.astype(BF)
    table = jnp.transpose(table_t)
    tb[...] = table.astype(BF)
    expert = lax.div(lax.broadcasted_iota(jnp.int32, (512, HD), 1), CAP)

    logits = nt(moe[...], w_router[...])
    e = jnp.exp(logits - jnp.max(logits, axis=-1, keepdims=True))
    probs = e / jnp.sum(e, axis=-1, keepdims=True)
    pr[...] = probs
    px = jnp.where(expert == 0, probs[:, 0:1], jnp.where(expert == 1, probs[:, 1:2], probs[:, 2:3]))
    gate_col = to_column(jnp.sum(table * px, axis=0, keepdims=True))

    hs[...] = jnp.zeros_like(hs)
    gsg[...] = jnp.zeros_like(gsg)
    gsu[...] = jnp.zeros_like(gsu)
    eo[...] = jnp.zeros_like(eo)
    gein[...] = jnp.zeros_like(gein)
    tmp[...] = jnp.zeros_like(tmp)

    def gather_in(i, carry):
        cols = pl.ds(pl.multiple_of(i * 512, 512), 512)
        ein[:, cols] = nn(tbt[...], moe[:, cols]).astype(BF)
        return carry

    lax.fori_loop(0, 4, gather_in, 0)
    loads[0].wait()
    loads[1].wait()

    def shared_in(i, carry):
        rr = pl.ds(pl.multiple_of(i * 256, 256), 256)
        g, u = nt(moe[rr, :], wsg[...]), nt(moe[rr, :], wsu[...])
        gt[rr, :] = g
        ut[rr, :] = u
        hs[rr, 0:SH] = (swish_parts(g, u)[1] * u).astype(BF)
        return carry

    lax.fori_loop(0, 2, shared_in, 0)
    for cp in loads[2:5]:
        cp.wait()
    for k in range(3):
        rr = pl.ds(k * CAP, CAP)
        g, u = nt(ein[rr, :], weg[k]), nt(ein[rr, :], weu[k])
        ge3[k] = g
        ue3[k] = u
        hid = (swish_parts(g, u)[1] * u).astype(BF)
        he3[k] = hid
        eo[rr, :] = nn(hid, wed[k])
    loads[5].wait()
    loads[6].wait()

    def slots_in(i, carry):
        cols = pl.ds(pl.multiple_of(i * 512, 512), 512)
        g = nn(tbt[...], cotv[:, cols])
        gsl[:, cols] = g.astype(BF)
        geo[:, cols] = (gate_col * g).astype(BF)
        gated[:, cols] = (gate_col * eo[:, cols]).astype(BF)
        return carry

    lax.fori_loop(0, 4, slots_in, 0)
    gate_part[...] = to_row(jnp.sum(eo[...] * gsl[...].astype(F32), axis=1, keepdims=True))
    all_in(count)
    mp_send_same(gate_part, gate_land, *mp1)

    def shared_back(i, carry):
        rr = pl.ds(pl.multiple_of(i * 256, 256), 256)
        gh = nt(cotv[rr, :], wsd[...])
        g, u = gt[rr, :], ut[rr, :]
        s, sw = swish_parts(g, u)
        gsg[rr, 0:SH] = (gh * u * s * (1.0 + g * (1.0 - s))).astype(BF)
        gsu[rr, 0:SH] = (gh * sw).astype(BF)
        return carry

    lax.fori_loop(0, 2, shared_back, 0)

    def put_block(i, k, val):
        rr = pl.ds(k * CAP, CAP)
        tmp[k, rr, 0:EF] = val.astype(F32)
        blk[pl.ds(EF * i, EF), :] = jnp.transpose(tmp[k])[0:EF].astype(BF)

    for k in range(3):
        rr = pl.ds(k * CAP, CAP)
        gh = nt(geo[rr, :], wed[k])
        g, u = ge3[k], ue3[k]
        s, sw = swish_parts(g, u)
        geg = (gh * u * s * (1.0 + g * (1.0 - s))).astype(BF)
        geu = (gh * sw).astype(BF)
        gein[rr, :] = (nn(geg, weg[k]) + nn(geu, weu[k])).astype(BF)
        put_block(k, k, geg)
        put_block(3 + k, k, geu)
        put_block(6 + k, k, he3[k])

    def back_cols(i, carry):
        cols = pl.ds(pl.multiple_of(i * 256, 256), 256)
        g = nn(gsg[:, 0:SH], wsg[:, cols]) + nn(gsu[:, 0:SH], wsu[:, cols]) + nn(tb[...], gein[:, cols])
        gmi[:, :, cols] = g.reshape(8, 64, 256).astype(BF)
        return carry

    mps = MpSum(gmi, sum_refs, CA)
    lax.fori_loop(0, CA // 256, back_cols, 0)
    mps.start_a()
    lax.fori_loop(CA // 256, 8, back_cols, 0)
    mps.start_b()

    amat[pl.ds(0, SH), :] = turned(gsg[...])[0:SH]
    amat[pl.ds(SH, SH), :] = turned(gsu[...])[0:SH]
    amat[pl.ds(2 * SH, SH), :] = turned(hs[...])[0:SH]
    rs = Scatter(rs_refs, 528)

    def piece(k):
        cols = pl.ds(pl.multiple_of(k * 256, 256), 256)
        for off, rows, lhs, rhs in (
            (0, 2 * SH, amat.at[pl.ds(0, 2 * SH)], moe),
            (2 * SH, SH, amat.at[pl.ds(2 * SH, SH)], cotv),
            (3 * SH, 6 * EF, blk.at[pl.ds(0, 6 * EF)], ein),
            (3 * SH + 6 * EF, 3 * EF, blk.at[pl.ds(6 * EF, 3 * EF)], geo),
        ):
            val = nn(lhs[...], rhs[:, cols]).astype(BF)
            one, two = val[:, 0:HD], val[:, HD:]
            rs.sums[k, pl.ds(off, rows), :] = jnp.where(core == 0, one, two)
            rs.to_sib[k, pl.ds(off, rows), :] = jnp.where(core == 0, two, one)
        rs.to_sibling(k)

    def pieces(i, carry):
        j = lax.div(i, 2)
        dy = lax.rem(2 - j + 3 * lax.div(j * (j - 1), 2), 4)
        piece(chip_at(dy, lax.rem(i, 2)))

        @pl.when(i == 2)
        def _():
            rs.merge(chip_at(2, 0))
            rs.merge(chip_at(2, 1))
            rs.far()

        return carry

    lax.fori_loop(0, 8, pieces, 0)

    def out_cols(i, carry):
        cols = pl.ds(pl.multiple_of(i * 256, 256), 256)
        o = nn(hs[:, 0:SH], wsd[:, cols]) + nn(tb[...], gated[:, cols])
        moe_part[:, :, cols] = o.reshape(8, 64, 256).astype(BF)
        return carry

    lax.fori_loop(0, 8, out_cols, 0)

    gate = gate_part[...]
    for d in range(1, 8):
        gate = gate + gate_land[mp_wait_recv(gate_land, *mp1, d)]
    lane2 = lax.broadcasted_iota(jnp.int32, (HD, 64), 0)
    col2 = lax.broadcasted_iota(jnp.int32, (HD, 64), 1)
    member = jnp.where((lax.div(lane2, CAP) == col2) & (col2 < 3), 1.0, 0.0)
    gate_probs = lax.dot_general(
        tb[...].astype(F32) * gate, member, (((1,), (0,)), ((), ())),
        precision=PRECISE, preferred_element_type=F32,
    )
    prob = pr[...]
    g_logits[...] = (prob * (gate_probs - jnp.sum(gate_probs * prob, axis=-1, keepdims=True))).astype(BF)

    mps.middle()
    for way, dy in ((0, 1), (1, 3)):
        rs.merge(chip_at(dy, 0))
        rs.merge(chip_at(dy, 1))
        rs.near(way)
    rs.merge(chip_at(0, 1))
    rs.merge(chip_at(0, 0))

    mine = pl.ds(pl.multiple_of(m * 64, 64), 64)
    total = nn(g_logits[mine, :], w_router[...]) + mps.finish()
    mx = mixed[...]
    n = lax.rsqrt(jnp.mean(mx * mx, axis=-1, keepdims=True) + EPSILON)
    gain_part[...] = jnp.sum(total * mx * n, axis=0, keepdims=True)
    gg = total * gain[...]
    gm = cotv[mine, :].astype(F32) + n * gg
    gm = gm - mx * (n * n * n) * jnp.mean(gg * mx, axis=-1, keepdims=True)
    g_mixed[...] = gm
    g_attn[m] = gm.astype(BF)
    mpg = MpGather(g_attn, ag_sems, CA)
    mpg.start()
    mpg.relay()

    rs.own(wown)
    rs.drain()
    mps.drain()
    mp_wait_send(gate_part, mp1[0])
    mpg.finish()


def experts(ids, moe, mixed, gain, w_router, cot, sg, su, sd, eg, eu, ed):
    vm = pltpu.VMEM
    return pl.pallas_call(
        k2_kernel,
        name="experts",
        out_shape=(
            sds((8, 64, D), BF),
            sds((64, D), F32),
            sds((1, D), F32),
            sds((2, R1, HD), BF),
            sds((8, 64, D), BF),
            sds((512, 64), BF),
        ),
        in_specs=[VMEM_SPEC] * 5 + [ANY_SPEC] * 7,
        out_specs=(VMEM_SPEC,) * 6,
        scratch_shapes=[
            vm((SH, D), BF), vm((SH, D), BF), vm((SH, D), BF),
            vm((3, EF, D), BF), vm((3, EF, D), BF), vm((3, EF, D), BF),
            vm((512, D), BF), vm((512, HD), BF), vm((HD, 512), BF), vm((512, 64), F32),
            vm((512, SH), F32), vm((512, SH), F32),
            vm((512, 384), BF), vm((512, 384), BF), vm((512, 384), BF),
            vm((HD, D), BF), vm((HD, D), BF), vm((HD, D), BF), vm((HD, D), BF),
            vm((HD, D), F32), vm((HD, D), BF),
            vm((3, CAP, EF), F32), vm((3, CAP, EF), F32), vm((3, CAP, EF), BF),
            vm((3, HD, 256), F32), vm((3 * SH, 512), BF), vm((9 * EF, HD), BF),
            vm((1, HD), F32), PARTS, vm((8, 1, HD), F32),
            DMA((7,)), Scatter.scratch(R1, HD), MP_SEMS, MpSum.scratch(CA), MpGather.sems(),
        ],
        compiler_params=params(2),
    )(ids, moe, mixed, gain, w_router, cot, sg, su, sd, eg, eu, ed)


def k3_kernel(
    order, q, kvall, lse, ot, g_attn, wout, moe_part, mixed, wown, cosf, sinf,
    output, w1, glin, fin_a,
    do, delta, dqt, zbuf, fin_b, dkz, dkv,
    s_loc, s_z, r_z, s_z2, r_z2, g_sems, rs_refs, sum_refs, ag_sems,
):
    y, z, core, m = place()
    chip = chip_at(0, 0)
    count = greet()
    g_att = nt(g_attn[...], wout[...])
    for n in range(2):
        for h in range(2):
            piece = g_att[n * 256 : n * 256 + 256, h * HD : h * HD + HD].astype(BF)
            do[n, h] = piece
            delta[n, h] = jnp.sum(jnp.transpose(piece.astype(F32)) * ot[n, h], axis=0, keepdims=True)
    dqt[...] = jnp.zeros_like(dqt)
    all_in(count)
    mps = MpSum(moe_part, sum_refs, CO)
    mps.start_a()
    mps.start_b()
    remote(wown.at[1], zbuf, s_z, r_z, peer(0, 1)).start()
    rs = Scatter(rs_refs, 256)
    gather = Gather(w1, g_sems)

    def terms(items):
        ps = [nt(k, qq) - ls for k, v, qq, dd, ls, de, mask in items]
        ps = [jnp.exp(p) for p in ps]
        ps = [p if i[6] is None else jnp.where(i[6], p, 0.0) for p, i in zip(ps, items)]
        ds = [(p * (nt(i[1], i[3]) - i[5])).astype(BF) for p, i in zip(ps, items)]
        dv = [nn(p.astype(BF), i[3]) for p, i in zip(ps, items)]
        dk = [nn(d, i[2]) for d, i in zip(ds, items)]
        dq = [tn(i[0], d) for d, i in zip(ds, items)]
        return list(zip(dk, dv, dq))

    def block(k, cr, dst):
        s = pick_of(order, k, cr)
        items = []
        for h in range(2):
            cols = pl.ds(h * HD, HD)
            items.append(
                (kvall[k, cr, 0, 0, :, cols], kvall[k, cr, 1, 0, :, cols], q[1, :, cols], do[1, h],
                 lse[1, h], delta[1, h], None)
            )
            items.append(
                (kvall[k, cr, 0, s, :, cols], kvall[k, cr, 1, s, :, cols], q[s, :, cols], do[s, h],
                 jnp.where(s == 0, lse[0, h], lse[1, h]), jnp.where(s == 0, delta[0, h], delta[1, h]), None)
            )
        got = terms(items)
        for h in range(2):
            cols = pl.ds(h * HD, HD)
            always, picked = got[2 * h], got[2 * h + 1]
            dqt[2, h] += always[2]
            for n in range(2):
                dqt[n, h] += jnp.where(s == n, picked[2], 0.0)
            for a in range(2):
                low = always[a] + jnp.where(s == 0, picked[a], 0.0)
                high = jnp.where(s == 1, picked[a], 0.0)
                dst[pl.ds(a * 512, 256), cols] = low.astype(BF)
                dst[pl.ds(a * 512 + 256, 256), cols] = high.astype(BF)

    def both_cores(k):
        block(k, 1 - core, rs.to_sib.at[k])
        rs.to_sibling(k)
        block(k, core, rs.sums.at[k])

    def ring_place(dy):
        def one(t, carry):
            both_cores(chip_at(dy, t))
            return carry

        lax.fori_loop(0, 2, one, 0)
        rs.merge(chip_at(dy, 0))
        rs.merge(chip_at(dy, 1))

    ring_place(2)
    rs.far()
    ring_place(1)
    rs.near(0)

    remote(zbuf, zbuf, s_z, r_z, peer(0, 1)).wait_recv()
    add_rows(fin_a, [wown.at[0, pl.ds(0, RA)], zbuf.at[pl.ds(0, RA)]], 528)
    add_rows(fin_b, [wown.at[0, pl.ds(RA, R1 - RA)], zbuf.at[pl.ds(RA, R1 - RA)]], 528)
    gather.start(fin_b)
    local = pltpu.make_async_copy(fin_b, w1.at[chip, core], s_loc)
    local.start()

    ring_place(3)
    rs.near(1)
    gather.hop(0, 1)
    mps.middle()

    both_cores(chip_at(0, 1))
    block(chip, 1 - core, rs.to_sib.at[chip])
    rs.to_sibling(chip)
    tri = lax.broadcasted_iota(jnp.int32, (256, 256), 0) <= lax.broadcasted_iota(
        jnp.int32, (256, 256), 1
    )
    for h in range(2):
        cols = pl.ds(h * HD, HD)
        kk = [kvall[chip, core, 0, n, :, cols] for n in range(2)]
        vv = [kvall[chip, core, 1, n, :, cols] for n in range(2)]
        items = [(kk[0], vv[0], q[1, :, cols], do[1, h], lse[1, h], delta[1, h], None)]
        for n in range(2):
            items.append((kk[n], vv[n], q[n, :, cols], do[n, h], lse[n, h], delta[n, h], tri))
        got = terms(items)
        dqt[2, h] += got[0][2]
        for n in range(2):
            dqt[n, h] += got[1 + n][2]
        for a in range(2):
            rs.sums[chip, pl.ds(a * 512, 256), cols] = (got[0][a] + got[1][a]).astype(BF)
            rs.sums[chip, pl.ds(a * 512 + 256, 256), cols] = got[2][a].astype(BF)
    rs.merge(chip_at(0, 1))
    rs.merge(chip)

    def back(x, rr):
        return (x * cosf[rr, :] - rolled(x) * sinf[rr, :]).astype(BF)

    for h in range(2):
        for n in range(2):
            rr = pl.ds(n * 256, 256)
            g = dqt[n, h] if n == 0 else dqt[1, h] + dqt[2, h]
            glin[0, rr, pl.ds(h * HD, HD)] = back(jnp.transpose(g) * (HD**-0.5), rr)

    output[m] = (mixed[...] + mps.finish()).astype(BF)
    mpg = MpGather(output, ag_sems, CO)
    mpg.start()

    gather.hop(3, 0)
    gather.hop(1, 0)
    rs.own(dkz)
    remote(dkz.at[1], dkv, s_z2, r_z2, peer(0, 1)).start()
    remote(dkv, dkv, s_z2, r_z2, peer(0, 1)).wait_recv()
    for n in range(2):
        rr = pl.ds(n * 256, 256)
        for h in range(2):
            cols = pl.ds(h * HD, HD)
            kr = pl.ds(n * 256, 256)
            vr = pl.ds(512 + n * 256, 256)
            g = dkz[0, kr, cols].astype(F32) + dkv[kr, cols].astype(F32)
            glin[1, rr, cols] = back(g, rr)
            glin[2, rr, cols] = (dkz[0, vr, cols].astype(F32) + dkv[vr, cols].astype(F32)).astype(BF)
    mpg.relay()
    for dy, t in HOPS[3:]:
        gather.hop(dy, t)

    remote(dkv, dkv, s_z2, s_z2, peer(0, 1)).wait_send()
    remote(zbuf, zbuf, s_z, s_z, peer(0, 1)).wait_send()
    rs.drain()
    mps.drain()
    mpg.finish()
    local.wait()
    gather.wait(chip, 1 - core)
    for dy, t in HOPS:
        gather.other_core(dy, t)
    gather.drain()


def attention_backward(order, q, kvall, lse, ot, g_attn, wout, moe_part, mixed, wown, cosf, sinf):
    vm = pltpu.VMEM
    return pl.pallas_call(
        k3_kernel,
        name="attend_backward",
        out_shape=(
            sds((8, 64, D), BF), sds((8, 2, R1 - RA, HD), BF), sds((3, 512, 256), BF), sds((RA, HD), BF),
        ),
        in_specs=[SMEM_SPEC] + [VMEM_SPEC] * 11,
        out_specs=(VMEM_SPEC, ANY_SPEC, VMEM_SPEC, VMEM_SPEC),
        scratch_shapes=[
            vm((2, 2, 256, HD), BF), vm((2, 2, 1, 256), F32), vm((3, 2, HD, 256), F32),
            vm((R1, HD), BF), vm((R1 - RA, HD), BF), vm((2, 1024, 256), BF), vm((1024, 256), BF),
            DMA, DMA, DMA, DMA, DMA, Gather.sems(), Scatter.scratch(1024, 256), MpSum.scratch(CO), MpGather.sems(),
        ],
        compiler_params=params(3),
    )(order, q, kvall, lse, ot, g_attn, wout, moe_part, mixed, wown, cosf, sinf)


def k4_kernel(
    glin, att, g_attn, g_logits, moe, normed, g_mixed, gain, gain_moe_part, fin_a, tokens, wq, wk, wv,
    g_tokens, w2out, gains, w1a,
    tok, w3, amat, gni, zbuf, fin, wown, gmine, gland, gsteps, gfar,
    s_in, s_loc, s_loc2, s_z, r_z, s_gx, r_gx, s_gy, r_gy, g_sems, g_sems2, rs_refs, sum_refs, ag_sems, mp3,
):
    y, z, core, m = place()
    chip = chip_at(0, 0)
    loads = [
        pltpu.make_async_copy(a, w3.at[i], s_in.at[i]) for i, a in enumerate((wq, wk, wv))
    ]
    mine = pl.ds(pl.multiple_of(m * 64, 64), 64)
    loads.append(pltpu.make_async_copy(tokens.at[mine, :], tok, s_in.at[3]))
    for cp in loads:
        cp.start()
    count = greet(far=True)
    for cp in loads:
        cp.wait()

    def back_cols(i, carry):
        cols = pl.ds(pl.multiple_of(i * 256, 256), 256)
        g = nt(glin[0], w3[0, cols, :]) + nt(glin[1], w3[1, cols, :]) + nt(glin[2], w3[2, cols, :])
        gni[:, :, cols] = g.reshape(8, 64, 256).astype(BF)
        return carry

    mps = MpSum(gni, sum_refs, CA)
    lax.fori_loop(0, CA // 256, back_cols, 0)
    all_in(count)
    mps.start_a()
    lax.fori_loop(CA // 256, 8, back_cols, 0)
    mps.start_b()
    first = Gather(w1a, g_sems2)
    first.start(fin_a)
    local2 = pltpu.make_async_copy(fin_a, w1a.at[chip, core], s_loc2)
    local2.start()

    amat[pl.ds(0, 64), :] = turned(g_logits[...])
    for i in range(3):
        amat[pl.ds(64 + 256 * i, 256), :] = turned(glin[i])
    amat[pl.ds(832, 256), :] = turned(att[...])
    rs = Scatter(rs_refs, 544)

    def piece(k):
        cols = pl.ds(pl.multiple_of(k * 256, 256), 256)
        for off, rows, rhs in ((0, 64, moe), (64, 768, normed), (832, 256, g_attn)):
            val = nn(amat[pl.ds(off, rows), :], rhs[:, cols]).astype(BF)
            one, two = val[:, 0:HD], val[:, HD:]
            rs.sums[k, pl.ds(off, rows), :] = jnp.where(core == 0, one, two)
            rs.to_sib[k, pl.ds(off, rows), :] = jnp.where(core == 0, two, one)
        rs.to_sibling(k)

    def pieces(i, carry):
        j = lax.div(i, 2)
        dy = lax.rem(2 - j + 3 * lax.div(j * (j - 1), 2), 4)
        piece(chip_at(dy, lax.rem(i, 2)))

        @pl.when(i == 2)
        def _():
            rs.merge(chip_at(2, 0))
            rs.merge(chip_at(2, 1))
            rs.far()

        return carry

    lax.fori_loop(0, 8, pieces, 0)
    first.hop(0, 1)
    for way, dy in ((0, 1), (1, 3)):
        rs.merge(chip_at(dy, 0))
        rs.merge(chip_at(dy, 1))
        rs.near(way)
        first.hop(3 if way == 0 else 1, 0)
        if way == 0:
            mps.middle()
    rs.merge(chip_at(0, 1))
    rs.merge(chip_at(0, 0))

    total = mps.finish()
    src = tok[...].astype(F32)
    n = lax.rsqrt(jnp.mean(src * src, axis=-1, keepdims=True) + EPSILON)
    gg = total * gain[...]
    gs = n * gg - src * (n * n * n) * jnp.mean(gg * src, axis=-1, keepdims=True)
    g_tokens[m] = (g_mixed[...] + gs).astype(BF)
    gmine[pl.ds(0, 1), :] = gain_moe_part[...]
    gmine[pl.ds(1, 1), :] = jnp.sum(total * src * n, axis=0, keepdims=True)
    mp_send_same(gmine, gland, *mp3)
    mpg = MpGather(g_tokens, ag_sems, CA)
    mpg.start()
    first.hop(3, 1)
    first.hop(1, 1)
    mpg.relay()

    rs.own(wown)
    remote(wown.at[1], zbuf, s_z, r_z, peer(0, 1)).start()

    def gain_step(i, dev):
        return remote(gsteps.at[2 * i], gsteps.at[2 * i + 1], s_gx.at[i], r_gx.at[i], dev)

    gsum = gmine[...]
    for d in range(1, 8):
        gsum = gsum + gland[mp_wait_recv(gland, *mp3, d)]
    gsteps[0] = gsum
    gain_step(0, sibling()).start()

    remote(zbuf, zbuf, s_z, r_z, peer(0, 1)).wait_recv()
    add_rows(fin, [wown.at[0], zbuf], 544)
    gather = Gather(w2out, g_sems)
    gather.start(fin)
    local = pltpu.make_async_copy(fin, w2out.at[chip, core], s_loc)
    local.start()

    gain_step(0, sibling()).wait_recv()
    gsteps[2] = gsteps[0] + gsteps[1]
    gain_step(1, peer(0, 1)).start()
    first.hop(2, 0)
    first.hop(2, 1)
    gain_step(1, peer(0, 1)).wait_recv()
    gfar[y] = gsteps[2] + gsteps[3]
    for d in range(1, 4):
        remote(gfar.at[y], gfar.at[y], s_gy.at[d - 1], r_gy.at[y], peer(d, 0)).start()
    for dy, t in HOPS:
        gather.hop(dy, t)
    for d in range(1, 4):
        yy = lax.rem(y + d, 4)
        remote(gfar.at[yy], gfar.at[yy], s_gy.at[0], r_gy.at[yy], peer(d, 0)).wait_recv()
    gains[...] = gfar[0] + gfar[1] + gfar[2] + gfar[3]

    for i, dev in enumerate((sibling(), peer(0, 1))):
        remote(gsteps.at[0], gsteps.at[0], s_gx.at[i], s_gx.at[i], dev).wait_send()
    for d in range(1, 4):
        remote(gfar.at[0], gfar.at[0], s_gy.at[d - 1], s_gy.at[d - 1], peer(d, 0)).wait_send()
    remote(zbuf, zbuf, s_z, s_z, peer(0, 1)).wait_send()
    rs.drain()
    mp_wait_send(gmine, mp3[0])
    mps.drain()
    mpg.finish()
    local.wait()
    local2.wait()
    for g in (first, gather):
        g.wait(chip, 1 - core)
        for dy, t in HOPS:
            g.other_core(dy, t)
        g.drain()


def first_norm_backward(*args):
    vm = pltpu.VMEM
    return pl.pallas_call(
        k4_kernel,
        name="first_norm_backward",
        out_shape=(
            sds((8, 64, D), BF), sds((8, 2, R2, HD), BF), sds((2, D), F32), sds((8, 2, RA, HD), BF),
        ),
        in_specs=[VMEM_SPEC] * 10 + [ANY_SPEC] * 4,
        out_specs=(VMEM_SPEC, ANY_SPEC, VMEM_SPEC, ANY_SPEC),
        scratch_shapes=[
            vm((64, D), BF), vm((3, D, 256), BF), vm((R2, 512), BF), PARTS, vm((R2, HD), BF), vm((R2, HD), BF),
            vm((2, R2, HD), BF), vm((2, D), F32), vm((8, 2, D), F32), vm((4, 2, D), F32), vm((4, 2, D), F32),
            DMA((4,)), DMA, DMA, DMA, DMA, DMA((2,)), DMA((2,)), DMA((3,)), DMA((4,)),
            Gather.sems(), Gather.sems(), Scatter.scratch(R2, HD), MpSum.scratch(CA), MpGather.sems(), MP_SEMS,
        ],
        compiler_params=params(4),
    )(*args)


def widen_kernel(
    wa, wb, w2, out_in, tok_in, gains,
    gq, gk, gv, go, gr, sg, su, sd, eg, eu, ed, out, tok, gain_a, gain_m,
):
    def flip(src, off):
        return jnp.transpose(src[0, 0, pl.ds(off, 256), :].astype(F32))

    gr[...] = w2[0, 0, pl.ds(0, 64), :].astype(F32)
    gq[...] = flip(w2, 64)
    gk[...] = flip(w2, 320)
    gv[...] = flip(w2, 576)
    go[...] = w2[0, 0, pl.ds(832, 256), :].astype(F32)
    for k, ref in enumerate((sg, su, sd)):
        ref[...] = wa[0, 0, pl.ds(k * SH, SH), :].astype(F32)
    for k in range(3):
        for j, ref in enumerate((eg, eu, ed)):
            ref[k] = wb[0, 0, pl.ds(EF * (3 * j + k), EF), :].astype(F32)
    out[...] = out_in[...]
    tok[...] = tok_in[...]
    gain_m[...] = gains[pl.ds(0, 1), :]
    gain_a[...] = gains[pl.ds(1, 1), :]


def widen(wa, wb, w2, out_in, tok_in, gains):
    def rows(width):
        return sds((D, width), F32), pl.BlockSpec((HD, width), lambda i: (i, 0))

    def cols(height):
        return sds((height, D), F32), pl.BlockSpec((height, HD), lambda i: (0, i))

    three = sds((3, EF, D), F32), pl.BlockSpec((3, EF, HD), lambda i: (0, 0, i))
    whole = pl.BlockSpec((32, D), lambda i: (i, 0))
    gain = sds((1, D), F32), pl.BlockSpec((1, HD), lambda i: (0, i))
    outs = [rows(256), rows(256), rows(256), cols(256), cols(64), cols(SH), cols(SH), cols(SH)]
    outs += [three, three, three, (sds((512, D), BF), whole), (sds((512, D), BF), whole), gain, gain]
    return pl.pallas_call(
        widen_kernel,
        name="widen",
        grid=(16,),
        out_shape=[o[0] for o in outs],
        in_specs=[
            pl.BlockSpec((1, 1, w.shape[2], HD), lambda i: (i // 2, i % 2, 0, 0)) for w in (wa, wb, w2)
        ]
        + [whole, whole, pl.BlockSpec((2, HD), lambda i: (0, i))],
        out_specs=[o[1] for o in outs],
        compiler_params=pltpu.CompilerParams(vmem_limit_bytes=VM),
    )(wa, wb, w2, out_in, tok_in, gains)


def on_device(
    tokens, cotangent, gain_attn, w_query, w_key, w_value, w_out, gain_moe, w_router,
    shared_gate, shared_up, shared_down, expert_gate, expert_up, expert_down, expert_ids, pair_order,
):
    rows = tokens.shape[0]
    inverse = ROPE_BASE ** (-2.0 * jnp.arange(HD // 2, dtype=F32) / HD)
    inverse = jnp.concatenate([inverse, inverse])[None]
    moe, mixed, lse, ot, q, kvall, normed, att, cosf, sinf = attention_forward(
        pair_order, tokens, w_query, w_key, w_value, w_out, inverse, gain_attn[None], gain_moe[None]
    )
    moe = moe.reshape(rows, D)
    g_attn, g_mixed, gain_moe_part, wown, moe_part, g_logits = experts(
        expert_ids.T, moe, mixed, gain_moe[None], w_router.T, cotangent, shared_gate.T, shared_up.T, shared_down,
        expert_gate.transpose(0, 2, 1), expert_up.transpose(0, 2, 1), expert_down,
    )
    g_attn = g_attn.reshape(rows, D)
    output, wb, glin, fin_a = attention_backward(
        pair_order, q, kvall, lse, ot, g_attn, w_out, moe_part, mixed, wown, cosf, sinf
    )
    g_tokens, w2, gains, wa = first_norm_backward(
        glin, att, g_attn, g_logits, moe, normed, g_mixed, gain_attn[None], gain_moe_part, fin_a,
        tokens, w_query, w_key, w_value,
    )
    gq, gk, gv, go, gr, sg, su, sd, eg, eu, ed, output, g_tokens, gain_a, gain_m = widen(
        wa, wb, w2, output.reshape(rows, D), g_tokens.reshape(rows, D), gains
    )
    return (
        output, g_tokens, gain_a.reshape(D), gq, gk, gv, go, gain_m.reshape(D), gr.T,
        sg.T, su.T, sd, eg.transpose(0, 2, 1), eu.transpose(0, 2, 1), ed,
    )


def solution(mesh):
    in_specs = (
        P("ctx", None), P("ctx", None), P(), P(None, "mp"), P(None, "mp"), P(None, "mp"),
        P("mp", None), P(), P(), P(None, "mp"), P(None, "mp"), P("mp", None),
        P(None, None, "mp"), P(None, None, "mp"), P(None, "mp", None), P("ctx", None), P(),
    )
    out_specs = (
        P("ctx", None), P("ctx", None), P(), P(None, "mp"), P(None, "mp"), P(None, "mp"),
        P("mp", None), P(), P(), P(None, "mp"), P(None, "mp"), P("mp", None),
        P(None, None, "mp"), P(None, None, "mp"), P(None, "mp", None),
    )
    return jax.shard_map(
        on_device, mesh=mesh, in_specs=in_specs, out_specs=out_specs, check_vma=False
    )
```

```python
import jax
import jax.numpy as jnp
from jax import lax
from jax.experimental import pallas as pl
from jax.experimental.pallas import tpu as pltpu
from jax.sharding import PartitionSpec as P

HD = 128
CAP = 32
EPSILON = 1e-06
ROPE_BASE = 10000.0
PRECISE = lax.Precision.HIGHEST
MESH = pl.DeviceIdType.MESH
BF = jnp.bfloat16
F32 = jnp.float32
D = 2048
SH = 352
EF = 176
RD = SH + 3 * EF
RG = 2 * SH + 6 * EF
RT = 64 + 2 * 256
R2 = 2 * 256
VM = 60 * 2**20
NEG = -1e30


def nt(a, b):
    return lax.dot_general(a, b, (((1,), (1,)), ((), ())), preferred_element_type=F32)


def nn(a, b):
    return lax.dot_general(a, b, (((1,), (0,)), ((), ())), preferred_element_type=F32)


def tn(a, b):
    return lax.dot_general(a, b, (((0,), (0,)), ((), ())), preferred_element_type=F32)


def turned(a):
    return jnp.transpose(a.astype(F32)).astype(BF)


def place():
    c = lax.axis_index("ctx")
    return lax.div(c, 4), lax.rem(lax.div(c, 2), 2), lax.rem(c, 2), lax.axis_index("mp")


def chip_at(dy, t):
    y, z, core, m = place()
    return lax.rem(y + dy, 4) * 2 + lax.rem(z + t, 2)


def peer(dy, t):
    y, z, core, m = place()
    return {"ctx": chip_at(dy, t) * 2 + core}


def sibling():
    y, z, core, m = place()
    return {"ctx": chip_at(0, 0) * 2 + 1 - core}


def mp_at(d):
    m = lax.axis_index("mp")
    return lax.rem(lax.div(m, 2) + d // 2, 4) * 2 + lax.rem(lax.rem(m, 2) + d % 2, 2)


def remote(src, dst, ssem, rsem, dev):
    return pltpu.make_async_remote_copy(
        src_ref=src, dst_ref=dst, send_sem=ssem, recv_sem=rsem, device_id=dev, device_id_type=MESH
    )


def greet(far=False):
    bar = pltpu.get_barrier_semaphore()
    devs = [sibling(), peer(0, 1), peer(1, 0), peer(3, 0)] + ([peer(2, 0)] if far else [])
    devs += [{"mp": mp_at(d)} for d in range(1, 8)]
    for dev in devs:
        pl.semaphore_signal(bar, inc=1, device_id=dev, device_id_type=MESH)
    return len(devs)


def all_in(count):
    pl.semaphore_wait(pltpu.get_barrier_semaphore(), count)


def mp_send_same(src, landing, ssem, rsem):
    m = lax.axis_index("mp")
    for d in range(1, 8):
        remote(src, landing.at[m], ssem.at[d - 1], rsem.at[m], {"mp": mp_at(d)}).start()


def mp_wait_recv(landing, ssem, rsem, d):
    t = mp_at(d)
    remote(landing.at[t], landing.at[t], ssem.at[0], rsem.at[t], {"mp": t}).wait_recv()
    return t


def mp_wait_send(src, ssem):
    for d in range(1, 8):
        remote(src, src, ssem.at[d - 1], ssem.at[d - 1], {"mp": mp_at(d)}).wait_send()


def mp_place():
    m = lax.axis_index("mp")
    return lax.div(m, 2), lax.rem(m, 2)


def x_peer(dx):
    x, zh = mp_place()
    return {"mp": lax.rem(x + dx, 4) * 2 + zh}


def zh_peer():
    x, zh = mp_place()
    return {"mp": x * 2 + 1 - zh}


class MpSum:
    def __init__(self, parts, refs, ca):
        self.parts, self.ca = parts, ca
        self.xa, self.za, self.zb, self.xs, self.xr, self.s, self.r = refs
        self.x, self.zh = mp_place()
        self.a, self.b = pl.ds(0, ca), pl.ds(ca, D - ca)

    @staticmethod
    def scratch(ca):
        cb, vm = D - ca, pltpu.VMEM
        return (
            vm((3, 2, 64, ca), BF), vm((2, 64, ca), BF), vm((4, 64, cb), BF),
            vm((3, 64, cb), BF), vm((3, 64, cb), BF),
            pltpu.SemaphoreType.DMA((11,)), pltpu.SemaphoreType.DMA((11,)),
        )

    def copy(self, n, src, dst, dev):
        return remote(src, dst, self.s.at[n], self.r.at[n], dev)

    def a_copy(self, dx):
        far = lax.rem(self.x + dx, 4)
        src = self.parts.at[pl.ds(far * 2, 2), :, self.a]
        return self.copy(dx - 1, src, self.xa.at[dx - 1], x_peer(dx))

    def b_copy(self, x):
        src = self.parts.at[x * 2 + 1 - self.zh, :, self.b]
        return self.copy(4 + x, src, self.zb.at[x], zh_peer())

    def x_copy(self, dx):
        return self.copy(7 + dx, self.xs.at[dx - 1], self.xr.at[dx - 1], x_peer(dx))

    def z_copy(self):
        return self.copy(3, self.za.at[0], self.za.at[1], zh_peer())

    def start_a(self):
        for dx in range(1, 4):
            self.a_copy(dx).start()

    def start_b(self):
        for x in range(4):
            self.b_copy(x).start()

    def middle(self):
        for x in range(4):
            self.b_copy(x).wait_recv()
        for dx in range(1, 4):
            far = lax.rem(self.x + dx, 4)
            val = self.parts[far * 2 + self.zh, :, self.b].astype(F32) + self.zb[far].astype(F32)
            self.xs[dx - 1] = val.astype(BF)
            self.x_copy(dx).start()
        for dx in range(1, 4):
            self.a_copy(dx).wait_recv()
        self.za[0] = self.over_x(1 - self.zh).astype(BF)
        self.z_copy().start()

    def over_x(self, zz):
        val = self.parts[self.x * 2 + zz, :, self.a].astype(F32)
        for n in range(3):
            val = val + self.xa[n, zz].astype(F32)
        return val

    def finish(self):
        one = self.over_x(self.zh)
        two = self.parts[self.x * 2 + self.zh, :, self.b].astype(F32) + self.zb[self.x].astype(F32)
        for dx in range(1, 4):
            self.x_copy(dx).wait_recv()
            two = two + self.xr[dx - 1].astype(F32)
        self.z_copy().wait_recv()
        one = one + self.za[1].astype(F32)
        return jnp.concatenate([one, two], axis=1)

    def drain(self):
        for dx in range(1, 4):
            self.a_copy(dx).wait_send()
            self.x_copy(dx).wait_send()
        for x in range(4):
            self.b_copy(x).wait_send()
        self.z_copy().wait_send()


class MpGather:
    def __init__(self, out, sems, ca):
        self.out, (self.s, self.r) = out, sems
        self.x, self.zh = mp_place()
        self.a, self.b = pl.ds(0, ca), pl.ds(ca, D - ca)

    @staticmethod
    def sems():
        return (pltpu.SemaphoreType.DMA((14,)), pltpu.SemaphoreType.DMA((14,)))

    def copy(self, n, x, zh, cols, dev):
        ref = self.out.at[x * 2 + zh, :, cols]
        return remote(ref, ref, self.s.at[n], self.r.at[n], dev)

    def start(self):
        x, zh = self.x, self.zh
        self.copy(0, x, zh, self.a, zh_peer()).start()
        for dx in range(1, 4):
            self.copy(dx, x, zh, self.b, x_peer(dx)).start()
        self.copy(4, x, zh, self.b, zh_peer()).start()
        for dx in range(1, 4):
            self.copy(4 + dx, x, zh, self.a, x_peer(dx)).start()

    def relay(self):
        x, zh = self.x, self.zh
        self.copy(0, x, 1 - zh, self.a, zh_peer()).wait_recv()
        for dx in range(1, 4):
            self.copy(7 + dx, x, 1 - zh, self.a, x_peer(dx)).start()
        for dx in (1, 3, 2):
            back = lax.rem(x + 4 - dx, 4)
            self.copy(dx, back, zh, self.b, x_peer(dx)).wait_recv()
            self.copy(10 + dx, back, zh, self.b, zh_peer()).start()

    def finish(self):
        x, zh = self.x, self.zh
        self.copy(4, x, 1 - zh, self.b, zh_peer()).wait_recv()
        for dx in range(1, 4):
            back = lax.rem(x + 4 - dx, 4)
            self.copy(4 + dx, back, zh, self.a, x_peer(dx)).wait_recv()
            self.copy(7 + dx, back, 1 - zh, self.a, x_peer(dx)).wait_recv()
            self.copy(10 + dx, back, 1 - zh, self.b, zh_peer()).wait_recv()
        for n in range(14):
            cols = self.a if n in (0, 5, 6, 7, 8, 9, 10) else self.b
            self.copy(n, x, zh, cols, zh_peer()).wait_send()


class Gather:
    def __init__(self, buf, sems, part=None):
        self.buf, self.part, (self.s, self.r) = buf, part, sems
        y, z, self.core, m = place()

    def at(self, chip, core):
        ref = self.buf.at[chip, core]
        return ref if self.part is None else ref.at[self.part]

    @staticmethod
    def sems():
        return (pltpu.SemaphoreType.DMA((15,)), pltpu.SemaphoreType.DMA((16,)))

    def send(self, src, chip, n, dev):
        dst = self.at(chip, self.core)
        remote(src, dst, self.s.at[n], self.r.at[chip * 2 + self.core], dev).start()

    def start(self, src):
        chip = chip_at(0, 0)
        for n, dev in enumerate([peer(0, 1), peer(1, 0), peer(3, 0), sibling()]):
            self.send(src, chip, n, dev)

    def wait(self, chip, core):
        ref = self.at(chip, core)
        remote(ref, ref, self.s.at[0], self.r.at[chip * 2 + core], sibling()).wait_recv()

    def hop(self, dy, t):
        chip = chip_at(dy, t)
        self.wait(chip, self.core)
        src = self.at(chip, self.core)
        n, devs = {
            (0, 1): (4, [peer(1, 0), peer(3, 0), sibling()]),
            (3, 0): (7, [peer(1, 0), sibling()]),
            (1, 0): (9, [sibling()]),
            (3, 1): (10, [sibling()]),
            (1, 1): (11, [peer(3, 0), sibling()]),
            (2, 0): (13, [sibling()]),
            (2, 1): (14, [sibling()]),
        }[dy, t]
        for i, dev in enumerate(devs):
            self.send(src, chip, n + i, dev)
        return chip

    def other_core(self, dy, t):
        chip = chip_at(dy, t)
        self.wait(chip, 1 - self.core)

    def drain(self):
        ref = self.at(0, 0)
        for n in range(15):
            remote(ref, ref, self.s.at[n], self.s.at[n], sibling()).wait_send()


class GatherRing(Gather):
    @staticmethod
    def sems():
        return (pltpu.SemaphoreType.DMA((16,)), pltpu.SemaphoreType.DMA((18,)))

    def half(self, n, way):
        chip = chip_at(2, 0) if way is None else chip_at(way, 0)
        ref = self.at(chip, self.core).at[n]
        return remote(ref, ref, self.s.at[4 + n], self.r.at[16 + n], peer(1 if n == 0 else 3, 0))

    def near(self, n):
        dy = 3 if n == 0 else 1
        chip = chip_at(dy, 0)
        self.wait(chip, self.core)
        self.half(n, dy).start()
        self.send(self.at(chip, self.core), chip, 6 + 2 * n, peer(0, 1))
        self.send(self.at(chip, self.core), chip, 7 + 2 * n, sibling())

    def far(self):
        chip = chip_at(2, 0)
        for n in range(2):
            self.half(n, None).wait_recv()
        self.send(self.at(chip, self.core), chip, 10, peer(0, 1))
        self.send(self.at(chip, self.core), chip, 11, sibling())

    def across(self, dy):
        chip = chip_at(dy, 1)
        self.wait(chip, self.core)
        self.send(self.at(chip, self.core), chip, 12 + dy, sibling())

    def drain(self):
        ref = self.at(0, 0)
        for n in range(16):
            one = ref.at[0] if n in (4, 5) else ref
            remote(one, one, self.s.at[n], self.s.at[n], sibling()).wait_send()


HOPS = ((0, 1), (3, 0), (1, 0), (3, 1), (1, 1), (2, 0), (2, 1))


def add_rows(dst, srcs, tile):
    def body(r, carry):
        rr = pl.ds(pl.multiple_of(r * tile, 16), tile)
        total = srcs[0][rr, :].astype(F32)
        for s in srcs[1:]:
            total = total + s[rr, :].astype(F32)
        dst[rr, :] = total.astype(dst.dtype)
        return carry

    lax.fori_loop(0, dst.shape[0] // tile, body, 0)


class Scatter:
    def __init__(self, refs, tile):
        (
            self.to_sib, self.from_sib, self.sums, self.half, self.pairs,
            self.s_sib, self.r_sib, self.s_half, self.r_half, self.s_pair, self.r_pair,
        ) = refs
        self.tile = tile
        self.y, self.z, self.core, m = place()

    @staticmethod
    def scratch(rows, cols):
        dma = pltpu.SemaphoreType.DMA
        eight = pltpu.VMEM((8, rows, cols), BF)
        return (
            eight, eight, eight, pltpu.VMEM((2, rows, cols), BF), pltpu.VMEM((2, 2, rows, cols), BF),
            dma((8,)), dma((8,)), dma((2,)), dma((2,)), dma((2,)), dma((2,)),
        )

    def add(self, dst, srcs):
        add_rows(dst, srcs, self.tile)

    def piece(self, chip, terms):
        cols = pl.ds(pl.multiple_of(chip * 256, 256), 256)
        for off, rows, lhs, rhs in terms:
            val = nn(lhs[...], rhs[:, cols]).astype(BF)
            one, two = val[:, 0:HD], val[:, HD:]
            self.sums[chip, pl.ds(off, rows), :] = jnp.where(self.core == 0, one, two)
            self.to_sib[chip, pl.ds(off, rows), :] = jnp.where(self.core == 0, two, one)
        self.to_sibling(chip)

    def to_sibling(self, chip):
        remote(
            self.to_sib.at[chip], self.from_sib.at[chip], self.s_sib.at[chip], self.r_sib.at[chip], sibling()
        ).start()

    def merge(self, chip):
        got = self.from_sib.at[chip]
        remote(got, got, self.s_sib.at[0], self.r_sib.at[chip], sibling()).wait_recv()
        self.add(self.sums.at[chip], [self.sums.at[chip], got])

    def pieces(self, terms):
        def one(i, carry):
            j = lax.div(i, 2)
            dy = lax.rem(2 - j + 3 * lax.div(j * (j - 1), 2), 4)
            self.piece(chip_at(dy, lax.rem(i, 2)), terms)
            return carry

        lax.fori_loop(0, 8, one, 0)

    def merge_place(self, dy):
        self.merge(chip_at(dy, 0))
        self.merge(chip_at(dy, 1))

    def far(self):
        for t, dy in ((0, 1), (1, 3)):
            remote(
                self.sums.at[chip_at(2, t)], self.half.at[t], self.s_half.at[t], self.r_half.at[t], peer(dy, 0)
            ).start()

    def near(self, way):
        dy = 1 if way == 0 else 3
        got = self.half.at[way]
        remote(got, got, self.s_half.at[0], self.r_half.at[way], sibling()).wait_recv()
        mid = self.sums.at[chip_at(dy, way)]
        self.add(mid, [mid, got])
        both = self.sums.at[pl.ds(lax.rem(self.y + dy, 4) * 2, 2)]
        remote(both, self.pairs.at[way], self.s_pair.at[way], self.r_pair.at[way], peer(dy, 0)).start()

    def own(self, dst):
        for way in range(2):
            got = self.pairs.at[way]
            remote(got, got, self.s_pair.at[0], self.r_pair.at[way], sibling()).wait_recv()
        for t in (1, 0):
            zz = lax.rem(self.z + t, 2)
            self.add(
                dst.at[t], [self.sums.at[chip_at(0, t)], self.pairs.at[0, zz], self.pairs.at[1, zz]]
            )

    def drain(self):
        one, two = self.sums.at[0], self.pairs.at[0]
        for k in range(8):
            remote(one, one, self.s_sib.at[k], self.s_sib.at[k], sibling()).wait_send()
        for k in range(2):
            remote(one, one, self.s_half.at[k], self.s_half.at[k], sibling()).wait_send()
            remote(two, two, self.s_pair.at[k], self.s_pair.at[k], sibling()).wait_send()


def sds(shape, dtype):
    return jax.ShapeDtypeStruct(shape, dtype)


VMEM_SPEC = pl.BlockSpec(memory_space=pltpu.VMEM)
SMEM_SPEC = pl.BlockSpec(memory_space=pltpu.SMEM)
ANY_SPEC = pl.BlockSpec(memory_space=pl.ANY)
DMA = pltpu.SemaphoreType.DMA
MP_SEMS = (DMA((7,)), DMA((8,)))
CA = 1024
CO = 1792
PARTS = pltpu.VMEM((8, 64, D), BF)


def params(cid):
    return pltpu.CompilerParams(collective_id=cid, has_side_effects=True, vmem_limit_bytes=VM)


def rolled(x):
    return pltpu.roll(x, 64, axis=1)


def pick_of(order, k, cr):
    return jnp.where(order[k * 2 + cr] < order[lax.axis_index("ctx")], 0, 1)


def k1_kernel(
    order, tokens, wq, wk, wv, wo, inverse, gain_a, gain_m,
    moe, mixed, lse, ot, q, kv_out, normed_out, att, cosf, sinf,
    kvall, normed, tok, w3, wov, st_m, st_l, st_a, parts, s_in, s_out, k_sems, v_sems, sum_refs, ag_sems,
):
    y, z, core, m = place()
    chip = chip_at(0, 0)
    loads = [
        pltpu.make_async_copy(a, b, s_in.at[i])
        for i, (a, b) in enumerate(
            [(tokens, tok), (wk, w3.at[0]), (wv, w3.at[1]), (wq, w3.at[2]), (wo, wov)]
        )
    ]
    for cp in loads:
        cp.start()
    count = greet()
    loads[0].wait()

    def norm_rows(i, carry):
        rr = pl.ds(pl.multiple_of(i * 128, 128), 128)
        x = tok[rr, :].astype(F32)
        n = lax.rsqrt(jnp.mean(x * x, axis=-1, keepdims=True) + EPSILON)
        normed[rr, :] = (x * n * gain_a[...]).astype(BF)
        return carry

    lax.fori_loop(0, 4, norm_rows, 0)
    own = kvall.at[chip, core]
    loads[2].wait()

    def values(n, carry):
        rr = pl.ds(pl.multiple_of(n * 256, 256), 256)
        own[1, n] = nn(normed[rr, :], w3[1]).astype(BF)
        return carry

    lax.fori_loop(0, 2, values, 0)
    all_in(count)
    gv = GatherRing(kvall, v_sems, 1)
    gv.start(own.at[1])

    pair = order[lax.axis_index("ctx")]
    sign = jnp.where(lax.broadcasted_iota(jnp.int32, (1, HD), 1) < HD // 2, -1.0, 1.0)
    for n, first in enumerate((pair, 31 - pair)):
        pos = (lax.broadcasted_iota(jnp.int32, (256, HD), 0) + first * 256).astype(F32)
        phase = pos * inverse[...]
        cosf[pl.ds(n * 256, 256), :] = jnp.cos(phase)
        sinf[pl.ds(n * 256, 256), :] = jnp.sin(phase) * sign
    def turn(lin, rr, h):
        x = lin[:, h * HD : h * HD + HD]
        return x * cosf[rr, :] + rolled(x) * sinf[rr, :]

    loads[1].wait()

    def keys(n, carry):
        rr = pl.ds(pl.multiple_of(n * 256, 256), 256)
        lin = nn(normed[rr, :], w3[0])
        for h in range(2):
            own[0, n, :, pl.ds(h * HD, HD)] = turn(lin, rr, h).astype(BF)
        return carry

    lax.fori_loop(0, 2, keys, 0)
    gk = Gather(kvall, k_sems, 0)
    gk.start(own.at[0])
    loads[3].wait()

    def queries(n, carry):
        rr = pl.ds(pl.multiple_of(n * 256, 256), 256)
        lin = nn(normed[rr, :], w3[2])
        for h in range(2):
            q[n, :, pl.ds(h * HD, HD)] = (turn(lin, rr, h) * (HD**-0.5)).astype(BF)
        return carry

    lax.fori_loop(0, 2, queries, 0)

    st_m[...] = jnp.full_like(st_m, NEG)
    st_l[...] = jnp.zeros_like(st_l)
    st_a[...] = jnp.zeros_like(st_a)

    def online(olds, sts, vs):
        mn = [jnp.maximum(o[0], jnp.max(s, axis=0, keepdims=True)) for o, s in zip(olds, sts)]
        ps = [jnp.exp(s - a) for s, a in zip(sts, mn)]
        al = [jnp.exp(o[0] - a) for o, a in zip(olds, mn)]
        ls = [a * o[1] + jnp.sum(p, axis=0, keepdims=True) for a, o, p in zip(al, olds, ps)]
        ac = [a * o[2] + tn(v, p.astype(BF)) for a, o, v, p in zip(al, olds, vs, ps)]
        return list(zip(mn, ls, ac))

    def keep(n, h, new):
        st_m[n, h], st_l[n, h], st_a[n, h] = new

    def block(k, cr):
        s = pick_of(order, k, cr)
        sts, vs, olds = [], [], []
        for h in range(2):
            cols = pl.ds(h * HD, HD)
            k0, k1 = kvall[k, cr, 0, 0, :, cols], kvall[k, cr, 0, 1, :, cols]
            v0, v1 = kvall[k, cr, 1, 0, :, cols], kvall[k, cr, 1, 1, :, cols]
            sts += [nt(k0, q[1, :, cols]), nt(jnp.where(s == 0, k0, k1), q[s, :, cols])]
            vs += [v0, jnp.where(s == 0, v0, v1)]
            olds.append((st_m[2, h], st_l[2, h], st_a[2, h]))
            olds.append(
                (
                    jnp.where(s == 0, st_m[0, h], st_m[1, h]),
                    jnp.where(s == 0, st_l[0, h], st_l[1, h]),
                    st_a[s, h],
                )
            )
        new = online(olds, sts, vs)
        for h in range(2):
            keep(2, h, new[2 * h])
            b = new[2 * h + 1]
            for n in range(2):
                st_m[n, h] = jnp.where(s == n, b[0], st_m[n, h])
                st_l[n, h] = jnp.where(s == n, b[1], st_l[n, h])
                st_a[n, h] = jnp.where(s == n, b[2], st_a[n, h])

    tri = lax.broadcasted_iota(jnp.int32, (256, 256), 0) <= lax.broadcasted_iota(
        jnp.int32, (256, 256), 1
    )
    for h in range(2):
        cols = pl.ds(h * HD, HD)
        names = [2, 0, 1]
        sts = [nt(own[0, 0, :, cols], q[1, :, cols])]
        sts += [jnp.where(tri, nt(own[0, n, :, cols], q[n, :, cols]), NEG) for n in range(2)]
        vs = [own[1, 0, :, cols], own[1, 0, :, cols], own[1, 1, :, cols]]
        olds = [(st_m[n, h], st_l[n, h], st_a[n, h]) for n in names]
        for n, new in zip(names, online(olds, sts, vs)):
            keep(n, h, new)

    def both(dy, t):
        k = chip_at(dy, t)

        def cores(i, carry):
            cr = lax.rem(core + i, 2)

            @pl.when(i == 1)
            def _():
                gk.wait(k, cr)
                gv.wait(k, cr)

            block(k, cr)
            return carry

        lax.fori_loop(0, 2, cores, 0)

    gv.near(0)
    gv.near(1)
    gk.wait(chip, 1 - core)
    gv.wait(chip, 1 - core)
    block(chip, 1 - core)
    gk.hop(0, 1)
    gv.across(0)
    gk.hop(3, 0)
    gk.hop(1, 0)
    both(0, 1)
    gv.far()
    both(3, 0)
    both(1, 0)
    gk.hop(3, 1)
    gk.hop(1, 1)
    gk.hop(2, 0)
    gv.across(3)
    gv.across(1)
    both(2, 0)
    both(3, 1)
    gk.hop(2, 1)
    both(1, 1)
    gv.across(2)
    both(2, 1)
    stores = [
        pltpu.make_async_copy(kvall, kv_out, s_out.at[0]),
        pltpu.make_async_copy(normed, normed_out, s_out.at[1]),
    ]
    for cp in stores:
        cp.start()

    for h in range(2):
        for n in range(2):
            m0, l0, a0 = st_m[n, h], st_l[n, h], st_a[n, h]
            if n == 1:
                m2, l2, a2 = st_m[2, h], st_l[2, h], st_a[2, h]
                mn = jnp.maximum(m0, m2)
                e0, e2 = jnp.exp(m0 - mn), jnp.exp(m2 - mn)
                m0, l0, a0 = mn, e0 * l0 + e2 * l2, e0 * a0 + e2 * a2
            lse[n, h] = m0 + jnp.log(l0)
            o = a0 / l0
            ot[n, h] = o
            att[pl.ds(n * 256, 256), pl.ds(h * HD, HD)] = jnp.transpose(o).astype(BF)

    loads[4].wait()

    def out_cols(i, carry):
        cols = pl.ds(pl.multiple_of(i * 256, 256), 256)
        parts[:, :, cols] = nn(att[...], wov[:, cols]).reshape(8, 64, 256).astype(BF)
        return carry

    mps = MpSum(parts, sum_refs, CA)
    lax.fori_loop(0, CA // 256, out_cols, 0)
    mps.start_a()
    lax.fori_loop(CA // 256, 8, out_cols, 0)
    mps.start_b()
    mps.middle()
    total = tok[pl.ds(pl.multiple_of(m * 64, 64), 64), :].astype(F32) + mps.finish()
    mixed[...] = total
    n = lax.rsqrt(jnp.mean(total * total, axis=-1, keepdims=True) + EPSILON)
    moe[m] = (total * n * gain_m[...]).astype(BF)
    mpg = MpGather(moe, ag_sems, CA)
    mpg.start()
    mpg.relay()

    gk.drain()
    gv.drain()
    mps.drain()
    mpg.finish()
    for cp in stores:
        cp.wait()


def attention_forward(order, tokens, wq, wk, wv, wo, inverse, gain_a, gain_m):
    return pl.pallas_call(
        k1_kernel,
        name="attend_forward",
        out_shape=(
            sds((8, 64, D), BF),
            sds((64, D), F32),
            sds((2, 2, 1, 256), F32),
            sds((2, 2, HD, 256), F32),
            sds((2, 256, 256), BF),
            sds((8, 2, 2, 2, 256, 256), BF),
            sds((512, D), BF),
            sds((512, 256), BF),
            sds((512, HD), F32),
            sds((512, HD), F32),
        ),
        in_specs=[SMEM_SPEC] + [ANY_SPEC] * 5 + [VMEM_SPEC] * 3,
        out_specs=(VMEM_SPEC,) * 5 + (ANY_SPEC,) * 2 + (VMEM_SPEC,) * 3,
        scratch_shapes=[
            pltpu.VMEM((8, 2, 2, 2, 256, 256), BF),
            pltpu.VMEM((512, D), BF),
            pltpu.VMEM((512, D), BF),
            pltpu.VMEM((3, D, 256), BF),
            pltpu.VMEM((256, D), BF),
            pltpu.VMEM((3, 2, 1, 256), F32),
            pltpu.VMEM((3, 2, 1, 256), F32),
            pltpu.VMEM((3, 2, HD, 256), F32),
            PARTS, DMA((5,)), DMA((2,)), Gather.sems(), GatherRing.sems(), MpSum.scratch(CA), MpGather.sems(),
        ],
        compiler_params=params(1),
    )(order, tokens, wq, wk, wv, wo, inverse, gain_a, gain_m)


def swish_parts(g, u):
    s = 1.0 / (1.0 + jnp.exp(-g))
    return s, g * s


def to_column(row):
    return jnp.transpose(jnp.broadcast_to(row, (HD, HD)))[:, 0:1]


def to_row(col):
    return jnp.transpose(jnp.broadcast_to(col, (HD, HD)))[0:1, :]


def k2_kernel(
    ids, moe, mixed, gain, w_router, cot, sg, su, sd, eg, eu, ed,
    g_attn, g_mixed, gain_part, wown, fin_d, moe_part_out, g_logits,
    moe_part, wsg, wsu, wsd, weg, weu, wed, cotv, tb, tbt, pr, gt, ut, hs, gsg, gsu,
    ein, gsl, geo, gated, eo, gein, ge3, ue3, he3, tmp, amat, blk, gate_part, gmi, gate_land,
    s_in, s_out, s_z, r_z, rd_refs, rs_refs, wd, zd, mp1, sum_refs, ag_sems,
):
    y, z, core, m = place()
    loads = [
        pltpu.make_async_copy(a, b, s_in.at[i])
        for i, (a, b) in enumerate(
            [(sg, wsg), (su, wsu), (eg, weg), (eu, weu), (ed, wed), (sd, wsd), (cot, cotv)]
        )
    ]
    for cp in loads:
        cp.start()
    count = greet()

    slot = lax.broadcasted_iota(jnp.int32, (HD, 512), 0)
    holder = lax.div(slot, CAP)
    chosen = holder == ids[0:1, :]
    for k in range(1, 6):
        chosen = chosen | (holder == ids[k : k + 1, :])
    chosen = jnp.where(chosen & (slot < 3 * CAP), 1.0, 0.0)
    upto = lax.broadcasted_iota(jnp.int32, (512, 512), 0) <= lax.broadcasted_iota(
        jnp.int32, (512, 512), 1
    )
    place_of = nn(chosen.astype(BF), jnp.where(upto, 1.0, 0.0).astype(BF)) - 1.0
    table_t = jnp.where(place_of == lax.rem(slot, CAP).astype(F32), chosen, 0.0)
    tbt[...] = table_t.astype(BF)
    table = jnp.transpose(table_t)
    tb[...] = table.astype(BF)
    expert = lax.div(lax.broadcasted_iota(jnp.int32, (512, HD), 1), CAP)

    logits = nt(moe[...], w_router[...])
    e = jnp.exp(logits - jnp.max(logits, axis=-1, keepdims=True))
    probs = e / jnp.sum(e, axis=-1, keepdims=True)
    pr[...] = probs
    px = jnp.where(expert == 0, probs[:, 0:1], jnp.where(expert == 1, probs[:, 1:2], probs[:, 2:3]))
    gate_col = to_column(jnp.sum(table * px, axis=0, keepdims=True))

    hs[...] = jnp.zeros_like(hs)
    gsg[...] = jnp.zeros_like(gsg)
    gsu[...] = jnp.zeros_like(gsu)
    eo[...] = jnp.zeros_like(eo)
    gein[...] = jnp.zeros_like(gein)
    tmp[...] = jnp.zeros_like(tmp)

    def gather_in(i, carry):
        cols = pl.ds(pl.multiple_of(i * 512, 512), 512)
        ein[:, cols] = nn(tbt[...], moe[:, cols]).astype(BF)
        return carry

    lax.fori_loop(0, 4, gather_in, 0)
    loads[0].wait()
    loads[1].wait()

    def shared_in(i, carry):
        rr = pl.ds(pl.multiple_of(i * 256, 256), 256)
        g, u = nt(moe[rr, :], wsg[...]), nt(moe[rr, :], wsu[...])
        gt[rr, :] = g
        ut[rr, :] = u
        hs[rr, 0:SH] = (swish_parts(g, u)[1] * u).astype(BF)
        return carry

    lax.fori_loop(0, 2, shared_in, 0)
    for cp in loads[2:5]:
        cp.wait()
    for k in range(3):
        rr = pl.ds(k * CAP, CAP)
        g, u = nt(ein[rr, :], weg[k]), nt(ein[rr, :], weu[k])
        ge3[k] = g
        ue3[k] = u
        hid = (swish_parts(g, u)[1] * u).astype(BF)
        he3[k] = hid
        eo[rr, :] = nn(hid, wed[k])
    loads[5].wait()
    loads[6].wait()

    def slots_in(i, carry):
        cols = pl.ds(pl.multiple_of(i * 512, 512), 512)
        g = nn(tbt[...], cotv[:, cols])
        gsl[:, cols] = g.astype(BF)
        geo[:, cols] = (gate_col * g).astype(BF)
        gated[:, cols] = (gate_col * eo[:, cols]).astype(BF)
        return carry

    lax.fori_loop(0, 4, slots_in, 0)
    gate_part[...] = to_row(jnp.sum(eo[...] * gsl[...].astype(F32), axis=1, keepdims=True))
    all_in(count)
    mp_send_same(gate_part, gate_land, *mp1)

    def put_block(i, k, val):
        rr = pl.ds(k * CAP, CAP)
        tmp[k, rr, 0:EF] = val.astype(F32)
        blk[pl.ds(EF * i, EF), :] = jnp.transpose(tmp[k])[0:EF].astype(BF)

    amat[pl.ds(2 * SH, SH), :] = turned(hs[...])[0:SH]
    for k in range(3):
        put_block(6 + k, k, he3[k])
    rd = Scatter(rd_refs, 176)
    terms_d = (
        (0, SH, amat.at[pl.ds(2 * SH, SH)], cotv),
        (SH, 3 * EF, blk.at[pl.ds(6 * EF, 3 * EF)], geo),
    )
    rd.pieces(terms_d)

    def shared_back(i, carry):
        rr = pl.ds(pl.multiple_of(i * 256, 256), 256)
        gh = nt(cotv[rr, :], wsd[...])
        g, u = gt[rr, :], ut[rr, :]
        s, sw = swish_parts(g, u)
        gsg[rr, 0:SH] = (gh * u * s * (1.0 + g * (1.0 - s))).astype(BF)
        gsu[rr, 0:SH] = (gh * sw).astype(BF)
        return carry

    lax.fori_loop(0, 2, shared_back, 0)

    for k in range(3):
        rr = pl.ds(k * CAP, CAP)
        gh = nt(geo[rr, :], wed[k])
        g, u = ge3[k], ue3[k]
        s, sw = swish_parts(g, u)
        geg = (gh * u * s * (1.0 + g * (1.0 - s))).astype(BF)
        geu = (gh * sw).astype(BF)
        gein[rr, :] = (nn(geg, weg[k]) + nn(geu, weu[k])).astype(BF)
        put_block(k, k, geg)
        put_block(3 + k, k, geu)

    rd.merge_place(2)
    rd.far()

    def back_cols(i, carry):
        cols = pl.ds(pl.multiple_of(i * 256, 256), 256)
        g = nn(gsg[:, 0:SH], wsg[:, cols]) + nn(gsu[:, 0:SH], wsu[:, cols]) + nn(tb[...], gein[:, cols])
        gmi[:, :, cols] = g.reshape(8, 64, 256).astype(BF)
        return carry

    mps = MpSum(gmi, sum_refs, CA)
    lax.fori_loop(0, CA // 256, back_cols, 0)
    mps.start_a()
    lax.fori_loop(CA // 256, 8, back_cols, 0)
    mps.start_b()

    amat[pl.ds(0, SH), :] = turned(gsg[...])[0:SH]
    amat[pl.ds(SH, SH), :] = turned(gsu[...])[0:SH]
    rs = Scatter(rs_refs, 352)
    terms = (
        (0, 2 * SH, amat.at[pl.ds(0, 2 * SH)], moe),
        (2 * SH, 6 * EF, blk.at[pl.ds(0, 6 * EF)], ein),
    )
    rd.merge_place(1)
    rd.near(0)
    rd.merge_place(3)
    rd.near(1)
    rs.pieces(terms)
    rd.merge_place(0)
    rs.merge_place(2)
    rs.far()

    def out_cols(i, carry):
        cols = pl.ds(pl.multiple_of(i * 256, 256), 256)
        o = nn(hs[:, 0:SH], wsd[:, cols]) + nn(tb[...], gated[:, cols])
        moe_part[:, :, cols] = o.reshape(8, 64, 256).astype(BF)
        return carry

    lax.fori_loop(0, 8, out_cols, 0)
    store = pltpu.make_async_copy(moe_part, moe_part_out, s_out)
    store.start()

    gate = gate_part[...]
    for d in range(1, 8):
        gate = gate + gate_land[mp_wait_recv(gate_land, *mp1, d)]
    lane2 = lax.broadcasted_iota(jnp.int32, (HD, 64), 0)
    col2 = lax.broadcasted_iota(jnp.int32, (HD, 64), 1)
    member = jnp.where((lax.div(lane2, CAP) == col2) & (col2 < 3), 1.0, 0.0)
    gate_probs = lax.dot_general(
        tb[...].astype(F32) * gate, member, (((1,), (0,)), ((), ())),
        precision=PRECISE, preferred_element_type=F32,
    )
    prob = pr[...]
    g_logits[...] = (prob * (gate_probs - jnp.sum(gate_probs * prob, axis=-1, keepdims=True))).astype(BF)

    mps.middle()
    for way, dy in ((0, 1), (1, 3)):
        rs.merge_place(dy)
        rs.near(way)
    rs.merge_place(0)
    rd.own(wd)
    remote(wd.at[1], zd, s_z, r_z, peer(0, 1)).start()

    mine = pl.ds(pl.multiple_of(m * 64, 64), 64)
    total = nn(g_logits[mine, :], w_router[...]) + mps.finish()
    mx = mixed[...]
    n = lax.rsqrt(jnp.mean(mx * mx, axis=-1, keepdims=True) + EPSILON)
    gain_part[...] = jnp.sum(total * mx * n, axis=0, keepdims=True)
    gg = total * gain[...]
    gm = cotv[mine, :].astype(F32) + n * gg
    gm = gm - mx * (n * n * n) * jnp.mean(gg * mx, axis=-1, keepdims=True)
    g_mixed[...] = gm
    g_attn[m] = gm.astype(BF)
    mpg = MpGather(g_attn, ag_sems, CA)
    mpg.start()
    mpg.relay()
    remote(zd, zd, s_z, r_z, peer(0, 1)).wait_recv()
    add_rows(fin_d, [wd.at[0], zd], 176)

    rs.own(wown)
    remote(zd, zd, s_z, s_z, peer(0, 1)).wait_send()
    rd.drain()
    rs.drain()
    mps.drain()
    mp_wait_send(gate_part, mp1[0])
    store.wait()
    mpg.finish()


def experts(ids, moe, mixed, gain, w_router, cot, sg, su, sd, eg, eu, ed):
    vm = pltpu.VMEM
    return pl.pallas_call(
        k2_kernel,
        name="experts",
        out_shape=(
            sds((8, 64, D), BF),
            sds((64, D), F32),
            sds((1, D), F32),
            sds((2, RG, HD), BF),
            sds((RD, HD), BF),
            sds((8, 64, D), BF),
            sds((512, 64), BF),
        ),
        in_specs=[VMEM_SPEC] * 5 + [ANY_SPEC] * 7,
        out_specs=(VMEM_SPEC,) * 5 + (ANY_SPEC, VMEM_SPEC),
        scratch_shapes=[
            PARTS, vm((SH, D), BF), vm((SH, D), BF), vm((SH, D), BF),
            vm((3, EF, D), BF), vm((3, EF, D), BF), vm((3, EF, D), BF),
            vm((512, D), BF), vm((512, HD), BF), vm((HD, 512), BF), vm((512, 64), F32),
            vm((512, SH), F32), vm((512, SH), F32),
            vm((512, 384), BF), vm((512, 384), BF), vm((512, 384), BF),
            vm((HD, D), BF), vm((HD, D), BF), vm((HD, D), BF), vm((HD, D), BF),
            vm((HD, D), F32), vm((HD, D), BF),
            vm((3, CAP, EF), F32), vm((3, CAP, EF), F32), vm((3, CAP, EF), BF),
            vm((3, HD, 256), F32), vm((3 * SH, 512), BF), vm((9 * EF, HD), BF),
            vm((1, HD), F32), PARTS, vm((8, 1, HD), F32),
            DMA((7,)), DMA, DMA, DMA, Scatter.scratch(RD, HD), Scatter.scratch(RG, HD),
            vm((2, RD, HD), BF), vm((RD, HD), BF), MP_SEMS, MpSum.scratch(CA), MpGather.sems(),
        ],
        compiler_params=params(2),
    )(ids, moe, mixed, gain, w_router, cot, sg, su, sd, eg, eu, ed)


def k3_kernel(
    order, q, lse, ot, g_attn, wout, mixed, cosf, sinf, att, g_logits, kv_in, moe_part_in, wown_in, fin_d, moe_in, normed_in,
    output, w1, glin, fin_a,
    moe, normed, amat, wtail, ztail, kvall, moe_part, wown, do, delta, dqt, zbuf, dkz, dkv,
    s_in, s_loc, s_z, r_z, s_z2, r_z2, s_z3, r_z3, g_sems, rs_refs, tail_refs, sum_refs, ag_sems,
):
    y, z, core, m = place()
    chip = chip_at(0, 0)
    loads = []
    for i, dy in enumerate((2, 1, 3, 0)):
        pair = pl.ds(lax.rem(y + dy, 4) * 2, 2)
        loads.append(pltpu.make_async_copy(kv_in.at[pair], kvall.at[pair], s_in.at[i]))
    loads.append(pltpu.make_async_copy(wown_in.at[0], wown, s_in.at[4]))
    loads.append(pltpu.make_async_copy(moe_part_in, moe_part, s_in.at[5]))
    loads.append(pltpu.make_async_copy(moe_in, moe, s_in.at[6]))
    loads.append(pltpu.make_async_copy(normed_in, normed, s_in.at[7]))
    for cp in loads:
        cp.start()
    all_in(greet())
    gather = Gather(w1, g_sems)
    gather.start(fin_d)
    local = pltpu.make_async_copy(fin_d, w1.at[chip, core], s_loc)
    local.start()
    remote(wown_in.at[1], zbuf, s_z, r_z, peer(0, 1)).start()
    g_att = nt(g_attn[...], wout[...])
    for n in range(2):
        for h in range(2):
            piece = g_att[n * 256 : n * 256 + 256, h * HD : h * HD + HD].astype(BF)
            do[n, h] = piece
            delta[n, h] = jnp.sum(jnp.transpose(piece.astype(F32)) * ot[n, h], axis=0, keepdims=True)
    dqt[...] = jnp.zeros_like(dqt)
    mps = MpSum(moe_part, sum_refs, CO)
    rs = Scatter(rs_refs, 256)

    def terms(items):
        ps = [nt(k, qq) - ls for k, v, qq, dd, ls, de, mask in items]
        ps = [jnp.exp(p) for p in ps]
        ps = [p if i[6] is None else jnp.where(i[6], p, 0.0) for p, i in zip(ps, items)]
        ds = [(p * (nt(i[1], i[3]) - i[5])).astype(BF) for p, i in zip(ps, items)]
        dv = [nn(p.astype(BF), i[3]) for p, i in zip(ps, items)]
        dk = [nn(d, i[2]) for d, i in zip(ds, items)]
        dq = [tn(i[0], d) for d, i in zip(ds, items)]
        return list(zip(dk, dv, dq))

    def block(k, cr, dst):
        s = pick_of(order, k, cr)
        items = []
        for h in range(2):
            cols = pl.ds(h * HD, HD)
            k0, k1 = kvall[k, cr, 0, 0, :, cols], kvall[k, cr, 0, 1, :, cols]
            v0, v1 = kvall[k, cr, 1, 0, :, cols], kvall[k, cr, 1, 1, :, cols]
            items.append((k0, v0, q[1, :, cols], do[1, h], lse[1, h], delta[1, h], None))
            items.append(
                (jnp.where(s == 0, k0, k1), jnp.where(s == 0, v0, v1), q[s, :, cols], do[s, h],
                 jnp.where(s == 0, lse[0, h], lse[1, h]), jnp.where(s == 0, delta[0, h], delta[1, h]), None)
            )
        got = terms(items)
        for h in range(2):
            cols = pl.ds(h * HD, HD)
            always, picked = got[2 * h], got[2 * h + 1]
            dqt[2, h] += always[2]
            for n in range(2):
                dqt[n, h] += jnp.where(s == n, picked[2], 0.0)
            for a in range(2):
                low = always[a] + jnp.where(s == 0, picked[a], 0.0)
                high = jnp.where(s == 1, picked[a], 0.0)
                dst[pl.ds(a * 512, 256), cols] = low.astype(BF)
                dst[pl.ds(a * 512 + 256, 256), cols] = high.astype(BF)

    def both_cores(k):
        block(k, 1 - core, rs.to_sib.at[k])
        rs.to_sibling(k)
        block(k, core, rs.sums.at[k])

    def ring_place(dy):
        loads[(2, 1, 3).index(dy)].wait()

        def one(t, carry):
            both_cores(chip_at(dy, t))
            return carry

        lax.fori_loop(0, 2, one, 0)
        rs.merge(chip_at(dy, 0))
        rs.merge(chip_at(dy, 1))

    ring_place(2)
    rs.far()
    loads[5].wait()
    mps.start_a()
    mps.start_b()
    gather.hop(0, 1)
    ring_place(1)
    rs.near(0)
    gather.hop(3, 0)
    gather.hop(1, 0)
    ring_place(3)
    rs.near(1)
    gather.hop(3, 1)
    gather.hop(1, 1)
    mps.middle()
    loads[3].wait()
    both_cores(chip_at(0, 1))
    block(chip, 1 - core, rs.to_sib.at[chip])
    rs.to_sibling(chip)
    tri = lax.broadcasted_iota(jnp.int32, (256, 256), 0) <= lax.broadcasted_iota(
        jnp.int32, (256, 256), 1
    )
    for h in range(2):
        cols = pl.ds(h * HD, HD)
        kk = [kvall[chip, core, 0, n, :, cols] for n in range(2)]
        vv = [kvall[chip, core, 1, n, :, cols] for n in range(2)]
        items = [(kk[0], vv[0], q[1, :, cols], do[1, h], lse[1, h], delta[1, h], None)]
        for n in range(2):
            items.append((kk[n], vv[n], q[n, :, cols], do[n, h], lse[n, h], delta[n, h], tri))
        got = terms(items)
        dqt[2, h] += got[0][2]
        for n in range(2):
            dqt[n, h] += got[1 + n][2]
        for a in range(2):
            rs.sums[chip, pl.ds(a * 512, 256), cols] = (got[0][a] + got[1][a]).astype(BF)
            rs.sums[chip, pl.ds(a * 512 + 256, 256), cols] = got[2][a].astype(BF)
    rs.merge(chip_at(0, 1))
    rs.merge(chip)

    def back(x, rr):
        return (x * cosf[rr, :] - rolled(x) * sinf[rr, :]).astype(BF)

    for h in range(2):
        for n in range(2):
            rr = pl.ds(n * 256, 256)
            g = dqt[n, h] if n == 0 else dqt[1, h] + dqt[2, h]
            glin[0, rr, pl.ds(h * HD, HD)] = back(jnp.transpose(g) * (HD**-0.5), rr)

    loads[6].wait()
    loads[7].wait()
    amat[pl.ds(0, 64), :] = turned(g_logits[...])
    amat[pl.ds(64, 256), :] = turned(att[...])
    amat[pl.ds(320, 256), :] = turned(glin[0])
    tail = Scatter(tail_refs, RT)
    terms_w = (
        (0, 64, amat.at[pl.ds(0, 64)], moe),
        (64, 256, amat.at[pl.ds(64, 256)], g_attn),
        (320, 256, amat.at[pl.ds(320, 256)], normed),
    )

    tail.pieces(terms_w)
    tail.merge_place(2)
    tail.far()
    rs.own(dkz)
    remote(dkz.at[1], dkv, s_z2, r_z2, peer(0, 1)).start()

    output[m] = (mixed[...] + mps.finish()).astype(BF)
    mpg = MpGather(output, ag_sems, CO)
    mpg.start()

    for way, dy in ((0, 1), (1, 3)):
        tail.merge_place(dy)
        tail.near(way)
    tail.merge_place(0)
    gather.hop(2, 0)
    gather.hop(2, 1)
    remote(zbuf, zbuf, s_z, r_z, peer(0, 1)).wait_recv()
    loads[4].wait()
    add_rows(fin_a.at[pl.ds(0, RG)], [wown, zbuf], 352)
    remote(dkv, dkv, s_z2, r_z2, peer(0, 1)).wait_recv()
    for n in range(2):
        rr = pl.ds(n * 256, 256)
        for h in range(2):
            cols = pl.ds(h * HD, HD)
            kr = pl.ds(n * 256, 256)
            vr = pl.ds(512 + n * 256, 256)
            g = dkz[0, kr, cols].astype(F32) + dkv[kr, cols].astype(F32)
            glin[1, rr, cols] = back(g, rr)
            glin[2, rr, cols] = (dkz[0, vr, cols].astype(F32) + dkv[vr, cols].astype(F32)).astype(BF)
    mpg.relay()
    tail.own(wtail)
    remote(wtail.at[1], ztail, s_z3, r_z3, peer(0, 1)).start()
    remote(ztail, ztail, s_z3, r_z3, peer(0, 1)).wait_recv()
    add_rows(fin_a.at[pl.ds(RG, RT)], [wtail.at[0], ztail], RT)

    remote(ztail, ztail, s_z3, s_z3, peer(0, 1)).wait_send()
    tail.drain()
    remote(dkv, dkv, s_z2, s_z2, peer(0, 1)).wait_send()
    remote(zbuf, zbuf, s_z, s_z, peer(0, 1)).wait_send()
    rs.drain()
    mps.drain()
    mpg.finish()
    local.wait()
    gather.wait(chip, 1 - core)
    for dy, t in HOPS:
        gather.other_core(dy, t)
    gather.drain()


def attention_backward(*args):
    vm = pltpu.VMEM
    return pl.pallas_call(
        k3_kernel,
        name="attend_backward",
        out_shape=(
            sds((8, 64, D), BF), sds((8, 2, RD, HD), BF), sds((3, 512, 256), BF), sds((RG + RT, HD), BF),
        ),
        in_specs=[SMEM_SPEC] + [VMEM_SPEC] * 10 + [ANY_SPEC] * 6,
        out_specs=(VMEM_SPEC, ANY_SPEC, VMEM_SPEC, VMEM_SPEC),
        scratch_shapes=[
            vm((512, D), BF), vm((512, D), BF), vm((RT, 512), BF), vm((2, RT, HD), BF), vm((RT, HD), BF),
            vm((8, 2, 2, 2, 256, 256), BF), PARTS, vm((RG, HD), BF),
            vm((2, 2, 256, HD), BF), vm((2, 2, 1, 256), F32), vm((3, 2, HD, 256), F32),
            vm((RG, HD), BF), vm((2, 1024, 256), BF), vm((1024, 256), BF),
            DMA((8,)), DMA, DMA, DMA, DMA, DMA, DMA, DMA, Gather.sems(), Scatter.scratch(1024, 256),
            Scatter.scratch(RT, HD), MpSum.scratch(CO), MpGather.sems(),
        ],
        compiler_params=params(3),
    )(*args)


def k4_kernel(
    glin, g_mixed, gain, gain_moe_part, fin_a, tokens, wq, wk, wv, normed_in,
    g_tokens, w2out, gains, w1a,
    normed, tok, w3, amat, gni, zbuf, fin, wown, gmine, gland, gsteps, gfar,
    s_in, s_loc, s_loc2, s_z, r_z, s_gx, r_gx, s_gy, r_gy, g_sems, g_sems2, rs_refs, sum_refs, ag_sems, mp3,
):
    y, z, core, m = place()
    chip = chip_at(0, 0)
    loads = [
        pltpu.make_async_copy(a, w3.at[i], s_in.at[i]) for i, a in enumerate((wq, wk, wv))
    ]
    mine = pl.ds(pl.multiple_of(m * 64, 64), 64)
    loads.append(pltpu.make_async_copy(tokens.at[mine, :], tok, s_in.at[3]))
    loads.append(pltpu.make_async_copy(normed_in, normed, s_in.at[4]))
    for cp in loads:
        cp.start()
    count = greet(far=True)
    for cp in loads[:3]:
        cp.wait()

    def back_cols(i, carry):
        cols = pl.ds(pl.multiple_of(i * 256, 256), 256)
        g = nt(glin[0], w3[0, cols, :]) + nt(glin[1], w3[1, cols, :]) + nt(glin[2], w3[2, cols, :])
        gni[:, :, cols] = g.reshape(8, 64, 256).astype(BF)
        return carry

    mps = MpSum(gni, sum_refs, CA)
    lax.fori_loop(0, CA // 256, back_cols, 0)
    all_in(count)
    mps.start_a()
    lax.fori_loop(CA // 256, 8, back_cols, 0)
    mps.start_b()
    first = Gather(w1a, g_sems2)
    first.start(fin_a)
    local2 = pltpu.make_async_copy(fin_a, w1a.at[chip, core], s_loc2)
    local2.start()

    for cp in loads[3:]:
        cp.wait()
    for i in range(2):
        amat[pl.ds(256 * i, 256), :] = turned(glin[1 + i])
    rs = Scatter(rs_refs, R2)
    terms = ((0, R2, amat, normed),)

    rs.pieces(terms)
    rs.merge_place(2)
    rs.far()
    rs.merge_place(1)
    rs.near(0)
    mps.middle()
    rs.merge_place(3)
    rs.near(1)
    first.hop(0, 1)
    first.hop(3, 0)
    rs.merge_place(0)

    total = mps.finish()
    src = tok[...].astype(F32)
    n = lax.rsqrt(jnp.mean(src * src, axis=-1, keepdims=True) + EPSILON)
    gg = total * gain[...]
    gs = n * gg - src * (n * n * n) * jnp.mean(gg * src, axis=-1, keepdims=True)
    g_tokens[m] = (g_mixed[...] + gs).astype(BF)
    gmine[pl.ds(0, 1), :] = gain_moe_part[...]
    gmine[pl.ds(1, 1), :] = jnp.sum(total * src * n, axis=0, keepdims=True)
    mp_send_same(gmine, gland, *mp3)
    mpg = MpGather(g_tokens, ag_sems, CA)
    mpg.start()
    first.hop(1, 0)
    rs.own(wown)
    remote(wown.at[1], zbuf, s_z, r_z, peer(0, 1)).start()
    mpg.relay()

    def gain_step(i, dev):
        return remote(gsteps.at[2 * i], gsteps.at[2 * i + 1], s_gx.at[i], r_gx.at[i], dev)

    remote(zbuf, zbuf, s_z, r_z, peer(0, 1)).wait_recv()
    add_rows(fin, [wown.at[0], zbuf], R2)
    gather = Gather(w2out, g_sems)
    gather.start(fin)
    first.hop(3, 1)
    first.hop(1, 1)
    local = pltpu.make_async_copy(fin, w2out.at[chip, core], s_loc)
    local.start()

    gsum = gmine[...]
    for d in range(1, 8):
        gsum = gsum + gland[mp_wait_recv(gland, *mp3, d)]
    gsteps[0] = gsum
    gain_step(0, sibling()).start()
    first.hop(2, 0)
    first.hop(2, 1)
    gain_step(0, sibling()).wait_recv()
    gsteps[2] = gsteps[0] + gsteps[1]
    gain_step(1, peer(0, 1)).start()
    gather.hop(0, 1)
    gain_step(1, peer(0, 1)).wait_recv()
    gfar[y] = gsteps[2] + gsteps[3]
    for d in range(1, 4):
        remote(gfar.at[y], gfar.at[y], s_gy.at[d - 1], r_gy.at[y], peer(d, 0)).start()
    for dy, t in HOPS[1:]:
        gather.hop(dy, t)
    for d in range(1, 4):
        yy = lax.rem(y + d, 4)
        remote(gfar.at[yy], gfar.at[yy], s_gy.at[0], r_gy.at[yy], peer(d, 0)).wait_recv()
    gains[...] = gfar[0] + gfar[1] + gfar[2] + gfar[3]

    for i, dev in enumerate((sibling(), peer(0, 1))):
        remote(gsteps.at[0], gsteps.at[0], s_gx.at[i], s_gx.at[i], dev).wait_send()
    for d in range(1, 4):
        remote(gfar.at[0], gfar.at[0], s_gy.at[d - 1], s_gy.at[d - 1], peer(d, 0)).wait_send()
    remote(zbuf, zbuf, s_z, s_z, peer(0, 1)).wait_send()
    rs.drain()
    mp_wait_send(gmine, mp3[0])
    mps.drain()
    mpg.finish()
    local.wait()
    local2.wait()
    for g in (first, gather):
        g.wait(chip, 1 - core)
        for dy, t in HOPS:
            g.other_core(dy, t)
        g.drain()


def first_norm_backward(*args):
    vm = pltpu.VMEM
    return pl.pallas_call(
        k4_kernel,
        name="first_norm_backward",
        out_shape=(
            sds((8, 64, D), BF), sds((8, 2, R2, HD), BF), sds((2, D), F32), sds((8, 2, RG + RT, HD), BF),
        ),
        in_specs=[VMEM_SPEC] * 5 + [ANY_SPEC] * 5,
        out_specs=(VMEM_SPEC, ANY_SPEC, VMEM_SPEC, ANY_SPEC),
        scratch_shapes=[
            vm((512, D), BF), vm((64, D), BF), vm((3, D, 256), BF), vm((R2, 512), BF), PARTS, vm((R2, HD), BF), vm((R2, HD), BF),
            vm((2, R2, HD), BF), vm((2, D), F32), vm((8, 2, D), F32), vm((4, 2, D), F32), vm((4, 2, D), F32),
            DMA((5,)), DMA, DMA, DMA, DMA, DMA((2,)), DMA((2,)), DMA((3,)), DMA((4,)),
            Gather.sems(), Gather.sems(), Scatter.scratch(R2, HD), MpSum.scratch(CA), MpGather.sems(), MP_SEMS,
        ],
        compiler_params=params(4),
    )(*args)


def widen_kernel(
    wa, wb, w2, out_in, tok_in, gains,
    gq, gk, gv, go, gr, sg, su, sd, eg, eu, ed, out, tok, gain_a, gain_m,
):
    def flip(src, off):
        return jnp.transpose(src[0, 0, pl.ds(off, 256), :].astype(F32))

    gr[...] = wa[0, 0, pl.ds(RG, 64), :].astype(F32)
    go[...] = wa[0, 0, pl.ds(RG + 64, 256), :].astype(F32)
    gq[...] = flip(wa, RG + 320)
    gk[...] = flip(w2, 0)
    gv[...] = flip(w2, 256)
    sg[...] = wa[0, 0, pl.ds(0, SH), :].astype(F32)
    su[...] = wa[0, 0, pl.ds(SH, SH), :].astype(F32)
    sd[...] = wb[0, 0, pl.ds(0, SH), :].astype(F32)
    for k in range(3):
        eg[k] = wa[0, 0, pl.ds(2 * SH + EF * k, EF), :].astype(F32)
        eu[k] = wa[0, 0, pl.ds(2 * SH + EF * (3 + k), EF), :].astype(F32)
        ed[k] = wb[0, 0, pl.ds(SH + EF * k, EF), :].astype(F32)
    out[...] = out_in[...]
    tok[...] = tok_in[...]
    gain_m[...] = gains[pl.ds(0, 1), :]
    gain_a[...] = gains[pl.ds(1, 1), :]


def widen(wa, wb, w2, out_in, tok_in, gains):
    def rows(width):
        return sds((D, width), F32), pl.BlockSpec((HD, width), lambda i: (i, 0))

    def cols(height):
        return sds((height, D), F32), pl.BlockSpec((height, HD), lambda i: (0, i))

    three = sds((3, EF, D), F32), pl.BlockSpec((3, EF, HD), lambda i: (0, 0, i))
    whole = pl.BlockSpec((32, D), lambda i: (i, 0))
    gain = sds((1, D), F32), pl.BlockSpec((1, HD), lambda i: (0, i))
    outs = [rows(256), rows(256), rows(256), cols(256), cols(64), cols(SH), cols(SH), cols(SH)]
    outs += [three, three, three, (sds((512, D), BF), whole), (sds((512, D), BF), whole), gain, gain]
    return pl.pallas_call(
        widen_kernel,
        name="widen",
        grid=(16,),
        out_shape=[o[0] for o in outs],
        in_specs=[
            pl.BlockSpec((1, 1, w.shape[2], HD), lambda i: (i // 2, i % 2, 0, 0)) for w in (wa, wb, w2)
        ]
        + [whole, whole, pl.BlockSpec((2, HD), lambda i: (0, i))],
        out_specs=[o[1] for o in outs],
        compiler_params=pltpu.CompilerParams(vmem_limit_bytes=VM),
    )(wa, wb, w2, out_in, tok_in, gains)


def on_device(
    tokens, cotangent, gain_attn, w_query, w_key, w_value, w_out, gain_moe, w_router,
    shared_gate, shared_up, shared_down, expert_gate, expert_up, expert_down, expert_ids, pair_order,
):
    rows = tokens.shape[0]
    inverse = ROPE_BASE ** (-2.0 * jnp.arange(HD // 2, dtype=F32) / HD)
    inverse = jnp.concatenate([inverse, inverse])[None]
    moe, mixed, lse, ot, q, kvall, normed, att, cosf, sinf = attention_forward(
        pair_order, tokens, w_query, w_key, w_value, w_out, inverse, gain_attn[None], gain_moe[None]
    )
    moe = moe.reshape(rows, D)
    g_attn, g_mixed, gain_moe_part, wown, fin_d, moe_part, g_logits = experts(
        expert_ids.T, moe, mixed, gain_moe[None], w_router.T, cotangent, shared_gate.T, shared_up.T, shared_down,
        expert_gate.transpose(0, 2, 1), expert_up.transpose(0, 2, 1), expert_down,
    )
    g_attn = g_attn.reshape(rows, D)
    output, wb, glin, fin_a = attention_backward(
        pair_order, q, lse, ot, g_attn, w_out, mixed, cosf, sinf, att, g_logits, kvall, moe_part, wown, fin_d, moe, normed
    )
    g_tokens, w2, gains, wa = first_norm_backward(
        glin, g_mixed, gain_attn[None], gain_moe_part, fin_a, tokens, w_query, w_key, w_value, normed,
    )
    gq, gk, gv, go, gr, sg, su, sd, eg, eu, ed, output, g_tokens, gain_a, gain_m = widen(
        wa, wb, w2, output.reshape(rows, D), g_tokens.reshape(rows, D), gains
    )
    return (
        output, g_tokens, gain_a.reshape(D), gq, gk, gv, go, gain_m.reshape(D), gr.T,
        sg.T, su.T, sd, eg.transpose(0, 2, 1), eu.transpose(0, 2, 1), ed,
    )


def solution(mesh):
    in_specs = (
        P("ctx", None), P("ctx", None), P(), P(None, "mp"), P(None, "mp"), P(None, "mp"),
        P("mp", None), P(), P(), P(None, "mp"), P(None, "mp"), P("mp", None),
        P(None, None, "mp"), P(None, None, "mp"), P(None, "mp", None), P("ctx", None), P(),
    )
    out_specs = (
        P("ctx", None), P("ctx", None), P(), P(None, "mp"), P(None, "mp"), P(None, "mp"),
        P("mp", None), P(), P(), P(None, "mp"), P(None, "mp"), P("mp", None),
        P(None, None, "mp"), P(None, None, "mp"), P(None, "mp", None),
    )
    return jax.shard_map(
        on_device, mesh=mesh, in_specs=in_specs, out_specs=out_specs, check_vma=False
    )
```

```python
import jax
import jax.numpy as jnp
from jax import lax
from jax.experimental import pallas as pl
from jax.experimental.pallas import tpu as pltpu
from jax.sharding import PartitionSpec as P

HD = 128
CAP = 32
EPSILON = 1e-06
ROPE_BASE = 10000.0
PRECISE = lax.Precision.HIGHEST
MESH = pl.DeviceIdType.MESH
BF = jnp.bfloat16
F32 = jnp.float32
D = 2048
SH = 352
EF = 176
RD = SH + 3 * EF
RG = 2 * SH + 6 * EF
RT = 64 + 2 * 256
R2 = 2 * 256
VM = 60 * 2**20
NEG = -1e30


def nt(a, b):
    return lax.dot_general(a, b, (((1,), (1,)), ((), ())), preferred_element_type=F32)


def nn(a, b):
    return lax.dot_general(a, b, (((1,), (0,)), ((), ())), preferred_element_type=F32)


def tn(a, b):
    return lax.dot_general(a, b, (((0,), (0,)), ((), ())), preferred_element_type=F32)


def turned(a):
    return jnp.transpose(a.astype(F32)).astype(BF)


def place():
    c = lax.axis_index("ctx")
    return lax.div(c, 4), lax.rem(lax.div(c, 2), 2), lax.rem(c, 2), lax.axis_index("mp")


def chip_at(dy, t):
    y, z, core, m = place()
    return lax.rem(y + dy, 4) * 2 + lax.rem(z + t, 2)


def peer(dy, t):
    y, z, core, m = place()
    return {"ctx": chip_at(dy, t) * 2 + core}


def sibling():
    y, z, core, m = place()
    return {"ctx": chip_at(0, 0) * 2 + 1 - core}


def mp_at(d):
    m = lax.axis_index("mp")
    return lax.rem(lax.div(m, 2) + d // 2, 4) * 2 + lax.rem(lax.rem(m, 2) + d % 2, 2)


def remote(src, dst, ssem, rsem, dev):
    return pltpu.make_async_remote_copy(
        src_ref=src, dst_ref=dst, send_sem=ssem, recv_sem=rsem, device_id=dev, device_id_type=MESH
    )


def greet(far=False):
    bar = pltpu.get_barrier_semaphore()
    devs = [sibling(), peer(0, 1), peer(1, 0), peer(3, 0)] + ([peer(2, 0)] if far else [])
    devs += [{"mp": mp_at(d)} for d in range(1, 8)]
    for dev in devs:
        pl.semaphore_signal(bar, inc=1, device_id=dev, device_id_type=MESH)
    return len(devs)


def all_in(count):
    pl.semaphore_wait(pltpu.get_barrier_semaphore(), count)


def mp_send_same(src, landing, ssem, rsem):
    m = lax.axis_index("mp")
    for d in range(1, 8):
        remote(src, landing.at[m], ssem.at[d - 1], rsem.at[m], {"mp": mp_at(d)}).start()


def mp_wait_recv(landing, ssem, rsem, d):
    t = mp_at(d)
    remote(landing.at[t], landing.at[t], ssem.at[0], rsem.at[t], {"mp": t}).wait_recv()
    return t


def mp_wait_send(src, ssem):
    for d in range(1, 8):
        remote(src, src, ssem.at[d - 1], ssem.at[d - 1], {"mp": mp_at(d)}).wait_send()


def mp_place():
    m = lax.axis_index("mp")
    return lax.div(m, 2), lax.rem(m, 2)


def x_peer(dx):
    x, zh = mp_place()
    return {"mp": lax.rem(x + dx, 4) * 2 + zh}


def zh_peer():
    x, zh = mp_place()
    return {"mp": x * 2 + 1 - zh}


class MpSum:
    def __init__(self, parts, refs, ca):
        self.parts, self.ca = parts, ca
        self.xa, self.za, self.zb, self.xs, self.xr, self.s, self.r = refs
        self.x, self.zh = mp_place()
        self.a, self.b = pl.ds(0, ca), pl.ds(ca, D - ca)

    @staticmethod
    def scratch(ca):
        cb, vm = D - ca, pltpu.VMEM
        return (
            vm((3, 2, 64, ca), BF), vm((2, 64, ca), BF), vm((4, 64, cb), BF),
            vm((3, 64, cb), BF), vm((3, 64, cb), BF),
            pltpu.SemaphoreType.DMA((11,)), pltpu.SemaphoreType.DMA((11,)),
        )

    def copy(self, n, src, dst, dev):
        return remote(src, dst, self.s.at[n], self.r.at[n], dev)

    def a_copy(self, dx):
        far = lax.rem(self.x + dx, 4)
        src = self.parts.at[pl.ds(far * 2, 2), :, self.a]
        return self.copy(dx - 1, src, self.xa.at[dx - 1], x_peer(dx))

    def b_copy(self, x):
        src = self.parts.at[x * 2 + 1 - self.zh, :, self.b]
        return self.copy(4 + x, src, self.zb.at[x], zh_peer())

    def x_copy(self, dx):
        return self.copy(7 + dx, self.xs.at[dx - 1], self.xr.at[dx - 1], x_peer(dx))

    def z_copy(self):
        return self.copy(3, self.za.at[0], self.za.at[1], zh_peer())

    def start_a(self):
        for dx in range(1, 4):
            self.a_copy(dx).start()

    def start_b(self):
        for x in range(4):
            self.b_copy(x).start()

    def middle(self):
        for x in range(4):
            self.b_copy(x).wait_recv()
        for dx in range(1, 4):
            far = lax.rem(self.x + dx, 4)
            val = self.parts[far * 2 + self.zh, :, self.b].astype(F32) + self.zb[far].astype(F32)
            self.xs[dx - 1] = val.astype(BF)
            self.x_copy(dx).start()
        for dx in range(1, 4):
            self.a_copy(dx).wait_recv()
        self.za[0] = self.over_x(1 - self.zh).astype(BF)
        self.z_copy().start()

    def over_x(self, zz):
        val = self.parts[self.x * 2 + zz, :, self.a].astype(F32)
        for n in range(3):
            val = val + self.xa[n, zz].astype(F32)
        return val

    def finish(self):
        one = self.over_x(self.zh)
        two = self.parts[self.x * 2 + self.zh, :, self.b].astype(F32) + self.zb[self.x].astype(F32)
        for dx in range(1, 4):
            self.x_copy(dx).wait_recv()
            two = two + self.xr[dx - 1].astype(F32)
        self.z_copy().wait_recv()
        one = one + self.za[1].astype(F32)
        return jnp.concatenate([one, two], axis=1)

    def drain(self):
        for dx in range(1, 4):
            self.a_copy(dx).wait_send()
            self.x_copy(dx).wait_send()
        for x in range(4):
            self.b_copy(x).wait_send()
        self.z_copy().wait_send()


class MpGather:
    def __init__(self, out, sems, ca):
        self.out, (self.s, self.r) = out, sems
        self.x, self.zh = mp_place()
        self.a, self.b = pl.ds(0, ca), pl.ds(ca, D - ca)

    @staticmethod
    def sems():
        return (pltpu.SemaphoreType.DMA((14,)), pltpu.SemaphoreType.DMA((14,)))

    def copy(self, n, x, zh, cols, dev):
        ref = self.out.at[x * 2 + zh, :, cols]
        return remote(ref, ref, self.s.at[n], self.r.at[n], dev)

    def start(self):
        x, zh = self.x, self.zh
        self.copy(0, x, zh, self.a, zh_peer()).start()
        for dx in range(1, 4):
            self.copy(dx, x, zh, self.b, x_peer(dx)).start()
        self.copy(4, x, zh, self.b, zh_peer()).start()
        for dx in range(1, 4):
            self.copy(4 + dx, x, zh, self.a, x_peer(dx)).start()

    def relay(self):
        x, zh = self.x, self.zh
        self.copy(0, x, 1 - zh, self.a, zh_peer()).wait_recv()
        for dx in range(1, 4):
            self.copy(7 + dx, x, 1 - zh, self.a, x_peer(dx)).start()
        for dx in (1, 3, 2):
            back = lax.rem(x + 4 - dx, 4)
            self.copy(dx, back, zh, self.b, x_peer(dx)).wait_recv()
            self.copy(10 + dx, back, zh, self.b, zh_peer()).start()

    def finish(self):
        x, zh = self.x, self.zh
        self.copy(4, x, 1 - zh, self.b, zh_peer()).wait_recv()
        for dx in range(1, 4):
            back = lax.rem(x + 4 - dx, 4)
            self.copy(4 + dx, back, zh, self.a, x_peer(dx)).wait_recv()
            self.copy(7 + dx, back, 1 - zh, self.a, x_peer(dx)).wait_recv()
            self.copy(10 + dx, back, 1 - zh, self.b, zh_peer()).wait_recv()
        for n in range(14):
            cols = self.a if n in (0, 5, 6, 7, 8, 9, 10) else self.b
            self.copy(n, x, zh, cols, zh_peer()).wait_send()


class Gather:
    def __init__(self, buf, sems, part=None):
        self.buf, self.part, (self.s, self.r) = buf, part, sems
        y, z, self.core, m = place()

    def at(self, chip, core):
        ref = self.buf.at[chip, core]
        return ref if self.part is None else ref.at[self.part]

    @staticmethod
    def sems():
        return (pltpu.SemaphoreType.DMA((15,)), pltpu.SemaphoreType.DMA((16,)))

    def send(self, src, chip, n, dev):
        dst = self.at(chip, self.core)
        remote(src, dst, self.s.at[n], self.r.at[chip * 2 + self.core], dev).start()

    def start(self, src):
        chip = chip_at(0, 0)
        for n, dev in enumerate([peer(0, 1), peer(1, 0), peer(3, 0), sibling()]):
            self.send(src, chip, n, dev)

    def wait(self, chip, core):
        ref = self.at(chip, core)
        remote(ref, ref, self.s.at[0], self.r.at[chip * 2 + core], sibling()).wait_recv()

    def hop(self, dy, t):
        chip = chip_at(dy, t)
        self.wait(chip, self.core)
        src = self.at(chip, self.core)
        n, devs = {
            (0, 1): (4, [peer(1, 0), peer(3, 0), sibling()]),
            (3, 0): (7, [peer(1, 0), sibling()]),
            (1, 0): (9, [sibling()]),
            (3, 1): (10, [sibling()]),
            (1, 1): (11, [peer(3, 0), sibling()]),
            (2, 0): (13, [sibling()]),
            (2, 1): (14, [sibling()]),
        }[dy, t]
        for i, dev in enumerate(devs):
            self.send(src, chip, n + i, dev)
        return chip

    def other_core(self, dy, t):
        chip = chip_at(dy, t)
        self.wait(chip, 1 - self.core)

    def drain(self):
        ref = self.at(0, 0)
        for n in range(15):
            remote(ref, ref, self.s.at[n], self.s.at[n], sibling()).wait_send()


class GatherPair(Gather):
    def start(self, own, other):
        here, across = chip_at(0, 0), chip_at(0, 1)
        self.send(own, here, 1, peer(1, 0))
        self.send(other, across, 5, peer(3, 0))
        self.send(other, across, 4, peer(1, 0))
        self.send(own, here, 2, peer(3, 0))
        self.send(own, here, 3, sibling())
        self.send(other, across, 6, sibling())

    def drain(self):
        ref = self.at(0, 0)
        for n in range(1, 15):
            remote(ref, ref, self.s.at[n], self.s.at[n], sibling()).wait_send()


class GatherRing(Gather):
    @staticmethod
    def sems():
        return (pltpu.SemaphoreType.DMA((16,)), pltpu.SemaphoreType.DMA((18,)))

    def half(self, n, way):
        chip = chip_at(2, 0) if way is None else chip_at(way, 0)
        ref = self.at(chip, self.core).at[n]
        return remote(ref, ref, self.s.at[4 + n], self.r.at[16 + n], peer(1 if n == 0 else 3, 0))

    def near(self, n):
        dy = 3 if n == 0 else 1
        chip = chip_at(dy, 0)
        self.wait(chip, self.core)
        self.half(n, dy).start()
        self.send(self.at(chip, self.core), chip, 6 + 2 * n, peer(0, 1))
        self.send(self.at(chip, self.core), chip, 7 + 2 * n, sibling())

    def far(self):
        chip = chip_at(2, 0)
        for n in range(2):
            self.half(n, None).wait_recv()
        self.send(self.at(chip, self.core), chip, 10, peer(0, 1))
        self.send(self.at(chip, self.core), chip, 11, sibling())

    def across(self, dy):
        chip = chip_at(dy, 1)
        self.wait(chip, self.core)
        self.send(self.at(chip, self.core), chip, 12 + dy, sibling())

    def drain(self):
        ref = self.at(0, 0)
        for n in range(16):
            one = ref.at[0] if n in (4, 5) else ref
            remote(one, one, self.s.at[n], self.s.at[n], sibling()).wait_send()


HOPS = ((0, 1), (3, 0), (1, 0), (3, 1), (1, 1), (2, 0), (2, 1))


def add_rows(dst, srcs, tile):
    def body(r, carry):
        rr = pl.ds(pl.multiple_of(r * tile, 16), tile)
        total = srcs[0][rr, :].astype(F32)
        for s in srcs[1:]:
            total = total + s[rr, :].astype(F32)
        dst[rr, :] = total.astype(dst.dtype)
        return carry

    lax.fori_loop(0, dst.shape[0] // tile, body, 0)


class Scatter:
    def __init__(self, refs, tile):
        (
            self.to_sib, self.from_sib, self.sums, self.half, self.pairs,
            self.s_sib, self.r_sib, self.s_half, self.r_half, self.s_pair, self.r_pair,
        ) = refs
        self.tile = tile
        self.y, self.z, self.core, m = place()

    @staticmethod
    def scratch(rows, cols):
        dma = pltpu.SemaphoreType.DMA
        eight = pltpu.VMEM((8, rows, cols), BF)
        return (
            eight, eight, eight, pltpu.VMEM((2, rows, cols), BF), pltpu.VMEM((2, 2, rows, cols), BF),
            dma((8,)), dma((8,)), dma((2,)), dma((2,)), dma((2,)), dma((2,)),
        )

    def add(self, dst, srcs):
        add_rows(dst, srcs, self.tile)

    def piece(self, chip, terms):
        cols = pl.ds(pl.multiple_of(chip * 256, 256), 256)
        for off, rows, lhs, rhs in terms:
            val = nn(lhs[...], rhs[:, cols]).astype(BF)
            one, two = val[:, 0:HD], val[:, HD:]
            self.sums[chip, pl.ds(off, rows), :] = jnp.where(self.core == 0, one, two)
            self.to_sib[chip, pl.ds(off, rows), :] = jnp.where(self.core == 0, two, one)
        self.to_sibling(chip)

    def to_sibling(self, chip):
        remote(
            self.to_sib.at[chip], self.from_sib.at[chip], self.s_sib.at[chip], self.r_sib.at[chip], sibling()
        ).start()

    def merge(self, chip):
        got = self.from_sib.at[chip]
        remote(got, got, self.s_sib.at[0], self.r_sib.at[chip], sibling()).wait_recv()
        self.add(self.sums.at[chip], [self.sums.at[chip], got])

    def pieces(self, terms):
        def one(i, carry):
            j = lax.div(i, 2)
            dy = lax.rem(2 - j + 3 * lax.div(j * (j - 1), 2), 4)
            self.piece(chip_at(dy, lax.rem(i, 2)), terms)
            return carry

        lax.fori_loop(0, 8, one, 0)

    def merge_place(self, dy):
        self.merge(chip_at(dy, 0))
        self.merge(chip_at(dy, 1))

    def far(self):
        for t, dy in ((0, 1), (1, 3)):
            remote(
                self.sums.at[chip_at(2, t)], self.half.at[t], self.s_half.at[t], self.r_half.at[t], peer(dy, 0)
            ).start()

    def near(self, way):
        dy = 1 if way == 0 else 3
        got = self.half.at[way]
        remote(got, got, self.s_half.at[0], self.r_half.at[way], sibling()).wait_recv()
        mid = self.sums.at[chip_at(dy, way)]
        self.add(mid, [mid, got])
        both = self.sums.at[pl.ds(lax.rem(self.y + dy, 4) * 2, 2)]
        remote(both, self.pairs.at[way], self.s_pair.at[way], self.r_pair.at[way], peer(dy, 0)).start()

    def own(self, dst):
        for way in range(2):
            got = self.pairs.at[way]
            remote(got, got, self.s_pair.at[0], self.r_pair.at[way], sibling()).wait_recv()
        for t in (1, 0):
            zz = lax.rem(self.z + t, 2)
            self.add(
                dst.at[t], [self.sums.at[chip_at(0, t)], self.pairs.at[0, zz], self.pairs.at[1, zz]]
            )

    def drain(self):
        one, two = self.sums.at[0], self.pairs.at[0]
        for k in range(8):
            remote(one, one, self.s_sib.at[k], self.s_sib.at[k], sibling()).wait_send()
        for k in range(2):
            remote(one, one, self.s_half.at[k], self.s_half.at[k], sibling()).wait_send()
            remote(two, two, self.s_pair.at[k], self.s_pair.at[k], sibling()).wait_send()


def sds(shape, dtype):
    return jax.ShapeDtypeStruct(shape, dtype)


VMEM_SPEC = pl.BlockSpec(memory_space=pltpu.VMEM)
SMEM_SPEC = pl.BlockSpec(memory_space=pltpu.SMEM)
ANY_SPEC = pl.BlockSpec(memory_space=pl.ANY)
DMA = pltpu.SemaphoreType.DMA
MP_SEMS = (DMA((7,)), DMA((8,)))
CA = 1024
CO = 1792
PARTS = pltpu.VMEM((8, 64, D), BF)


def params(cid, vmem=VM):
    return pltpu.CompilerParams(collective_id=cid, has_side_effects=True, vmem_limit_bytes=vmem)


def rolled(x):
    return pltpu.roll(x, 64, axis=1)


def pick_of(order, k, cr):
    return jnp.where(order[k * 2 + cr] < order[lax.axis_index("ctx")], 0, 1)


def k1_kernel(
    order, tokens, wq, wk, wv, wo, inverse, gain_a, gain_m,
    moe, mixed, lse, ot, q, kv_out, normed_out, att, cosf, sinf,
    kvall, normed, tok, w3, wov, st_m, st_l, st_a, parts, s_in, s_out, k_sems, v_sems, sum_refs, ag_sems,
):
    y, z, core, m = place()
    chip = chip_at(0, 0)
    loads = [
        pltpu.make_async_copy(a, b, s_in.at[i])
        for i, (a, b) in enumerate(
            [(tokens, tok), (wk, w3.at[0]), (wv, w3.at[1]), (wq, w3.at[2]), (wo, wov)]
        )
    ]
    for cp in loads:
        cp.start()
    count = greet()
    loads[0].wait()

    def norm_rows(i, carry):
        rr = pl.ds(pl.multiple_of(i * 128, 128), 128)
        x = tok[rr, :].astype(F32)
        n = lax.rsqrt(jnp.mean(x * x, axis=-1, keepdims=True) + EPSILON)
        normed[rr, :] = (x * n * gain_a[...]).astype(BF)
        return carry

    lax.fori_loop(0, 4, norm_rows, 0)
    own = kvall.at[chip, core]
    loads[2].wait()

    def values(n, carry):
        rr = pl.ds(pl.multiple_of(n * 256, 256), 256)
        own[1, n] = nn(normed[rr, :], w3[1]).astype(BF)
        return carry

    lax.fori_loop(0, 2, values, 0)
    all_in(count)
    gv = GatherRing(kvall, v_sems, 1)
    gv.start(own.at[1])

    pair = order[lax.axis_index("ctx")]
    sign = jnp.where(lax.broadcasted_iota(jnp.int32, (1, HD), 1) < HD // 2, -1.0, 1.0)
    for n, first in enumerate((pair, 31 - pair)):
        pos = (lax.broadcasted_iota(jnp.int32, (256, HD), 0) + first * 256).astype(F32)
        phase = pos * inverse[...]
        cosf[pl.ds(n * 256, 256), :] = jnp.cos(phase)
        sinf[pl.ds(n * 256, 256), :] = jnp.sin(phase) * sign
    def turn(lin, rr, h):
        x = lin[:, h * HD : h * HD + HD]
        return x * cosf[rr, :] + rolled(x) * sinf[rr, :]

    loads[1].wait()

    def keys(n, carry):
        rr = pl.ds(pl.multiple_of(n * 256, 256), 256)
        lin = nn(normed[rr, :], w3[0])
        for h in range(2):
            own[0, n, :, pl.ds(h * HD, HD)] = turn(lin, rr, h).astype(BF)
        return carry

    lax.fori_loop(0, 2, keys, 0)
    gk = Gather(kvall, k_sems, 0)
    gk.start(own.at[0])
    loads[3].wait()

    def queries(n, carry):
        rr = pl.ds(pl.multiple_of(n * 256, 256), 256)
        lin = nn(normed[rr, :], w3[2])
        for h in range(2):
            q[n, :, pl.ds(h * HD, HD)] = (turn(lin, rr, h) * (HD**-0.5)).astype(BF)
        return carry

    lax.fori_loop(0, 2, queries, 0)

    st_m[...] = jnp.full_like(st_m, NEG)
    st_l[...] = jnp.zeros_like(st_l)
    st_a[...] = jnp.zeros_like(st_a)

    def online(olds, sts, vs):
        mn = [jnp.maximum(o[0], jnp.max(s, axis=0, keepdims=True)) for o, s in zip(olds, sts)]
        ps = [jnp.exp(s - a) for s, a in zip(sts, mn)]
        al = [jnp.exp(o[0] - a) for o, a in zip(olds, mn)]
        ls = [a * o[1] + jnp.sum(p, axis=0, keepdims=True) for a, o, p in zip(al, olds, ps)]
        ac = [a * o[2] + tn(v, p.astype(BF)) for a, o, v, p in zip(al, olds, vs, ps)]
        return list(zip(mn, ls, ac))

    def keep(n, h, new):
        st_m[n, h], st_l[n, h], st_a[n, h] = new

    def block(k, cr):
        s = pick_of(order, k, cr)
        sts, vs, olds = [], [], []
        for h in range(2):
            cols = pl.ds(h * HD, HD)
            k0, k1 = kvall[k, cr, 0, 0, :, cols], kvall[k, cr, 0, 1, :, cols]
            v0, v1 = kvall[k, cr, 1, 0, :, cols], kvall[k, cr, 1, 1, :, cols]
            sts += [nt(k0, q[1, :, cols]), nt(jnp.where(s == 0, k0, k1), q[s, :, cols])]
            vs += [v0, jnp.where(s == 0, v0, v1)]
            olds.append((st_m[2, h], st_l[2, h], st_a[2, h]))
            olds.append(
                (
                    jnp.where(s == 0, st_m[0, h], st_m[1, h]),
                    jnp.where(s == 0, st_l[0, h], st_l[1, h]),
                    st_a[s, h],
                )
            )
        new = online(olds, sts, vs)
        for h in range(2):
            keep(2, h, new[2 * h])
            b = new[2 * h + 1]
            for n in range(2):
                st_m[n, h] = jnp.where(s == n, b[0], st_m[n, h])
                st_l[n, h] = jnp.where(s == n, b[1], st_l[n, h])
                st_a[n, h] = jnp.where(s == n, b[2], st_a[n, h])

    tri = lax.broadcasted_iota(jnp.int32, (256, 256), 0) <= lax.broadcasted_iota(
        jnp.int32, (256, 256), 1
    )
    for h in range(2):
        cols = pl.ds(h * HD, HD)
        names = [2, 0, 1]
        sts = [nt(own[0, 0, :, cols], q[1, :, cols])]
        sts += [jnp.where(tri, nt(own[0, n, :, cols], q[n, :, cols]), NEG) for n in range(2)]
        vs = [own[1, 0, :, cols], own[1, 0, :, cols], own[1, 1, :, cols]]
        olds = [(st_m[n, h], st_l[n, h], st_a[n, h]) for n in names]
        for n, new in zip(names, online(olds, sts, vs)):
            keep(n, h, new)

    def both(dy, t):
        k = chip_at(dy, t)

        def cores(i, carry):
            cr = lax.rem(core + i, 2)

            @pl.when(i == 1)
            def _():
                gk.wait(k, cr)
                gv.wait(k, cr)

            block(k, cr)
            return carry

        lax.fori_loop(0, 2, cores, 0)

    gv.near(0)
    gv.near(1)
    gk.wait(chip, 1 - core)
    gv.wait(chip, 1 - core)
    block(chip, 1 - core)
    gk.hop(0, 1)
    gv.across(0)
    gk.hop(3, 0)
    gk.hop(1, 0)
    both(0, 1)
    gv.far()
    both(3, 0)
    both(1, 0)
    gk.hop(3, 1)
    gk.hop(1, 1)
    gk.hop(2, 0)
    gv.across(3)
    gv.across(1)
    both(2, 0)
    both(3, 1)
    gk.hop(2, 1)
    both(1, 1)
    gv.across(2)
    both(2, 1)
    stores = [
        pltpu.make_async_copy(kvall, kv_out, s_out.at[0]),
        pltpu.make_async_copy(normed, normed_out, s_out.at[1]),
    ]
    for cp in stores:
        cp.start()

    for h in range(2):
        for n in range(2):
            m0, l0, a0 = st_m[n, h], st_l[n, h], st_a[n, h]
            if n == 1:
                m2, l2, a2 = st_m[2, h], st_l[2, h], st_a[2, h]
                mn = jnp.maximum(m0, m2)
                e0, e2 = jnp.exp(m0 - mn), jnp.exp(m2 - mn)
                m0, l0, a0 = mn, e0 * l0 + e2 * l2, e0 * a0 + e2 * a2
            lse[n, h] = m0 + jnp.log(l0)
            o = a0 / l0
            ot[n, h] = o
            att[pl.ds(n * 256, 256), pl.ds(h * HD, HD)] = jnp.transpose(o).astype(BF)

    loads[4].wait()

    def out_cols(i, carry):
        cols = pl.ds(pl.multiple_of(i * 256, 256), 256)
        parts[:, :, cols] = nn(att[...], wov[:, cols]).reshape(8, 64, 256).astype(BF)
        return carry

    mps = MpSum(parts, sum_refs, CA)
    lax.fori_loop(0, CA // 256, out_cols, 0)
    mps.start_a()
    lax.fori_loop(CA // 256, 8, out_cols, 0)
    mps.start_b()
    mps.middle()
    total = tok[pl.ds(pl.multiple_of(m * 64, 64), 64), :].astype(F32) + mps.finish()
    mixed[...] = total
    n = lax.rsqrt(jnp.mean(total * total, axis=-1, keepdims=True) + EPSILON)
    moe[m] = (total * n * gain_m[...]).astype(BF)
    mpg = MpGather(moe, ag_sems, CA)
    mpg.start()
    mpg.relay()

    gk.drain()
    gv.drain()
    mps.drain()
    mpg.finish()
    for cp in stores:
        cp.wait()


def attention_forward(order, tokens, wq, wk, wv, wo, inverse, gain_a, gain_m):
    return pl.pallas_call(
        k1_kernel,
        name="attend_forward",
        out_shape=(
            sds((8, 64, D), BF),
            sds((64, D), F32),
            sds((2, 2, 1, 256), F32),
            sds((2, 2, HD, 256), F32),
            sds((2, 256, 256), BF),
            sds((8, 2, 2, 2, 256, 256), BF),
            sds((512, D), BF),
            sds((512, 256), BF),
            sds((512, HD), F32),
            sds((512, HD), F32),
        ),
        in_specs=[SMEM_SPEC] + [ANY_SPEC] * 5 + [VMEM_SPEC] * 3,
        out_specs=(VMEM_SPEC,) * 5 + (ANY_SPEC,) * 2 + (VMEM_SPEC,) * 3,
        scratch_shapes=[
            pltpu.VMEM((8, 2, 2, 2, 256, 256), BF),
            pltpu.VMEM((512, D), BF),
            pltpu.VMEM((512, D), BF),
            pltpu.VMEM((3, D, 256), BF),
            pltpu.VMEM((256, D), BF),
            pltpu.VMEM((3, 2, 1, 256), F32),
            pltpu.VMEM((3, 2, 1, 256), F32),
            pltpu.VMEM((3, 2, HD, 256), F32),
            PARTS, DMA((5,)), DMA((2,)), Gather.sems(), GatherRing.sems(), MpSum.scratch(CA), MpGather.sems(),
        ],
        compiler_params=params(1),
    )(order, tokens, wq, wk, wv, wo, inverse, gain_a, gain_m)


def swish_parts(g, u):
    s = 1.0 / (1.0 + jnp.exp(-g))
    return s, g * s


def to_column(row):
    return jnp.transpose(jnp.broadcast_to(row, (HD, HD)))[:, 0:1]


def to_row(col):
    return jnp.transpose(jnp.broadcast_to(col, (HD, HD)))[0:1, :]


def k2_kernel(
    ids, moe, mixed, gain, w_router, cot, sg, su, sd, eg, eu, ed,
    g_attn, g_mixed, gain_part, wown, fin_d, moe_part_out, g_logits,
    moe_part, wsg, wsu, wsd, weg, weu, wed, cotv, tb, tbt, pr, gt, ut, hs, gsg, gsu,
    ein, gsl, geo, gated, eo, gein, ge3, ue3, he3, tmp, amat, blk, gate_part, gmi, gate_land,
    s_in, s_out, s_z, r_z, rd_refs, rs_refs, wd, zd, mp1, sum_refs, ag_sems,
):
    y, z, core, m = place()
    loads = [
        pltpu.make_async_copy(a, b, s_in.at[i])
        for i, (a, b) in enumerate(
            [(sg, wsg), (su, wsu), (eg, weg), (eu, weu), (ed, wed), (sd, wsd), (cot, cotv)]
        )
    ]
    for cp in loads:
        cp.start()
    count = greet()

    slot = lax.broadcasted_iota(jnp.int32, (HD, 512), 0)
    holder = lax.div(slot, CAP)
    chosen = holder == ids[0:1, :]
    for k in range(1, 6):
        chosen = chosen | (holder == ids[k : k + 1, :])
    chosen = jnp.where(chosen & (slot < 3 * CAP), 1.0, 0.0)
    upto = lax.broadcasted_iota(jnp.int32, (512, 512), 0) <= lax.broadcasted_iota(
        jnp.int32, (512, 512), 1
    )
    place_of = nn(chosen.astype(BF), jnp.where(upto, 1.0, 0.0).astype(BF)) - 1.0
    table_t = jnp.where(place_of == lax.rem(slot, CAP).astype(F32), chosen, 0.0)
    tbt[...] = table_t.astype(BF)
    table = jnp.transpose(table_t)
    tb[...] = table.astype(BF)
    expert = lax.div(lax.broadcasted_iota(jnp.int32, (512, HD), 1), CAP)

    logits = nt(moe[...], w_router[...])
    e = jnp.exp(logits - jnp.max(logits, axis=-1, keepdims=True))
    probs = e / jnp.sum(e, axis=-1, keepdims=True)
    pr[...] = probs
    px = jnp.where(expert == 0, probs[:, 0:1], jnp.where(expert == 1, probs[:, 1:2], probs[:, 2:3]))
    gate_col = to_column(jnp.sum(table * px, axis=0, keepdims=True))

    hs[...] = jnp.zeros_like(hs)
    gsg[...] = jnp.zeros_like(gsg)
    gsu[...] = jnp.zeros_like(gsu)
    eo[...] = jnp.zeros_like(eo)
    gein[...] = jnp.zeros_like(gein)
    tmp[...] = jnp.zeros_like(tmp)

    def gather_in(i, carry):
        cols = pl.ds(pl.multiple_of(i * 512, 512), 512)
        ein[:, cols] = nn(tbt[...], moe[:, cols]).astype(BF)
        return carry

    lax.fori_loop(0, 4, gather_in, 0)
    loads[0].wait()
    loads[1].wait()

    def shared_in(i, carry):
        rr = pl.ds(pl.multiple_of(i * 256, 256), 256)
        g, u = nt(moe[rr, :], wsg[...]), nt(moe[rr, :], wsu[...])
        gt[rr, :] = g
        ut[rr, :] = u
        hs[rr, 0:SH] = (swish_parts(g, u)[1] * u).astype(BF)
        return carry

    lax.fori_loop(0, 2, shared_in, 0)
    for cp in loads[2:5]:
        cp.wait()
    for k in range(3):
        rr = pl.ds(k * CAP, CAP)
        g, u = nt(ein[rr, :], weg[k]), nt(ein[rr, :], weu[k])
        ge3[k] = g
        ue3[k] = u
        hid = (swish_parts(g, u)[1] * u).astype(BF)
        he3[k] = hid
        eo[rr, :] = nn(hid, wed[k])
    loads[5].wait()
    loads[6].wait()

    def slots_in(i, carry):
        cols = pl.ds(pl.multiple_of(i * 512, 512), 512)
        g = nn(tbt[...], cotv[:, cols])
        gsl[:, cols] = g.astype(BF)
        geo[:, cols] = (gate_col * g).astype(BF)
        gated[:, cols] = (gate_col * eo[:, cols]).astype(BF)
        return carry

    lax.fori_loop(0, 4, slots_in, 0)
    gate_part[...] = to_row(jnp.sum(eo[...] * gsl[...].astype(F32), axis=1, keepdims=True))
    all_in(count)
    mp_send_same(gate_part, gate_land, *mp1)

    def put_block(i, k, val):
        rr = pl.ds(k * CAP, CAP)
        tmp[k, rr, 0:EF] = val.astype(F32)
        blk[pl.ds(EF * i, EF), :] = jnp.transpose(tmp[k])[0:EF].astype(BF)

    amat[pl.ds(2 * SH, SH), :] = turned(hs[...])[0:SH]
    for k in range(3):
        put_block(6 + k, k, he3[k])
    rd = Scatter(rd_refs, 176)
    terms_d = (
        (0, SH, amat.at[pl.ds(2 * SH, SH)], cotv),
        (SH, 3 * EF, blk.at[pl.ds(6 * EF, 3 * EF)], geo),
    )
    rd.pieces(terms_d)

    def shared_back(i, carry):
        rr = pl.ds(pl.multiple_of(i * 256, 256), 256)
        gh = nt(cotv[rr, :], wsd[...])
        g, u = gt[rr, :], ut[rr, :]
        s, sw = swish_parts(g, u)
        gsg[rr, 0:SH] = (gh * u * s * (1.0 + g * (1.0 - s))).astype(BF)
        gsu[rr, 0:SH] = (gh * sw).astype(BF)
        return carry

    lax.fori_loop(0, 2, shared_back, 0)

    for k in range(3):
        rr = pl.ds(k * CAP, CAP)
        gh = nt(geo[rr, :], wed[k])
        g, u = ge3[k], ue3[k]
        s, sw = swish_parts(g, u)
        geg = (gh * u * s * (1.0 + g * (1.0 - s))).astype(BF)
        geu = (gh * sw).astype(BF)
        gein[rr, :] = (nn(geg, weg[k]) + nn(geu, weu[k])).astype(BF)
        put_block(k, k, geg)
        put_block(3 + k, k, geu)

    rd.merge_place(2)
    rd.far()

    def back_cols(i, carry):
        cols = pl.ds(pl.multiple_of(i * 256, 256), 256)
        g = nn(gsg[:, 0:SH], wsg[:, cols]) + nn(gsu[:, 0:SH], wsu[:, cols]) + nn(tb[...], gein[:, cols])
        gmi[:, :, cols] = g.reshape(8, 64, 256).astype(BF)
        return carry

    mps = MpSum(gmi, sum_refs, CA)
    lax.fori_loop(0, CA // 256, back_cols, 0)
    mps.start_a()
    lax.fori_loop(CA // 256, 8, back_cols, 0)
    mps.start_b()

    amat[pl.ds(0, SH), :] = turned(gsg[...])[0:SH]
    amat[pl.ds(SH, SH), :] = turned(gsu[...])[0:SH]
    rs = Scatter(rs_refs, 352)
    terms = (
        (0, 2 * SH, amat.at[pl.ds(0, 2 * SH)], moe),
        (2 * SH, 6 * EF, blk.at[pl.ds(0, 6 * EF)], ein),
    )
    rd.merge_place(1)
    rd.near(0)
    rd.merge_place(3)
    rd.near(1)
    rs.pieces(terms)
    rd.merge_place(0)
    rs.merge_place(2)
    rs.far()

    def out_cols(i, carry):
        cols = pl.ds(pl.multiple_of(i * 256, 256), 256)
        o = nn(hs[:, 0:SH], wsd[:, cols]) + nn(tb[...], gated[:, cols])
        moe_part[:, :, cols] = o.reshape(8, 64, 256).astype(BF)
        return carry

    lax.fori_loop(0, 8, out_cols, 0)
    store = pltpu.make_async_copy(moe_part, moe_part_out, s_out)
    store.start()

    gate = gate_part[...]
    for d in range(1, 8):
        gate = gate + gate_land[mp_wait_recv(gate_land, *mp1, d)]
    lane2 = lax.broadcasted_iota(jnp.int32, (HD, 64), 0)
    col2 = lax.broadcasted_iota(jnp.int32, (HD, 64), 1)
    member = jnp.where((lax.div(lane2, CAP) == col2) & (col2 < 3), 1.0, 0.0)
    gate_probs = lax.dot_general(
        tb[...].astype(F32) * gate, member, (((1,), (0,)), ((), ())),
        precision=PRECISE, preferred_element_type=F32,
    )
    prob = pr[...]
    g_logits[...] = (prob * (gate_probs - jnp.sum(gate_probs * prob, axis=-1, keepdims=True))).astype(BF)

    mps.middle()
    for way, dy in ((0, 1), (1, 3)):
        rs.merge_place(dy)
        rs.near(way)
    rs.merge_place(0)
    rd.own(wd)
    remote(wd.at[1], zd, s_z, r_z, peer(0, 1)).start()

    mine = pl.ds(pl.multiple_of(m * 64, 64), 64)
    total = nn(g_logits[mine, :], w_router[...]) + mps.finish()
    mx = mixed[...]
    n = lax.rsqrt(jnp.mean(mx * mx, axis=-1, keepdims=True) + EPSILON)
    gain_part[...] = jnp.sum(total * mx * n, axis=0, keepdims=True)
    gg = total * gain[...]
    gm = cotv[mine, :].astype(F32) + n * gg
    gm = gm - mx * (n * n * n) * jnp.mean(gg * mx, axis=-1, keepdims=True)
    g_mixed[...] = gm
    g_attn[m] = gm.astype(BF)
    mpg = MpGather(g_attn, ag_sems, CA)
    mpg.start()
    mpg.relay()
    remote(zd, zd, s_z, r_z, peer(0, 1)).wait_recv()
    add_rows(fin_d, [wd.at[0], zd], 176)

    rs.own(wown)
    remote(zd, zd, s_z, s_z, peer(0, 1)).wait_send()
    rd.drain()
    rs.drain()
    mps.drain()
    mp_wait_send(gate_part, mp1[0])
    store.wait()
    mpg.finish()


def experts(ids, moe, mixed, gain, w_router, cot, sg, su, sd, eg, eu, ed):
    vm = pltpu.VMEM
    return pl.pallas_call(
        k2_kernel,
        name="experts",
        out_shape=(
            sds((8, 64, D), BF),
            sds((64, D), F32),
            sds((1, D), F32),
            sds((2, RG, HD), BF),
            sds((RD, HD), BF),
            sds((8, 64, D), BF),
            sds((512, 64), BF),
        ),
        in_specs=[VMEM_SPEC] * 5 + [ANY_SPEC] * 7,
        out_specs=(VMEM_SPEC,) * 5 + (ANY_SPEC, VMEM_SPEC),
        scratch_shapes=[
            PARTS, vm((SH, D), BF), vm((SH, D), BF), vm((SH, D), BF),
            vm((3, EF, D), BF), vm((3, EF, D), BF), vm((3, EF, D), BF),
            vm((512, D), BF), vm((512, HD), BF), vm((HD, 512), BF), vm((512, 64), F32),
            vm((512, SH), F32), vm((512, SH), F32),
            vm((512, 384), BF), vm((512, 384), BF), vm((512, 384), BF),
            vm((HD, D), BF), vm((HD, D), BF), vm((HD, D), BF), vm((HD, D), BF),
            vm((HD, D), F32), vm((HD, D), BF),
            vm((3, CAP, EF), F32), vm((3, CAP, EF), F32), vm((3, CAP, EF), BF),
            vm((3, HD, 256), F32), vm((3 * SH, 512), BF), vm((9 * EF, HD), BF),
            vm((1, HD), F32), PARTS, vm((8, 1, HD), F32),
            DMA((7,)), DMA, DMA, DMA, Scatter.scratch(RD, HD), Scatter.scratch(RG, HD),
            vm((2, RD, HD), BF), vm((RD, HD), BF), MP_SEMS, MpSum.scratch(CA), MpGather.sems(),
        ],
        compiler_params=params(2),
    )(ids, moe, mixed, gain, w_router, cot, sg, su, sd, eg, eu, ed)


def k3_kernel(
    order, q, lse, ot, g_attn, wout, mixed, cosf, sinf, att, g_logits, g_mixed, gain, gain_moe_part,
    kv_in, moe_part_in, wown_in, fin_d, moe_in, normed_in, tokens, wq, wk, wv,
    output, g_tokens, gains, w1d, w1g, w1t, w2out,
    glin, fin_g, fin_t, fin, moe, normed, amat, wtail, ztail, kvall, moe_part, wown, do, delta, dqt, zbuf, dkz, dkv,
    tok, zlast, wlast, gmine, gland, gsteps, gfar,
    s_in, s_loc, s_z, r_z, s_gx, r_gx, s_gy, r_gy, d_sems, g_sems, t_sems, l_sems, rs_refs, tail_refs, last_refs,
    osum_refs, oag_sems, sum_refs, ag_sems, mp3,
):
    y, z, core, m = place()
    chip = chip_at(0, 0)
    mine = pl.ds(pl.multiple_of(m * 64, 64), 64)
    loads = []
    for i, dy in enumerate((2, 1, 3, 0)):
        pair = pl.ds(lax.rem(y + dy, 4) * 2, 2)
        loads.append(pltpu.make_async_copy(kv_in.at[pair], kvall.at[pair], s_in.at[i]))
    for a, b in (
        (wown_in.at[0], wown), (moe_part_in, moe_part), (moe_in, moe), (normed_in, normed),
        (tokens.at[mine, :], tok),
    ):
        loads.append(pltpu.make_async_copy(a, b, s_in.at[len(loads)]))
    for cp in loads[5:6] + loads[:5] + loads[6:]:
        cp.start()
    all_in(greet(far=True))
    stores = []

    def store(src, dst):
        cp = pltpu.make_async_copy(src, dst, s_loc.at[len(stores)])
        cp.start()
        stores.append(cp)

    def swap(i, src, dst):
        return remote(src, dst, s_z.at[i], r_z.at[i], peer(0, 1))

    down = Gather(w1d, d_sems)
    down.start(fin_d)
    store(fin_d, w1d.at[chip, core])
    swap(0, wown_in.at[1], zbuf).start()
    loads[5].wait()
    mps = MpSum(moe_part, osum_refs, CO)
    mps.start_a()
    mps.start_b()
    g_att = nt(g_attn[...], wout[...])
    for n in range(2):
        for h in range(2):
            piece = g_att[n * 256 : n * 256 + 256, h * HD : h * HD + HD].astype(BF)
            do[n, h] = piece
            delta[n, h] = jnp.sum(jnp.transpose(piece.astype(F32)) * ot[n, h], axis=0, keepdims=True)
    dqt[...] = jnp.zeros_like(dqt)
    rs = Scatter(rs_refs, 256)

    def terms(items):
        ps = [nt(k, qq) - ls for k, v, qq, dd, ls, de, mask in items]
        ps = [jnp.exp(p) for p in ps]
        ps = [p if i[6] is None else jnp.where(i[6], p, 0.0) for p, i in zip(ps, items)]
        ds = [(p * (nt(i[1], i[3]) - i[5])).astype(BF) for p, i in zip(ps, items)]
        dv = [nn(p.astype(BF), i[3]) for p, i in zip(ps, items)]
        dk = [nn(d, i[2]) for d, i in zip(ds, items)]
        dq = [tn(i[0], d) for d, i in zip(ds, items)]
        return list(zip(dk, dv, dq))

    def block(k, cr, dst):
        s = pick_of(order, k, cr)
        items = []
        for h in range(2):
            cols = pl.ds(h * HD, HD)
            k0, k1 = kvall[k, cr, 0, 0, :, cols], kvall[k, cr, 0, 1, :, cols]
            v0, v1 = kvall[k, cr, 1, 0, :, cols], kvall[k, cr, 1, 1, :, cols]
            items.append((k0, v0, q[1, :, cols], do[1, h], lse[1, h], delta[1, h], None))
            items.append(
                (jnp.where(s == 0, k0, k1), jnp.where(s == 0, v0, v1), q[s, :, cols], do[s, h],
                 jnp.where(s == 0, lse[0, h], lse[1, h]), jnp.where(s == 0, delta[0, h], delta[1, h]), None)
            )
        got = terms(items)
        for h in range(2):
            cols = pl.ds(h * HD, HD)
            always, picked = got[2 * h], got[2 * h + 1]
            dqt[2, h] += always[2]
            for n in range(2):
                dqt[n, h] += jnp.where(s == n, picked[2], 0.0)
            for a in range(2):
                low = always[a] + jnp.where(s == 0, picked[a], 0.0)
                high = jnp.where(s == 1, picked[a], 0.0)
                dst[pl.ds(a * 512, 256), cols] = low.astype(BF)
                dst[pl.ds(a * 512 + 256, 256), cols] = high.astype(BF)

    def both_cores(k):
        block(k, 1 - core, rs.to_sib.at[k])
        rs.to_sibling(k)
        block(k, core, rs.sums.at[k])

    def ring_place(dy):
        loads[(2, 1, 3).index(dy)].wait()

        def one(t, carry):
            both_cores(chip_at(dy, t))
            return carry

        lax.fori_loop(0, 2, one, 0)
        rs.merge_place(dy)

    ring_place(2)
    rs.far()
    down.hop(0, 1)
    ring_place(1)
    rs.near(0)
    mps.middle()
    swap(0, wown_in.at[1], zbuf).wait_recv()
    loads[4].wait()
    add_rows(fin_g.at[0], [wown, zbuf], 352)
    swap(1, fin_g.at[0], fin_g.at[1]).start()
    down.hop(3, 0)
    down.hop(1, 0)
    ring_place(3)
    rs.near(1)
    output[m] = (mixed[...] + mps.finish()).astype(BF)
    mpg = MpGather(output, oag_sems, CO)
    mpg.start()
    down.hop(3, 1)
    down.hop(1, 1)
    loads[3].wait()
    both_cores(chip_at(0, 1))
    block(chip, 1 - core, rs.to_sib.at[chip])
    rs.to_sibling(chip)
    tri = lax.broadcasted_iota(jnp.int32, (256, 256), 0) <= lax.broadcasted_iota(
        jnp.int32, (256, 256), 1
    )
    for h in range(2):
        cols = pl.ds(h * HD, HD)
        kk = [kvall[chip, core, 0, n, :, cols] for n in range(2)]
        vv = [kvall[chip, core, 1, n, :, cols] for n in range(2)]
        items = [(kk[0], vv[0], q[1, :, cols], do[1, h], lse[1, h], delta[1, h], None)]
        for n in range(2):
            items.append((kk[n], vv[n], q[n, :, cols], do[n, h], lse[n, h], delta[n, h], tri))
        got = terms(items)
        dqt[2, h] += got[0][2]
        for n in range(2):
            dqt[n, h] += got[1 + n][2]
        for a in range(2):
            rs.sums[chip, pl.ds(a * 512, 256), cols] = (got[0][a] + got[1][a]).astype(BF)
            rs.sums[chip, pl.ds(a * 512 + 256, 256), cols] = got[2][a].astype(BF)
    w3 = [kvall.at[:, 0, 0, 0], kvall.at[:, 0, 1, 0], kvall.at[:, 1, 0, 0]]
    for w, dst in zip((wq, wk, wv), w3):
        loads.append(pltpu.make_async_copy(w, dst, s_in.at[len(loads)]))
        loads[-1].start()
    rs.merge(chip_at(0, 1))
    rs.merge(chip)
    mpg.relay()

    def back(x, rr):
        return (x * cosf[rr, :] - rolled(x) * sinf[rr, :]).astype(BF)

    for h in range(2):
        for n in range(2):
            rr = pl.ds(n * 256, 256)
            g = dqt[n, h] if n == 0 else dqt[1, h] + dqt[2, h]
            glin[0, rr, pl.ds(h * HD, HD)] = back(jnp.transpose(g) * (HD**-0.5), rr)

    loads[6].wait()
    loads[7].wait()
    amat[pl.ds(0, 64), :] = turned(g_logits[...])
    amat[pl.ds(64, 256), :] = turned(att[...])
    amat[pl.ds(320, 256), :] = turned(glin[0])
    tail = Scatter(tail_refs, RT)
    tail.pieces(
        (
            (0, 64, amat.at[pl.ds(0, 64)], moe),
            (64, 256, amat.at[pl.ds(64, 256)], g_attn),
            (320, 256, amat.at[pl.ds(320, 256)], normed),
        )
    )
    tail.merge_place(2)
    tail.far()
    rs.own(dkz)
    swap(2, dkz.at[1], dkv).start()
    swap(1, fin_g.at[0], fin_g.at[1]).wait_recv()
    big = GatherPair(w1g, g_sems)
    big.start(fin_g.at[0], fin_g.at[1])
    store(fin_g.at[0], w1g.at[chip, core])
    store(fin_g.at[1], w1g.at[chip_at(0, 1), core])
    tail.merge_place(1)
    tail.near(0)
    tail.merge_place(3)
    tail.near(1)
    tail.merge_place(0)
    down.hop(2, 0)
    down.hop(2, 1)
    for cp in loads[8:]:
        cp.wait()
    mps.drain()
    gni = moe_part
    swap(2, dkz.at[1], dkv).wait_recv()
    for n in range(2):
        rr = pl.ds(n * 256, 256)
        for h in range(2):
            cols = pl.ds(h * HD, HD)
            kr = pl.ds(n * 256, 256)
            vr = pl.ds(512 + n * 256, 256)
            g = dkz[0, kr, cols].astype(F32) + dkv[kr, cols].astype(F32)
            glin[1, rr, cols] = back(g, rr)
            glin[2, rr, cols] = (dkz[0, vr, cols].astype(F32) + dkv[vr, cols].astype(F32)).astype(BF)

    def back_cols(i, carry):
        cols = pl.ds(pl.multiple_of(i * 256, 256), 256)
        g = nt(glin[0], w3[0][i]) + nt(glin[1], w3[1][i]) + nt(glin[2], w3[2][i])
        gni[:, :, cols] = g.reshape(8, 64, 256).astype(BF)
        return carry

    mps2 = MpSum(gni, sum_refs, CA)
    lax.fori_loop(0, CA // 256, back_cols, 0)
    mps2.start_a()
    lax.fori_loop(CA // 256, 8, back_cols, 0)
    mps2.start_b()
    for i in range(2):
        amat[pl.ds(256 * i, 256), :] = turned(glin[1 + i])
    last = Scatter(last_refs, R2)
    last.pieces(((0, R2, amat.at[pl.ds(0, R2)], normed),))
    last.merge_place(2)
    last.far()
    big.hop(3, 0)
    big.hop(1, 1)
    last.merge_place(1)
    last.near(0)
    mps2.middle()
    last.merge_place(3)
    last.near(1)
    last.merge_place(0)
    tail.own(wtail)
    swap(3, wtail.at[1], ztail).start()

    total = mps2.finish()
    src = tok[...].astype(F32)
    n = lax.rsqrt(jnp.mean(src * src, axis=-1, keepdims=True) + EPSILON)
    gg = total * gain[...]
    gs = n * gg - src * (n * n * n) * jnp.mean(gg * src, axis=-1, keepdims=True)
    g_tokens[m] = (g_mixed[...] + gs).astype(BF)
    gmine[pl.ds(0, 1), :] = gain_moe_part[...]
    gmine[pl.ds(1, 1), :] = jnp.sum(total * src * n, axis=0, keepdims=True)
    mp_send_same(gmine, gland, *mp3)
    mpg2 = MpGather(g_tokens, ag_sems, CA)
    mpg2.start()
    last.own(wlast)
    swap(4, wlast.at[1], zlast).start()
    swap(3, wtail.at[1], ztail).wait_recv()
    add_rows(fin_t, [wtail.at[0], ztail], RT)
    third = Gather(w1t, t_sems)
    third.start(fin_t)
    store(fin_t, w1t.at[chip, core])
    mpg2.relay()
    swap(4, wlast.at[1], zlast).wait_recv()
    add_rows(fin, [wlast.at[0], zlast], R2)
    final = Gather(w2out, l_sems)
    final.start(fin)
    store(fin, w2out.at[chip, core])
    big.hop(1, 0)
    big.hop(3, 1)

    def gain_step(i, dev):
        return remote(gsteps.at[2 * i], gsteps.at[2 * i + 1], s_gx.at[i], r_gx.at[i], dev)

    gsum = gmine[...]
    for d in range(1, 8):
        gsum = gsum + gland[mp_wait_recv(gland, *mp3, d)]
    gsteps[0] = gsum
    gain_step(0, sibling()).start()
    third.hop(0, 1)
    final.hop(0, 1)
    gain_step(0, sibling()).wait_recv()
    gsteps[2] = gsteps[0] + gsteps[1]
    gain_step(1, peer(0, 1)).start()
    third.hop(3, 0)
    third.hop(1, 1)
    gain_step(1, peer(0, 1)).wait_recv()
    gfar[y] = gsteps[2] + gsteps[3]
    for d in range(1, 4):
        remote(gfar.at[y], gfar.at[y], s_gy.at[d - 1], r_gy.at[y], peer(d, 0)).start()
    final.hop(3, 0)
    final.hop(1, 1)
    big.hop(2, 0)
    big.hop(2, 1)
    for g in (third, final):
        g.hop(1, 0)
        g.hop(3, 1)
    for g in (third, final):
        g.hop(2, 0)
        g.hop(2, 1)
    for d in range(1, 4):
        yy = lax.rem(y + d, 4)
        remote(gfar.at[yy], gfar.at[yy], s_gy.at[0], r_gy.at[yy], peer(d, 0)).wait_recv()
    gains[...] = gfar[0] + gfar[1] + gfar[2] + gfar[3]

    for i, ref in enumerate((zbuf, fin_g.at[0], dkv, ztail, zlast)):
        swap(i, ref, ref).wait_send()
    for i, dev in enumerate((sibling(), peer(0, 1))):
        remote(gsteps.at[0], gsteps.at[0], s_gx.at[i], s_gx.at[i], dev).wait_send()
    for d in range(1, 4):
        remote(gfar.at[0], gfar.at[0], s_gy.at[d - 1], s_gy.at[d - 1], peer(d, 0)).wait_send()
    mp_wait_send(gmine, mp3[0])
    for part in (rs, tail, last, mps2):
        part.drain()
    mpg.finish()
    mpg2.finish()
    for cp in stores:
        cp.wait()
    for g in (down, big, third, final):
        g.wait(chip, 1 - core)
        for dy, t in HOPS:
            g.other_core(dy, t)
        g.drain()


def attention_backward(*args):
    vm = pltpu.VMEM
    return pl.pallas_call(
        k3_kernel,
        name="attend_backward",
        out_shape=(
            sds((8, 64, D), BF), sds((8, 64, D), BF), sds((2, D), F32),
            sds((8, 2, RD, HD), BF), sds((8, 2, RG, HD), BF), sds((8, 2, RT, HD), BF), sds((8, 2, R2, HD), BF),
        ),
        in_specs=[SMEM_SPEC] + [VMEM_SPEC] * 13 + [ANY_SPEC] * 10,
        out_specs=(VMEM_SPEC,) * 3 + (ANY_SPEC,) * 4,
        scratch_shapes=[
            vm((3, 512, 256), BF), vm((2, RG, HD), BF), vm((RT, HD), BF), vm((R2, HD), BF),
            vm((512, D), BF), vm((512, D), BF), vm((RT, 512), BF), vm((2, RT, HD), BF), vm((RT, HD), BF),
            vm((8, 2, 2, 2, 256, 256), BF), PARTS, vm((RG, HD), BF),
            vm((2, 2, 256, HD), BF), vm((2, 2, 1, 256), F32), vm((3, 2, HD, 256), F32),
            vm((RG, HD), BF), vm((2, 1024, 256), BF), vm((1024, 256), BF),
            vm((64, D), BF), vm((R2, HD), BF), vm((2, R2, HD), BF), vm((2, D), F32), vm((8, 2, D), F32), vm((4, 2, D), F32), vm((4, 2, D), F32),
            DMA((12,)), DMA((5,)), DMA((5,)), DMA((5,)), DMA((2,)), DMA((2,)), DMA((3,)), DMA((4,)),
            Gather.sems(), GatherPair.sems(), Gather.sems(), Gather.sems(),
            Scatter.scratch(1024, 256), Scatter.scratch(RT, HD), Scatter.scratch(R2, HD),
            MpSum.scratch(CO), MpGather.sems(), MpSum.scratch(CA), MpGather.sems(), MP_SEMS,
        ],
        compiler_params=params(3, 63 * 2**20),
    )(*args)


def widen_kernel(
    wa, wb, wt, w2, out_in, tok_in, gains,
    gq, gk, gv, go, gr, sg, su, sd, eg, eu, ed, out, tok, gain_a, gain_m,
):
    def flip(src, off):
        return jnp.transpose(src[0, 0, pl.ds(off, 256), :].astype(F32))

    gr[...] = wt[0, 0, pl.ds(0, 64), :].astype(F32)
    go[...] = wt[0, 0, pl.ds(64, 256), :].astype(F32)
    gq[...] = flip(wt, 320)
    gk[...] = flip(w2, 0)
    gv[...] = flip(w2, 256)
    sg[...] = wa[0, 0, pl.ds(0, SH), :].astype(F32)
    su[...] = wa[0, 0, pl.ds(SH, SH), :].astype(F32)
    sd[...] = wb[0, 0, pl.ds(0, SH), :].astype(F32)
    for k in range(3):
        eg[k] = wa[0, 0, pl.ds(2 * SH + EF * k, EF), :].astype(F32)
        eu[k] = wa[0, 0, pl.ds(2 * SH + EF * (3 + k), EF), :].astype(F32)
        ed[k] = wb[0, 0, pl.ds(SH + EF * k, EF), :].astype(F32)
    out[...] = out_in[...]
    tok[...] = tok_in[...]
    gain_m[...] = gains[pl.ds(0, 1), :]
    gain_a[...] = gains[pl.ds(1, 1), :]


def widen(wa, wb, wt, w2, out_in, tok_in, gains):
    def rows(width):
        return sds((D, width), F32), pl.BlockSpec((HD, width), lambda i: (i, 0))

    def cols(height):
        return sds((height, D), F32), pl.BlockSpec((height, HD), lambda i: (0, i))

    three = sds((3, EF, D), F32), pl.BlockSpec((3, EF, HD), lambda i: (0, 0, i))
    whole = pl.BlockSpec((32, D), lambda i: (i, 0))
    gain = sds((1, D), F32), pl.BlockSpec((1, HD), lambda i: (0, i))
    outs = [rows(256), rows(256), rows(256), cols(256), cols(64), cols(SH), cols(SH), cols(SH)]
    outs += [three, three, three, (sds((512, D), BF), whole), (sds((512, D), BF), whole), gain, gain]
    return pl.pallas_call(
        widen_kernel,
        name="widen",
        grid=(16,),
        out_shape=[o[0] for o in outs],
        in_specs=[
            pl.BlockSpec((1, 1, w.shape[2], HD), lambda i: (i // 2, i % 2, 0, 0)) for w in (wa, wb, wt, w2)
        ]
        + [whole, whole, pl.BlockSpec((2, HD), lambda i: (0, i))],
        out_specs=[o[1] for o in outs],
        compiler_params=pltpu.CompilerParams(vmem_limit_bytes=VM),
    )(wa, wb, wt, w2, out_in, tok_in, gains)


def on_device(
    tokens, cotangent, gain_attn, w_query, w_key, w_value, w_out, gain_moe, w_router,
    shared_gate, shared_up, shared_down, expert_gate, expert_up, expert_down, expert_ids, pair_order,
):
    rows = tokens.shape[0]
    inverse = ROPE_BASE ** (-2.0 * jnp.arange(HD // 2, dtype=F32) / HD)
    inverse = jnp.concatenate([inverse, inverse])[None]
    moe, mixed, lse, ot, q, kvall, normed, att, cosf, sinf = attention_forward(
        pair_order, tokens, w_query, w_key, w_value, w_out, inverse, gain_attn[None], gain_moe[None]
    )
    moe = moe.reshape(rows, D)
    g_attn, g_mixed, gain_moe_part, wown, fin_d, moe_part, g_logits = experts(
        expert_ids.T, moe, mixed, gain_moe[None], w_router.T, cotangent, shared_gate.T, shared_up.T, shared_down,
        expert_gate.transpose(0, 2, 1), expert_up.transpose(0, 2, 1), expert_down,
    )
    g_attn = g_attn.reshape(rows, D)
    output, g_tokens, gains, wb, wa, wt, w2 = attention_backward(
        pair_order, q, lse, ot, g_attn, w_out, mixed, cosf, sinf, att, g_logits, g_mixed, gain_attn[None],
        gain_moe_part, kvall, moe_part, wown, fin_d, moe, normed, tokens, w_query.reshape(8, 256, 256), w_key.reshape(8, 256, 256),
        w_value.reshape(8, 256, 256),
    )
    gq, gk, gv, go, gr, sg, su, sd, eg, eu, ed, output, g_tokens, gain_a, gain_m = widen(
        wa, wb, wt, w2, output.reshape(rows, D), g_tokens.reshape(rows, D), gains
    )
    return (
        output, g_tokens, gain_a.reshape(D), gq, gk, gv, go, gain_m.reshape(D), gr.T,
        sg.T, su.T, sd, eg.transpose(0, 2, 1), eu.transpose(0, 2, 1), ed,
    )


def solution(mesh):
    in_specs = (
        P("ctx", None), P("ctx", None), P(), P(None, "mp"), P(None, "mp"), P(None, "mp"),
        P("mp", None), P(), P(), P(None, "mp"), P(None, "mp"), P("mp", None),
        P(None, None, "mp"), P(None, None, "mp"), P(None, "mp", None), P("ctx", None), P(),
    )
    out_specs = (
        P("ctx", None), P("ctx", None), P(), P(None, "mp"), P(None, "mp"), P(None, "mp"),
        P("mp", None), P(), P(), P(None, "mp"), P(None, "mp"), P("mp", None),
        P(None, None, "mp"), P(None, None, "mp"), P(None, "mp", None),
    )
    return jax.shard_map(
        on_device, mesh=mesh, in_specs=in_specs, out_specs=out_specs, check_vma=False
    )
```

```python
import jax
import jax.numpy as jnp
from jax import lax
from jax.experimental import pallas as pl
from jax.experimental.pallas import tpu as pltpu
from jax.sharding import PartitionSpec as P

HD = 128
CAP = 32
EPSILON = 1e-06
ROPE_BASE = 10000.0
PRECISE = lax.Precision.HIGHEST
MESH = pl.DeviceIdType.MESH
BF = jnp.bfloat16
F32 = jnp.float32
D = 2048
SH = 352
EF = 176
RD = SH + 3 * EF
RG = 2 * SH + 6 * EF
RT = 64 + 2 * 256
R2 = 2 * 256
VM = 60 * 2**20
NEG = -1e30


def nt(a, b):
    return lax.dot_general(a, b, (((1,), (1,)), ((), ())), preferred_element_type=F32)


def nn(a, b):
    return lax.dot_general(a, b, (((1,), (0,)), ((), ())), preferred_element_type=F32)


def tn(a, b):
    return lax.dot_general(a, b, (((0,), (0,)), ((), ())), preferred_element_type=F32)


def turned(a):
    return jnp.transpose(a.astype(F32)).astype(BF)


def place():
    c = lax.axis_index("ctx")
    return lax.div(c, 4), lax.rem(lax.div(c, 2), 2), lax.rem(c, 2), lax.axis_index("mp")


def chip_at(dy, t):
    y, z, core, m = place()
    return lax.rem(y + dy, 4) * 2 + lax.rem(z + t, 2)


def peer(dy, t):
    y, z, core, m = place()
    return {"ctx": chip_at(dy, t) * 2 + core}


def sibling():
    y, z, core, m = place()
    return {"ctx": chip_at(0, 0) * 2 + 1 - core}


def mp_at(d):
    m = lax.axis_index("mp")
    return lax.rem(lax.div(m, 2) + d // 2, 4) * 2 + lax.rem(lax.rem(m, 2) + d % 2, 2)


def remote(src, dst, ssem, rsem, dev):
    return pltpu.make_async_remote_copy(
        src_ref=src, dst_ref=dst, send_sem=ssem, recv_sem=rsem, device_id=dev, device_id_type=MESH
    )


def greet(far=False):
    bar = pltpu.get_barrier_semaphore()
    devs = [sibling(), peer(0, 1), peer(1, 0), peer(3, 0)] + ([peer(2, 0)] if far else [])
    devs += [{"mp": mp_at(d)} for d in range(1, 8)]
    for dev in devs:
        pl.semaphore_signal(bar, inc=1, device_id=dev, device_id_type=MESH)
    return len(devs)


def all_in(count):
    pl.semaphore_wait(pltpu.get_barrier_semaphore(), count)


def mp_send_same(src, landing, ssem, rsem):
    m = lax.axis_index("mp")
    for d in range(1, 8):
        remote(src, landing.at[m], ssem.at[d - 1], rsem.at[m], {"mp": mp_at(d)}).start()


def mp_wait_recv(landing, ssem, rsem, d):
    t = mp_at(d)
    remote(landing.at[t], landing.at[t], ssem.at[0], rsem.at[t], {"mp": t}).wait_recv()
    return t


def mp_wait_send(src, ssem):
    for d in range(1, 8):
        remote(src, src, ssem.at[d - 1], ssem.at[d - 1], {"mp": mp_at(d)}).wait_send()


def mp_place():
    m = lax.axis_index("mp")
    return lax.div(m, 2), lax.rem(m, 2)


def x_peer(dx):
    x, zh = mp_place()
    return {"mp": lax.rem(x + dx, 4) * 2 + zh}


def zh_peer():
    x, zh = mp_place()
    return {"mp": x * 2 + 1 - zh}


class MpSum:
    def __init__(self, parts, refs, ca):
        self.parts, self.ca = parts, ca
        self.xa, self.za, self.zb, self.xs, self.xr, self.s, self.r = refs
        self.x, self.zh = mp_place()
        self.a, self.b = pl.ds(0, ca), pl.ds(ca, D - ca)

    @staticmethod
    def scratch(ca):
        cb, vm = D - ca, pltpu.VMEM
        return (
            vm((3, 2, 64, ca), BF), vm((2, 64, ca), BF), vm((4, 64, cb), BF),
            vm((3, 64, cb), BF), vm((3, 64, cb), BF),
            pltpu.SemaphoreType.DMA((11,)), pltpu.SemaphoreType.DMA((11,)),
        )

    def copy(self, n, src, dst, dev):
        return remote(src, dst, self.s.at[n], self.r.at[n], dev)

    def a_copy(self, dx):
        far = lax.rem(self.x + dx, 4)
        src = self.parts.at[pl.ds(far * 2, 2), :, self.a]
        return self.copy(dx - 1, src, self.xa.at[dx - 1], x_peer(dx))

    def b_copy(self, x):
        src = self.parts.at[x * 2 + 1 - self.zh, :, self.b]
        return self.copy(4 + x, src, self.zb.at[x], zh_peer())

    def x_copy(self, dx):
        return self.copy(7 + dx, self.xs.at[dx - 1], self.xr.at[dx - 1], x_peer(dx))

    def z_copy(self):
        return self.copy(3, self.za.at[0], self.za.at[1], zh_peer())

    def start_a(self):
        for dx in range(1, 4):
            self.a_copy(dx).start()

    def start_b(self):
        for x in range(4):
            self.b_copy(x).start()

    def middle(self):
        for x in range(4):
            self.b_copy(x).wait_recv()
        for dx in range(1, 4):
            far = lax.rem(self.x + dx, 4)
            val = self.parts[far * 2 + self.zh, :, self.b].astype(F32) + self.zb[far].astype(F32)
            self.xs[dx - 1] = val.astype(BF)
            self.x_copy(dx).start()
        for dx in range(1, 4):
            self.a_copy(dx).wait_recv()
        self.za[0] = self.over_x(1 - self.zh).astype(BF)
        self.z_copy().start()

    def over_x(self, zz):
        val = self.parts[self.x * 2 + zz, :, self.a].astype(F32)
        for n in range(3):
            val = val + self.xa[n, zz].astype(F32)
        return val

    def finish(self):
        one = self.over_x(self.zh)
        two = self.parts[self.x * 2 + self.zh, :, self.b].astype(F32) + self.zb[self.x].astype(F32)
        for dx in range(1, 4):
            self.x_copy(dx).wait_recv()
            two = two + self.xr[dx - 1].astype(F32)
        self.z_copy().wait_recv()
        one = one + self.za[1].astype(F32)
        return jnp.concatenate([one, two], axis=1)

    def drain(self):
        for dx in range(1, 4):
            self.a_copy(dx).wait_send()
            self.x_copy(dx).wait_send()
        for x in range(4):
            self.b_copy(x).wait_send()
        self.z_copy().wait_send()


class MpGather:
    def __init__(self, out, sems, ca):
        self.out, (self.s, self.r) = out, sems
        self.x, self.zh = mp_place()
        self.a, self.b = pl.ds(0, ca), pl.ds(ca, D - ca)

    @staticmethod
    def sems():
        return (pltpu.SemaphoreType.DMA((14,)), pltpu.SemaphoreType.DMA((14,)))

    def copy(self, n, x, zh, cols, dev):
        ref = self.out.at[x * 2 + zh, :, cols]
        return remote(ref, ref, self.s.at[n], self.r.at[n], dev)

    def start(self):
        x, zh = self.x, self.zh
        self.copy(0, x, zh, self.a, zh_peer()).start()
        for dx in range(1, 4):
            self.copy(dx, x, zh, self.b, x_peer(dx)).start()
        self.copy(4, x, zh, self.b, zh_peer()).start()
        for dx in range(1, 4):
            self.copy(4 + dx, x, zh, self.a, x_peer(dx)).start()

    def relay(self):
        x, zh = self.x, self.zh
        self.copy(0, x, 1 - zh, self.a, zh_peer()).wait_recv()
        for dx in range(1, 4):
            self.copy(7 + dx, x, 1 - zh, self.a, x_peer(dx)).start()
        for dx in (1, 3, 2):
            back = lax.rem(x + 4 - dx, 4)
            self.copy(dx, back, zh, self.b, x_peer(dx)).wait_recv()
            self.copy(10 + dx, back, zh, self.b, zh_peer()).start()

    def finish(self):
        x, zh = self.x, self.zh
        self.copy(4, x, 1 - zh, self.b, zh_peer()).wait_recv()
        for dx in range(1, 4):
            back = lax.rem(x + 4 - dx, 4)
            self.copy(4 + dx, back, zh, self.a, x_peer(dx)).wait_recv()
            self.copy(7 + dx, back, 1 - zh, self.a, x_peer(dx)).wait_recv()
            self.copy(10 + dx, back, 1 - zh, self.b, zh_peer()).wait_recv()
        for n in range(14):
            cols = self.a if n in (0, 5, 6, 7, 8, 9, 10) else self.b
            self.copy(n, x, zh, cols, zh_peer()).wait_send()


class Gather:
    def __init__(self, buf, sems, part=None):
        self.buf, self.part, (self.s, self.r) = buf, part, sems
        y, z, self.core, m = place()

    def at(self, chip, core):
        ref = self.buf.at[chip, core]
        return ref if self.part is None else ref.at[self.part]

    @staticmethod
    def sems():
        return (pltpu.SemaphoreType.DMA((15,)), pltpu.SemaphoreType.DMA((16,)))

    def send(self, src, chip, n, dev):
        dst = self.at(chip, self.core)
        remote(src, dst, self.s.at[n], self.r.at[chip * 2 + self.core], dev).start()

    def start(self, src):
        chip = chip_at(0, 0)
        for n, dev in enumerate([peer(0, 1), peer(1, 0), peer(3, 0), sibling()]):
            self.send(src, chip, n, dev)

    def wait(self, chip, core):
        ref = self.at(chip, core)
        remote(ref, ref, self.s.at[0], self.r.at[chip * 2 + core], sibling()).wait_recv()

    def hop(self, dy, t):
        chip = chip_at(dy, t)
        self.wait(chip, self.core)
        src = self.at(chip, self.core)
        n, devs = {
            (0, 1): (4, [peer(1, 0), peer(3, 0), sibling()]),
            (3, 0): (7, [peer(1, 0), sibling()]),
            (1, 0): (9, [sibling()]),
            (3, 1): (10, [sibling()]),
            (1, 1): (11, [peer(3, 0), sibling()]),
            (2, 0): (13, [sibling()]),
            (2, 1): (14, [sibling()]),
        }[dy, t]
        for i, dev in enumerate(devs):
            self.send(src, chip, n + i, dev)
        return chip

    def other_core(self, dy, t):
        chip = chip_at(dy, t)
        self.wait(chip, 1 - self.core)

    def drain(self):
        ref = self.at(0, 0)
        for n in range(15):
            remote(ref, ref, self.s.at[n], self.s.at[n], sibling()).wait_send()


class GatherPair(Gather):
    def start(self, own, other):
        here, across = chip_at(0, 0), chip_at(0, 1)
        self.send(own, here, 1, peer(1, 0))
        self.send(other, across, 5, peer(3, 0))
        self.send(other, across, 4, peer(1, 0))
        self.send(own, here, 2, peer(3, 0))
        self.send(own, here, 3, sibling())
        self.send(other, across, 6, sibling())

    def drain(self):
        ref = self.at(0, 0)
        for n in range(1, 15):
            remote(ref, ref, self.s.at[n], self.s.at[n], sibling()).wait_send()


class GatherRing(Gather):
    @staticmethod
    def sems():
        return (pltpu.SemaphoreType.DMA((16,)), pltpu.SemaphoreType.DMA((18,)))

    def half(self, n, way):
        chip = chip_at(2, 0) if way is None else chip_at(way, 0)
        ref = self.at(chip, self.core).at[n]
        return remote(ref, ref, self.s.at[4 + n], self.r.at[16 + n], peer(1 if n == 0 else 3, 0))

    def near(self, n):
        dy = 3 if n == 0 else 1
        chip = chip_at(dy, 0)
        self.wait(chip, self.core)
        self.half(n, dy).start()
        self.send(self.at(chip, self.core), chip, 6 + 2 * n, peer(0, 1))
        self.send(self.at(chip, self.core), chip, 7 + 2 * n, sibling())

    def far(self):
        chip = chip_at(2, 0)
        for n in range(2):
            self.half(n, None).wait_recv()
        self.send(self.at(chip, self.core), chip, 10, peer(0, 1))
        self.send(self.at(chip, self.core), chip, 11, sibling())

    def across(self, dy):
        chip = chip_at(dy, 1)
        self.wait(chip, self.core)
        self.send(self.at(chip, self.core), chip, 12 + dy, sibling())

    def drain(self):
        ref = self.at(0, 0)
        for n in range(16):
            one = ref.at[0] if n in (4, 5) else ref
            remote(one, one, self.s.at[n], self.s.at[n], sibling()).wait_send()


HOPS = ((0, 1), (3, 0), (1, 0), (3, 1), (1, 1), (2, 0), (2, 1))


def add_rows(dst, srcs, tile):
    def body(r, carry):
        rr = pl.ds(pl.multiple_of(r * tile, 16), tile)
        total = srcs[0][rr, :].astype(F32)
        for s in srcs[1:]:
            total = total + s[rr, :].astype(F32)
        dst[rr, :] = total.astype(dst.dtype)
        return carry

    lax.fori_loop(0, dst.shape[0] // tile, body, 0)


class Scatter:
    def __init__(self, refs, tile):
        (
            self.to_sib, self.from_sib, self.sums, self.half, self.pairs,
            self.s_sib, self.r_sib, self.s_half, self.r_half, self.s_pair, self.r_pair,
        ) = refs
        self.tile = tile
        self.y, self.z, self.core, m = place()

    @staticmethod
    def scratch(rows, cols):
        dma = pltpu.SemaphoreType.DMA
        eight = pltpu.VMEM((8, rows, cols), BF)
        return (
            eight, eight, eight, pltpu.VMEM((2, rows, cols), BF), pltpu.VMEM((2, 2, rows, cols), BF),
            dma((8,)), dma((8,)), dma((2,)), dma((2,)), dma((4,)), dma((4,)),
        )

    def add(self, dst, srcs):
        add_rows(dst, srcs, self.tile)

    def piece(self, chip, terms):
        cols = pl.ds(pl.multiple_of(chip * 256, 256), 256)
        for off, rows, lhs, rhs in terms:
            val = nn(lhs[...], rhs[:, cols]).astype(BF)
            one, two = val[:, 0:HD], val[:, HD:]
            self.sums[chip, pl.ds(off, rows), :] = jnp.where(self.core == 0, one, two)
            self.to_sib[chip, pl.ds(off, rows), :] = jnp.where(self.core == 0, two, one)
        self.to_sibling(chip)

    def to_sibling(self, chip):
        remote(
            self.to_sib.at[chip], self.from_sib.at[chip], self.s_sib.at[chip], self.r_sib.at[chip], sibling()
        ).start()

    def merge(self, chip):
        got = self.from_sib.at[chip]
        remote(got, got, self.s_sib.at[0], self.r_sib.at[chip], sibling()).wait_recv()
        self.add(self.sums.at[chip], [self.sums.at[chip], got])

    def pieces(self, terms):
        def one(i, carry):
            j = lax.div(i, 2)
            dy = lax.rem(2 - j + 3 * lax.div(j * (j - 1), 2), 4)
            self.piece(chip_at(dy, lax.rem(i, 2)), terms)
            return carry

        lax.fori_loop(0, 8, one, 0)

    def merge_place(self, dy):
        self.merge(chip_at(dy, 0))
        self.merge(chip_at(dy, 1))

    def far(self):
        for t, dy in ((0, 1), (1, 3)):
            remote(
                self.sums.at[chip_at(2, t)], self.half.at[t], self.s_half.at[t], self.r_half.at[t], peer(dy, 0)
            ).start()

    def pair_copy(self, way, t):
        dy = 1 if way == 0 else 3
        dst = self.pairs.at[way, lax.rem(self.z + t, 2)]
        n = 2 * way + t
        return remote(self.sums.at[chip_at(dy, t)], dst, self.s_pair.at[n], self.r_pair.at[n], peer(dy, 0))

    def early(self, way):
        self.pair_copy(way, 1 - way).start()

    def near(self, way):
        dy = 1 if way == 0 else 3
        got = self.half.at[way]
        remote(got, got, self.s_half.at[0], self.r_half.at[way], sibling()).wait_recv()
        mid = self.sums.at[chip_at(dy, way)]
        self.add(mid, [mid, got])
        self.pair_copy(way, way).start()

    def own(self, dst):
        for way in range(2):
            for t in range(2):
                self.pair_copy(way, t).wait_recv()
        for t in (1, 0):
            zz = lax.rem(self.z + t, 2)
            self.add(
                dst.at[t], [self.sums.at[chip_at(0, t)], self.pairs.at[0, zz], self.pairs.at[1, zz]]
            )

    def drain(self):
        one = self.sums.at[0]
        for k in range(8):
            remote(one, one, self.s_sib.at[k], self.s_sib.at[k], sibling()).wait_send()
        for k in range(2):
            remote(one, one, self.s_half.at[k], self.s_half.at[k], sibling()).wait_send()
        for k in range(4):
            remote(one, one, self.s_pair.at[k], self.s_pair.at[k], sibling()).wait_send()


def sds(shape, dtype):
    return jax.ShapeDtypeStruct(shape, dtype)


VMEM_SPEC = pl.BlockSpec(memory_space=pltpu.VMEM)
SMEM_SPEC = pl.BlockSpec(memory_space=pltpu.SMEM)
ANY_SPEC = pl.BlockSpec(memory_space=pl.ANY)
DMA = pltpu.SemaphoreType.DMA
MP_SEMS = (DMA((7,)), DMA((8,)))
CA = 1024
CO = 1792
CT = 1536
PARTS = pltpu.VMEM((8, 64, D), BF)


def params(cid, vmem=VM):
    return pltpu.CompilerParams(collective_id=cid, has_side_effects=True, vmem_limit_bytes=vmem)


def rolled(x):
    return pltpu.roll(x, 64, axis=1)


def pick_of(order, k, cr):
    return jnp.where(order[k * 2 + cr] < order[lax.axis_index("ctx")], 0, 1)


def k1_kernel(
    order, tokens, wq, wk, wv, wo, inverse, gain_a, gain_m,
    moe, mixed, lse, ot, q, kv_out, normed_out, att, cosf, sinf,
    kvall, normed, tok, w3, wov, st_m, st_l, st_a, parts, s_in, s_out, k_sems, v_sems, sum_refs, ag_sems,
):
    y, z, core, m = place()
    chip = chip_at(0, 0)
    loads = [
        pltpu.make_async_copy(a, b, s_in.at[i])
        for i, (a, b) in enumerate(
            [(tokens, tok), (wk, w3.at[0]), (wv, w3.at[1]), (wq, w3.at[2]), (wo, wov)]
        )
    ]
    for cp in loads:
        cp.start()
    count = greet()
    loads[0].wait()

    def norm_rows(i, carry):
        rr = pl.ds(pl.multiple_of(i * 128, 128), 128)
        x = tok[rr, :].astype(F32)
        n = lax.rsqrt(jnp.mean(x * x, axis=-1, keepdims=True) + EPSILON)
        normed[rr, :] = (x * n * gain_a[...]).astype(BF)
        return carry

    lax.fori_loop(0, 4, norm_rows, 0)
    own = kvall.at[chip, core]
    loads[2].wait()

    def values(n, carry):
        rr = pl.ds(pl.multiple_of(n * 256, 256), 256)
        own[1, n] = nn(normed[rr, :], w3[1]).astype(BF)
        return carry

    lax.fori_loop(0, 2, values, 0)
    all_in(count)
    gv = GatherRing(kvall, v_sems, 1)
    gv.start(own.at[1])

    pair = order[lax.axis_index("ctx")]
    sign = jnp.where(lax.broadcasted_iota(jnp.int32, (1, HD), 1) < HD // 2, -1.0, 1.0)
    for n, first in enumerate((pair, 31 - pair)):
        pos = (lax.broadcasted_iota(jnp.int32, (256, HD), 0) + first * 256).astype(F32)
        phase = pos * inverse[...]
        cosf[pl.ds(n * 256, 256), :] = jnp.cos(phase)
        sinf[pl.ds(n * 256, 256), :] = jnp.sin(phase) * sign
    def turn(lin, rr, h):
        x = lin[:, h * HD : h * HD + HD]
        return x * cosf[rr, :] + rolled(x) * sinf[rr, :]

    loads[1].wait()

    def keys(n, carry):
        rr = pl.ds(pl.multiple_of(n * 256, 256), 256)
        lin = nn(normed[rr, :], w3[0])
        for h in range(2):
            own[0, n, :, pl.ds(h * HD, HD)] = turn(lin, rr, h).astype(BF)
        return carry

    lax.fori_loop(0, 2, keys, 0)
    gk = Gather(kvall, k_sems, 0)
    gk.start(own.at[0])
    loads[3].wait()

    def queries(n, carry):
        rr = pl.ds(pl.multiple_of(n * 256, 256), 256)
        lin = nn(normed[rr, :], w3[2])
        for h in range(2):
            q[n, :, pl.ds(h * HD, HD)] = (turn(lin, rr, h) * (HD**-0.5)).astype(BF)
        return carry

    lax.fori_loop(0, 2, queries, 0)

    st_m[...] = jnp.full_like(st_m, NEG)
    st_l[...] = jnp.zeros_like(st_l)
    st_a[...] = jnp.zeros_like(st_a)

    def online(olds, sts, vs):
        mn = [jnp.maximum(o[0], jnp.max(s, axis=0, keepdims=True)) for o, s in zip(olds, sts)]
        ps = [jnp.exp(s - a) for s, a in zip(sts, mn)]
        al = [jnp.exp(o[0] - a) for o, a in zip(olds, mn)]
        ls = [a * o[1] + jnp.sum(p, axis=0, keepdims=True) for a, o, p in zip(al, olds, ps)]
        ac = [a * o[2] + tn(v, p.astype(BF)) for a, o, v, p in zip(al, olds, vs, ps)]
        return list(zip(mn, ls, ac))

    def keep(n, h, new):
        st_m[n, h], st_l[n, h], st_a[n, h] = new

    def block(k, cr):
        s = pick_of(order, k, cr)
        sts, vs, olds = [], [], []
        for h in range(2):
            cols = pl.ds(h * HD, HD)
            k0, k1 = kvall[k, cr, 0, 0, :, cols], kvall[k, cr, 0, 1, :, cols]
            v0, v1 = kvall[k, cr, 1, 0, :, cols], kvall[k, cr, 1, 1, :, cols]
            sts += [nt(k0, q[1, :, cols]), nt(jnp.where(s == 0, k0, k1), q[s, :, cols])]
            vs += [v0, jnp.where(s == 0, v0, v1)]
            olds.append((st_m[2, h], st_l[2, h], st_a[2, h]))
            olds.append(
                (
                    jnp.where(s == 0, st_m[0, h], st_m[1, h]),
                    jnp.where(s == 0, st_l[0, h], st_l[1, h]),
                    st_a[s, h],
                )
            )
        new = online(olds, sts, vs)
        for h in range(2):
            keep(2, h, new[2 * h])
            b = new[2 * h + 1]
            for n in range(2):
                st_m[n, h] = jnp.where(s == n, b[0], st_m[n, h])
                st_l[n, h] = jnp.where(s == n, b[1], st_l[n, h])
                st_a[n, h] = jnp.where(s == n, b[2], st_a[n, h])

    tri = lax.broadcasted_iota(jnp.int32, (256, 256), 0) <= lax.broadcasted_iota(
        jnp.int32, (256, 256), 1
    )
    for h in range(2):
        cols = pl.ds(h * HD, HD)
        names = [2, 0, 1]
        sts = [nt(own[0, 0, :, cols], q[1, :, cols])]
        sts += [jnp.where(tri, nt(own[0, n, :, cols], q[n, :, cols]), NEG) for n in range(2)]
        vs = [own[1, 0, :, cols], own[1, 0, :, cols], own[1, 1, :, cols]]
        olds = [(st_m[n, h], st_l[n, h], st_a[n, h]) for n in names]
        for n, new in zip(names, online(olds, sts, vs)):
            keep(n, h, new)

    def both(dy, t):
        k = chip_at(dy, t)

        def cores(i, carry):
            cr = lax.rem(core + i, 2)

            @pl.when(i == 1)
            def _():
                gk.wait(k, cr)
                gv.wait(k, cr)

            block(k, cr)
            return carry

        lax.fori_loop(0, 2, cores, 0)

    gv.near(0)
    gv.near(1)
    gk.wait(chip, 1 - core)
    gv.wait(chip, 1 - core)
    block(chip, 1 - core)
    gk.hop(0, 1)
    gv.across(0)
    gk.hop(3, 0)
    gk.hop(1, 0)
    both(0, 1)
    gv.far()
    both(3, 0)
    both(1, 0)
    gk.hop(3, 1)
    gk.hop(1, 1)
    gk.hop(2, 0)
    gv.across(3)
    gv.across(1)
    both(2, 0)
    both(3, 1)
    gk.hop(2, 1)
    both(1, 1)
    gv.across(2)
    both(2, 1)
    stores = [
        pltpu.make_async_copy(kvall, kv_out, s_out.at[0]),
        pltpu.make_async_copy(normed, normed_out, s_out.at[1]),
    ]
    for cp in stores:
        cp.start()

    for h in range(2):
        for n in range(2):
            m0, l0, a0 = st_m[n, h], st_l[n, h], st_a[n, h]
            if n == 1:
                m2, l2, a2 = st_m[2, h], st_l[2, h], st_a[2, h]
                mn = jnp.maximum(m0, m2)
                e0, e2 = jnp.exp(m0 - mn), jnp.exp(m2 - mn)
                m0, l0, a0 = mn, e0 * l0 + e2 * l2, e0 * a0 + e2 * a2
            lse[n, h] = m0 + jnp.log(l0)
            o = a0 / l0
            ot[n, h] = o
            att[pl.ds(n * 256, 256), pl.ds(h * HD, HD)] = jnp.transpose(o).astype(BF)

    loads[4].wait()

    def out_cols(i, carry):
        cols = pl.ds(pl.multiple_of(i * 256, 256), 256)
        parts[:, :, cols] = nn(att[...], wov[:, cols]).reshape(8, 64, 256).astype(BF)
        return carry

    mps = MpSum(parts, sum_refs, CA)
    lax.fori_loop(0, CA // 256, out_cols, 0)
    mps.start_a()
    lax.fori_loop(CA // 256, 8, out_cols, 0)
    mps.start_b()
    mps.middle()
    total = tok[pl.ds(pl.multiple_of(m * 64, 64), 64), :].astype(F32) + mps.finish()
    mixed[...] = total
    n = lax.rsqrt(jnp.mean(total * total, axis=-1, keepdims=True) + EPSILON)
    moe[m] = (total * n * gain_m[...]).astype(BF)
    mpg = MpGather(moe, ag_sems, CA)
    mpg.start()
    mpg.relay()

    gk.drain()
    gv.drain()
    mps.drain()
    mpg.finish()
    for cp in stores:
        cp.wait()


def attention_forward(order, tokens, wq, wk, wv, wo, inverse, gain_a, gain_m):
    return pl.pallas_call(
        k1_kernel,
        name="attend_forward",
        out_shape=(
            sds((8, 64, D), BF),
            sds((64, D), F32),
            sds((2, 2, 1, 256), F32),
            sds((2, 2, HD, 256), F32),
            sds((2, 256, 256), BF),
            sds((8, 2, 2, 2, 256, 256), BF),
            sds((512, D), BF),
            sds((512, 256), BF),
            sds((512, HD), F32),
            sds((512, HD), F32),
        ),
        in_specs=[SMEM_SPEC] + [ANY_SPEC] * 5 + [VMEM_SPEC] * 3,
        out_specs=(VMEM_SPEC,) * 5 + (ANY_SPEC,) * 2 + (VMEM_SPEC,) * 3,
        scratch_shapes=[
            pltpu.VMEM((8, 2, 2, 2, 256, 256), BF),
            pltpu.VMEM((512, D), BF),
            pltpu.VMEM((512, D), BF),
            pltpu.VMEM((3, D, 256), BF),
            pltpu.VMEM((256, D), BF),
            pltpu.VMEM((3, 2, 1, 256), F32),
            pltpu.VMEM((3, 2, 1, 256), F32),
            pltpu.VMEM((3, 2, HD, 256), F32),
            PARTS, DMA((5,)), DMA((2,)), Gather.sems(), GatherRing.sems(), MpSum.scratch(CA), MpGather.sems(),
        ],
        compiler_params=params(1),
    )(order, tokens, wq, wk, wv, wo, inverse, gain_a, gain_m)


def swish_parts(g, u):
    s = 1.0 / (1.0 + jnp.exp(-g))
    return s, g * s


def to_column(row):
    return jnp.transpose(jnp.broadcast_to(row, (HD, HD)))[:, 0:1]


def to_row(col):
    return jnp.transpose(jnp.broadcast_to(col, (HD, HD)))[0:1, :]


def k2_kernel(
    ids, moe, mixed, gain, w_router, cot, sg, su, sd, eg, eu, ed,
    g_attn, g_mixed, gain_part, wown, fin_d, moe_part_out, g_logits,
    moe_part, wsg, wsu, wsd, weg, weu, wed, cotv, tb, tbt, pr, gt, ut, hs, gsg, gsu,
    ein, gsl, geo, gated, eo, gein, ge3, ue3, he3, tmp, amat, blk, gate_part, gmi, gate_land,
    s_in, s_out, s_z, r_z, rd_refs, rs_refs, wd, zd, mp1, sum_refs, ag_sems,
):
    y, z, core, m = place()
    loads = [
        pltpu.make_async_copy(a, b, s_in.at[i])
        for i, (a, b) in enumerate(
            [(sg, wsg), (su, wsu), (eg, weg), (eu, weu), (ed, wed), (sd, wsd), (cot, cotv)]
        )
    ]
    for cp in loads:
        cp.start()
    count = greet()

    slot = lax.broadcasted_iota(jnp.int32, (HD, 512), 0)
    holder = lax.div(slot, CAP)
    chosen = holder == ids[0:1, :]
    for k in range(1, 6):
        chosen = chosen | (holder == ids[k : k + 1, :])
    chosen = jnp.where(chosen & (slot < 3 * CAP), 1.0, 0.0)
    upto = lax.broadcasted_iota(jnp.int32, (512, 512), 0) <= lax.broadcasted_iota(
        jnp.int32, (512, 512), 1
    )
    place_of = nn(chosen.astype(BF), jnp.where(upto, 1.0, 0.0).astype(BF)) - 1.0
    table_t = jnp.where(place_of == lax.rem(slot, CAP).astype(F32), chosen, 0.0)
    tbt[...] = table_t.astype(BF)
    table = jnp.transpose(table_t)
    tb[...] = table.astype(BF)
    expert = lax.div(lax.broadcasted_iota(jnp.int32, (512, HD), 1), CAP)

    logits = nt(moe[...], w_router[...])
    e = jnp.exp(logits - jnp.max(logits, axis=-1, keepdims=True))
    probs = e / jnp.sum(e, axis=-1, keepdims=True)
    pr[...] = probs
    px = jnp.where(expert == 0, probs[:, 0:1], jnp.where(expert == 1, probs[:, 1:2], probs[:, 2:3]))
    gate_col = to_column(jnp.sum(table * px, axis=0, keepdims=True))

    hs[...] = jnp.zeros_like(hs)
    gsg[...] = jnp.zeros_like(gsg)
    gsu[...] = jnp.zeros_like(gsu)
    eo[...] = jnp.zeros_like(eo)
    gein[...] = jnp.zeros_like(gein)
    tmp[...] = jnp.zeros_like(tmp)

    def gather_in(i, carry):
        cols = pl.ds(pl.multiple_of(i * 512, 512), 512)
        ein[:, cols] = nn(tbt[...], moe[:, cols]).astype(BF)
        return carry

    lax.fori_loop(0, 4, gather_in, 0)
    loads[0].wait()
    loads[1].wait()

    def shared_in(i, carry):
        rr = pl.ds(pl.multiple_of(i * 256, 256), 256)
        g, u = nt(moe[rr, :], wsg[...]), nt(moe[rr, :], wsu[...])
        gt[rr, :] = g
        ut[rr, :] = u
        hs[rr, 0:SH] = (swish_parts(g, u)[1] * u).astype(BF)
        return carry

    lax.fori_loop(0, 2, shared_in, 0)
    for cp in loads[2:5]:
        cp.wait()
    for k in range(3):
        rr = pl.ds(k * CAP, CAP)
        g, u = nt(ein[rr, :], weg[k]), nt(ein[rr, :], weu[k])
        ge3[k] = g
        ue3[k] = u
        hid = (swish_parts(g, u)[1] * u).astype(BF)
        he3[k] = hid
        eo[rr, :] = nn(hid, wed[k])
    loads[5].wait()
    loads[6].wait()

    def slots_in(i, carry):
        cols = pl.ds(pl.multiple_of(i * 512, 512), 512)
        g = nn(tbt[...], cotv[:, cols])
        gsl[:, cols] = g.astype(BF)
        geo[:, cols] = (gate_col * g).astype(BF)
        gated[:, cols] = (gate_col * eo[:, cols]).astype(BF)
        return carry

    lax.fori_loop(0, 4, slots_in, 0)
    gate_part[...] = to_row(jnp.sum(eo[...] * gsl[...].astype(F32), axis=1, keepdims=True))
    all_in(count)
    mp_send_same(gate_part, gate_land, *mp1)

    def put_block(i, k, val):
        rr = pl.ds(k * CAP, CAP)
        tmp[k, rr, 0:EF] = val.astype(F32)
        blk[pl.ds(EF * i, EF), :] = jnp.transpose(tmp[k])[0:EF].astype(BF)

    amat[pl.ds(2 * SH, SH), :] = turned(hs[...])[0:SH]
    for k in range(3):
        put_block(6 + k, k, he3[k])
    rd = Scatter(rd_refs, 176)
    terms_d = (
        (0, SH, amat.at[pl.ds(2 * SH, SH)], cotv),
        (SH, 3 * EF, blk.at[pl.ds(6 * EF, 3 * EF)], geo),
    )
    rd.pieces(terms_d)

    def shared_back(i, carry):
        rr = pl.ds(pl.multiple_of(i * 256, 256), 256)
        gh = nt(cotv[rr, :], wsd[...])
        g, u = gt[rr, :], ut[rr, :]
        s, sw = swish_parts(g, u)
        gsg[rr, 0:SH] = (gh * u * s * (1.0 + g * (1.0 - s))).astype(BF)
        gsu[rr, 0:SH] = (gh * sw).astype(BF)
        return carry

    lax.fori_loop(0, 2, shared_back, 0)

    for k in range(3):
        rr = pl.ds(k * CAP, CAP)
        gh = nt(geo[rr, :], wed[k])
        g, u = ge3[k], ue3[k]
        s, sw = swish_parts(g, u)
        geg = (gh * u * s * (1.0 + g * (1.0 - s))).astype(BF)
        geu = (gh * sw).astype(BF)
        gein[rr, :] = (nn(geg, weg[k]) + nn(geu, weu[k])).astype(BF)
        put_block(k, k, geg)
        put_block(3 + k, k, geu)

    rd.merge_place(2)
    rd.far()
    rd.merge_place(1)
    rd.early(0)
    rd.merge_place(3)
    rd.early(1)

    def back_cols(i, carry):
        cols = pl.ds(pl.multiple_of(i * 256, 256), 256)
        g = nn(gsg[:, 0:SH], wsg[:, cols]) + nn(gsu[:, 0:SH], wsu[:, cols]) + nn(tb[...], gein[:, cols])
        gmi[:, :, cols] = g.reshape(8, 64, 256).astype(BF)
        return carry

    mps = MpSum(gmi, sum_refs, CA)
    lax.fori_loop(0, CA // 256, back_cols, 0)
    mps.start_a()
    lax.fori_loop(CA // 256, 8, back_cols, 0)
    mps.start_b()

    amat[pl.ds(0, SH), :] = turned(gsg[...])[0:SH]
    amat[pl.ds(SH, SH), :] = turned(gsu[...])[0:SH]
    rs = Scatter(rs_refs, 352)
    terms = (
        (0, 2 * SH, amat.at[pl.ds(0, 2 * SH)], moe),
        (2 * SH, 6 * EF, blk.at[pl.ds(0, 6 * EF)], ein),
    )
    rd.near(0)
    rd.near(1)
    rs.pieces(terms)
    rd.merge_place(0)
    rs.merge_place(2)
    rs.far()
    rs.merge_place(1)
    rs.early(0)
    rs.merge_place(3)
    rs.early(1)

    def out_cols(i, carry):
        cols = pl.ds(pl.multiple_of(i * 256, 256), 256)
        o = nn(hs[:, 0:SH], wsd[:, cols]) + nn(tb[...], gated[:, cols])
        moe_part[:, :, cols] = o.reshape(8, 64, 256).astype(BF)
        return carry

    lax.fori_loop(0, 8, out_cols, 0)
    store = pltpu.make_async_copy(moe_part, moe_part_out, s_out)
    store.start()

    gate = gate_part[...]
    for d in range(1, 8):
        gate = gate + gate_land[mp_wait_recv(gate_land, *mp1, d)]
    lane2 = lax.broadcasted_iota(jnp.int32, (HD, 64), 0)
    col2 = lax.broadcasted_iota(jnp.int32, (HD, 64), 1)
    member = jnp.where((lax.div(lane2, CAP) == col2) & (col2 < 3), 1.0, 0.0)
    gate_probs = lax.dot_general(
        tb[...].astype(F32) * gate, member, (((1,), (0,)), ((), ())),
        precision=PRECISE, preferred_element_type=F32,
    )
    prob = pr[...]
    g_logits[...] = (prob * (gate_probs - jnp.sum(gate_probs * prob, axis=-1, keepdims=True))).astype(BF)

    mps.middle()
    rs.near(0)
    rs.near(1)
    rs.merge_place(0)
    rd.own(wd)
    remote(wd.at[1], zd, s_z, r_z, peer(0, 1)).start()

    mine = pl.ds(pl.multiple_of(m * 64, 64), 64)
    total = nn(g_logits[mine, :], w_router[...]) + mps.finish()
    mx = mixed[...]
    n = lax.rsqrt(jnp.mean(mx * mx, axis=-1, keepdims=True) + EPSILON)
    gain_part[...] = jnp.sum(total * mx * n, axis=0, keepdims=True)
    gg = total * gain[...]
    gm = cotv[mine, :].astype(F32) + n * gg
    gm = gm - mx * (n * n * n) * jnp.mean(gg * mx, axis=-1, keepdims=True)
    g_mixed[...] = gm
    g_attn[m] = gm.astype(BF)
    mpg = MpGather(g_attn, ag_sems, CA)
    mpg.start()
    mpg.relay()
    remote(zd, zd, s_z, r_z, peer(0, 1)).wait_recv()
    add_rows(fin_d, [wd.at[0], zd], 176)

    rs.own(wown)
    remote(zd, zd, s_z, s_z, peer(0, 1)).wait_send()
    rd.drain()
    rs.drain()
    mps.drain()
    mp_wait_send(gate_part, mp1[0])
    store.wait()
    mpg.finish()


def experts(ids, moe, mixed, gain, w_router, cot, sg, su, sd, eg, eu, ed):
    vm = pltpu.VMEM
    return pl.pallas_call(
        k2_kernel,
        name="experts",
        out_shape=(
            sds((8, 64, D), BF),
            sds((64, D), F32),
            sds((1, D), F32),
            sds((2, RG, HD), BF),
            sds((RD, HD), BF),
            sds((8, 64, D), BF),
            sds((512, 64), BF),
        ),
        in_specs=[VMEM_SPEC] * 5 + [ANY_SPEC] * 7,
        out_specs=(VMEM_SPEC,) * 5 + (ANY_SPEC, VMEM_SPEC),
        scratch_shapes=[
            PARTS, vm((SH, D), BF), vm((SH, D), BF), vm((SH, D), BF),
            vm((3, EF, D), BF), vm((3, EF, D), BF), vm((3, EF, D), BF),
            vm((512, D), BF), vm((512, HD), BF), vm((HD, 512), BF), vm((512, 64), F32),
            vm((512, SH), F32), vm((512, SH), F32),
            vm((512, 384), BF), vm((512, 384), BF), vm((512, 384), BF),
            vm((HD, D), BF), vm((HD, D), BF), vm((HD, D), BF), vm((HD, D), BF),
            vm((HD, D), F32), vm((HD, D), BF),
            vm((3, CAP, EF), F32), vm((3, CAP, EF), F32), vm((3, CAP, EF), BF),
            vm((3, HD, 256), F32), vm((3 * SH, 512), BF), vm((9 * EF, HD), BF),
            vm((1, HD), F32), PARTS, vm((8, 1, HD), F32),
            DMA((7,)), DMA, DMA, DMA, Scatter.scratch(RD, HD), Scatter.scratch(RG, HD),
            vm((2, RD, HD), BF), vm((RD, HD), BF), MP_SEMS, MpSum.scratch(CA), MpGather.sems(),
        ],
        compiler_params=params(2),
    )(ids, moe, mixed, gain, w_router, cot, sg, su, sd, eg, eu, ed)


def k3_kernel(
    order, q, lse, ot, g_attn, wout, mixed, cosf, sinf, att, g_logits, g_mixed, gain, gain_moe_part,
    kv_in, moe_part_in, wown_in, fin_d, moe_in, normed_in, tokens, wq, wk, wv,
    output, g_tokens, gains, w1d, w1g, w1t, w2out,
    glin, fin_g, fin_t, fin, moe, normed, amat, wtail, ztail, kvall, moe_part, wown, do, delta, dqt, zbuf, dkz, dkv,
    tok, zlast, wlast, gmine, gland, gsteps, gfar,
    s_in, s_loc, s_z, r_z, s_gx, r_gx, s_gy, r_gy, d_sems, g_sems, t_sems, l_sems, rs_refs, tail_refs, last_refs,
    osum_refs, oag_sems, sum_refs, ag_sems, mp3,
):
    y, z, core, m = place()
    chip = chip_at(0, 0)
    mine = pl.ds(pl.multiple_of(m * 64, 64), 64)
    loads = []
    for i, dy in enumerate((2, 1, 3, 0)):
        pair = pl.ds(lax.rem(y + dy, 4) * 2, 2)
        loads.append(pltpu.make_async_copy(kv_in.at[pair], kvall.at[pair], s_in.at[i]))
    for a, b in (
        (wown_in.at[0], wown), (moe_part_in, moe_part), (moe_in, moe), (normed_in, normed),
        (tokens.at[mine, :], tok),
    ):
        loads.append(pltpu.make_async_copy(a, b, s_in.at[len(loads)]))
    for cp in loads[5:6] + loads[:5] + loads[6:]:
        cp.start()
    all_in(greet(far=True))
    stores = []

    def store(src, dst):
        cp = pltpu.make_async_copy(src, dst, s_loc.at[len(stores)])
        cp.start()
        stores.append(cp)

    def swap(i, src, dst):
        return remote(src, dst, s_z.at[i], r_z.at[i], peer(0, 1))

    down = Gather(w1d, d_sems)
    down.start(fin_d)
    store(fin_d, w1d.at[chip, core])
    swap(0, wown_in.at[1], zbuf).start()
    loads[5].wait()
    mps = MpSum(moe_part, osum_refs, CO)
    mps.start_a()
    mps.start_b()
    g_att = nt(g_attn[...], wout[...])
    for n in range(2):
        for h in range(2):
            piece = g_att[n * 256 : n * 256 + 256, h * HD : h * HD + HD].astype(BF)
            do[n, h] = piece
            delta[n, h] = jnp.sum(jnp.transpose(piece.astype(F32)) * ot[n, h], axis=0, keepdims=True)
    dqt[...] = jnp.zeros_like(dqt)
    rs = Scatter(rs_refs, 256)

    def terms(items):
        ps = [nt(k, qq) - ls for k, v, qq, dd, ls, de, mask in items]
        ps = [jnp.exp(p) for p in ps]
        ps = [p if i[6] is None else jnp.where(i[6], p, 0.0) for p, i in zip(ps, items)]
        ds = [(p * (nt(i[1], i[3]) - i[5])).astype(BF) for p, i in zip(ps, items)]
        dv = [nn(p.astype(BF), i[3]) for p, i in zip(ps, items)]
        dk = [nn(d, i[2]) for d, i in zip(ds, items)]
        dq = [tn(i[0], d) for d, i in zip(ds, items)]
        return list(zip(dk, dv, dq))

    def block(k, cr, dst):
        s = pick_of(order, k, cr)
        items = []
        for h in range(2):
            cols = pl.ds(h * HD, HD)
            k0, k1 = kvall[k, cr, 0, 0, :, cols], kvall[k, cr, 0, 1, :, cols]
            v0, v1 = kvall[k, cr, 1, 0, :, cols], kvall[k, cr, 1, 1, :, cols]
            items.append((k0, v0, q[1, :, cols], do[1, h], lse[1, h], delta[1, h], None))
            items.append(
                (jnp.where(s == 0, k0, k1), jnp.where(s == 0, v0, v1), q[s, :, cols], do[s, h],
                 jnp.where(s == 0, lse[0, h], lse[1, h]), jnp.where(s == 0, delta[0, h], delta[1, h]), None)
            )
        got = terms(items)
        for h in range(2):
            cols = pl.ds(h * HD, HD)
            always, picked = got[2 * h], got[2 * h + 1]
            dqt[2, h] += always[2]
            for n in range(2):
                dqt[n, h] += jnp.where(s == n, picked[2], 0.0)
            for a in range(2):
                low = always[a] + jnp.where(s == 0, picked[a], 0.0)
                high = jnp.where(s == 1, picked[a], 0.0)
                dst[pl.ds(a * 512, 256), cols] = low.astype(BF)
                dst[pl.ds(a * 512 + 256, 256), cols] = high.astype(BF)

    def both_cores(k):
        block(k, 1 - core, rs.to_sib.at[k])
        rs.to_sibling(k)
        block(k, core, rs.sums.at[k])

    def ring_place(dy):
        loads[(2, 1, 3).index(dy)].wait()

        def one(t, carry):
            both_cores(chip_at(dy, t))
            return carry

        lax.fori_loop(0, 2, one, 0)
        rs.merge_place(dy)

    ring_place(2)
    rs.far()
    down.hop(0, 1)
    ring_place(1)
    rs.early(0)
    ring_place(3)
    rs.early(1)
    mps.middle()
    rs.near(0)
    rs.near(1)
    swap(0, wown_in.at[1], zbuf).wait_recv()
    loads[4].wait()
    add_rows(fin_g.at[0], [wown, zbuf], 352)
    swap(1, fin_g.at[0], fin_g.at[1]).start()
    down.hop(3, 0)
    down.hop(1, 0)
    output[m] = (mixed[...] + mps.finish()).astype(BF)
    mpg = MpGather(output, oag_sems, CO)
    mpg.start()
    down.hop(3, 1)
    down.hop(1, 1)
    loads[3].wait()
    both_cores(chip_at(0, 1))
    block(chip, 1 - core, rs.to_sib.at[chip])
    rs.to_sibling(chip)
    tri = lax.broadcasted_iota(jnp.int32, (256, 256), 0) <= lax.broadcasted_iota(
        jnp.int32, (256, 256), 1
    )
    for h in range(2):
        cols = pl.ds(h * HD, HD)
        kk = [kvall[chip, core, 0, n, :, cols] for n in range(2)]
        vv = [kvall[chip, core, 1, n, :, cols] for n in range(2)]
        items = [(kk[0], vv[0], q[1, :, cols], do[1, h], lse[1, h], delta[1, h], None)]
        for n in range(2):
            items.append((kk[n], vv[n], q[n, :, cols], do[n, h], lse[n, h], delta[n, h], tri))
        got = terms(items)
        dqt[2, h] += got[0][2]
        for n in range(2):
            dqt[n, h] += got[1 + n][2]
        for a in range(2):
            rs.sums[chip, pl.ds(a * 512, 256), cols] = (got[0][a] + got[1][a]).astype(BF)
            rs.sums[chip, pl.ds(a * 512 + 256, 256), cols] = got[2][a].astype(BF)
    w3 = [kvall.at[:, 0, 0, 0], kvall.at[:, 0, 1, 0], kvall.at[:, 1, 0, 0]]
    for w, dst in zip((wq, wk, wv), w3):
        loads.append(pltpu.make_async_copy(w, dst, s_in.at[len(loads)]))
        loads[-1].start()
    rs.merge(chip_at(0, 1))
    rs.merge(chip)
    mpg.relay()

    def back(x, rr):
        return (x * cosf[rr, :] - rolled(x) * sinf[rr, :]).astype(BF)

    for h in range(2):
        for n in range(2):
            rr = pl.ds(n * 256, 256)
            g = dqt[n, h] if n == 0 else dqt[1, h] + dqt[2, h]
            glin[0, rr, pl.ds(h * HD, HD)] = back(jnp.transpose(g) * (HD**-0.5), rr)

    loads[6].wait()
    loads[7].wait()
    amat[pl.ds(0, 64), :] = turned(g_logits[...])
    amat[pl.ds(64, 256), :] = turned(att[...])
    amat[pl.ds(320, 256), :] = turned(glin[0])
    tail = Scatter(tail_refs, RT)
    tail.pieces(
        (
            (0, 64, amat.at[pl.ds(0, 64)], moe),
            (64, 256, amat.at[pl.ds(64, 256)], g_attn),
            (320, 256, amat.at[pl.ds(320, 256)], normed),
        )
    )
    tail.merge_place(2)
    tail.far()
    tail.merge_place(1)
    tail.early(0)
    tail.merge_place(3)
    tail.early(1)
    rs.own(dkz)
    swap(2, dkz.at[1], dkv).start()
    swap(1, fin_g.at[0], fin_g.at[1]).wait_recv()
    big = GatherPair(w1g, g_sems)
    big.start(fin_g.at[0], fin_g.at[1])
    store(fin_g.at[0], w1g.at[chip, core])
    store(fin_g.at[1], w1g.at[chip_at(0, 1), core])
    tail.near(0)
    tail.near(1)
    tail.merge_place(0)
    down.hop(2, 0)
    down.hop(2, 1)
    for cp in loads[8:]:
        cp.wait()
    mps.drain()
    gni = moe_part
    swap(2, dkz.at[1], dkv).wait_recv()
    for n in range(2):
        rr = pl.ds(n * 256, 256)
        for h in range(2):
            cols = pl.ds(h * HD, HD)
            kr = pl.ds(n * 256, 256)
            vr = pl.ds(512 + n * 256, 256)
            g = dkz[0, kr, cols].astype(F32) + dkv[kr, cols].astype(F32)
            glin[1, rr, cols] = back(g, rr)
            glin[2, rr, cols] = (dkz[0, vr, cols].astype(F32) + dkv[vr, cols].astype(F32)).astype(BF)

    def back_cols(i, carry):
        cols = pl.ds(pl.multiple_of(i * 256, 256), 256)
        g = nt(glin[0], w3[0][i]) + nt(glin[1], w3[1][i]) + nt(glin[2], w3[2][i])
        gni[:, :, cols] = g.reshape(8, 64, 256).astype(BF)
        return carry

    mps2 = MpSum(gni, sum_refs, CT)
    lax.fori_loop(0, CT // 256, back_cols, 0)
    mps2.start_a()
    lax.fori_loop(CT // 256, 8, back_cols, 0)
    mps2.start_b()
    for i in range(2):
        amat[pl.ds(256 * i, 256), :] = turned(glin[1 + i])
    last = Scatter(last_refs, R2)
    last.pieces(((0, R2, amat.at[pl.ds(0, R2)], normed),))
    last.merge_place(2)
    last.far()
    last.merge_place(1)
    last.early(0)
    last.merge_place(3)
    last.early(1)
    big.hop(3, 0)
    big.hop(1, 1)
    last.near(0)
    last.near(1)
    mps2.middle()
    last.merge_place(0)
    tail.own(wtail)
    swap(3, wtail.at[1], ztail).start()

    total = mps2.finish()
    src = tok[...].astype(F32)
    n = lax.rsqrt(jnp.mean(src * src, axis=-1, keepdims=True) + EPSILON)
    gg = total * gain[...]
    gs = n * gg - src * (n * n * n) * jnp.mean(gg * src, axis=-1, keepdims=True)
    g_tokens[m] = (g_mixed[...] + gs).astype(BF)
    gmine[pl.ds(0, 1), :] = gain_moe_part[...]
    gmine[pl.ds(1, 1), :] = jnp.sum(total * src * n, axis=0, keepdims=True)
    mp_send_same(gmine, gland, *mp3)
    mpg2 = MpGather(g_tokens, ag_sems, CT)
    mpg2.start()
    last.own(wlast)
    swap(4, wlast.at[1], zlast).start()
    swap(3, wtail.at[1], ztail).wait_recv()
    add_rows(fin_t, [wtail.at[0], ztail], RT)
    third = Gather(w1t, t_sems)
    third.start(fin_t)
    store(fin_t, w1t.at[chip, core])
    mpg2.relay()
    swap(4, wlast.at[1], zlast).wait_recv()
    add_rows(fin, [wlast.at[0], zlast], R2)
    final = Gather(w2out, l_sems)
    final.start(fin)
    store(fin, w2out.at[chip, core])
    big.hop(1, 0)
    big.hop(3, 1)

    def gain_step(i, dev):
        return remote(gsteps.at[2 * i], gsteps.at[2 * i + 1], s_gx.at[i], r_gx.at[i], dev)

    gsum = gmine[...]
    for d in range(1, 8):
        gsum = gsum + gland[mp_wait_recv(gland, *mp3, d)]
    gsteps[0] = gsum
    gain_step(0, sibling()).start()
    third.hop(0, 1)
    final.hop(0, 1)
    gain_step(0, sibling()).wait_recv()
    gsteps[2] = gsteps[0] + gsteps[1]
    gain_step(1, peer(0, 1)).start()
    third.hop(3, 0)
    third.hop(1, 1)
    gain_step(1, peer(0, 1)).wait_recv()
    gfar[y] = gsteps[2] + gsteps[3]
    for d in range(1, 4):
        remote(gfar.at[y], gfar.at[y], s_gy.at[d - 1], r_gy.at[y], peer(d, 0)).start()
    final.hop(3, 0)
    final.hop(1, 1)
    big.hop(2, 0)
    big.hop(2, 1)
    for g in (third, final):
        g.hop(1, 0)
        g.hop(3, 1)
    for g in (third, final):
        g.hop(2, 0)
        g.hop(2, 1)
    for d in range(1, 4):
        yy = lax.rem(y + d, 4)
        remote(gfar.at[yy], gfar.at[yy], s_gy.at[0], r_gy.at[yy], peer(d, 0)).wait_recv()
    gains[...] = gfar[0] + gfar[1] + gfar[2] + gfar[3]

    for i, ref in enumerate((zbuf, fin_g.at[0], dkv, ztail, zlast)):
        swap(i, ref, ref).wait_send()
    for i, dev in enumerate((sibling(), peer(0, 1))):
        remote(gsteps.at[0], gsteps.at[0], s_gx.at[i], s_gx.at[i], dev).wait_send()
    for d in range(1, 4):
        remote(gfar.at[0], gfar.at[0], s_gy.at[d - 1], s_gy.at[d - 1], peer(d, 0)).wait_send()
    mp_wait_send(gmine, mp3[0])
    for part in (rs, tail, last, mps2):
        part.drain()
    mpg.finish()
    mpg2.finish()
    for cp in stores:
        cp.wait()
    for g in (down, big, third, final):
        g.wait(chip, 1 - core)
        for dy, t in HOPS:
            g.other_core(dy, t)
        g.drain()


def attention_backward(*args):
    vm = pltpu.VMEM
    return pl.pallas_call(
        k3_kernel,
        name="attend_backward",
        out_shape=(
            sds((8, 64, D), BF), sds((8, 64, D), BF), sds((2, D), F32),
            sds((8, 2, RD, HD), BF), sds((8, 2, RG, HD), BF), sds((8, 2, RT, HD), BF), sds((8, 2, R2, HD), BF),
        ),
        in_specs=[SMEM_SPEC] + [VMEM_SPEC] * 13 + [ANY_SPEC] * 10,
        out_specs=(VMEM_SPEC,) * 3 + (ANY_SPEC,) * 4,
        scratch_shapes=[
            vm((3, 512, 256), BF), vm((2, RG, HD), BF), vm((RT, HD), BF), vm((R2, HD), BF),
            vm((512, D), BF), vm((512, D), BF), vm((RT, 512), BF), vm((2, RT, HD), BF), vm((RT, HD), BF),
            vm((8, 2, 2, 2, 256, 256), BF), PARTS, vm((RG, HD), BF),
            vm((2, 2, 256, HD), BF), vm((2, 2, 1, 256), F32), vm((3, 2, HD, 256), F32),
            vm((RG, HD), BF), vm((2, 1024, 256), BF), vm((1024, 256), BF),
            vm((64, D), BF), vm((R2, HD), BF), vm((2, R2, HD), BF), vm((2, D), F32), vm((8, 2, D), F32), vm((4, 2, D), F32), vm((4, 2, D), F32),
            DMA((12,)), DMA((5,)), DMA((5,)), DMA((5,)), DMA((2,)), DMA((2,)), DMA((3,)), DMA((4,)),
            Gather.sems(), GatherPair.sems(), Gather.sems(), Gather.sems(),
            Scatter.scratch(1024, 256), Scatter.scratch(RT, HD), Scatter.scratch(R2, HD),
            MpSum.scratch(CO), MpGather.sems(), MpSum.scratch(CT), MpGather.sems(), MP_SEMS,
        ],
        compiler_params=params(3, 63 * 2**20),
    )(*args)


def widen_kernel(
    wa, wb, wt, w2, out_in, tok_in, gains,
    gq, gk, gv, go, gr, sg, su, sd, eg, eu, ed, out, tok, gain_a, gain_m,
):
    def flip(src, off, c):
        return jnp.transpose(src[0, c, pl.ds(off, 256), :].astype(F32))

    for c in range(2):
        gr[:, pl.ds(c * HD, HD)] = wt[0, c, pl.ds(0, 64), :].astype(F32)
        go[:, pl.ds(c * HD, HD)] = wt[0, c, pl.ds(64, 256), :].astype(F32)
        gq[pl.ds(c * HD, HD), :] = flip(wt, 320, c)
        gk[pl.ds(c * HD, HD), :] = flip(w2, 0, c)
        gv[pl.ds(c * HD, HD), :] = flip(w2, 256, c)
        sg[:, pl.ds(c * HD, HD)] = wa[0, c, pl.ds(0, SH), :].astype(F32)
        su[:, pl.ds(c * HD, HD)] = wa[0, c, pl.ds(SH, SH), :].astype(F32)
        sd[:, pl.ds(c * HD, HD)] = wb[0, c, pl.ds(0, SH), :].astype(F32)
        for k in range(3):
            eg[k, :, pl.ds(c * HD, HD)] = wa[0, c, pl.ds(2 * SH + EF * k, EF), :].astype(F32)
            eu[k, :, pl.ds(c * HD, HD)] = wa[0, c, pl.ds(2 * SH + EF * (3 + k), EF), :].astype(F32)
            ed[k, :, pl.ds(c * HD, HD)] = wb[0, c, pl.ds(SH + EF * k, EF), :].astype(F32)
    out[...] = out_in[...]
    tok[...] = tok_in[...]
    gain_m[...] = gains[pl.ds(0, 1), :]
    gain_a[...] = gains[pl.ds(1, 1), :]


def widen(wa, wb, wt, w2, out_in, tok_in, gains):
    def rows(width):
        return sds((D, width), F32), pl.BlockSpec((2 * HD, width), lambda i: (i, 0))

    def cols(height):
        return sds((height, D), F32), pl.BlockSpec((height, 2 * HD), lambda i: (0, i))

    three = sds((3, EF, D), F32), pl.BlockSpec((3, EF, 2 * HD), lambda i: (0, 0, i))
    whole = pl.BlockSpec((64, D), lambda i: (i, 0))
    gain = sds((1, D), F32), pl.BlockSpec((1, 2 * HD), lambda i: (0, i))
    outs = [rows(256), rows(256), rows(256), cols(256), cols(64), cols(SH), cols(SH), cols(SH)]
    outs += [three, three, three, (sds((512, D), BF), whole), (sds((512, D), BF), whole), gain, gain]
    return pl.pallas_call(
        widen_kernel,
        name="widen",
        grid=(8,),
        out_shape=[o[0] for o in outs],
        in_specs=[
            pl.BlockSpec((1, 2, w.shape[2], HD), lambda i: (i, 0, 0, 0)) for w in (wa, wb, wt, w2)
        ]
        + [whole, whole, pl.BlockSpec((2, 2 * HD), lambda i: (0, i))],
        out_specs=[o[1] for o in outs],
        compiler_params=pltpu.CompilerParams(vmem_limit_bytes=VM),
    )(wa, wb, wt, w2, out_in, tok_in, gains)


def on_device(
    tokens, cotangent, gain_attn, w_query, w_key, w_value, w_out, gain_moe, w_router,
    shared_gate, shared_up, shared_down, expert_gate, expert_up, expert_down, expert_ids, pair_order,
):
    rows = tokens.shape[0]
    inverse = ROPE_BASE ** (-2.0 * jnp.arange(HD // 2, dtype=F32) / HD)
    inverse = jnp.concatenate([inverse, inverse])[None]
    moe, mixed, lse, ot, q, kvall, normed, att, cosf, sinf = attention_forward(
        pair_order, tokens, w_query, w_key, w_value, w_out, inverse, gain_attn[None], gain_moe[None]
    )
    moe = moe.reshape(rows, D)
    g_attn, g_mixed, gain_moe_part, wown, fin_d, moe_part, g_logits = experts(
        expert_ids.T, moe, mixed, gain_moe[None], w_router.T, cotangent, shared_gate.T, shared_up.T, shared_down,
        expert_gate.transpose(0, 2, 1), expert_up.transpose(0, 2, 1), expert_down,
    )
    g_attn = g_attn.reshape(rows, D)
    output, g_tokens, gains, wb, wa, wt, w2 = attention_backward(
        pair_order, q, lse, ot, g_attn, w_out, mixed, cosf, sinf, att, g_logits, g_mixed, gain_attn[None],
        gain_moe_part, kvall, moe_part, wown, fin_d, moe, normed, tokens, w_query.reshape(8, 256, 256), w_key.reshape(8, 256, 256),
        w_value.reshape(8, 256, 256),
    )
    gq, gk, gv, go, gr, sg, su, sd, eg, eu, ed, output, g_tokens, gain_a, gain_m = widen(
        wa, wb, wt, w2, output.reshape(rows, D), g_tokens.reshape(rows, D), gains
    )
    return (
        output, g_tokens, gain_a.reshape(D), gq, gk, gv, go, gain_m.reshape(D), gr.T,
        sg.T, su.T, sd, eg.transpose(0, 2, 1), eu.transpose(0, 2, 1), ed,
    )


def solution(mesh):
    in_specs = (
        P("ctx", None), P("ctx", None), P(), P(None, "mp"), P(None, "mp"), P(None, "mp"),
        P("mp", None), P(), P(), P(None, "mp"), P(None, "mp"), P("mp", None),
        P(None, None, "mp"), P(None, None, "mp"), P(None, "mp", None), P("ctx", None), P(),
    )
    out_specs = (
        P("ctx", None), P("ctx", None), P(), P(None, "mp"), P(None, "mp"), P(None, "mp"),
        P("mp", None), P(), P(), P(None, "mp"), P(None, "mp"), P("mp", None),
        P(None, None, "mp"), P(None, None, "mp"), P(None, "mp", None),
    )
    return jax.shard_map(
        on_device, mesh=mesh, in_specs=in_specs, out_specs=out_specs, check_vma=False
    )
```

```python
import jax
import jax.numpy as jnp
from jax import lax
from jax.experimental import pallas as pl
from jax.experimental.pallas import tpu as pltpu
from jax.sharding import PartitionSpec as P

HD = 128
CAP = 32
EPSILON = 1e-06
ROPE_BASE = 10000.0
PRECISE = lax.Precision.HIGHEST
MESH = pl.DeviceIdType.MESH
BF = jnp.bfloat16
F32 = jnp.float32
D = 2048
SH = 352
EF = 176
RD = SH + 3 * EF
RG = 2 * SH + 6 * EF
RT = 64 + 2 * 256
R2 = 2 * 256
VM = 60 * 2**20
NEG = -1e30


def nt(a, b):
    return lax.dot_general(a, b, (((1,), (1,)), ((), ())), preferred_element_type=F32)


def nn(a, b):
    return lax.dot_general(a, b, (((1,), (0,)), ((), ())), preferred_element_type=F32)


def tn(a, b):
    return lax.dot_general(a, b, (((0,), (0,)), ((), ())), preferred_element_type=F32)


def turned(a):
    return jnp.transpose(a.astype(F32)).astype(BF)


def place():
    c = lax.axis_index("ctx")
    return lax.div(c, 4), lax.rem(lax.div(c, 2), 2), lax.rem(c, 2), lax.axis_index("mp")


def chip_at(dy, t):
    y, z, core, m = place()
    return lax.rem(y + dy, 4) * 2 + lax.rem(z + t, 2)


def peer(dy, t):
    y, z, core, m = place()
    return {"ctx": chip_at(dy, t) * 2 + core}


def sibling():
    y, z, core, m = place()
    return {"ctx": chip_at(0, 0) * 2 + 1 - core}


def mp_at(d):
    m = lax.axis_index("mp")
    return lax.rem(lax.div(m, 2) + d // 2, 4) * 2 + lax.rem(lax.rem(m, 2) + d % 2, 2)


def remote(src, dst, ssem, rsem, dev):
    return pltpu.make_async_remote_copy(
        src_ref=src, dst_ref=dst, send_sem=ssem, recv_sem=rsem, device_id=dev, device_id_type=MESH
    )


def greet(far=False):
    bar = pltpu.get_barrier_semaphore()
    devs = [sibling(), peer(0, 1), peer(1, 0), peer(3, 0)] + ([peer(2, 0)] if far else [])
    devs += [{"mp": mp_at(d)} for d in range(1, 8)]
    for dev in devs:
        pl.semaphore_signal(bar, inc=1, device_id=dev, device_id_type=MESH)
    return len(devs)


def all_in(count):
    pl.semaphore_wait(pltpu.get_barrier_semaphore(), count)


def mp_send_same(src, landing, ssem, rsem):
    m = lax.axis_index("mp")
    for d in range(1, 8):
        remote(src, landing.at[m], ssem.at[d - 1], rsem.at[m], {"mp": mp_at(d)}).start()


def mp_wait_recv(landing, ssem, rsem, d):
    t = mp_at(d)
    remote(landing.at[t], landing.at[t], ssem.at[0], rsem.at[t], {"mp": t}).wait_recv()
    return t


def mp_wait_send(src, ssem):
    for d in range(1, 8):
        remote(src, src, ssem.at[d - 1], ssem.at[d - 1], {"mp": mp_at(d)}).wait_send()


def mp_place():
    m = lax.axis_index("mp")
    return lax.div(m, 2), lax.rem(m, 2)


def x_peer(dx):
    x, zh = mp_place()
    return {"mp": lax.rem(x + dx, 4) * 2 + zh}


def zh_peer():
    x, zh = mp_place()
    return {"mp": x * 2 + 1 - zh}


class MpSum:
    def __init__(self, parts, refs, ca):
        self.parts, self.ca = parts, ca
        self.xa, self.za, self.zb, self.xs, self.xr, self.s, self.r = refs
        self.x, self.zh = mp_place()
        self.a, self.b = pl.ds(0, ca), pl.ds(ca, D - ca)

    @staticmethod
    def scratch(ca):
        cb, vm = D - ca, pltpu.VMEM
        return (
            vm((3, 2, 64, ca), BF), vm((2, 64, ca), BF), vm((4, 64, cb), BF),
            vm((3, 64, cb), BF), vm((3, 64, cb), BF),
            pltpu.SemaphoreType.DMA((11,)), pltpu.SemaphoreType.DMA((11,)),
        )

    def copy(self, n, src, dst, dev):
        return remote(src, dst, self.s.at[n], self.r.at[n], dev)

    def a_copy(self, dx):
        far = lax.rem(self.x + dx, 4)
        src = self.parts.at[pl.ds(far * 2, 2), :, self.a]
        return self.copy(dx - 1, src, self.xa.at[dx - 1], x_peer(dx))

    def b_copy(self, x):
        src = self.parts.at[x * 2 + 1 - self.zh, :, self.b]
        return self.copy(4 + x, src, self.zb.at[x], zh_peer())

    def x_copy(self, dx):
        return self.copy(7 + dx, self.xs.at[dx - 1], self.xr.at[dx - 1], x_peer(dx))

    def z_copy(self):
        return self.copy(3, self.za.at[0], self.za.at[1], zh_peer())

    def start_a(self):
        for dx in range(1, 4):
            self.a_copy(dx).start()

    def start_b(self):
        for x in range(4):
            self.b_copy(x).start()

    def middle(self):
        for x in range(4):
            self.b_copy(x).wait_recv()
        for dx in range(1, 4):
            far = lax.rem(self.x + dx, 4)
            val = self.parts[far * 2 + self.zh, :, self.b].astype(F32) + self.zb[far].astype(F32)
            self.xs[dx - 1] = val.astype(BF)
            self.x_copy(dx).start()
        for dx in range(1, 4):
            self.a_copy(dx).wait_recv()
        self.za[0] = self.over_x(1 - self.zh).astype(BF)
        self.z_copy().start()

    def over_x(self, zz):
        val = self.parts[self.x * 2 + zz, :, self.a].astype(F32)
        for n in range(3):
            val = val + self.xa[n, zz].astype(F32)
        return val

    def finish(self):
        one = self.over_x(self.zh)
        two = self.parts[self.x * 2 + self.zh, :, self.b].astype(F32) + self.zb[self.x].astype(F32)
        for dx in range(1, 4):
            self.x_copy(dx).wait_recv()
            two = two + self.xr[dx - 1].astype(F32)
        self.z_copy().wait_recv()
        one = one + self.za[1].astype(F32)
        return jnp.concatenate([one, two], axis=1)

    def drain(self):
        for dx in range(1, 4):
            self.a_copy(dx).wait_send()
            self.x_copy(dx).wait_send()
        for x in range(4):
            self.b_copy(x).wait_send()
        self.z_copy().wait_send()


class MpGather:
    def __init__(self, out, sems, ca):
        self.out, (self.s, self.r) = out, sems
        self.x, self.zh = mp_place()
        self.a, self.b = pl.ds(0, ca), pl.ds(ca, D - ca)

    @staticmethod
    def sems():
        return (pltpu.SemaphoreType.DMA((14,)), pltpu.SemaphoreType.DMA((14,)))

    def copy(self, n, x, zh, cols, dev):
        ref = self.out.at[x * 2 + zh, :, cols]
        return remote(ref, ref, self.s.at[n], self.r.at[n], dev)

    def start(self):
        x, zh = self.x, self.zh
        self.copy(0, x, zh, self.a, zh_peer()).start()
        for dx in range(1, 4):
            self.copy(dx, x, zh, self.b, x_peer(dx)).start()
        self.copy(4, x, zh, self.b, zh_peer()).start()
        for dx in range(1, 4):
            self.copy(4 + dx, x, zh, self.a, x_peer(dx)).start()

    def relay(self):
        x, zh = self.x, self.zh
        self.copy(0, x, 1 - zh, self.a, zh_peer()).wait_recv()
        for dx in range(1, 4):
            self.copy(7 + dx, x, 1 - zh, self.a, x_peer(dx)).start()
        for dx in (1, 3, 2):
            back = lax.rem(x + 4 - dx, 4)
            self.copy(dx, back, zh, self.b, x_peer(dx)).wait_recv()
            self.copy(10 + dx, back, zh, self.b, zh_peer()).start()

    def finish(self):
        x, zh = self.x, self.zh
        self.copy(4, x, 1 - zh, self.b, zh_peer()).wait_recv()
        for dx in range(1, 4):
            back = lax.rem(x + 4 - dx, 4)
            self.copy(4 + dx, back, zh, self.a, x_peer(dx)).wait_recv()
            self.copy(7 + dx, back, 1 - zh, self.a, x_peer(dx)).wait_recv()
            self.copy(10 + dx, back, 1 - zh, self.b, zh_peer()).wait_recv()
        for n in range(14):
            cols = self.a if n in (0, 5, 6, 7, 8, 9, 10) else self.b
            self.copy(n, x, zh, cols, zh_peer()).wait_send()


class Gather:
    def __init__(self, buf, sems, part=None):
        self.buf, self.part, (self.s, self.r) = buf, part, sems
        y, z, self.core, m = place()

    def at(self, chip, core):
        ref = self.buf.at[chip, core]
        return ref if self.part is None else ref.at[self.part]

    @staticmethod
    def sems():
        return (pltpu.SemaphoreType.DMA((15,)), pltpu.SemaphoreType.DMA((16,)))

    def send(self, src, chip, n, dev):
        dst = self.at(chip, self.core)
        remote(src, dst, self.s.at[n], self.r.at[chip * 2 + self.core], dev).start()

    def start(self, src):
        chip = chip_at(0, 0)
        for n, dev in enumerate([peer(0, 1), peer(1, 0), peer(3, 0), sibling()]):
            self.send(src, chip, n, dev)

    def wait(self, chip, core):
        ref = self.at(chip, core)
        remote(ref, ref, self.s.at[0], self.r.at[chip * 2 + core], sibling()).wait_recv()

    def hop(self, dy, t):
        chip = chip_at(dy, t)
        self.wait(chip, self.core)
        src = self.at(chip, self.core)
        n, devs = {
            (0, 1): (4, [peer(1, 0), peer(3, 0), sibling()]),
            (3, 0): (7, [peer(1, 0), sibling()]),
            (1, 0): (9, [sibling()]),
            (3, 1): (10, [sibling()]),
            (1, 1): (11, [peer(3, 0), sibling()]),
            (2, 0): (13, [sibling()]),
            (2, 1): (14, [sibling()]),
        }[dy, t]
        for i, dev in enumerate(devs):
            self.send(src, chip, n + i, dev)
        return chip

    def other_core(self, dy, t):
        chip = chip_at(dy, t)
        self.wait(chip, 1 - self.core)

    def drain(self):
        ref = self.at(0, 0)
        for n in range(15):
            remote(ref, ref, self.s.at[n], self.s.at[n], sibling()).wait_send()


class GatherPair(Gather):
    def start(self, own, other):
        here, across = chip_at(0, 0), chip_at(0, 1)
        self.send(own, here, 1, peer(1, 0))
        self.send(other, across, 5, peer(3, 0))
        self.send(other, across, 4, peer(1, 0))
        self.send(own, here, 2, peer(3, 0))
        self.send(own, here, 3, sibling())
        self.send(other, across, 6, sibling())

    def drain(self):
        ref = self.at(0, 0)
        for n in range(1, 15):
            remote(ref, ref, self.s.at[n], self.s.at[n], sibling()).wait_send()


class GatherRing(Gather):
    @staticmethod
    def sems():
        return (pltpu.SemaphoreType.DMA((16,)), pltpu.SemaphoreType.DMA((18,)))

    def half(self, n, way):
        chip = chip_at(2, 0) if way is None else chip_at(way, 0)
        ref = self.at(chip, self.core).at[n]
        return remote(ref, ref, self.s.at[4 + n], self.r.at[16 + n], peer(1 if n == 0 else 3, 0))

    def near(self, n):
        dy = 3 if n == 0 else 1
        chip = chip_at(dy, 0)
        self.wait(chip, self.core)
        self.half(n, dy).start()
        self.send(self.at(chip, self.core), chip, 6 + 2 * n, peer(0, 1))
        self.send(self.at(chip, self.core), chip, 7 + 2 * n, sibling())

    def far(self):
        chip = chip_at(2, 0)
        for n in range(2):
            self.half(n, None).wait_recv()
        self.send(self.at(chip, self.core), chip, 10, peer(0, 1))
        self.send(self.at(chip, self.core), chip, 11, sibling())

    def across(self, dy):
        chip = chip_at(dy, 1)
        self.wait(chip, self.core)
        self.send(self.at(chip, self.core), chip, 12 + dy, sibling())

    def drain(self):
        ref = self.at(0, 0)
        for n in range(16):
            one = ref.at[0] if n in (4, 5) else ref
            remote(one, one, self.s.at[n], self.s.at[n], sibling()).wait_send()


HOPS = ((0, 1), (3, 0), (1, 0), (3, 1), (1, 1), (2, 0), (2, 1))


def add_rows(dst, srcs, tile):
    def body(r, carry):
        rr = pl.ds(pl.multiple_of(r * tile, 16), tile)
        total = srcs[0][rr, :].astype(F32)
        for s in srcs[1:]:
            total = total + s[rr, :].astype(F32)
        dst[rr, :] = total.astype(dst.dtype)
        return carry

    lax.fori_loop(0, dst.shape[0] // tile, body, 0)


class Scatter:
    def __init__(self, refs, tile):
        (
            self.to_sib, self.from_sib, self.sums, self.half, self.pairs,
            self.s_sib, self.r_sib, self.s_half, self.r_half, self.s_pair, self.r_pair,
        ) = refs
        self.tile = tile
        self.y, self.z, self.core, m = place()

    @staticmethod
    def scratch(rows, cols):
        dma = pltpu.SemaphoreType.DMA
        eight = pltpu.VMEM((8, rows, cols), BF)
        return (
            eight, eight, eight, pltpu.VMEM((2, rows, cols), BF), pltpu.VMEM((2, 2, rows, cols), BF),
            dma((8,)), dma((8,)), dma((2,)), dma((2,)), dma((4,)), dma((4,)),
        )

    def add(self, dst, srcs):
        add_rows(dst, srcs, self.tile)

    def piece(self, chip, terms):
        cols = pl.ds(pl.multiple_of(chip * 256, 256), 256)
        for off, rows, lhs, rhs in terms:
            val = nn(lhs[...], rhs[:, cols]).astype(BF)
            one, two = val[:, 0:HD], val[:, HD:]
            self.sums[chip, pl.ds(off, rows), :] = jnp.where(self.core == 0, one, two)
            self.to_sib[chip, pl.ds(off, rows), :] = jnp.where(self.core == 0, two, one)
        self.to_sibling(chip)

    def to_sibling(self, chip):
        remote(
            self.to_sib.at[chip], self.from_sib.at[chip], self.s_sib.at[chip], self.r_sib.at[chip], sibling()
        ).start()

    def merge(self, chip):
        got = self.from_sib.at[chip]
        remote(got, got, self.s_sib.at[0], self.r_sib.at[chip], sibling()).wait_recv()
        self.add(self.sums.at[chip], [self.sums.at[chip], got])

    def pieces(self, terms):
        def one(i, carry):
            j = lax.div(i, 2)
            dy = lax.rem(2 - j + 3 * lax.div(j * (j - 1), 2), 4)
            self.piece(chip_at(dy, lax.rem(i, 2)), terms)
            return carry

        lax.fori_loop(0, 8, one, 0)

    def merge_place(self, dy):
        self.merge(chip_at(dy, 0))
        self.merge(chip_at(dy, 1))

    def far(self):
        for t, dy in ((0, 1), (1, 3)):
            remote(
                self.sums.at[chip_at(2, t)], self.half.at[t], self.s_half.at[t], self.r_half.at[t], peer(dy, 0)
            ).start()

    def pair_copy(self, way, t):
        dy = 1 if way == 0 else 3
        dst = self.pairs.at[way, lax.rem(self.z + t, 2)]
        n = 2 * way + t
        return remote(self.sums.at[chip_at(dy, t)], dst, self.s_pair.at[n], self.r_pair.at[n], peer(dy, 0))

    def early(self, way):
        self.pair_copy(way, 1 - way).start()

    def near(self, way):
        dy = 1 if way == 0 else 3
        got = self.half.at[way]
        remote(got, got, self.s_half.at[0], self.r_half.at[way], sibling()).wait_recv()
        mid = self.sums.at[chip_at(dy, way)]
        self.add(mid, [mid, got])
        self.pair_copy(way, way).start()

    def own(self, dst):
        for way in range(2):
            for t in range(2):
                self.pair_copy(way, t).wait_recv()
        for t in (1, 0):
            zz = lax.rem(self.z + t, 2)
            self.add(
                dst.at[t], [self.sums.at[chip_at(0, t)], self.pairs.at[0, zz], self.pairs.at[1, zz]]
            )

    def drain(self):
        one = self.sums.at[0]
        for k in range(8):
            remote(one, one, self.s_sib.at[k], self.s_sib.at[k], sibling()).wait_send()
        for k in range(2):
            remote(one, one, self.s_half.at[k], self.s_half.at[k], sibling()).wait_send()
        for k in range(4):
            remote(one, one, self.s_pair.at[k], self.s_pair.at[k], sibling()).wait_send()


def sds(shape, dtype):
    return jax.ShapeDtypeStruct(shape, dtype)


VMEM_SPEC = pl.BlockSpec(memory_space=pltpu.VMEM)
SMEM_SPEC = pl.BlockSpec(memory_space=pltpu.SMEM)
ANY_SPEC = pl.BlockSpec(memory_space=pl.ANY)
DMA = pltpu.SemaphoreType.DMA
MP_SEMS = (DMA((7,)), DMA((8,)))
CA = 1024
CO = 1792
CT = 1536
PARTS = pltpu.VMEM((8, 64, D), BF)


def params(cid, vmem=VM):
    return pltpu.CompilerParams(collective_id=cid, has_side_effects=True, vmem_limit_bytes=vmem)


def rolled(x):
    return pltpu.roll(x, 64, axis=1)


def pick_of(order, k, cr):
    return jnp.where(order[k * 2 + cr] < order[lax.axis_index("ctx")], 0, 1)


def k1_kernel(
    order, tokens, wq, wk, wv, wo, inverse, gain_a, gain_m,
    moe, mixed, lse, ot, q, kv_out, normed_out, att, cosf, sinf,
    kvall, normed, tok, w3, wov, st_m, st_l, st_a, parts, s_in, s_out, k_sems, v_sems, sum_refs, ag_sems,
):
    y, z, core, m = place()
    chip = chip_at(0, 0)
    loads = [
        pltpu.make_async_copy(a, b, s_in.at[i])
        for i, (a, b) in enumerate(
            [(tokens, tok), (wk, w3.at[0]), (wv, w3.at[1]), (wq, w3.at[2]), (wo, wov)]
        )
    ]
    for cp in loads:
        cp.start()
    count = greet()
    loads[0].wait()

    def norm_rows(i, carry):
        rr = pl.ds(pl.multiple_of(i * 128, 128), 128)
        x = tok[rr, :].astype(F32)
        n = lax.rsqrt(jnp.mean(x * x, axis=-1, keepdims=True) + EPSILON)
        normed[rr, :] = (x * n * gain_a[...]).astype(BF)
        return carry

    lax.fori_loop(0, 4, norm_rows, 0)
    own = kvall.at[chip, core]
    loads[2].wait()

    def values(n, carry):
        rr = pl.ds(pl.multiple_of(n * 256, 256), 256)
        own[1, n] = nn(normed[rr, :], w3[1]).astype(BF)
        return carry

    lax.fori_loop(0, 2, values, 0)
    all_in(count)
    gv = GatherRing(kvall, v_sems, 1)
    gv.start(own.at[1])

    pair = order[lax.axis_index("ctx")]
    sign = jnp.where(lax.broadcasted_iota(jnp.int32, (1, HD), 1) < HD // 2, -1.0, 1.0)
    for n, first in enumerate((pair, 31 - pair)):
        pos = (lax.broadcasted_iota(jnp.int32, (256, HD), 0) + first * 256).astype(F32)
        phase = pos * inverse[...]
        cosf[pl.ds(n * 256, 256), :] = jnp.cos(phase)
        sinf[pl.ds(n * 256, 256), :] = jnp.sin(phase) * sign
    def turn(lin, rr, h):
        x = lin[:, h * HD : h * HD + HD]
        return x * cosf[rr, :] + rolled(x) * sinf[rr, :]

    loads[1].wait()

    def keys(n, carry):
        rr = pl.ds(pl.multiple_of(n * 256, 256), 256)
        lin = nn(normed[rr, :], w3[0])
        for h in range(2):
            own[0, n, :, pl.ds(h * HD, HD)] = turn(lin, rr, h).astype(BF)
        return carry

    lax.fori_loop(0, 2, keys, 0)
    gk = Gather(kvall, k_sems, 0)
    gk.start(own.at[0])
    loads[3].wait()

    def queries(n, carry):
        rr = pl.ds(pl.multiple_of(n * 256, 256), 256)
        lin = nn(normed[rr, :], w3[2])
        for h in range(2):
            q[n, :, pl.ds(h * HD, HD)] = (turn(lin, rr, h) * (HD**-0.5)).astype(BF)
        return carry

    lax.fori_loop(0, 2, queries, 0)

    st_m[...] = jnp.full_like(st_m, NEG)
    st_l[...] = jnp.zeros_like(st_l)
    st_a[...] = jnp.zeros_like(st_a)

    def online(olds, sts, vs):
        mn = [jnp.maximum(o[0], jnp.max(s, axis=0, keepdims=True)) for o, s in zip(olds, sts)]
        ps = [jnp.exp(s - a) for s, a in zip(sts, mn)]
        al = [jnp.exp(o[0] - a) for o, a in zip(olds, mn)]
        ls = [a * o[1] + jnp.sum(p, axis=0, keepdims=True) for a, o, p in zip(al, olds, ps)]
        ac = [a * o[2] + tn(v, p.astype(BF)) for a, o, v, p in zip(al, olds, vs, ps)]
        return list(zip(mn, ls, ac))

    def keep(n, h, new):
        st_m[n, h], st_l[n, h], st_a[n, h] = new

    def block(k, cr):
        s = pick_of(order, k, cr)
        sts, vs, olds = [], [], []
        for h in range(2):
            cols = pl.ds(h * HD, HD)
            k0, k1 = kvall[k, cr, 0, 0, :, cols], kvall[k, cr, 0, 1, :, cols]
            v0, v1 = kvall[k, cr, 1, 0, :, cols], kvall[k, cr, 1, 1, :, cols]
            sts += [nt(k0, q[1, :, cols]), nt(jnp.where(s == 0, k0, k1), q[s, :, cols])]
            vs += [v0, jnp.where(s == 0, v0, v1)]
            olds.append((st_m[2, h], st_l[2, h], st_a[2, h]))
            olds.append(
                (
                    jnp.where(s == 0, st_m[0, h], st_m[1, h]),
                    jnp.where(s == 0, st_l[0, h], st_l[1, h]),
                    st_a[s, h],
                )
            )
        new = online(olds, sts, vs)
        for h in range(2):
            keep(2, h, new[2 * h])
            b = new[2 * h + 1]
            for n in range(2):
                st_m[n, h] = jnp.where(s == n, b[0], st_m[n, h])
                st_l[n, h] = jnp.where(s == n, b[1], st_l[n, h])
                st_a[n, h] = jnp.where(s == n, b[2], st_a[n, h])

    tri = lax.broadcasted_iota(jnp.int32, (256, 256), 0) <= lax.broadcasted_iota(
        jnp.int32, (256, 256), 1
    )
    for h in range(2):
        cols = pl.ds(h * HD, HD)
        names = [2, 0, 1]
        sts = [nt(own[0, 0, :, cols], q[1, :, cols])]
        sts += [jnp.where(tri, nt(own[0, n, :, cols], q[n, :, cols]), NEG) for n in range(2)]
        vs = [own[1, 0, :, cols], own[1, 0, :, cols], own[1, 1, :, cols]]
        olds = [(st_m[n, h], st_l[n, h], st_a[n, h]) for n in names]
        for n, new in zip(names, online(olds, sts, vs)):
            keep(n, h, new)

    def both(dy, t):
        k = chip_at(dy, t)

        def cores(i, carry):
            cr = lax.rem(core + i, 2)

            @pl.when(i == 1)
            def _():
                gk.wait(k, cr)
                gv.wait(k, cr)

            block(k, cr)
            return carry

        lax.fori_loop(0, 2, cores, 0)

    gv.near(0)
    gv.near(1)
    gk.wait(chip, 1 - core)
    gv.wait(chip, 1 - core)
    block(chip, 1 - core)
    gk.hop(0, 1)
    gv.across(0)
    gk.hop(3, 0)
    gk.hop(1, 0)
    both(0, 1)
    gv.far()
    both(3, 0)
    both(1, 0)
    gk.hop(3, 1)
    gk.hop(1, 1)
    gk.hop(2, 0)
    gv.across(3)
    gv.across(1)
    both(2, 0)
    both(3, 1)
    gk.hop(2, 1)
    both(1, 1)
    gv.across(2)
    both(2, 1)
    stores = [
        pltpu.make_async_copy(kvall, kv_out, s_out.at[0]),
        pltpu.make_async_copy(normed, normed_out, s_out.at[1]),
    ]
    for cp in stores:
        cp.start()

    for h in range(2):
        for n in range(2):
            m0, l0, a0 = st_m[n, h], st_l[n, h], st_a[n, h]
            if n == 1:
                m2, l2, a2 = st_m[2, h], st_l[2, h], st_a[2, h]
                mn = jnp.maximum(m0, m2)
                e0, e2 = jnp.exp(m0 - mn), jnp.exp(m2 - mn)
                m0, l0, a0 = mn, e0 * l0 + e2 * l2, e0 * a0 + e2 * a2
            lse[n, h] = m0 + jnp.log(l0)
            o = a0 / l0
            ot[n, h] = o
            att[pl.ds(n * 256, 256), pl.ds(h * HD, HD)] = jnp.transpose(o).astype(BF)

    loads[4].wait()

    def out_cols(i, carry):
        cols = pl.ds(pl.multiple_of(i * 256, 256), 256)
        parts[:, :, cols] = nn(att[...], wov[:, cols]).reshape(8, 64, 256).astype(BF)
        return carry

    mps = MpSum(parts, sum_refs, CA)
    lax.fori_loop(0, CA // 256, out_cols, 0)
    mps.start_a()
    lax.fori_loop(CA // 256, 8, out_cols, 0)
    mps.start_b()
    mps.middle()
    total = tok[pl.ds(pl.multiple_of(m * 64, 64), 64), :].astype(F32) + mps.finish()
    mixed[...] = total
    n = lax.rsqrt(jnp.mean(total * total, axis=-1, keepdims=True) + EPSILON)
    moe[m] = (total * n * gain_m[...]).astype(BF)
    mpg = MpGather(moe, ag_sems, CA)
    mpg.start()
    mpg.relay()

    gk.drain()
    gv.drain()
    mps.drain()
    mpg.finish()
    for cp in stores:
        cp.wait()


def attention_forward(order, tokens, wq, wk, wv, wo, inverse, gain_a, gain_m):
    return pl.pallas_call(
        k1_kernel,
        name="attend_forward",
        out_shape=(
            sds((8, 64, D), BF),
            sds((64, D), F32),
            sds((2, 2, 1, 256), F32),
            sds((2, 2, HD, 256), F32),
            sds((2, 256, 256), BF),
            sds((8, 2, 2, 2, 256, 256), BF),
            sds((512, D), BF),
            sds((512, 256), BF),
            sds((512, HD), F32),
            sds((512, HD), F32),
        ),
        in_specs=[SMEM_SPEC] + [ANY_SPEC] * 5 + [VMEM_SPEC] * 3,
        out_specs=(VMEM_SPEC,) * 5 + (ANY_SPEC,) * 2 + (VMEM_SPEC,) * 3,
        scratch_shapes=[
            pltpu.VMEM((8, 2, 2, 2, 256, 256), BF),
            pltpu.VMEM((512, D), BF),
            pltpu.VMEM((512, D), BF),
            pltpu.VMEM((3, D, 256), BF),
            pltpu.VMEM((256, D), BF),
            pltpu.VMEM((3, 2, 1, 256), F32),
            pltpu.VMEM((3, 2, 1, 256), F32),
            pltpu.VMEM((3, 2, HD, 256), F32),
            PARTS, DMA((5,)), DMA((2,)), Gather.sems(), GatherRing.sems(), MpSum.scratch(CA), MpGather.sems(),
        ],
        compiler_params=params(1),
    )(order, tokens, wq, wk, wv, wo, inverse, gain_a, gain_m)


def swish_parts(g, u):
    s = 1.0 / (1.0 + jnp.exp(-g))
    return s, g * s


def to_column(row):
    return jnp.transpose(jnp.broadcast_to(row, (HD, HD)))[:, 0:1]


def to_row(col):
    return jnp.transpose(jnp.broadcast_to(col, (HD, HD)))[0:1, :]


def k2_kernel(
    ids, moe, mixed, gain, w_router, cot, sg, su, sd, eg, eu, ed,
    g_attn, g_mixed, gain_part, wown, fin_d, moe_part_out, g_logits,
    moe_part, wsg, wsu, wsd, weg, weu, wed, cotv, tb, tbt, pr, gt, ut, hs, gsg, gsu,
    ein, gsl, geo, gated, eo, gein, ge3, ue3, he3, tmp, amat, blk, gate_part, gmi, gate_land,
    s_in, s_out, s_z, r_z, rd_refs, rs_refs, wd, zd, mp1, sum_refs, ag_sems,
):
    y, z, core, m = place()
    loads = [
        pltpu.make_async_copy(a, b, s_in.at[i])
        for i, (a, b) in enumerate(
            [(sg, wsg), (su, wsu), (eg, weg), (eu, weu), (ed, wed), (sd, wsd), (cot, cotv)]
        )
    ]
    for cp in loads:
        cp.start()
    count = greet()

    slot = lax.broadcasted_iota(jnp.int32, (HD, 512), 0)
    holder = lax.div(slot, CAP)
    chosen = holder == ids[0:1, :]
    for k in range(1, 6):
        chosen = chosen | (holder == ids[k : k + 1, :])
    chosen = jnp.where(chosen & (slot < 3 * CAP), 1.0, 0.0)
    upto = lax.broadcasted_iota(jnp.int32, (512, 512), 0) <= lax.broadcasted_iota(
        jnp.int32, (512, 512), 1
    )
    place_of = nn(chosen.astype(BF), jnp.where(upto, 1.0, 0.0).astype(BF)) - 1.0
    table_t = jnp.where(place_of == lax.rem(slot, CAP).astype(F32), chosen, 0.0)
    tbt[...] = table_t.astype(BF)
    table = jnp.transpose(table_t)
    tb[...] = table.astype(BF)
    expert = lax.div(lax.broadcasted_iota(jnp.int32, (512, HD), 1), CAP)

    logits = nt(moe[...], w_router[...])
    e = jnp.exp(logits - jnp.max(logits, axis=-1, keepdims=True))
    probs = e / jnp.sum(e, axis=-1, keepdims=True)
    pr[...] = probs
    px = jnp.where(expert == 0, probs[:, 0:1], jnp.where(expert == 1, probs[:, 1:2], probs[:, 2:3]))
    gate_col = to_column(jnp.sum(table * px, axis=0, keepdims=True))

    hs[...] = jnp.zeros_like(hs)
    gsg[...] = jnp.zeros_like(gsg)
    gsu[...] = jnp.zeros_like(gsu)
    eo[...] = jnp.zeros_like(eo)
    gein[...] = jnp.zeros_like(gein)
    tmp[...] = jnp.zeros_like(tmp)

    def gather_in(i, carry):
        cols = pl.ds(pl.multiple_of(i * 512, 512), 512)
        ein[:, cols] = nn(tbt[...], moe[:, cols]).astype(BF)
        return carry

    lax.fori_loop(0, 4, gather_in, 0)
    loads[0].wait()
    loads[1].wait()

    def shared_in(i, carry):
        rr = pl.ds(pl.multiple_of(i * 256, 256), 256)
        g, u = nt(moe[rr, :], wsg[...]), nt(moe[rr, :], wsu[...])
        gt[rr, :] = g
        ut[rr, :] = u
        hs[rr, 0:SH] = (swish_parts(g, u)[1] * u).astype(BF)
        return carry

    lax.fori_loop(0, 2, shared_in, 0)
    for cp in loads[2:5]:
        cp.wait()
    for k in range(3):
        rr = pl.ds(k * CAP, CAP)
        g, u = nt(ein[rr, :], weg[k]), nt(ein[rr, :], weu[k])
        ge3[k] = g
        ue3[k] = u
        hid = (swish_parts(g, u)[1] * u).astype(BF)
        he3[k] = hid
        eo[rr, :] = nn(hid, wed[k])
    loads[5].wait()
    loads[6].wait()

    def slots_in(i, carry):
        cols = pl.ds(pl.multiple_of(i * 512, 512), 512)
        g = nn(tbt[...], cotv[:, cols])
        gsl[:, cols] = g.astype(BF)
        geo[:, cols] = (gate_col * g).astype(BF)
        gated[:, cols] = (gate_col * eo[:, cols]).astype(BF)
        return carry

    lax.fori_loop(0, 4, slots_in, 0)
    gate_part[...] = to_row(jnp.sum(eo[...] * gsl[...].astype(F32), axis=1, keepdims=True))
    all_in(count)
    mp_send_same(gate_part, gate_land, *mp1)

    def put_block(i, k, val):
        rr = pl.ds(k * CAP, CAP)
        tmp[k, rr, 0:EF] = val.astype(F32)
        blk[pl.ds(EF * i, EF), :] = jnp.transpose(tmp[k])[0:EF].astype(BF)

    amat[pl.ds(2 * SH, SH), :] = turned(hs[...])[0:SH]
    for k in range(3):
        put_block(6 + k, k, he3[k])
    rd = Scatter(rd_refs, 176)
    terms_d = (
        (0, SH, amat.at[pl.ds(2 * SH, SH)], cotv),
        (SH, 3 * EF, blk.at[pl.ds(6 * EF, 3 * EF)], geo),
    )
    rd.pieces(terms_d)

    def shared_back(i, carry):
        rr = pl.ds(pl.multiple_of(i * 256, 256), 256)
        gh = nt(cotv[rr, :], wsd[...])
        g, u = gt[rr, :], ut[rr, :]
        s, sw = swish_parts(g, u)
        gsg[rr, 0:SH] = (gh * u * s * (1.0 + g * (1.0 - s))).astype(BF)
        gsu[rr, 0:SH] = (gh * sw).astype(BF)
        return carry

    lax.fori_loop(0, 2, shared_back, 0)

    for k in range(3):
        rr = pl.ds(k * CAP, CAP)
        gh = nt(geo[rr, :], wed[k])
        g, u = ge3[k], ue3[k]
        s, sw = swish_parts(g, u)
        geg = (gh * u * s * (1.0 + g * (1.0 - s))).astype(BF)
        geu = (gh * sw).astype(BF)
        gein[rr, :] = (nn(geg, weg[k]) + nn(geu, weu[k])).astype(BF)
        put_block(k, k, geg)
        put_block(3 + k, k, geu)

    rd.merge_place(2)
    rd.far()
    rd.merge_place(1)
    rd.early(0)
    rd.merge_place(3)
    rd.early(1)

    def back_cols(i, carry):
        cols = pl.ds(pl.multiple_of(i * 256, 256), 256)
        g = nn(gsg[:, 0:SH], wsg[:, cols]) + nn(gsu[:, 0:SH], wsu[:, cols]) + nn(tb[...], gein[:, cols])
        gmi[:, :, cols] = g.reshape(8, 64, 256).astype(BF)
        return carry

    mps = MpSum(gmi, sum_refs, CA)
    lax.fori_loop(0, CA // 256, back_cols, 0)
    mps.start_a()
    lax.fori_loop(CA // 256, 8, back_cols, 0)
    mps.start_b()

    amat[pl.ds(0, SH), :] = turned(gsg[...])[0:SH]
    amat[pl.ds(SH, SH), :] = turned(gsu[...])[0:SH]
    rs = Scatter(rs_refs, 352)
    terms = (
        (0, 2 * SH, amat.at[pl.ds(0, 2 * SH)], moe),
        (2 * SH, 6 * EF, blk.at[pl.ds(0, 6 * EF)], ein),
    )
    rd.near(0)
    rd.near(1)
    rs.pieces(terms)
    rd.merge_place(0)
    rs.merge_place(2)
    rs.far()
    rs.merge_place(1)
    rs.early(0)
    rs.merge_place(3)
    rs.early(1)

    def out_cols(i, carry):
        cols = pl.ds(pl.multiple_of(i * 256, 256), 256)
        o = nn(hs[:, 0:SH], wsd[:, cols]) + nn(tb[...], gated[:, cols])
        moe_part[:, :, cols] = o.reshape(8, 64, 256).astype(BF)
        return carry


    gate = gate_part[...]
    for d in range(1, 8):
        gate = gate + gate_land[mp_wait_recv(gate_land, *mp1, d)]
    lane2 = lax.broadcasted_iota(jnp.int32, (HD, 64), 0)
    col2 = lax.broadcasted_iota(jnp.int32, (HD, 64), 1)
    member = jnp.where((lax.div(lane2, CAP) == col2) & (col2 < 3), 1.0, 0.0)
    gate_probs = lax.dot_general(
        tb[...].astype(F32) * gate, member, (((1,), (0,)), ((), ())),
        precision=PRECISE, preferred_element_type=F32,
    )
    prob = pr[...]
    g_logits[...] = (prob * (gate_probs - jnp.sum(gate_probs * prob, axis=-1, keepdims=True))).astype(BF)

    mps.middle()
    rs.near(0)
    rs.near(1)
    rs.merge_place(0)
    rd.own(wd)
    remote(wd.at[1], zd, s_z, r_z, peer(0, 1)).start()

    mine = pl.ds(pl.multiple_of(m * 64, 64), 64)
    total = nn(g_logits[mine, :], w_router[...]) + mps.finish()
    mx = mixed[...]
    n = lax.rsqrt(jnp.mean(mx * mx, axis=-1, keepdims=True) + EPSILON)
    gain_part[...] = jnp.sum(total * mx * n, axis=0, keepdims=True)
    gg = total * gain[...]
    gm = cotv[mine, :].astype(F32) + n * gg
    gm = gm - mx * (n * n * n) * jnp.mean(gg * mx, axis=-1, keepdims=True)
    g_mixed[...] = gm
    g_attn[m] = gm.astype(BF)
    mpg = MpGather(g_attn, ag_sems, CA)
    mpg.start()
    lax.fori_loop(0, 8, out_cols, 0)
    store = pltpu.make_async_copy(moe_part, moe_part_out, s_out)
    store.start()
    mpg.relay()
    remote(zd, zd, s_z, r_z, peer(0, 1)).wait_recv()
    add_rows(fin_d, [wd.at[0], zd], 176)

    rs.own(wown)
    remote(zd, zd, s_z, s_z, peer(0, 1)).wait_send()
    rd.drain()
    rs.drain()
    mps.drain()
    mp_wait_send(gate_part, mp1[0])
    store.wait()
    mpg.finish()


def experts(ids, moe, mixed, gain, w_router, cot, sg, su, sd, eg, eu, ed):
    vm = pltpu.VMEM
    return pl.pallas_call(
        k2_kernel,
        name="experts",
        out_shape=(
            sds((8, 64, D), BF),
            sds((64, D), F32),
            sds((1, D), F32),
            sds((2, RG, HD), BF),
            sds((RD, HD), BF),
            sds((8, 64, D), BF),
            sds((512, 64), BF),
        ),
        in_specs=[VMEM_SPEC] * 5 + [ANY_SPEC] * 7,
        out_specs=(VMEM_SPEC,) * 5 + (ANY_SPEC, VMEM_SPEC),
        scratch_shapes=[
            PARTS, vm((SH, D), BF), vm((SH, D), BF), vm((SH, D), BF),
            vm((3, EF, D), BF), vm((3, EF, D), BF), vm((3, EF, D), BF),
            vm((512, D), BF), vm((512, HD), BF), vm((HD, 512), BF), vm((512, 64), F32),
            vm((512, SH), F32), vm((512, SH), F32),
            vm((512, 384), BF), vm((512, 384), BF), vm((512, 384), BF),
            vm((HD, D), BF), vm((HD, D), BF), vm((HD, D), BF), vm((HD, D), BF),
            vm((HD, D), F32), vm((HD, D), BF),
            vm((3, CAP, EF), F32), vm((3, CAP, EF), F32), vm((3, CAP, EF), BF),
            vm((3, HD, 256), F32), vm((3 * SH, 512), BF), vm((9 * EF, HD), BF),
            vm((1, HD), F32), PARTS, vm((8, 1, HD), F32),
            DMA((7,)), DMA, DMA, DMA, Scatter.scratch(RD, HD), Scatter.scratch(RG, HD),
            vm((2, RD, HD), BF), vm((RD, HD), BF), MP_SEMS, MpSum.scratch(CA), MpGather.sems(),
        ],
        compiler_params=params(2),
    )(ids, moe, mixed, gain, w_router, cot, sg, su, sd, eg, eu, ed)


def k3_kernel(
    order, q, lse, ot, g_attn, wout, mixed, cosf, sinf, att, g_logits, g_mixed, gain, gain_moe_part,
    kv_in, moe_part_in, wown_in, fin_d, moe_in, normed_in, tokens, wq, wk, wv,
    output, g_tokens, gains, w1d, w1g, w1t, w2out,
    glin, fin_g, fin_t, fin, moe, normed, amat, wtail, ztail, kvall, moe_part, wown, do, delta, dqt, zbuf, dkz, dkv,
    tok, zlast, wlast, gmine, gland, gsteps, gfar,
    s_in, s_loc, s_z, r_z, s_gx, r_gx, s_gy, r_gy, d_sems, g_sems, t_sems, l_sems, rs_refs, tail_refs, last_refs,
    osum_refs, oag_sems, sum_refs, ag_sems, mp3,
):
    y, z, core, m = place()
    chip = chip_at(0, 0)
    mine = pl.ds(pl.multiple_of(m * 64, 64), 64)
    loads = []
    for i, dy in enumerate((2, 1, 3, 0)):
        pair = pl.ds(lax.rem(y + dy, 4) * 2, 2)
        loads.append(pltpu.make_async_copy(kv_in.at[pair], kvall.at[pair], s_in.at[i]))
    for a, b in (
        (wown_in.at[0], wown), (moe_part_in, moe_part), (moe_in, moe), (normed_in, normed),
        (tokens.at[mine, :], tok),
    ):
        loads.append(pltpu.make_async_copy(a, b, s_in.at[len(loads)]))
    for cp in loads[5:6] + loads[:5] + loads[6:]:
        cp.start()
    all_in(greet(far=True))
    stores = []

    def store(src, dst):
        cp = pltpu.make_async_copy(src, dst, s_loc.at[len(stores)])
        cp.start()
        stores.append(cp)

    def swap(i, src, dst):
        return remote(src, dst, s_z.at[i], r_z.at[i], peer(0, 1))

    down = Gather(w1d, d_sems)
    down.start(fin_d)
    store(fin_d, w1d.at[chip, core])
    swap(0, wown_in.at[1], zbuf).start()
    loads[5].wait()
    mps = MpSum(moe_part, osum_refs, CO)
    mps.start_a()
    mps.start_b()
    g_att = nt(g_attn[...], wout[...])
    for n in range(2):
        for h in range(2):
            piece = g_att[n * 256 : n * 256 + 256, h * HD : h * HD + HD].astype(BF)
            do[n, h] = piece
            delta[n, h] = jnp.sum(jnp.transpose(piece.astype(F32)) * ot[n, h], axis=0, keepdims=True)
    dqt[...] = jnp.zeros_like(dqt)
    rs = Scatter(rs_refs, 256)

    def terms(items):
        ps = [nt(k, qq) - ls for k, v, qq, dd, ls, de, mask in items]
        ps = [jnp.exp(p) for p in ps]
        ps = [p if i[6] is None else jnp.where(i[6], p, 0.0) for p, i in zip(ps, items)]
        ds = [(p * (nt(i[1], i[3]) - i[5])).astype(BF) for p, i in zip(ps, items)]
        dv = [nn(p.astype(BF), i[3]) for p, i in zip(ps, items)]
        dk = [nn(d, i[2]) for d, i in zip(ds, items)]
        dq = [tn(i[0], d) for d, i in zip(ds, items)]
        return list(zip(dk, dv, dq))

    def block(k, cr, dst):
        s = pick_of(order, k, cr)
        items = []
        for h in range(2):
            cols = pl.ds(h * HD, HD)
            k0, k1 = kvall[k, cr, 0, 0, :, cols], kvall[k, cr, 0, 1, :, cols]
            v0, v1 = kvall[k, cr, 1, 0, :, cols], kvall[k, cr, 1, 1, :, cols]
            items.append((k0, v0, q[1, :, cols], do[1, h], lse[1, h], delta[1, h], None))
            items.append(
                (jnp.where(s == 0, k0, k1), jnp.where(s == 0, v0, v1), q[s, :, cols], do[s, h],
                 jnp.where(s == 0, lse[0, h], lse[1, h]), jnp.where(s == 0, delta[0, h], delta[1, h]), None)
            )
        got = terms(items)
        for h in range(2):
            cols = pl.ds(h * HD, HD)
            always, picked = got[2 * h], got[2 * h + 1]
            dqt[2, h] += always[2]
            for n in range(2):
                dqt[n, h] += jnp.where(s == n, picked[2], 0.0)
            for a in range(2):
                low = always[a] + jnp.where(s == 0, picked[a], 0.0)
                high = jnp.where(s == 1, picked[a], 0.0)
                dst[pl.ds(a * 512, 256), cols] = low.astype(BF)
                dst[pl.ds(a * 512 + 256, 256), cols] = high.astype(BF)

    def both_cores(k):
        block(k, 1 - core, rs.to_sib.at[k])
        rs.to_sibling(k)
        block(k, core, rs.sums.at[k])

    def ring_place(dy):
        loads[(2, 1, 3).index(dy)].wait()

        def one(t, carry):
            both_cores(chip_at(dy, t))
            return carry

        lax.fori_loop(0, 2, one, 0)
        rs.merge_place(dy)

    ring_place(2)
    rs.far()
    down.hop(0, 1)
    ring_place(1)
    rs.early(0)
    ring_place(3)
    rs.early(1)
    mps.middle()
    rs.near(0)
    rs.near(1)
    swap(0, wown_in.at[1], zbuf).wait_recv()
    loads[4].wait()
    add_rows(fin_g.at[0], [wown, zbuf], 352)
    swap(1, fin_g.at[0], fin_g.at[1]).start()
    down.hop(3, 0)
    down.hop(1, 0)
    output[m] = (mixed[...] + mps.finish()).astype(BF)
    mpg = MpGather(output, oag_sems, CO)
    mpg.start()
    down.hop(3, 1)
    down.hop(1, 1)
    loads[3].wait()
    both_cores(chip_at(0, 1))
    block(chip, 1 - core, rs.to_sib.at[chip])
    rs.to_sibling(chip)
    tri = lax.broadcasted_iota(jnp.int32, (256, 256), 0) <= lax.broadcasted_iota(
        jnp.int32, (256, 256), 1
    )
    for h in range(2):
        cols = pl.ds(h * HD, HD)
        kk = [kvall[chip, core, 0, n, :, cols] for n in range(2)]
        vv = [kvall[chip, core, 1, n, :, cols] for n in range(2)]
        items = [(kk[0], vv[0], q[1, :, cols], do[1, h], lse[1, h], delta[1, h], None)]
        for n in range(2):
            items.append((kk[n], vv[n], q[n, :, cols], do[n, h], lse[n, h], delta[n, h], tri))
        got = terms(items)
        dqt[2, h] += got[0][2]
        for n in range(2):
            dqt[n, h] += got[1 + n][2]
        for a in range(2):
            rs.sums[chip, pl.ds(a * 512, 256), cols] = (got[0][a] + got[1][a]).astype(BF)
            rs.sums[chip, pl.ds(a * 512 + 256, 256), cols] = got[2][a].astype(BF)
    w3 = [kvall.at[:, 0, 0, 0], kvall.at[:, 0, 1, 0], kvall.at[:, 1, 0, 0]]
    for w, dst in zip((wq, wk, wv), w3):
        loads.append(pltpu.make_async_copy(w, dst, s_in.at[len(loads)]))
        loads[-1].start()
    rs.merge(chip_at(0, 1))
    rs.merge(chip)
    mpg.relay()

    def back(x, rr):
        return (x * cosf[rr, :] - rolled(x) * sinf[rr, :]).astype(BF)

    for h in range(2):
        for n in range(2):
            rr = pl.ds(n * 256, 256)
            g = dqt[n, h] if n == 0 else dqt[1, h] + dqt[2, h]
            glin[0, rr, pl.ds(h * HD, HD)] = back(jnp.transpose(g) * (HD**-0.5), rr)

    loads[6].wait()
    loads[7].wait()
    amat[pl.ds(0, 64), :] = turned(g_logits[...])
    amat[pl.ds(64, 256), :] = turned(att[...])
    amat[pl.ds(320, 256), :] = turned(glin[0])
    tail = Scatter(tail_refs, RT)
    tail.pieces(
        (
            (0, 64, amat.at[pl.ds(0, 64)], moe),
            (64, 256, amat.at[pl.ds(64, 256)], g_attn),
            (320, 256, amat.at[pl.ds(320, 256)], normed),
        )
    )
    tail.merge_place(2)
    tail.far()
    tail.merge_place(1)
    tail.early(0)
    tail.merge_place(3)
    tail.early(1)
    rs.own(dkz)
    swap(2, dkz.at[1], dkv).start()
    swap(1, fin_g.at[0], fin_g.at[1]).wait_recv()
    big = GatherPair(w1g, g_sems)
    big.start(fin_g.at[0], fin_g.at[1])
    store(fin_g.at[0], w1g.at[chip, core])
    store(fin_g.at[1], w1g.at[chip_at(0, 1), core])
    tail.near(0)
    tail.near(1)
    tail.merge_place(0)
    down.hop(2, 0)
    down.hop(2, 1)
    for cp in loads[8:]:
        cp.wait()
    mps.drain()
    gni = moe_part
    swap(2, dkz.at[1], dkv).wait_recv()
    for n in range(2):
        rr = pl.ds(n * 256, 256)
        for h in range(2):
            cols = pl.ds(h * HD, HD)
            kr = pl.ds(n * 256, 256)
            vr = pl.ds(512 + n * 256, 256)
            g = dkz[0, kr, cols].astype(F32) + dkv[kr, cols].astype(F32)
            glin[1, rr, cols] = back(g, rr)
            glin[2, rr, cols] = (dkz[0, vr, cols].astype(F32) + dkv[vr, cols].astype(F32)).astype(BF)

    def back_cols(i, carry):
        cols = pl.ds(pl.multiple_of(i * 256, 256), 256)
        g = nt(glin[0], w3[0][i]) + nt(glin[1], w3[1][i]) + nt(glin[2], w3[2][i])
        gni[:, :, cols] = g.reshape(8, 64, 256).astype(BF)
        return carry

    mps2 = MpSum(gni, sum_refs, CT)
    lax.fori_loop(0, CT // 256, back_cols, 0)
    mps2.start_a()
    lax.fori_loop(CT // 256, 8, back_cols, 0)
    mps2.start_b()
    for i in range(2):
        amat[pl.ds(256 * i, 256), :] = turned(glin[1 + i])
    last = Scatter(last_refs, R2)
    last.pieces(((0, R2, amat.at[pl.ds(0, R2)], normed),))
    last.merge_place(2)
    last.far()
    last.merge_place(1)
    last.early(0)
    last.merge_place(3)
    last.early(1)
    big.hop(3, 0)
    big.hop(1, 1)
    last.near(0)
    last.near(1)
    mps2.middle()
    last.merge_place(0)
    tail.own(wtail)
    swap(3, wtail.at[1], ztail).start()

    total = mps2.finish()
    src = tok[...].astype(F32)
    n = lax.rsqrt(jnp.mean(src * src, axis=-1, keepdims=True) + EPSILON)
    gg = total * gain[...]
    gs = n * gg - src * (n * n * n) * jnp.mean(gg * src, axis=-1, keepdims=True)
    g_tokens[m] = (g_mixed[...] + gs).astype(BF)
    gmine[pl.ds(0, 1), :] = gain_moe_part[...]
    gmine[pl.ds(1, 1), :] = jnp.sum(total * src * n, axis=0, keepdims=True)
    mp_send_same(gmine, gland, *mp3)
    mpg2 = MpGather(g_tokens, ag_sems, CT)
    mpg2.start()
    last.own(wlast)
    swap(4, wlast.at[1], zlast).start()
    swap(3, wtail.at[1], ztail).wait_recv()
    add_rows(fin_t, [wtail.at[0], ztail], RT)
    third = Gather(w1t, t_sems)
    third.start(fin_t)
    store(fin_t, w1t.at[chip, core])
    mpg2.relay()
    swap(4, wlast.at[1], zlast).wait_recv()
    add_rows(fin, [wlast.at[0], zlast], R2)
    final = Gather(w2out, l_sems)
    final.start(fin)
    store(fin, w2out.at[chip, core])
    big.hop(1, 0)
    big.hop(3, 1)

    def gain_step(i, dev):
        return remote(gsteps.at[2 * i], gsteps.at[2 * i + 1], s_gx.at[i], r_gx.at[i], dev)

    gsum = gmine[...]
    for d in range(1, 8):
        gsum = gsum + gland[mp_wait_recv(gland, *mp3, d)]
    gsteps[0] = gsum
    gain_step(0, sibling()).start()
    third.hop(0, 1)
    final.hop(0, 1)
    gain_step(0, sibling()).wait_recv()
    gsteps[2] = gsteps[0] + gsteps[1]
    gain_step(1, peer(0, 1)).start()
    third.hop(3, 0)
    third.hop(1, 1)
    gain_step(1, peer(0, 1)).wait_recv()
    gfar[y] = gsteps[2] + gsteps[3]
    for d in range(1, 4):
        remote(gfar.at[y], gfar.at[y], s_gy.at[d - 1], r_gy.at[y], peer(d, 0)).start()
    final.hop(3, 0)
    final.hop(1, 1)
    big.hop(2, 0)
    big.hop(2, 1)
    for g in (third, final):
        g.hop(1, 0)
        g.hop(3, 1)
    for g in (third, final):
        g.hop(2, 0)
        g.hop(2, 1)
    for d in range(1, 4):
        yy = lax.rem(y + d, 4)
        remote(gfar.at[yy], gfar.at[yy], s_gy.at[0], r_gy.at[yy], peer(d, 0)).wait_recv()
    gains[...] = gfar[0] + gfar[1] + gfar[2] + gfar[3]

    for i, ref in enumerate((zbuf, fin_g.at[0], dkv, ztail, zlast)):
        swap(i, ref, ref).wait_send()
    for i, dev in enumerate((sibling(), peer(0, 1))):
        remote(gsteps.at[0], gsteps.at[0], s_gx.at[i], s_gx.at[i], dev).wait_send()
    for d in range(1, 4):
        remote(gfar.at[0], gfar.at[0], s_gy.at[d - 1], s_gy.at[d - 1], peer(d, 0)).wait_send()
    mp_wait_send(gmine, mp3[0])
    for part in (rs, tail, last, mps2):
        part.drain()
    mpg.finish()
    mpg2.finish()
    for cp in stores:
        cp.wait()
    for g in (down, big, third, final):
        g.wait(chip, 1 - core)
        for dy, t in HOPS:
            g.other_core(dy, t)
        g.drain()


def attention_backward(*args):
    vm = pltpu.VMEM
    return pl.pallas_call(
        k3_kernel,
        name="attend_backward",
        out_shape=(
            sds((8, 64, D), BF), sds((8, 64, D), BF), sds((2, D), F32),
            sds((8, 2, RD, HD), BF), sds((8, 2, RG, HD), BF), sds((8, 2, RT, HD), BF), sds((8, 2, R2, HD), BF),
        ),
        in_specs=[SMEM_SPEC] + [VMEM_SPEC] * 13 + [ANY_SPEC] * 10,
        out_specs=(VMEM_SPEC,) * 3 + (ANY_SPEC,) * 4,
        scratch_shapes=[
            vm((3, 512, 256), BF), vm((2, RG, HD), BF), vm((RT, HD), BF), vm((R2, HD), BF),
            vm((512, D), BF), vm((512, D), BF), vm((RT, 512), BF), vm((2, RT, HD), BF), vm((RT, HD), BF),
            vm((8, 2, 2, 2, 256, 256), BF), PARTS, vm((RG, HD), BF),
            vm((2, 2, 256, HD), BF), vm((2, 2, 1, 256), F32), vm((3, 2, HD, 256), F32),
            vm((RG, HD), BF), vm((2, 1024, 256), BF), vm((1024, 256), BF),
            vm((64, D), BF), vm((R2, HD), BF), vm((2, R2, HD), BF), vm((2, D), F32), vm((8, 2, D), F32), vm((4, 2, D), F32), vm((4, 2, D), F32),
            DMA((12,)), DMA((5,)), DMA((5,)), DMA((5,)), DMA((2,)), DMA((2,)), DMA((3,)), DMA((4,)),
            Gather.sems(), GatherPair.sems(), Gather.sems(), Gather.sems(),
            Scatter.scratch(1024, 256), Scatter.scratch(RT, HD), Scatter.scratch(R2, HD),
            MpSum.scratch(CO), MpGather.sems(), MpSum.scratch(CT), MpGather.sems(), MP_SEMS,
        ],
        compiler_params=params(3, 63 * 2**20),
    )(*args)


def widen_kernel(
    wa, wb, wt, w2, out_in, tok_in, gains,
    gq, gk, gv, go, gr, sg, su, sd, eg, eu, ed, out, tok, gain_a, gain_m,
):
    def flip(src, off, c):
        return jnp.transpose(src[0, c, pl.ds(off, 256), :].astype(F32))

    for c in range(2):
        gr[:, pl.ds(c * HD, HD)] = wt[0, c, pl.ds(0, 64), :].astype(F32)
        go[:, pl.ds(c * HD, HD)] = wt[0, c, pl.ds(64, 256), :].astype(F32)
        gq[pl.ds(c * HD, HD), :] = flip(wt, 320, c)
        gk[pl.ds(c * HD, HD), :] = flip(w2, 0, c)
        gv[pl.ds(c * HD, HD), :] = flip(w2, 256, c)
        sg[:, pl.ds(c * HD, HD)] = wa[0, c, pl.ds(0, SH), :].astype(F32)
        su[:, pl.ds(c * HD, HD)] = wa[0, c, pl.ds(SH, SH), :].astype(F32)
        sd[:, pl.ds(c * HD, HD)] = wb[0, c, pl.ds(0, SH), :].astype(F32)
        for k in range(3):
            eg[k, :, pl.ds(c * HD, HD)] = wa[0, c, pl.ds(2 * SH + EF * k, EF), :].astype(F32)
            eu[k, :, pl.ds(c * HD, HD)] = wa[0, c, pl.ds(2 * SH + EF * (3 + k), EF), :].astype(F32)
            ed[k, :, pl.ds(c * HD, HD)] = wb[0, c, pl.ds(SH + EF * k, EF), :].astype(F32)
    out[...] = out_in[...]
    tok[...] = tok_in[...]
    gain_m[...] = gains[pl.ds(0, 1), :]
    gain_a[...] = gains[pl.ds(1, 1), :]


def widen(wa, wb, wt, w2, out_in, tok_in, gains):
    def rows(width):
        return sds((D, width), F32), pl.BlockSpec((2 * HD, width), lambda i: (i, 0))

    def cols(height):
        return sds((height, D), F32), pl.BlockSpec((height, 2 * HD), lambda i: (0, i))

    three = sds((3, EF, D), F32), pl.BlockSpec((3, EF, 2 * HD), lambda i: (0, 0, i))
    whole = pl.BlockSpec((64, D), lambda i: (i, 0))
    gain = sds((1, D), F32), pl.BlockSpec((1, 2 * HD), lambda i: (0, i))
    outs = [rows(256), rows(256), rows(256), cols(256), cols(64), cols(SH), cols(SH), cols(SH)]
    outs += [three, three, three, (sds((512, D), BF), whole), (sds((512, D), BF), whole), gain, gain]
    return pl.pallas_call(
        widen_kernel,
        name="widen",
        grid=(8,),
        out_shape=[o[0] for o in outs],
        in_specs=[
            pl.BlockSpec((1, 2, w.shape[2], HD), lambda i: (i, 0, 0, 0)) for w in (wa, wb, wt, w2)
        ]
        + [whole, whole, pl.BlockSpec((2, 2 * HD), lambda i: (0, i))],
        out_specs=[o[1] for o in outs],
        compiler_params=pltpu.CompilerParams(vmem_limit_bytes=VM),
    )(wa, wb, wt, w2, out_in, tok_in, gains)


def on_device(
    tokens, cotangent, gain_attn, w_query, w_key, w_value, w_out, gain_moe, w_router,
    shared_gate, shared_up, shared_down, expert_gate, expert_up, expert_down, expert_ids, pair_order,
):
    rows = tokens.shape[0]
    inverse = ROPE_BASE ** (-2.0 * jnp.arange(HD // 2, dtype=F32) / HD)
    inverse = jnp.concatenate([inverse, inverse])[None]
    moe, mixed, lse, ot, q, kvall, normed, att, cosf, sinf = attention_forward(
        pair_order, tokens, w_query, w_key, w_value, w_out, inverse, gain_attn[None], gain_moe[None]
    )
    moe = moe.reshape(rows, D)
    g_attn, g_mixed, gain_moe_part, wown, fin_d, moe_part, g_logits = experts(
        expert_ids.T, moe, mixed, gain_moe[None], w_router.T, cotangent, shared_gate.T, shared_up.T, shared_down,
        expert_gate.transpose(0, 2, 1), expert_up.transpose(0, 2, 1), expert_down,
    )
    g_attn = g_attn.reshape(rows, D)
    output, g_tokens, gains, wb, wa, wt, w2 = attention_backward(
        pair_order, q, lse, ot, g_attn, w_out, mixed, cosf, sinf, att, g_logits, g_mixed, gain_attn[None],
        gain_moe_part, kvall, moe_part, wown, fin_d, moe, normed, tokens, w_query.reshape(8, 256, 256), w_key.reshape(8, 256, 256),
        w_value.reshape(8, 256, 256),
    )
    gq, gk, gv, go, gr, sg, su, sd, eg, eu, ed, output, g_tokens, gain_a, gain_m = widen(
        wa, wb, wt, w2, output.reshape(rows, D), g_tokens.reshape(rows, D), gains
    )
    return (
        output, g_tokens, gain_a.reshape(D), gq, gk, gv, go, gain_m.reshape(D), gr.T,
        sg.T, su.T, sd, eg.transpose(0, 2, 1), eu.transpose(0, 2, 1), ed,
    )


def solution(mesh):
    in_specs = (
        P("ctx", None), P("ctx", None), P(), P(None, "mp"), P(None, "mp"), P(None, "mp"),
        P("mp", None), P(), P(), P(None, "mp"), P(None, "mp"), P("mp", None),
        P(None, None, "mp"), P(None, None, "mp"), P(None, "mp", None), P("ctx", None), P(),
    )
    out_specs = (
        P("ctx", None), P("ctx", None), P(), P(None, "mp"), P(None, "mp"), P(None, "mp"),
        P("mp", None), P(), P(), P(None, "mp"), P(None, "mp"), P("mp", None),
        P(None, None, "mp"), P(None, None, "mp"), P(None, "mp", None),
    )
    return jax.shard_map(
        on_device, mesh=mesh, in_specs=in_specs, out_specs=out_specs, check_vma=False
    )
```
